32 devices in a mesh: pipe: 4 (over y, x), dp: 8 (over z, core).
Axes of the slice: x: 2, y: 2, z: 4, core: 2. Of those that a mesh axis runs over, the one named last changes fastest.
Arguments:
- tokens: bfloat16 [12480, 768], P('dp', 'pipe'), may hold values from -6 to 6
- cotangent: bfloat16 [12480, 768], P('dp', 'pipe'), may hold values from -6 to 6
- captions: int32 [120], P('dp'), may hold values from 5 to 60, as said below
- projection: bfloat16 [4, 768, 1152], P('pipe'), may hold values from -0.21875 to 0.21875
- biases: bfloat16 [4, 768], P('pipe'), may hold values from -1.5 to 1.5
- combiner: bfloat16 [4, 384, 768], P('pipe'), may hold values from -2 to 2
- offsets: bfloat16 [4, 384], P('pipe'), may hold values from -1.5 to 1.5
- scaling: bfloat16 [4, 384], P('pipe'), may hold values from 0.5 to 1.5
- centring: bfloat16 [4, 384], P('pipe'), may hold values from -1.5 to 1.5
- expansion: bfloat16 [4, 768, 1536], P('pipe'), may hold values from -0.21875 to 0.21875
- lifting: bfloat16 [4, 1536], P('pipe'), may hold values from -1.5 to 1.5
- reduction: bfloat16 [4, 1536, 768], P('pipe'), may hold values from -0.109375 to 0.109375
- settling: bfloat16 [4, 384], P('pipe'), may hold values from -1.5 to 1.5
- stretch: bfloat16 [4, 384], P('pipe'), may hold values from 0.5 to 1.5
- translate: bfloat16 [4, 384], P('pipe'), may hold values from -1.5 to 1.5
Outputs:
- encoded: bfloat16 [12480, 768], P('dp', 'pipe')
- tokens_grad: float32 [12480, 768], P('dp', 'pipe')
- projection_grad: float32 [4, 768, 1152], P('pipe', 'dp')
- biases_grad: float32 [4, 768], P('pipe', 'dp')
- combiner_grad: float32 [4, 384, 768], P('pipe', 'dp')
- offsets_grad: float32 [4, 384], P('pipe', 'dp')
- scaling_grad: float32 [4, 384], P('pipe', 'dp')
- centring_grad: float32 [4, 384], P('pipe', 'dp')
- expansion_grad: float32 [4, 768, 1536], P('pipe', 'dp')
- lifting_grad: float32 [4, 1536], P('pipe', 'dp')
- reduction_grad: float32 [4, 1536, 768], P('pipe', 'dp')
- settling_grad: float32 [4, 384], P('pipe', 'dp')
- stretch_grad: float32 [4, 384], P('pipe', 'dp')
- translate_grad: float32 [4, 384], P('pipe', 'dp')
The draws below stay inside these ranges and needn't reach their ends.
Inputs may be any that keep to these rules, and one draw needn't show every extreme that they name: `captions`: word slots at or beyond a pair's caption length are padding keys; some pair has 5 and some 60; lengths lean to short ones.
All inputs are finite; a program needn't handle non-finite values.
Results may differ from the reference program's by a relative error of at most 0.025.
Values may be sent and summed in bfloat16 or wider, within the bound.
A program may use at most 320 MiB of HBM per device.

```python
import jax
import jax.numpy as jnp
from jax import lax

D = 768
HEADS = 12
HEAD_DIM = 64
FF = 3072
LAYERS = 2
WORDS = 64
CAP_MIN = 5
CAP_MAX = 60
PAIR_ROWS = 104
PAIRS_DEV = 15
PAIRS = 120
TOKENS = 12480
N_DP = 8


def draw_captions(key, part):
    key = jax.random.fold_in(key, 7)
    first_key, second_key = jax.random.split(key, 2)
    span_words = CAP_MAX - CAP_MIN
    raw_draw = jax.random.randint(first_key, (PAIRS,), 0, span_words + 1)
    lengths = CAP_MIN + raw_draw * raw_draw * raw_draw // (span_words * span_words)
    longest_at = jax.random.randint(second_key, (), 0, PAIRS)
    indices = jnp.arange(PAIRS)
    lengths = jnp.where(indices == longest_at, CAP_MAX, lengths)
    lengths = jnp.where(indices == (longest_at + 1) % PAIRS, CAP_MIN, lengths)
    return lengths.astype(jnp.int32)


def shard_levels(rng, extent, cuts, smallest, top_value):
    factor_of = 1.0
    for position, parts in cuts:
        heights = jax.random.uniform(jax.random.fold_in(jax.random.fold_in(rng, 6), position), (parts,), jnp.float32, smallest / len(cuts), top_value / len(cuts))
        factor_of = factor_of * jnp.repeat(jnp.exp(heights), extent[position] // parts).reshape((-1,) + (1,) * (len(extent) - 1 - position))
    return factor_of


def scatter_about(own_key, extent, scale, limit, cuts=(), kind=jnp.bfloat16):
    array = scale * jax.random.normal(own_key, extent, jnp.float32)
    if cuts:
        array = array * shard_levels(own_key, extent, cuts, -0.22, 0.18)
    return jnp.clip(array, -limit, limit).astype(kind)


def setup_inputs(seed: int = 0) -> dict:
    seeds = jax.random.split(jax.random.key(seed), 16)
    return {
        "tokens": scatter_about(seeds[0], (TOKENS, D), 1.0, 6.0, ((0, 8), (1, 4))),
        "cotangent": scatter_about(seeds[1], (TOKENS, D), 1.0, 6.0, ((0, 8), (1, 4))),
        "captions": draw_captions(jax.random.fold_in(seeds[15], 71), 0),
        "projection": scatter_about(seeds[3], (2 * LAYERS, D, 3 * D // 2), D ** -0.5, 0.21875, ((0, 4),)),
        "biases": scatter_about(seeds[4], (2 * LAYERS, D), 0.3, 1.5, ((0, 4),)),
        "combiner": scatter_about(seeds[5], (2 * LAYERS, D // 2, D), (D // PAIR_ROWS) ** -0.5, 2.0, ((0, 4),)),
        "offsets": scatter_about(seeds[6], (2 * LAYERS, D // 2), 0.3, 1.5, ((0, 4),)),
        "scaling": jnp.clip(1.0 + 0.1 * jax.random.normal(seeds[7], (2 * LAYERS, D // 2), jnp.float32), 0.5, 1.5).astype(jnp.bfloat16),
        "centring": scatter_about(seeds[8], (2 * LAYERS, D // 2), 0.3, 1.5, ((0, 4),)),
        "expansion": scatter_about(seeds[9], (2 * LAYERS, D, FF // 2), D ** -0.5, 0.21875, ((0, 4),)),
        "lifting": scatter_about(seeds[10], (2 * LAYERS, FF // 2), 0.3, 1.5, ((0, 4),)),
        "reduction": scatter_about(seeds[11], (2 * LAYERS, FF // 2, D), FF ** -0.5, 0.109375, ((0, 4),)),
        "settling": scatter_about(seeds[12], (2 * LAYERS, D // 2), 0.3, 1.5, ((0, 4),)),
        "stretch": jnp.clip(1.0 + 0.1 * jax.random.normal(seeds[13], (2 * LAYERS, D // 2), jnp.float32), 0.5, 1.5).astype(jnp.bfloat16),
        "translate": scatter_about(seeds[14], (2 * LAYERS, D // 2), 0.3, 1.5, ((0, 4),)),
    }


@jax.custom_vjp
def low(v):
    return lax.optimization_barrier(v.astype(jnp.bfloat16)).astype(jnp.float32)

@jax.custom_vjp
def low_back(v):
    return v

def low_keep(v):
    return (low(v), None)

def low_pass(kept, grad):
    return (grad,)

def back_keep(v):
    return (v, None)

def back_low(kept, grad):
    return (low(grad),)
low.defvjp(low_keep, low_pass)
low_back.defvjp(back_keep, back_low)
EPSILON = 1e-05
NEGATIVE = -1e+30
HIGHEST = lax.Precision.HIGHEST

def matmul(left_side, right_side):
    return jnp.dot(left_side, right_side, precision=HIGHEST, preferred_element_type=jnp.float32)

def layer_norm(residual, gain_row, shift_row):
    average = lax.optimization_barrier(jnp.mean(residual, axis=-1, keepdims=True))
    centred = residual - average
    variance = lax.optimization_barrier(jnp.mean(centred * centred, axis=-1, keepdims=True))
    return centred * lax.rsqrt(variance + EPSILON) * gain_row + shift_row

def unpack_layer(weights, layer_index):
    lower = 2 * layer_index
    pairs = [member[lower:lower + 2] for member in weights]
    half_width = D // 2
    joint_weight = pairs[0].reshape(2, D, 3, half_width).transpose(1, 2, 0, 3).reshape(D, 3 * D)
    query_value = pairs[1].reshape(2, 2, half_width).transpose(1, 0, 2).reshape(2, D)
    joint_bias = jnp.concatenate([query_value[0], jnp.zeros((D,), jnp.float32), query_value[1]])
    attention = (joint_weight, joint_bias, pairs[2].reshape(D, D), pairs[3].reshape(D), pairs[4].reshape(D), pairs[5].reshape(D))
    expand_weight = pairs[6].transpose(1, 0, 2).reshape(D, FF)
    dense = (expand_weight, pairs[7].reshape(FF), pairs[8].reshape(FF, D), pairs[9].reshape(D), pairs[10].reshape(D), pairs[11].reshape(D))
    return (attention, dense)

def attention_block(inputs, visible_keys, weights):
    joint_weight, joint_bias, mixing_weight, mixing_bias, gain_row, shift_row = weights
    group_pairs = inputs.shape[0] // PAIR_ROWS
    projected = low_back(low(matmul(inputs, joint_weight) + joint_bias))
    heads_view = projected.reshape(group_pairs, PAIR_ROWS, 3, HEADS, HEAD_DIM)
    query_heads = heads_view[:, :, 0]
    key_heads = heads_view[:, :, 1]
    value_heads = heads_view[:, :, 2]
    scores = jnp.einsum('pqhd,pkhd->phqk', query_heads, key_heads, precision=HIGHEST) * HEAD_DIM ** (-0.5)
    scores = low_back(scores)
    scores = jnp.where(visible_keys[:, None, None, :], scores, NEGATIVE)
    highest = lax.optimization_barrier(jnp.max(scores, axis=-1, keepdims=True))
    exponent = jnp.exp(scores - highest)
    probabilities = low(exponent / lax.optimization_barrier(jnp.sum(exponent, axis=-1, keepdims=True)))
    context = jnp.einsum('phqk,pkhd->pqhd', probabilities, value_heads, precision=HIGHEST)
    context = low_back(low(context.reshape(inputs.shape[0], D)))
    residual = inputs + low_back(matmul(context, mixing_weight)) + mixing_bias
    return layer_norm(residual, gain_row, shift_row)

def dense_block(inputs, weights):
    expand_weight, expand_bias, reduce_weight, reduce_bias, gain_row, shift_row = weights
    expanded = low_back(matmul(inputs, expand_weight)) + expand_bias
    hidden = low(jax.nn.gelu(expanded, approximate=False))
    residual = inputs + low_back(matmul(hidden, reduce_weight)) + reduce_bias
    return layer_norm(residual, gain_row, shift_row)

def reference(tokens, cotangent, captions, projection, biases, combiner, offsets, scaling, centring, expansion, lifting, reduction, settling, stretch, translate):
    position_rows = jnp.arange(PAIR_ROWS, dtype=jnp.int32)
    visible = (position_rows[None, :] < captions[:, None]) | (position_rows[None, :] >= WORDS)
    group_rows = PAIRS_DEV * PAIR_ROWS

    def whole(inputs, *weights):
        layers = [unpack_layer(weights, layer_index) for layer_index in range(LAYERS)]

        def group_forward(item):
            current, visible_group = item
            for layer_index in range(LAYERS):
                current = attention_block(current, visible_group, layers[layer_index][0])
                current = low_back(low(current))
                current = dense_block(current, layers[layer_index][1])
                if layer_index + 1 < LAYERS:
                    current = low_back(low(current))
            return current
        outcome = lax.map(jax.checkpoint(group_forward), (inputs.reshape(N_DP, group_rows, D), visible.reshape(N_DP, PAIRS_DEV, PAIR_ROWS)))
        return outcome.reshape(TOKENS, D)
    params = (projection, biases, combiner, offsets, scaling, centring, expansion, lifting, reduction, settling, stretch, translate)
    params = tuple((member.astype(jnp.float32) for member in params))
    result, pullback = jax.vjp(whole, tokens.astype(jnp.float32), *params)
    grads = pullback(cotangent.astype(jnp.float32))
    return (result.astype(jnp.bfloat16), grads[0], grads[1], grads[2], grads[3], grads[4], grads[5], grads[6], grads[7], grads[8], grads[9], grads[10], grads[11], grads[12])
```

```python
import functools

import jax
import jax.numpy as jnp
from jax import lax
from jax.experimental import pallas as pl
from jax.experimental.pallas import tpu as pltpu
from jax.sharding import PartitionSpec as P

D = 768
HEADS = 12
HEAD_DIM = 64
FF = 3072
WORDS = 64
PAIR_ROWS = 104
HALF = D // 2
HIDDEN_HALF = FF // 2
QUARTER = D // 4
PIPE = 4
KEYS = 128
GROUP = 4
GROUP_WIDTH = GROUP * HEAD_DIM
GROUPS = HEADS // GROUP

EPSILON = 1e-05
NEGATIVE = -1e30
SCALE = HEAD_DIM ** (-0.5)

MESH = pl.DeviceIdType.MESH
BF = jnp.bfloat16
F32 = jnp.float32
VMEM_LIMIT = 60 << 20


def dot_nn(left, right):
    return lax.dot_general(left, right, (((1,), (0,)), ((), ())), preferred_element_type=F32)


def dot_nt(left, right):
    return lax.dot_general(left, right, (((1,), (1,)), ((), ())), preferred_element_type=F32)


def dot_tn(left, right):
    return lax.dot_general(left, right, (((0,), (0,)), ((), ())), preferred_element_type=F32)


def place():
    pipe = lax.axis_index("pipe")
    dp = lax.axis_index("dp")
    layer = pipe // 2
    half = pipe % 2
    across_x = pipe + 1 - 2 * half
    across_y = (pipe + 2) % 4
    core = dp % 2
    other_core = dp + 1 - 2 * core
    return pipe, dp, layer, half, across_x, across_y, core, other_core


def greet(devices):
    barrier = pltpu.get_barrier_semaphore()
    for device in devices:
        pl.semaphore_signal(barrier, inc=1, device_id=device, device_id_type=MESH)
    pl.semaphore_wait(barrier, len(devices))


def remote(source, target, send, recv, device):
    return pltpu.make_async_remote_copy(
        src_ref=source,
        dst_ref=target,
        send_sem=send,
        recv_sem=recv,
        device_id=device,
        device_id_type=MESH,
    )


def gather_kernel(
    rows,
    both, projection, combiner, expansion, reduction, vectors,
    pieces, joint, mixing, expand, reduce, whole_vectors,
    send, recv, local_sem, piece_send, piece_recv, vec_sem,
):
    pipe, dp, layer, half, across_x, across_y, core, other_core = place()
    diagonal = (across_x + 2) % 4
    parity = (dp // 2) % 2
    across_z = dp + 2 - 4 * parity
    greet([(across_x, dp), (across_y, dp), (diagonal, dp), (pipe, across_z), (pipe, other_core)])

    def regions(owner_half, quarter):
        found = []
        for part in range(3):
            r = D // 4
            found.append((
                projection.at[pl.ds(quarter * r, r), pl.ds(part * HALF, HALF)],
                joint.at[pl.ds(quarter * r, r), pl.ds(pl.multiple_of(part * D + owner_half * HALF, 128), HALF)],
            ))
        r = HALF // 4
        found.append((
            combiner.at[pl.ds(quarter * r, r)],
            mixing.at[pl.ds(owner_half * HALF + quarter * r, r)],
        ))
        r = D // 4
        found.append((
            expansion.at[pl.ds(quarter * r, r)],
            expand.at[pl.ds(quarter * r, r), pl.ds(pl.multiple_of(owner_half * HIDDEN_HALF, 128), HIDDEN_HALF)],
        ))
        r = HIDDEN_HALF // 4
        found.append((
            reduction.at[pl.ds(quarter * r, r)],
            reduce.at[pl.ds(owner_half * HIDDEN_HALF + quarter * r, r)],
        ))
        return found

    mine = 2 * parity + core
    paired = 2 * (1 - parity) + core
    own = regions(half, mine)
    got_x = regions(1 - half, mine)
    got_z = regions(1 - half, paired)
    n = len(own)
    sent = []

    vec_copy = remote(vectors, whole_vectors.at[half], vec_sem.at[0], vec_sem.at[1], (across_x, dp))
    vec_copy.start()
    x_copies = []
    for i in range(4):
        copy = remote(own[i][0], own[i][1], send.at[0, i], recv.at[0, i], (across_x, dp))
        copy.start()
        x_copies.append(copy)
    piece_copies = []
    for j, target in enumerate((across_x, across_y, diagonal)):
        copy = remote(
            both.at[target // 2, pl.ds((target % 2) * rows, rows)],
            pieces.at[pipe],
            piece_send.at[j], piece_recv.at[j],
            (target, dp),
        )
        copy.start()
        piece_copies.append(copy)
    for i in range(4, n):
        copy = remote(own[i][0], own[i][1], send.at[0, i], recv.at[0, i], (across_x, dp))
        copy.start()
        x_copies.append(copy)

    locals_ = [
        pltpu.make_async_copy(both.at[layer, pl.ds(half * rows, rows)], pieces.at[pipe], local_sem.at[0]),
        pltpu.make_async_copy(vectors, whole_vectors.at[half], local_sem.at[1]),
        pltpu.make_async_copy(combiner, mixing.at[pl.ds(half * HALF, HALF)], local_sem.at[2]),
        pltpu.make_async_copy(
            expansion, expand.at[:, pl.ds(pl.multiple_of(half * HIDDEN_HALF, 128), HIDDEN_HALF)], local_sem.at[3]
        ),
        pltpu.make_async_copy(reduction, reduce.at[pl.ds(half * HIDDEN_HALF, HIDDEN_HALF)], local_sem.at[4]),
    ]
    for part in range(3):
        locals_.append(
            pltpu.make_async_copy(
                projection.at[:, pl.ds(part * HALF, HALF)],
                joint.at[:, pl.ds(pl.multiple_of(part * D + half * HALF, 128), HALF)],
                local_sem.at[5 + part],
            )
        )
    for copy in locals_:
        copy.start()

    z_copies = []
    core_copies = []
    for i in range(n):
        x_copies[i].wait_recv()
        copy = remote(got_x[i][1], got_x[i][1], send.at[1, i], recv.at[1, i], (pipe, across_z))
        copy.start()
        z_copies.append(copy)
        copy = remote(got_x[i][1], got_x[i][1], send.at[2, i], recv.at[2, i], (pipe, other_core))
        copy.start()
        core_copies.append(copy)
    for i in range(n):
        z_copies[i].wait_recv()
        copy = remote(got_z[i][1], got_z[i][1], send.at[3, i], recv.at[3, i], (pipe, other_core))
        copy.start()
        core_copies.append(copy)
    for copy in core_copies:
        copy.wait_recv()
    for copy in x_copies + z_copies + core_copies:
        copy.wait_send()
    for copy in piece_copies + [vec_copy]:
        copy.wait()
    for copy in locals_:
        copy.wait()


def gather(rows, both, projection, combiner, expansion, reduction, vectors):
    hbm = pl.BlockSpec(memory_space=pl.ANY)
    return pl.pallas_call(
        functools.partial(gather_kernel, rows),
        out_shape=(
            jax.ShapeDtypeStruct((PIPE, rows, QUARTER), BF),
            jax.ShapeDtypeStruct((D, 3 * D), BF),
            jax.ShapeDtypeStruct((D, D), BF),
            jax.ShapeDtypeStruct((D, FF), BF),
            jax.ShapeDtypeStruct((FF, D), BF),
            jax.ShapeDtypeStruct((2,) + vectors.shape, BF),
        ),
        in_specs=[hbm] * 6,
        out_specs=(hbm,) * 6,
        scratch_shapes=[
            pltpu.SemaphoreType.DMA((4, 6)),
            pltpu.SemaphoreType.DMA((4, 6)),
            pltpu.SemaphoreType.DMA((8,)),
            pltpu.SemaphoreType.DMA((3,)),
            pltpu.SemaphoreType.DMA((3,)),
            pltpu.SemaphoreType.DMA((2,)),
        ],
        compiler_params=pltpu.CompilerParams(collective_id=0, has_side_effects=True, vmem_limit_bytes=VMEM_LIMIT),
        name="gather_weights",
    )(both, projection, combiner, expansion, reduction, vectors)


def head_of_lane():
    return lax.broadcasted_iota(jnp.int32, (KEYS, GROUP_WIDTH), 1) // HEAD_DIM


def stacked_keys(values, scale=None):
    padded = jnp.concatenate([values, jnp.zeros((KEYS - PAIR_ROWS, GROUP_WIDTH), F32)], 0)
    if scale is not None:
        padded = padded * scale
    owner = head_of_lane()
    return jnp.concatenate([jnp.where(owner == i, padded, 0.0) for i in range(GROUP)], 0).astype(BF)


def own_lanes(stacked):
    left = lax.broadcasted_iota(jnp.int32, (KEYS, KEYS), 1) < HEAD_DIM
    low = jnp.where(left, stacked[0:KEYS, :KEYS], stacked[KEYS : 2 * KEYS, :KEYS])
    high = jnp.where(left, stacked[2 * KEYS : 3 * KEYS, KEYS:], stacked[3 * KEYS :, KEYS:])
    return jnp.concatenate([low, high], 1)[:PAIR_ROWS]


def normalized(residual):
    average = jnp.mean(residual, axis=-1, keepdims=True)
    centred = residual - average
    variance = jnp.mean(centred * centred, axis=-1, keepdims=True)
    inverse = lax.rsqrt(variance + EPSILON)
    return centred * inverse, inverse


def forward_kernel(
    micros, block,
    pieces, masks, joint, mixing, expand, reduce, vectors,
    a0_out, qkv_out, prob_out, context_out, n1_out, r1_out, a1_out, hidden_out, slope_out, n2_out, r2_out, y2_out,
    slots, outgoing, a_s, qkv_s, prob_s, context_s, send, recv,
):
    pipe, dp, layer, half, across_x, across_y, core, other_core = place()
    micro = pl.program_id(0)
    pairs = block // PAIR_ROWS

    @pl.when(micro == 0)
    def _():
        greet([(across_y, dp)])

    def copy_of(index):
        return remote(outgoing.at[index], slots.at[index], send.at[index], recv.at[index], (across_y, dp))

    @pl.when(layer == 0)
    def _():
        a_s[...] = jnp.concatenate([pieces[i] for i in range(PIPE)], 1)

    @pl.when(layer == 1)
    def _():
        copy_of(micro).wait_recv()
        a_s[...] = slots[micro]

    inputs = a_s[...]
    a0_out[...] = inputs
    for part in range(3):
        cols = slice(part * D, (part + 1) * D)
        value = dot_nn(inputs, joint[:, cols]) + vectors[0:1, cols]
        qkv_s[:, cols] = value
        qkv_out[:, cols] = value.astype(BF)
    for pair in range(pairs):
        rows = slice(pair * PAIR_ROWS, (pair + 1) * PAIR_ROWS)
        mask = masks[pl.ds(micro * pairs + pair, 1), :]
        for group in range(GROUPS):
            lanes = slice(group * GROUP_WIDTH, (group + 1) * GROUP_WIDTH)
            query = qkv_s[rows, group * GROUP_WIDTH : (group + 1) * GROUP_WIDTH].astype(BF)
            keys = stacked_keys(qkv_s[rows, D + group * GROUP_WIDTH : D + (group + 1) * GROUP_WIDTH], SCALE)
            values = stacked_keys(qkv_s[rows, 2 * D + group * GROUP_WIDTH : 2 * D + (group + 1) * GROUP_WIDTH])
            scores = dot_nt(query, keys)
            found = []
            for i in range(GROUP):
                score = scores[:, i * KEYS : (i + 1) * KEYS] + mask
                exponent = jnp.exp(score - jnp.max(score, axis=-1, keepdims=True))
                found.append(exponent * (1.0 / jnp.sum(exponent, axis=-1, keepdims=True)))
            probs = jnp.concatenate(found, 1)
            prob_s[rows, group * GROUP * KEYS : (group + 1) * GROUP * KEYS] = probs
            context_s[rows, lanes] = dot_nn(probs.astype(BF), values)
    prob_out[...] = prob_s[...].astype(BF)
    context = context_s[...].astype(BF)
    context_out[...] = context
    residual = inputs.astype(F32) + dot_nn(context, mixing[...]) + vectors[1:2, :D]
    norm, inverse = normalized(residual)
    n1_out[...] = norm.astype(BF)
    r1_out[...] = inverse
    attended = (norm * vectors[2:3, :D] + vectors[3:4, :D]).astype(BF)
    a1_out[...] = attended

    chunk = 512
    residual = attended.astype(F32) + vectors[5:6, :D]
    for start in range(0, FF, chunk):
        cols = slice(start, start + chunk)
        raised = dot_nn(attended, expand[:, cols]) + vectors[4:5, cols]
        below = 0.5 * (1.0 + lax.erf(raised * (0.5**0.5)))
        hidden = (raised * below).astype(BF)
        hidden_out[:, cols] = hidden
        density = jnp.exp(raised * raised * (-0.5)) * 0.3989422804014327
        slope_out[:, cols] = (below + raised * density).astype(BF)
        residual = residual + dot_nn(hidden, reduce[cols, :])
    norm, inverse = normalized(residual)
    n2_out[...] = norm.astype(BF)
    r2_out[...] = inverse
    result = (norm * vectors[6:7, :D] + vectors[7:8, :D]).astype(BF)
    for i in range(PIPE):
        y2_out[i] = result[:, i * QUARTER : (i + 1) * QUARTER]

    @pl.when(layer == 0)
    def _():
        outgoing[micro] = result
        copy_of(micro).start()

    @pl.when((layer == 0) & (micro == micros - 1))
    def _():
        for index in range(micros):
            copy_of(index).wait_send()


def forward(micros, block, pieces, masks, joint, mixing, expand, reduce, vectors):
    rows = micros * block

    def whole(array):
        return pl.BlockSpec(array.shape, lambda m: (0,) * array.ndim, pipeline_mode=pl.Buffered(1))

    def by_rows(width):
        return pl.BlockSpec((block, width), lambda m: (m, 0))

    by_pieces = pl.BlockSpec((PIPE, block, QUARTER), lambda m: (0, m, 0))
    widths = [D, 3 * D, HEADS * KEYS, D, D, 1, D, FF, FF, D, 1]
    types = [BF, BF, BF, BF, BF, F32, BF, BF, BF, BF, F32]
    return pl.pallas_call(
        functools.partial(forward_kernel, micros, block),
        grid=(micros,),
        out_shape=[jax.ShapeDtypeStruct((rows, w), t) for w, t in zip(widths, types)]
        + [jax.ShapeDtypeStruct((PIPE, rows, QUARTER), BF)],
        in_specs=[by_pieces] + [whole(a) for a in (masks, joint, mixing, expand, reduce, vectors)],
        out_specs=[by_rows(w) for w in widths] + [by_pieces],
        scratch_shapes=[
            pltpu.VMEM((micros, block, D), BF),
            pltpu.VMEM((micros, block, D), BF),
            pltpu.VMEM((block, D), BF),
            pltpu.VMEM((block, 3 * D), F32),
            pltpu.VMEM((block, HEADS * KEYS), F32),
            pltpu.VMEM((block, D), F32),
            pltpu.SemaphoreType.DMA((micros,)),
            pltpu.SemaphoreType.DMA((micros,)),
        ],
        compiler_params=pltpu.CompilerParams(collective_id=1, has_side_effects=True, vmem_limit_bytes=VMEM_LIMIT),
        name="layer_forward",
    )(pieces, masks, joint, mixing, expand, reduce, vectors)


def norm_backward(gradient, norm, inverse, gain):
    scaled = gradient * gain
    first = jnp.mean(scaled, axis=-1, keepdims=True)
    second = jnp.mean(scaled * norm, axis=-1, keepdims=True)
    return (scaled - first - norm * second) * inverse


def column_sums(value):
    return jnp.sum(value, axis=0, keepdims=True)


def backward_kernel(
    micros, block,
    pieces, joint, mixing, expand, reduce, vectors,
    n2, r2, slope, n1, r1, qkv, prob,
    dr2_out, du_out, dr1_out, dqkv_out, da_out, sums_out,
    slots, outgoing, g_s, qkv_s, prob_s, dc_s, dqkv_s, send, recv,
):
    pipe, dp, layer, half, across_x, across_y, core, other_core = place()
    micro = pl.program_id(0)
    pairs = block // PAIR_ROWS

    @pl.when(micro == 0)
    def _():
        greet([(across_y, dp)])
        sums_out[...] = jnp.zeros_like(sums_out)

    def copy_of(index):
        return remote(outgoing.at[index], slots.at[index], send.at[index], recv.at[index], (across_y, dp))

    @pl.when(layer == 1)
    def _():
        g_s[...] = jnp.concatenate([pieces[i] for i in range(PIPE)], 1)

    @pl.when(layer == 0)
    def _():
        copy_of(micro).wait_recv()
        g_s[...] = slots[micro]

    def add_sum(row, value):
        width = value.shape[1]
        sums_out[row : row + 1, :width] += column_sums(value)

    gradient = g_s[...].astype(F32)
    norm = n2[...].astype(F32)
    add_sum(6, gradient * norm)
    add_sum(7, gradient)
    grad_residual = norm_backward(gradient, norm, r2[...], vectors[6:7, :D])
    add_sum(5, grad_residual)
    branch = grad_residual.astype(BF)
    dr2_out[...] = branch
    chunk = 512
    total = grad_residual
    for start in range(0, FF, chunk):
        cols = slice(start, start + chunk)
        raised = dot_nt(branch, reduce[cols, :]) * slope[:, cols].astype(F32)
        sums_out[4:5, cols] += column_sums(raised)
        raised = raised.astype(BF)
        du_out[:, cols] = raised
        total = total + dot_nt(raised, expand[:, cols])

    gradient = total.astype(BF).astype(F32)
    norm = n1[...].astype(F32)
    add_sum(2, gradient * norm)
    add_sum(3, gradient)
    grad_residual = norm_backward(gradient, norm, r1[...], vectors[2:3, :D])
    add_sum(1, grad_residual)
    branch = grad_residual.astype(BF)
    dr1_out[...] = branch
    dc_s[...] = dot_nt(branch, mixing[...])
    qkv_s[...] = qkv[...].astype(F32)
    prob_s[...] = prob[...].astype(F32)
    for pair in range(pairs):
        rows = slice(pair * PAIR_ROWS, (pair + 1) * PAIR_ROWS)
        for group in range(GROUPS):
            lanes = [
                slice(part * D + group * GROUP_WIDTH, part * D + (group + 1) * GROUP_WIDTH) for part in range(3)
            ]
            query = qkv_s[rows, lanes[0]].astype(BF)
            keys = stacked_keys(qkv_s[rows, lanes[1]], SCALE)
            values = stacked_keys(qkv_s[rows, lanes[2]])
            grad_context = dc_s[rows, lanes[0]].astype(BF)
            probs = prob_s[rows, group * GROUP * KEYS : (group + 1) * GROUP * KEYS]
            grad_probs = dot_nt(grad_context, values)
            found = []
            for i in range(GROUP):
                at = slice(i * KEYS, (i + 1) * KEYS)
                weighted = probs[:, at] * grad_probs[:, at]
                found.append(weighted - probs[:, at] * jnp.sum(weighted, axis=-1, keepdims=True))
            grad_scores = jnp.concatenate(found, 1).astype(BF)
            dqkv_s[rows, lanes[0]] = dot_nn(grad_scores, keys)
            dqkv_s[rows, lanes[1]] = own_lanes(dot_tn(grad_scores, query)) * SCALE
            dqkv_s[rows, lanes[2]] = own_lanes(dot_tn(probs.astype(BF), grad_context))
    total = grad_residual
    for part in range(3):
        cols = slice(part * D, (part + 1) * D)
        value = dqkv_s[:, cols].astype(BF)
        dqkv_out[:, cols] = value
        sums_out[0:1, cols] += column_sums(value.astype(F32))
        total = total + dot_nt(value, joint[:, cols])
    result = total.astype(BF)
    for i in range(PIPE):
        da_out[i] = result[:, i * QUARTER : (i + 1) * QUARTER]

    @pl.when(layer == 1)
    def _():
        outgoing[micro] = result
        copy_of(micro).start()

    @pl.when((layer == 1) & (micro == micros - 1))
    def _():
        for index in range(micros):
            copy_of(index).wait_send()


def backward(micros, block, pieces, joint, mixing, expand, reduce, vectors, n2, r2, slope, n1, r1, qkv, prob):
    rows = micros * block

    def whole(array):
        return pl.BlockSpec(array.shape, lambda m: (0,) * array.ndim, pipeline_mode=pl.Buffered(1))

    def by_rows(width):
        return pl.BlockSpec((block, width), lambda m: (m, 0))

    by_pieces = pl.BlockSpec((PIPE, block, QUARTER), lambda m: (0, m, 0))
    kept = (n2, r2, slope, n1, r1, qkv, prob)
    widths = [D, FF, D, 3 * D]
    return pl.pallas_call(
        functools.partial(backward_kernel, micros, block),
        grid=(micros,),
        out_shape=[jax.ShapeDtypeStruct((rows, w), BF) for w in widths]
        + [jax.ShapeDtypeStruct((PIPE, rows, QUARTER), BF), jax.ShapeDtypeStruct((8, FF), F32)],
        in_specs=[by_pieces]
        + [whole(a) for a in (joint, mixing, expand, reduce, vectors)]
        + [by_rows(a.shape[1]) for a in kept],
        out_specs=[by_rows(w) for w in widths] + [by_pieces, pl.BlockSpec((8, FF), lambda m: (0, 0))],
        scratch_shapes=[
            pltpu.VMEM((micros, block, D), BF),
            pltpu.VMEM((micros, block, D), BF),
            pltpu.VMEM((block, D), BF),
            pltpu.VMEM((block, 3 * D), F32),
            pltpu.VMEM((block, HEADS * KEYS), F32),
            pltpu.VMEM((block, D), F32),
            pltpu.VMEM((block, 3 * D), F32),
            pltpu.SemaphoreType.DMA((micros,)),
            pltpu.SemaphoreType.DMA((micros,)),
        ],
        compiler_params=pltpu.CompilerParams(collective_id=2, has_side_effects=True, vmem_limit_bytes=VMEM_LIMIT),
        name="layer_backward",
    )(pieces, joint, mixing, expand, reduce, vectors, *kept)


TILE = 384


def weights_kernel(
    n_dp,
    a0, dqkv, context, dr1, a1, du, hidden, dr2, sums, y2, da,
    g_proj, g_comb, g_exp, g_red, sums_out, pieces_out,
    b_proj, b_comb, b_exp, b_red,
    c_proj, c_comb, c_exp, c_red,
    x_proj, x_comb, x_exp, x_red,
    z_proj, z_comb, z_exp, z_red,
    sums_core, sums_x, sums_z, sums_a, sums_b,
    core_send, core_recv, x_send, x_recv, z_send, z_recv, piece_send, piece_recv, local_sem,
):
    pipe, dp, layer, half, across_x, across_y, core, other_core = place()
    diagonal = (across_x + 2) % 4
    n_z = n_dp // 2
    z = dp // 2
    z_others = [(z + step) % n_z for step in range(1, n_z)]
    greet(
        [(across_x, dp), (across_y, dp), (diagonal, dp), (pipe, other_core)]
        + [(pipe, 2 * other + core) for other in z_others]
    )

    waits = []
    for j, target in enumerate((across_x, across_y, diagonal)):

        @pl.when(layer == 0)
        def _():
            remote(da.at[target], pieces_out.at[pipe], piece_send.at[j], piece_recv.at[j], (target, dp)).start()

        @pl.when(layer == 1)
        def _():
            remote(y2.at[target], pieces_out.at[pipe], piece_send.at[j], piece_recv.at[j], (target, dp)).start()

        waits.append(remote(da.at[target], pieces_out.at[pipe], piece_send.at[j], piece_recv.at[j], (target, dp)))

    @pl.when(layer == 0)
    def _():
        pltpu.make_async_copy(da.at[pipe], pieces_out.at[pipe], local_sem.at[0]).start()

    @pl.when(layer == 1)
    def _():
        pltpu.make_async_copy(y2.at[pipe], pieces_out.at[pipe], local_sem.at[0]).start()

    own_piece = pltpu.make_async_copy(da.at[pipe], pieces_out.at[pipe], local_sem.at[0])

    mine = [b_red, b_exp, b_proj, b_comb]
    from_core = [c_red, c_exp, c_proj, c_comb]
    from_x = [x_red, x_exp, x_proj, x_comb]
    from_z = [z_red, z_exp, z_proj, z_comb]
    outs = [g_red, g_exp, g_proj, g_comb]

    def fill_red(i, carry):
        lanes = pl.ds(pl.multiple_of(i * TILE, 128), TILE)
        tile = dot_tn(hidden[:, lanes], dr2[...])
        per_half = HIDDEN_HALF // TILE
        r = b_red.shape[3]
        per = TILE // r // 2
        for k in range(per):
            for c in range(2):
                b_red[c, i // per_half, (i % per_half) * per + k] = tile[(2 * k + c) * r : (2 * k + c + 1) * r].astype(BF)
        return carry

    def fill_exp(step, carry):
        i, j = step // 4, step % 4
        r = b_exp.shape[3]
        per = TILE // r // 2
        tile = dot_tn(
            a1[:, pl.ds(pl.multiple_of(i * TILE, 128), TILE)], du[:, pl.ds(pl.multiple_of(j * D, 128), D)]
        )
        lanes = pl.ds(pl.multiple_of((j % 2) * D, 128), D)
        for k in range(per):
            for c in range(2):
                b_exp[c, j // 2, i * per + k, :, lanes] = tile[(2 * k + c) * r : (2 * k + c + 1) * r].astype(BF)
        return carry

    def fill_proj(step, carry):
        i, j = step // 3, step % 3
        r = b_proj.shape[3]
        per = TILE // r // 2
        tile = dot_tn(
            a0[:, pl.ds(pl.multiple_of(i * TILE, 128), TILE)], dqkv[:, pl.ds(pl.multiple_of(j * D, 128), D)]
        )
        lanes = pl.ds(pl.multiple_of(j * HALF, 128), HALF)
        for k in range(per):
            for c in range(2):
                rows = tile[(2 * k + c) * r : (2 * k + c + 1) * r].astype(BF)
                b_proj[c, 0, i * per + k, :, lanes] = rows[:, :HALF]
                b_proj[c, 1, i * per + k, :, lanes] = rows[:, HALF:]
        return carry

    def fill_comb(i, carry):
        r = b_comb.shape[3]
        per = TILE // r // 2
        tile = dot_tn(context[:, pl.ds(pl.multiple_of(i * TILE, 128), TILE)], dr1[...])
        for k in range(per):
            for c in range(2):
                b_comb[c, i, k] = tile[(2 * k + c) * r : (2 * k + c + 1) * r].astype(BF)
        return carry

    fills = [(fill_red, FF // TILE), (fill_exp, 4 * D // TILE), (fill_proj, 3 * D // TILE), (fill_comb, D // TILE)]

    def core_copy(a):
        return remote(mine[a].at[1 - core], from_core[a], core_send.at[a], core_recv.at[a], (pipe, other_core))

    def x_copy(a):
        return remote(mine[a].at[core, 1 - half], from_x[a], x_send.at[a], x_recv.at[a], (across_x, dp))

    def z_copy(a, step):
        other = z_others[step]
        return remote(
            mine[a].at[core, half, other], from_z[a].at[step], z_send.at[a, step], z_recv.at[a, step],
            (pipe, 2 * other + core),
        )

    def after_core(a):
        core_copy(a).wait()

        @pl.loop(0, n_z)
        def _(k):
            total = mine[a][core, 1 - half, k].astype(F32) + from_core[a][1 - half, k].astype(F32)
            mine[a][core, 1 - half, k] = total.astype(BF)

        x_copy(a).start()

    def after_x(a):
        x_copy(a).wait()

        def total_of(k):
            return (
                mine[a][core, half, k].astype(F32) + from_core[a][half, k].astype(F32) + from_x[a][k].astype(F32)
            )

        for step, other in enumerate(z_others):
            mine[a][core, half, other] = total_of(other).astype(BF)
            z_copy(a, step).start()
        outs[a][...] = total_of(z)

    def after_z(a):
        for step in range(n_z - 1):
            z_copy(a, step).wait()
        total = outs[a][...]
        for step in range(n_z - 1):
            total = total + from_z[a][step].astype(F32)
        outs[a][...] = total

    small = 4
    sums_copy_core = remote(sums, sums_core, core_send.at[small], core_recv.at[small], (pipe, other_core))
    sums_copy_x = remote(sums_a, sums_x, x_send.at[small], x_recv.at[small], (across_x, dp))
    sums_copies_z = [
        remote(
            sums_b, sums_z.at[step], z_send.at[small, step], z_recv.at[small, step], (pipe, 2 * other + core)
        )
        for step, other in enumerate(z_others)
    ]

    sums_copy_core.start()
    for a, (fill, count) in enumerate(fills):
        lax.fori_loop(0, count, fill, 0)
        core_copy(a).start()
        if a == 0:
            sums_copy_core.wait()
            sums_a[...] = sums[...] + sums_core[...]
            sums_copy_x.start()
        else:
            after_core(a - 1)
    after_core(3)
    sums_copy_x.wait()
    sums_b[...] = sums_a[...] + sums_x[...]
    for copy in sums_copies_z:
        copy.start()
    for a in range(4):
        after_x(a)
    for a in range(4):
        after_z(a)
    total = sums_b[...]
    for step in range(n_z - 1):
        sums_copies_z[step].wait()
        total = total + sums_z[step]
    sums_out[...] = total
    own_piece.wait()
    for copy in waits:
        copy.wait()


def weight_gradients(n_dp, a0, dqkv, context, dr1, a1, du, hidden, dr2, sums, y2, da):
    vmem = pl.BlockSpec(memory_space=pltpu.VMEM)
    hbm = pl.BlockSpec(memory_space=pl.ANY)
    n_z = n_dp // 2
    shapes = [(D // n_dp, 3 * HALF), (HALF // n_dp, D), (D // n_dp, HIDDEN_HALF), (HIDDEN_HALF // n_dp, D)]
    return pl.pallas_call(
        functools.partial(weights_kernel, n_dp),
        out_shape=[jax.ShapeDtypeStruct(s, F32) for s in shapes]
        + [jax.ShapeDtypeStruct(sums.shape, F32), jax.ShapeDtypeStruct(y2.shape, BF)],
        in_specs=[vmem] * 9 + [hbm] * 2,
        out_specs=[vmem] * 5 + [hbm],
        scratch_shapes=[pltpu.VMEM((2, 2, n_z) + s, BF) for s in shapes]
        + [pltpu.VMEM((2, n_z) + s, BF) for s in shapes]
        + [pltpu.VMEM((n_z,) + s, BF) for s in shapes]
        + [pltpu.VMEM((n_z - 1,) + s, BF) for s in shapes]
        + [
            pltpu.VMEM(sums.shape, F32),
            pltpu.VMEM(sums.shape, F32),
            pltpu.VMEM((n_z - 1,) + sums.shape, F32),
            pltpu.VMEM(sums.shape, F32),
            pltpu.VMEM(sums.shape, F32),
            pltpu.SemaphoreType.DMA((5,)),
            pltpu.SemaphoreType.DMA((5,)),
            pltpu.SemaphoreType.DMA((5,)),
            pltpu.SemaphoreType.DMA((5,)),
            pltpu.SemaphoreType.DMA((5, n_z - 1)),
            pltpu.SemaphoreType.DMA((5, n_z - 1)),
            pltpu.SemaphoreType.DMA((3,)),
            pltpu.SemaphoreType.DMA((3,)),
            pltpu.SemaphoreType.DMA((1,)),
        ],
        compiler_params=pltpu.CompilerParams(collective_id=3, has_side_effects=True, vmem_limit_bytes=VMEM_LIMIT),
        name="weight_gradients",
    )(a0, dqkv, context, dr1, a1, du, hidden, dr2, sums, y2, da)


def weight_gradients_by_scatter(n_dp, a0, dqkv, context, dr1, a1, du, hidden, dr2, sums, y2, da):
    half = lax.axis_index("pipe") % 2
    layer = lax.axis_index("pipe") // 2
    halves = (
        dot_tn(a0, dqkv).reshape(D, 3, 2, HALF).transpose(2, 0, 1, 3).reshape(2, D, 3 * HALF),
        dot_tn(context, dr1).reshape(2, HALF, D),
        dot_tn(a1, du).reshape(D, 2, HIDDEN_HALF).transpose(1, 0, 2),
        dot_tn(hidden, dr2).reshape(2, HIDDEN_HALF, D),
    )
    swap = [(i, i ^ 1) for i in range(PIPE)]
    found = []
    for member in halves:
        part = lax.psum_scatter(member, "dp", scatter_dimension=1, tiled=True)
        keep = lax.dynamic_index_in_dim(part, half, 0, keepdims=False)
        send = lax.dynamic_index_in_dim(part, 1 - half, 0, keepdims=False)
        found.append(keep + lax.ppermute(send.astype(BF), "pipe", swap).astype(F32))
    small = lax.psum(sums, "dp")
    small = small + lax.ppermute(small, "pipe", swap)
    mine = jnp.where(layer == 1, y2, da)
    pieces = lax.all_to_all(mine, "pipe", 0, 0, tiled=False)
    return found + [small, pieces]


def shards(
    n_dp,
    tokens, cotangent, captions, projection, biases, combiner, offsets, scaling, centring,
    expansion, lifting, reduction, settling, stretch, translate,
):
    pipe = lax.axis_index("pipe")
    dp = lax.axis_index("dp")
    half = pipe % 2
    local_rows = tokens.shape[0]
    local_pairs = local_rows // PAIR_ROWS
    pairs = 2 * ((local_pairs + 3) // 4)
    rows = pairs * PAIR_ROWS
    spare = 2 * rows - local_rows
    block = 2 * PAIR_ROWS
    micros = rows // block

    both = jnp.pad(jnp.stack([tokens, cotangent]), ((0, 0), (0, spare), (0, 0)))
    wide = [jnp.pad(v[0], (0, HIDDEN_HALF - v.shape[1])) for v in (
        biases, offsets, scaling, centring, lifting, settling, stretch, translate
    )]
    packed = jnp.pad(jnp.stack(wide), ((0, 8), (0, 0)))
    pieces, joint, mixing, expand, reduce, halves = gather(
        rows, both, projection[0], combiner[0], expansion[0], reduction[0], packed
    )
    halves = halves.astype(F32)

    def joined(index, width):
        return jnp.pad(halves[:, index, :width].reshape(2 * width), (0, FF - 2 * width))

    joint_bias = jnp.pad(
        jnp.concatenate([
            halves[:, 0, :HALF].reshape(D), jnp.zeros((D,), F32), halves[:, 0, HALF:D].reshape(D)
        ]),
        (0, FF - 3 * D),
    )
    vectors = jnp.stack([
        joint_bias, joined(1, HALF), joined(2, HALF), joined(3, HALF),
        joined(4, HIDDEN_HALF), joined(5, HALF), joined(6, HALF), joined(7, HALF),
    ])
    lengths = lax.dynamic_slice_in_dim(jnp.pad(captions, (0, 2 * pairs - local_pairs)), half * pairs, pairs)
    key = jnp.arange(KEYS)[None, :]
    visible = (key < PAIR_ROWS) & ((key >= WORDS) | (key < lengths[:, None]))
    masks = jnp.where(visible, 0.0, NEGATIVE).astype(F32)

    a0, qkv, prob, context, n1, r1, a1, hidden, slope, n2, r2, y2 = forward(
        micros, block, pieces, masks, joint, mixing, expand, reduce, vectors
    )
    dr2, du, dr1, dqkv, da, sums = backward(
        micros, block, pieces, joint, mixing, expand, reduce, vectors, n2, r2, slope, n1, r1, qkv, prob
    )
    whole_tiles = HALF % (16 * n_dp) == 0
    collect = weight_gradients if whole_tiles else weight_gradients_by_scatter
    g_proj, g_comb, g_exp, g_red, small, outs = collect(
        n_dp, a0, dqkv, context, dr1, a1, du, hidden, dr2, sums, y2, da
    )
    tokens_grad = jnp.concatenate([outs[0], outs[1]])[:local_rows].astype(F32)
    encoded = jnp.concatenate([outs[2], outs[3]])[:local_rows]

    def own(row, start, width):
        count = width // n_dp
        return lax.dynamic_slice(small, (row, start + half * width + dp * count), (1, count))

    per_bias = jnp.concatenate([
        lax.dynamic_slice(small, (0, half * HALF), (1, HALF)),
        lax.dynamic_slice(small, (0, 2 * D + half * HALF), (1, HALF)),
    ], 1)
    g_bias = lax.dynamic_slice(per_bias, (0, dp * (D // n_dp)), (1, D // n_dp))
    return (
        encoded,
        tokens_grad,
        g_proj[None],
        g_bias,
        g_comb[None],
        own(1, 0, HALF),
        own(2, 0, HALF),
        own(3, 0, HALF),
        g_exp[None],
        own(4, 0, HIDDEN_HALF),
        g_red[None],
        own(5, 0, HALF),
        own(6, 0, HALF),
        own(7, 0, HALF),
    )


def solution(mesh):
    rows = P("dp", "pipe")
    matrix = P("pipe", None, None)
    vector = P("pipe", None)
    matrix_out = P("pipe", "dp", None)
    vector_out = P("pipe", "dp")
    in_specs = (
        rows, rows, P("dp"), matrix, vector, matrix, vector, vector, vector,
        matrix, vector, matrix, vector, vector, vector,
    )
    out_specs = (
        rows, rows, matrix_out, vector_out, matrix_out, vector_out, vector_out, vector_out,
        matrix_out, vector_out, matrix_out, vector_out, vector_out, vector_out,
    )
    return jax.shard_map(
        functools.partial(shards, mesh.shape["dp"]),
        mesh=mesh, in_specs=in_specs, out_specs=out_specs, check_vma=False,
    )
```

```python
import functools

import jax
import jax.numpy as jnp
from jax import lax
from jax.experimental import pallas as pl
from jax.experimental.pallas import tpu as pltpu
from jax.sharding import PartitionSpec as P

D = 768
HEADS = 12
HEAD_DIM = 64
FF = 3072
WORDS = 64
PAIR_ROWS = 104
HALF = D // 2
HIDDEN_HALF = FF // 2
QUARTER = D // 4
PIPE = 4
KEYS = 128
GROUP = 4
GROUP_WIDTH = GROUP * HEAD_DIM
GROUPS = HEADS // GROUP

EPSILON = 1e-05
NEGATIVE = -1e30
SCALE = HEAD_DIM ** (-0.5)

MESH = pl.DeviceIdType.MESH
BF = jnp.bfloat16
F32 = jnp.float32
VMEM_LIMIT = 60 << 20


def dot_nn(left, right):
    return lax.dot_general(left, right, (((1,), (0,)), ((), ())), preferred_element_type=F32)


def dot_nt(left, right):
    return lax.dot_general(left, right, (((1,), (1,)), ((), ())), preferred_element_type=F32)


def dot_tn(left, right):
    return lax.dot_general(left, right, (((0,), (0,)), ((), ())), preferred_element_type=F32)


def place():
    pipe = lax.axis_index("pipe")
    dp = lax.axis_index("dp")
    layer = pipe // 2
    half = pipe % 2
    across_x = pipe + 1 - 2 * half
    across_y = (pipe + 2) % 4
    core = dp % 2
    other_core = dp + 1 - 2 * core
    return pipe, dp, layer, half, across_x, across_y, core, other_core


def greet(devices):
    barrier = pltpu.get_barrier_semaphore()
    for device in devices:
        pl.semaphore_signal(barrier, inc=1, device_id=device, device_id_type=MESH)
    pl.semaphore_wait(barrier, len(devices))


def remote(source, target, send, recv, device):
    return pltpu.make_async_remote_copy(
        src_ref=source,
        dst_ref=target,
        send_sem=send,
        recv_sem=recv,
        device_id=device,
        device_id_type=MESH,
    )


WEIGHT_SHAPES = [(D, 3 * HALF), (HALF, D), (D, HIDDEN_HALF), (HIDDEN_HALF, D)]
WEIGHT_SCRATCH = [pltpu.VMEM((2,) + shape, BF) for shape in WEIGHT_SHAPES]
CHUNKS = [(0, 0, 96), (0, 96, 96), (1, 0, 96), (2, 0, 96), (2, 96, 96), (3, 0, 192), (3, 192, 192)]
ATTENTION_CHUNKS = 3
DEPTH = 3


def head_of_lane():
    return lax.broadcasted_iota(jnp.int32, (KEYS, GROUP_WIDTH), 1) // HEAD_DIM


def stacked_keys(values, scale=None):
    padded = jnp.concatenate([values, jnp.zeros((KEYS - PAIR_ROWS, GROUP_WIDTH), F32)], 0)
    if scale is not None:
        padded = padded * scale
    owner = head_of_lane()
    return jnp.concatenate([jnp.where(owner == i, padded, 0.0) for i in range(GROUP)], 0).astype(BF)


def own_lanes(stacked):
    left = lax.broadcasted_iota(jnp.int32, (KEYS, KEYS), 1) < HEAD_DIM
    low = jnp.where(left, stacked[0:KEYS, :KEYS], stacked[KEYS : 2 * KEYS, :KEYS])
    high = jnp.where(left, stacked[2 * KEYS : 3 * KEYS, KEYS:], stacked[3 * KEYS :, KEYS:])
    return jnp.concatenate([low, high], 1)[:PAIR_ROWS]


def normalized(residual):
    average = jnp.mean(residual, axis=-1, keepdims=True)
    centred = residual - average
    variance = jnp.mean(centred * centred, axis=-1, keepdims=True)
    inverse = lax.rsqrt(variance + EPSILON)
    return centred * inverse, inverse


def forward_kernel(
    micros, block,
    own_vectors, masks, both, own_proj, own_comb, own_exp, own_red,
    a0_out, qkv_out, prob_out, context_out, n1_out, r1_out, a1_out, hidden_out, slope_out, n2_out, r2_out, y2_out,
    vectors, pieces_out, other_proj, other_comb, other_exp, other_red,
    slots, outgoing, a_s, qkv_s, prob_s, context_s, send, recv,
    joint, mixing, expand, reduce, pieces, other_vectors,
    x_send, x_recv, z_send, z_recv, near_send, near_recv, far_send, far_recv,
    own_sem, piece_send, piece_recv, vec_sem, out_sem,
):
    pipe, dp, layer, half, across_x, across_y, core, other_core = place()
    micro = pl.program_id(0)
    pairs = block // PAIR_ROWS
    rows = micros * block
    diagonal = (across_x + 2) % 4
    parity = (dp // 2) % 2
    across_z = dp + 2 - 4 * parity
    mine = 2 * parity + core
    paired = 2 * (1 - parity) + core
    owned = [own_proj, own_comb, own_exp, own_red]
    held = [joint, mixing, expand, reduce]
    others = [other_proj, other_comb, other_exp, other_red]

    def span(chunk, quarter):
        which, start, count = chunk
        return pl.ds(quarter * (WEIGHT_SHAPES[which][0] // 4) + start, count)

    def x_copy(k):
        at = span(CHUNKS[k], mine)
        which = CHUNKS[k][0]
        return remote(owned[which].at[at], held[which].at[half, at], x_send.at[k], x_recv.at[k], (across_x, dp))

    def z_copy(k):
        region = held[CHUNKS[k][0]].at[1 - half, span(CHUNKS[k], mine)]
        return remote(region, region, z_send.at[k], z_recv.at[k], (pipe, across_z))

    def near_copy(k):
        region = held[CHUNKS[k][0]].at[1 - half, span(CHUNKS[k], mine)]
        return remote(region, region, near_send.at[k], near_recv.at[k], (pipe, other_core))

    def far_copy(k):
        region = held[CHUNKS[k][0]].at[1 - half, span(CHUNKS[k], paired)]
        return remote(region, region, far_send.at[k], far_recv.at[k], (pipe, other_core))

    own_copies = [pltpu.make_async_copy(owned[i], held[i].at[half], own_sem.at[i]) for i in range(4)]
    own_piece = pltpu.make_async_copy(both.at[layer, pl.ds(half * rows, rows)], pieces.at[pipe], own_sem.at[4])
    vec_copy = remote(own_vectors, other_vectors, vec_sem.at[0], vec_sem.at[1], (across_x, dp))
    piece_copies = [
        remote(
            both.at[target // 2, pl.ds((target % 2) * rows, rows)],
            pieces.at[pipe],
            piece_send.at[j], piece_recv.at[j],
            (target, dp),
        )
        for j, target in enumerate((across_x, across_y, diagonal))
    ]
    out_copies = [pltpu.make_async_copy(held[i].at[1 - half], others[i], out_sem.at[i]) for i in range(4)] + [
        pltpu.make_async_copy(pieces, pieces_out, out_sem.at[4])
    ]
    n = len(CHUNKS)

    def gathered(first, last):
        for k in range(first, last):
            x_copy(k).wait_recv()
            z_copy(k).start()
            near_copy(k).start()
            if k + DEPTH < n:
                x_copy(k).wait_send()
                x_copy(k + DEPTH).start()
            if k + DEPTH == n - 1:
                send_pieces(1)
        for k in range(first, last):
            z_copy(k).wait_recv()
            far_copy(k).start()
        for k in range(first, last):
            near_copy(k).wait_recv()
            far_copy(k).wait_recv()

    def send_pieces(to_layer):
        for j, target in enumerate((across_x, across_y, diagonal)):
            @pl.when(target // 2 == to_layer)
            def _():
                piece_copies[j].start()

    def rest_gathered():
        gathered(ATTENTION_CHUNKS, n)
        own_copies[2].wait()
        own_copies[3].wait()
        for copy in out_copies[:4]:
            copy.start()

    @pl.when(micro == 0)
    def _():
        own_piece.start()
        for copy in own_copies:
            copy.start()
        greet([(across_x, dp), (across_y, dp), (diagonal, dp), (pipe, across_z), (pipe, other_core)])
        vec_copy.start()
        send_pieces(0)
        for k in range(DEPTH):
            x_copy(k).start()
        vec_copy.wait_recv()
        for which in range(2):
            value = jnp.where(half == which, own_vectors[...], other_vectors[...]).astype(F32)
            vectors[0:1, which * 3 * HALF : which * 3 * HALF + HALF] = value[0:1, :HALF]
            vectors[0:1, which * 3 * HALF + HALF : which * 3 * HALF + D] = jnp.zeros((1, HALF), F32)
            vectors[0:1, which * 3 * HALF + D : (which + 1) * 3 * HALF] = value[0:1, HALF:D]
            for i in (1, 2, 3, 5, 6, 7):
                vectors[i : i + 1, which * HALF : (which + 1) * HALF] = value[i : i + 1, :HALF]
            vectors[4:5, which * HIDDEN_HALF : (which + 1) * HIDDEN_HALF] = value[4:5, :]
        own_piece.wait()

        @pl.when(layer == 0)
        def _():
            for copy in piece_copies:
                copy.wait_recv()

        gathered(0, ATTENTION_CHUNKS)
        own_copies[0].wait()
        own_copies[1].wait()

        @pl.when(layer == 1)
        def _():
            rest_gathered()

    def copy_of(index):
        return remote(outgoing.at[index], slots.at[index], send.at[index], recv.at[index], (across_y, dp))

    @pl.when(layer == 0)
    def _():
        at = pl.ds(pl.multiple_of(micro * block, 16), block)
        a_s[...] = jnp.concatenate([pieces[i, at, :] for i in range(PIPE)], 1)

    @pl.when(layer == 1)
    def _():
        copy_of(micro).wait_recv()
        a_s[...] = slots[micro]

    inputs = a_s[...]
    a0_out[...] = inputs
    for which in range(2):
        value = dot_nn(inputs, joint[which]) + vectors[0:1, which * 3 * HALF : (which + 1) * 3 * HALF]
        for part in range(3):
            cols = slice(part * D + which * HALF, part * D + (which + 1) * HALF)
            found = value[:, part * HALF : (part + 1) * HALF]
            qkv_s[:, cols] = found
            qkv_out[:, cols] = found.astype(BF)
    for pair in range(pairs):
        rows_at = slice(pair * PAIR_ROWS, (pair + 1) * PAIR_ROWS)
        mask = masks[pl.ds(micro * pairs + pair, 1), :]
        for group in range(GROUPS):
            lanes = slice(group * GROUP_WIDTH, (group + 1) * GROUP_WIDTH)
            query = qkv_s[rows_at, group * GROUP_WIDTH : (group + 1) * GROUP_WIDTH].astype(BF)
            keys = stacked_keys(qkv_s[rows_at, D + group * GROUP_WIDTH : D + (group + 1) * GROUP_WIDTH], SCALE)
            values = stacked_keys(qkv_s[rows_at, 2 * D + group * GROUP_WIDTH : 2 * D + (group + 1) * GROUP_WIDTH])
            scores = dot_nt(query, keys)
            found = []
            for i in range(GROUP):
                score = scores[:, i * KEYS : (i + 1) * KEYS] + mask
                exponent = jnp.exp(score - jnp.max(score, axis=-1, keepdims=True))
                found.append(exponent * (1.0 / jnp.sum(exponent, axis=-1, keepdims=True)))
            probs = jnp.concatenate(found, 1)
            prob_s[rows_at, group * GROUP * KEYS : (group + 1) * GROUP * KEYS] = probs
            context_s[rows_at, lanes] = dot_nn(probs.astype(BF), values)
    prob_out[...] = prob_s[...].astype(BF)
    context = context_s[...].astype(BF)
    context_out[...] = context
    residual = inputs.astype(F32) + dot_nn(context, mixing[...].reshape(D, D)) + vectors[1:2, :D]
    norm, inverse = normalized(residual)
    n1_out[...] = norm.astype(BF)
    r1_out[...] = inverse
    attended = (norm * vectors[2:3, :D] + vectors[3:4, :D]).astype(BF)
    a1_out[...] = attended

    @pl.when((micro == 0) & (layer == 0))
    def _():
        rest_gathered()

    chunk = 512
    residual = attended.astype(F32) + vectors[5:6, :D]
    for which in range(2):
        for start in range(0, HIDDEN_HALF, chunk):
            at = slice(start, start + chunk)
            cols = slice(which * HIDDEN_HALF + start, which * HIDDEN_HALF + start + chunk)
            raised = dot_nn(attended, expand[which, :, at]) + vectors[4:5, cols]
            below = 0.5 * (1.0 + lax.erf(raised * (0.5**0.5)))
            hidden = (raised * below).astype(BF)
            hidden_out[:, cols] = hidden
            density = jnp.exp(raised * raised * (-0.5)) * 0.3989422804014327
            slope_out[:, cols] = (below + raised * density).astype(BF)
            residual = residual + dot_nn(hidden, reduce[which, at, :])
    norm, inverse = normalized(residual)
    n2_out[...] = norm.astype(BF)
    r2_out[...] = inverse
    result = (norm * vectors[6:7, :D] + vectors[7:8, :D]).astype(BF)
    for i in range(PIPE):
        y2_out[i] = result[:, i * QUARTER : (i + 1) * QUARTER]

    @pl.when(layer == 0)
    def _():
        outgoing[micro] = result
        copy_of(micro).start()

    @pl.when(micro == micros - 1)
    def _():
        @pl.when(layer == 0)
        def _():
            for index in range(micros):
                copy_of(index).wait_send()

        for k in range(n):
            if k + DEPTH >= n:
                x_copy(k).wait_send()
            z_copy(k).wait_send()
            near_copy(k).wait_send()
            far_copy(k).wait_send()
        for copy in piece_copies + [vec_copy]:
            copy.wait_send()

        @pl.when(layer == 1)
        def _():
            for copy in piece_copies:
                copy.wait_recv()

        out_copies[4].start()
        for copy in out_copies:
            copy.wait()


def forward(micros, block, own_vectors, masks, both, owned):
    rows = micros * block
    n = len(CHUNKS)

    def by_rows(width):
        return pl.BlockSpec((block, width), lambda m: (m, 0))

    vmem = pl.BlockSpec(memory_space=pltpu.VMEM)
    hbm = pl.BlockSpec(memory_space=pl.ANY)
    by_pieces = pl.BlockSpec((PIPE, block, QUARTER), lambda m: (0, m, 0))
    widths = [D, 3 * D, HEADS * KEYS, D, D, 1, D, FF, FF, D, 1]
    types = [BF, BF, BF, BF, BF, F32, BF, BF, BF, BF, F32]
    pieces = jax.ShapeDtypeStruct((PIPE, rows, QUARTER), BF)
    return pl.pallas_call(
        functools.partial(forward_kernel, micros, block),
        grid=(micros,),
        out_shape=[jax.ShapeDtypeStruct((rows, w), t) for w, t in zip(widths, types)]
        + [pieces, jax.ShapeDtypeStruct((8, FF), F32), pieces]
        + [jax.ShapeDtypeStruct(shape, BF) for shape in WEIGHT_SHAPES],
        in_specs=[vmem, vmem] + [hbm] * 5,
        out_specs=[by_rows(w) for w in widths] + [by_pieces, vmem] + [hbm] * 5,
        scratch_shapes=[
            pltpu.VMEM((micros, block, D), BF),
            pltpu.VMEM((micros, block, D), BF),
            pltpu.VMEM((block, D), BF),
            pltpu.VMEM((block, 3 * D), F32),
            pltpu.VMEM((block, HEADS * KEYS), F32),
            pltpu.VMEM((block, D), F32),
            pltpu.SemaphoreType.DMA((micros,)),
            pltpu.SemaphoreType.DMA((micros,)),
        ]
        + WEIGHT_SCRATCH
        + [pltpu.VMEM((PIPE, rows, QUARTER), BF), pltpu.VMEM(own_vectors.shape, BF)]
        + [pltpu.SemaphoreType.DMA((n,))] * 8
        + [
            pltpu.SemaphoreType.DMA((5,)),
            pltpu.SemaphoreType.DMA((3,)),
            pltpu.SemaphoreType.DMA((3,)),
            pltpu.SemaphoreType.DMA((2,)),
            pltpu.SemaphoreType.DMA((5,)),
        ],
        compiler_params=pltpu.CompilerParams(collective_id=1, has_side_effects=True, vmem_limit_bytes=VMEM_LIMIT),
        name="layer_forward",
    )(own_vectors, masks, both, *owned)


def norm_backward(gradient, norm, inverse, gain):
    scaled = gradient * gain
    first = jnp.mean(scaled, axis=-1, keepdims=True)
    second = jnp.mean(scaled * norm, axis=-1, keepdims=True)
    return (scaled - first - norm * second) * inverse


def column_sums(value):
    return jnp.sum(value, axis=0, keepdims=True)


def backward_kernel(
    micros, block,
    pieces, vectors,
    own_proj, own_comb, own_exp, own_red, other_proj, other_comb, other_exp, other_red,
    n2, r2, slope, n1, r1, qkv, prob,
    dr2_out, du_out, dr1_out, dqkv_out, da_out, sums_out,
    slots, outgoing, g_s, qkv_s, prob_s, dc_s, dqkv_s, send, recv,
    joint, mixing, expand, reduce, weight_sem,
):
    pipe, dp, layer, half, across_x, across_y, core, other_core = place()
    micro = pl.program_id(0)
    pairs = block // PAIR_ROWS

    owned = [own_proj, own_comb, own_exp, own_red]
    others = [other_proj, other_comb, other_exp, other_red]
    held = [joint, mixing, expand, reduce]
    loads = [
        [
            pltpu.make_async_copy(owned[i], held[i].at[half], weight_sem.at[0, i]),
            pltpu.make_async_copy(others[i], held[i].at[1 - half], weight_sem.at[1, i]),
        ]
        for i in range(4)
    ]

    def loaded(*which):
        @pl.when(micro == 0)
        def _():
            for index in which:
                for copy in loads[index]:
                    copy.wait()

    @pl.when(micro == 0)
    def _():
        for index in (3, 2, 1, 0):
            for copy in loads[index]:
                copy.start()
        greet([(across_y, dp)])
        sums_out[...] = jnp.zeros_like(sums_out)

    def copy_of(index):
        return remote(outgoing.at[index], slots.at[index], send.at[index], recv.at[index], (across_y, dp))

    @pl.when(layer == 1)
    def _():
        g_s[...] = jnp.concatenate([pieces[i] for i in range(PIPE)], 1)

    @pl.when(layer == 0)
    def _():
        copy_of(micro).wait_recv()
        g_s[...] = slots[micro]

    def add_sum(row, value):
        width = value.shape[1]
        sums_out[row : row + 1, :width] += column_sums(value)

    gradient = g_s[...].astype(F32)
    norm = n2[...].astype(F32)
    add_sum(6, gradient * norm)
    add_sum(7, gradient)
    grad_residual = norm_backward(gradient, norm, r2[...], vectors[6:7, :D])
    add_sum(5, grad_residual)
    branch = grad_residual.astype(BF)
    dr2_out[...] = branch
    loaded(3, 2)
    chunk = 512
    total = grad_residual
    for which in range(2):
        for start in range(0, HIDDEN_HALF, chunk):
            at = slice(start, start + chunk)
            cols = slice(which * HIDDEN_HALF + start, which * HIDDEN_HALF + start + chunk)
            raised = dot_nt(branch, reduce[which, at, :]) * slope[:, cols].astype(F32)
            sums_out[4:5, cols] += column_sums(raised)
            raised = raised.astype(BF)
            du_out[:, cols] = raised
            total = total + dot_nt(raised, expand[which, :, at])

    gradient = total.astype(BF).astype(F32)
    norm = n1[...].astype(F32)
    add_sum(2, gradient * norm)
    add_sum(3, gradient)
    grad_residual = norm_backward(gradient, norm, r1[...], vectors[2:3, :D])
    add_sum(1, grad_residual)
    branch = grad_residual.astype(BF)
    dr1_out[...] = branch
    loaded(1, 0)
    dc_s[...] = dot_nt(branch, mixing[...].reshape(D, D))
    qkv_s[...] = qkv[...].astype(F32)
    prob_s[...] = prob[...].astype(F32)
    for pair in range(pairs):
        rows = slice(pair * PAIR_ROWS, (pair + 1) * PAIR_ROWS)
        for group in range(GROUPS):
            lanes = [
                slice(part * D + group * GROUP_WIDTH, part * D + (group + 1) * GROUP_WIDTH) for part in range(3)
            ]
            query = qkv_s[rows, lanes[0]].astype(BF)
            keys = stacked_keys(qkv_s[rows, lanes[1]], SCALE)
            values = stacked_keys(qkv_s[rows, lanes[2]])
            grad_context = dc_s[rows, lanes[0]].astype(BF)
            probs = prob_s[rows, group * GROUP * KEYS : (group + 1) * GROUP * KEYS]
            grad_probs = dot_nt(grad_context, values)
            found = []
            for i in range(GROUP):
                at = slice(i * KEYS, (i + 1) * KEYS)
                weighted = probs[:, at] * grad_probs[:, at]
                found.append(weighted - probs[:, at] * jnp.sum(weighted, axis=-1, keepdims=True))
            grad_scores = jnp.concatenate(found, 1).astype(BF)
            dqkv_s[rows, lanes[0]] = dot_nn(grad_scores, keys)
            dqkv_s[rows, lanes[1]] = own_lanes(dot_tn(grad_scores, query)) * SCALE
            dqkv_s[rows, lanes[2]] = own_lanes(dot_tn(probs.astype(BF), grad_context))
    total = grad_residual
    for which in range(2):
        value = jnp.concatenate(
            [dqkv_s[:, part * D + which * HALF : part * D + (which + 1) * HALF] for part in range(3)], 1
        ).astype(BF)
        cols = slice(which * 3 * HALF, (which + 1) * 3 * HALF)
        dqkv_out[:, cols] = value
        sums_out[0:1, cols] += column_sums(value.astype(F32))
        total = total + dot_nt(value, joint[which])
    result = total.astype(BF)
    for i in range(PIPE):
        da_out[i] = result[:, i * QUARTER : (i + 1) * QUARTER]

    @pl.when(layer == 1)
    def _():
        outgoing[micro] = result
        copy_of(micro).start()

    @pl.when((layer == 1) & (micro == micros - 1))
    def _():
        for index in range(micros):
            copy_of(index).wait_send()


def backward(micros, block, pieces, vectors, owned, others, n2, r2, slope, n1, r1, qkv, prob):
    rows = micros * block

    def whole(array):
        return pl.BlockSpec(array.shape, lambda m: (0,) * array.ndim, pipeline_mode=pl.Buffered(1))

    def by_rows(width):
        return pl.BlockSpec((block, width), lambda m: (m, 0))

    by_pieces = pl.BlockSpec((PIPE, block, QUARTER), lambda m: (0, m, 0))
    kept = (n2, r2, slope, n1, r1, qkv, prob)
    widths = [D, FF, D, 3 * D]
    return pl.pallas_call(
        functools.partial(backward_kernel, micros, block),
        grid=(micros,),
        out_shape=[jax.ShapeDtypeStruct((rows, w), BF) for w in widths]
        + [jax.ShapeDtypeStruct((PIPE, rows, QUARTER), BF), jax.ShapeDtypeStruct((8, FF), F32)],
        in_specs=[by_pieces, whole(vectors)]
        + [pl.BlockSpec(memory_space=pl.ANY)] * 8
        + [by_rows(a.shape[1]) for a in kept],
        out_specs=[by_rows(w) for w in widths] + [by_pieces, pl.BlockSpec((8, FF), lambda m: (0, 0))],
        scratch_shapes=[
            pltpu.VMEM((micros, block, D), BF),
            pltpu.VMEM((micros, block, D), BF),
            pltpu.VMEM((block, D), BF),
            pltpu.VMEM((block, 3 * D), F32),
            pltpu.VMEM((block, HEADS * KEYS), F32),
            pltpu.VMEM((block, D), F32),
            pltpu.VMEM((block, 3 * D), F32),
            pltpu.SemaphoreType.DMA((micros,)),
            pltpu.SemaphoreType.DMA((micros,)),
        ]
        + WEIGHT_SCRATCH
        + [pltpu.SemaphoreType.DMA((2, 4))],
        compiler_params=pltpu.CompilerParams(collective_id=2, has_side_effects=True, vmem_limit_bytes=VMEM_LIMIT),
        name="layer_backward",
    )(pieces, vectors, *owned, *others, *kept)


TILE = 384


def weights_kernel(
    n_dp,
    a0_in, dqkv_in, context_in, dr1_in, a1_in, du_in, hidden_in, dr2_in, sums, y2, da,
    g_proj, g_comb, g_exp, g_red, sums_out, pieces_out,
    b_proj, b_comb, b_exp, b_red,
    c_proj, c_comb, c_exp, c_red,
    x_proj, x_comb, x_exp, x_red,
    z_proj, z_comb, z_exp, z_red,
    sums_core, sums_x, sums_z, sums_a, sums_b,
    a0, dqkv, context, dr1, a1, du, hidden, dr2,
    core_send, core_recv, x_send, x_recv, z_send, z_recv, piece_send, piece_recv, local_sem,
    small_send, small_recv, load_sem,
):
    pipe, dp, layer, half, across_x, across_y, core, other_core = place()
    diagonal = (across_x + 2) % 4
    n_z = n_dp // 2
    z = dp // 2
    offsets = sorted(range(1, n_z), key=lambda off: -min(off, n_z - off)) + [0]
    z_order = [(z + off) % n_z for off in offsets]
    z_others = z_order[:-1]
    loads = [
        pltpu.make_async_copy(source, target, load_sem.at[i])
        for i, (source, target) in enumerate((
            (hidden_in, hidden), (dr2_in, dr2), (a1_in, a1), (du_in, du),
            (a0_in, a0), (dqkv_in, dqkv), (context_in, context), (dr1_in, dr1),
        ))
    ]
    for copy in loads:
        copy.start()
    greet(
        [(across_x, dp), (across_y, dp), (diagonal, dp), (pipe, other_core)]
        + [(pipe, 2 * other + core) for other in z_others]
    )

    waits = []
    for j, target in enumerate((across_x, across_y, diagonal)):

        @pl.when(layer == 0)
        def _():
            remote(da.at[target], pieces_out.at[pipe], piece_send.at[j], piece_recv.at[j], (target, dp)).start()

        @pl.when(layer == 1)
        def _():
            remote(y2.at[target], pieces_out.at[pipe], piece_send.at[j], piece_recv.at[j], (target, dp)).start()

        waits.append(remote(da.at[target], pieces_out.at[pipe], piece_send.at[j], piece_recv.at[j], (target, dp)))

    @pl.when(layer == 0)
    def _():
        pltpu.make_async_copy(da.at[pipe], pieces_out.at[pipe], local_sem.at[0]).start()

    @pl.when(layer == 1)
    def _():
        pltpu.make_async_copy(y2.at[pipe], pieces_out.at[pipe], local_sem.at[0]).start()

    own_piece = pltpu.make_async_copy(da.at[pipe], pieces_out.at[pipe], local_sem.at[0])

    mine = [b_red, b_exp, b_proj, b_comb]
    from_core = [c_red, c_exp, c_proj, c_comb]
    from_x = [x_red, x_exp, x_proj, x_comb]
    from_z = [z_red, z_exp, z_proj, z_comb]
    outs = [g_red, g_exp, g_proj, g_comb]

    def fill_red(i, carry):
        lanes = pl.ds(pl.multiple_of(i * TILE, 128), TILE)
        tile = dot_tn(hidden[:, lanes], dr2[...])
        per_half = HIDDEN_HALF // TILE
        r = b_red.shape[3]
        per = TILE // r // 2
        for k in range(per):
            for c in range(2):
                b_red[c, i // per_half, (i % per_half) * per + k] = tile[(2 * k + c) * r : (2 * k + c + 1) * r].astype(BF)
        return carry

    def fill_exp(step, carry):
        i, j = step // 4, step % 4
        r = b_exp.shape[3]
        per = TILE // r // 2
        tile = dot_tn(
            a1[:, pl.ds(pl.multiple_of(i * TILE, 128), TILE)], du[:, pl.ds(pl.multiple_of(j * D, 128), D)]
        )
        lanes = pl.ds(pl.multiple_of((j % 2) * D, 128), D)
        for k in range(per):
            for c in range(2):
                b_exp[c, j // 2, i * per + k, :, lanes] = tile[(2 * k + c) * r : (2 * k + c + 1) * r].astype(BF)
        return carry

    def fill_proj(step, carry):
        i, h = step // 2, step % 2
        r = b_proj.shape[3]
        per = TILE // r // 2
        tile = dot_tn(
            a0[:, pl.ds(pl.multiple_of(i * TILE, 128), TILE)],
            dqkv[:, pl.ds(pl.multiple_of(h * 3 * HALF, 128), 3 * HALF)],
        )
        for k in range(per):
            for c in range(2):
                b_proj[c, h, i * per + k] = tile[(2 * k + c) * r : (2 * k + c + 1) * r].astype(BF)
        return carry

    def fill_comb(i, carry):
        r = b_comb.shape[3]
        per = TILE // r // 2
        tile = dot_tn(context[:, pl.ds(pl.multiple_of(i * TILE, 128), TILE)], dr1[...])
        for k in range(per):
            for c in range(2):
                b_comb[c, i, k] = tile[(2 * k + c) * r : (2 * k + c + 1) * r].astype(BF)
        return carry

    def core_copy(a, which):
        at = 1 - half if which == 0 else half
        return remote(
            mine[a].at[1 - core, at], from_core[a].at[at], core_send.at[a, which], core_recv.at[a, which],
            (pipe, other_core),
        )

    def x_copy(k):
        a, i = chunks[k]
        return remote(
            mine[a].at[core, 1 - half, z_order[i]], from_x[a].at[z_order[i]], x_send.at[a, i], x_recv.at[a, i],
            (across_x, dp),
        )

    def z_copy(a, i):
        other = z_order[i]
        return remote(
            mine[a].at[core, half, other], from_z[a].at[i], z_send.at[a, i], z_recv.at[a, i],
            (pipe, 2 * other + core),
        )

    chunks = [(a, i) for a in range(4) for i in range(n_z)]

    def start_x(k):
        if k >= len(chunks):
            return
        a, i = chunks[k]
        at = z_order[i]
        total = mine[a][core, 1 - half, at].astype(F32) + from_core[a][1 - half, at].astype(F32)
        mine[a][core, 1 - half, at] = total.astype(BF)
        x_copy(k).start()

    def after_x(k):
        a, i = chunks[k]
        at = z_order[i]
        x_copy(k).wait()
        start_x(k + DEPTH)
        if i == 0:
            core_copy(a, 1).wait_recv()
        total = mine[a][core, half, at].astype(F32) + from_core[a][half, at].astype(F32) + from_x[a][at].astype(F32)
        if i < n_z - 1:
            mine[a][core, half, at] = total.astype(BF)
            z_copy(a, i).start()
        else:
            outs[a][...] = total

    def after_z(a):
        total = outs[a][...]
        for i in range(n_z - 1):
            z_copy(a, i).wait()
            total = total + from_z[a][i].astype(F32)
        outs[a][...] = total

    sums_copy_core = remote(sums, sums_core, small_send.at[0], small_recv.at[0], (pipe, other_core))
    sums_copy_x = remote(sums_a, sums_x, small_send.at[1], small_recv.at[1], (across_x, dp))
    sums_copies_z = [
        remote(sums_b, sums_z.at[i], small_send.at[2 + i], small_recv.at[2 + i], (pipe, 2 * other + core))
        for i, other in enumerate(z_others)
    ]

    sums_copy_core.start()
    loads[0].wait()
    loads[1].wait()
    per_half = HIDDEN_HALF // TILE
    lax.fori_loop(0, per_half, lambda i, carry: fill_red((1 - half) * per_half + i, carry), 0)
    core_copy(0, 0).start()
    lax.fori_loop(0, per_half, lambda i, carry: fill_red(half * per_half + i, carry), 0)
    core_copy(0, 1).start()
    core_copy(0, 0).wait_recv()
    for k in range(DEPTH):
        start_x(k)
    loads[2].wait()
    loads[3].wait()
    lax.fori_loop(0, 4 * D // TILE, fill_exp, 0)
    core_copy(1, 0).start()
    core_copy(1, 1).start()
    sums_copy_core.wait()
    sums_a[...] = sums[...] + sums_core[...]
    sums_copy_x.start()
    core_copy(1, 0).wait_recv()
    after_x(0)
    loads[4].wait()
    loads[5].wait()
    lax.fori_loop(0, 2 * D // TILE, fill_proj, 0)
    core_copy(2, 0).start()
    core_copy(2, 1).start()
    after_x(1)
    loads[6].wait()
    loads[7].wait()
    lax.fori_loop(0, D // TILE, fill_comb, 0)
    core_copy(3, 0).start()
    core_copy(3, 1).start()
    sums_copy_x.wait()
    sums_b[...] = sums_a[...] + sums_x[...]
    for copy in sums_copies_z:
        copy.start()
    core_copy(2, 0).wait_recv()
    core_copy(3, 0).wait_recv()
    for k in range(2, len(chunks)):
        after_x(k)
        if k % n_z == n_z - 2 and k >= n_z:
            after_z(k // n_z - 1)
    after_z(3)
    for a in range(4):
        for which in range(2):
            core_copy(a, which).wait_send()
    total = sums_b[...]
    for i in range(n_z - 1):
        sums_copies_z[i].wait()
        total = total + sums_z[i]
    sums_out[...] = total
    own_piece.wait()
    for copy in waits:
        copy.wait()


def weight_gradients(n_dp, a0, dqkv, context, dr1, a1, du, hidden, dr2, sums, y2, da):
    vmem = pl.BlockSpec(memory_space=pltpu.VMEM)
    hbm = pl.BlockSpec(memory_space=pl.ANY)
    n_z = n_dp // 2
    shapes = [(D // n_dp, 3 * HALF), (HALF // n_dp, D), (D // n_dp, HIDDEN_HALF), (HIDDEN_HALF // n_dp, D)]
    return pl.pallas_call(
        functools.partial(weights_kernel, n_dp),
        out_shape=[jax.ShapeDtypeStruct(s, F32) for s in shapes]
        + [jax.ShapeDtypeStruct(sums.shape, F32), jax.ShapeDtypeStruct(y2.shape, BF)],
        in_specs=[hbm] * 8 + [vmem] + [hbm] * 2,
        out_specs=[vmem] * 5 + [hbm],
        scratch_shapes=[pltpu.VMEM((2, 2, n_z) + s, BF) for s in shapes]
        + [pltpu.VMEM((2, n_z) + s, BF) for s in shapes]
        + [pltpu.VMEM((n_z,) + s, BF) for s in shapes]
        + [pltpu.VMEM((n_z - 1,) + s, BF) for s in shapes]
        + [
            pltpu.VMEM(sums.shape, F32),
            pltpu.VMEM(sums.shape, F32),
            pltpu.VMEM((n_z - 1,) + sums.shape, F32),
            pltpu.VMEM(sums.shape, F32),
            pltpu.VMEM(sums.shape, F32),
        ]
        + [pltpu.VMEM(v.shape, BF) for v in (a0, dqkv, context, dr1, a1, du, hidden, dr2)]
        + [
            pltpu.SemaphoreType.DMA((4, 2)),
            pltpu.SemaphoreType.DMA((4, 2)),
            pltpu.SemaphoreType.DMA((4, n_z)),
            pltpu.SemaphoreType.DMA((4, n_z)),
            pltpu.SemaphoreType.DMA((4, n_z - 1)),
            pltpu.SemaphoreType.DMA((4, n_z - 1)),
            pltpu.SemaphoreType.DMA((3,)),
            pltpu.SemaphoreType.DMA((3,)),
            pltpu.SemaphoreType.DMA((1,)),
            pltpu.SemaphoreType.DMA((n_z + 1,)),
            pltpu.SemaphoreType.DMA((n_z + 1,)),
            pltpu.SemaphoreType.DMA((8,)),
        ],
        compiler_params=pltpu.CompilerParams(collective_id=3, has_side_effects=True, vmem_limit_bytes=VMEM_LIMIT),
        name="weight_gradients",
    )(a0, dqkv, context, dr1, a1, du, hidden, dr2, sums, y2, da)


def weight_gradients_by_scatter(n_dp, a0, dqkv, context, dr1, a1, du, hidden, dr2, sums, y2, da):
    half = lax.axis_index("pipe") % 2
    layer = lax.axis_index("pipe") // 2
    halves = (
        dot_tn(a0, dqkv).reshape(D, 2, 3 * HALF).transpose(1, 0, 2),
        dot_tn(context, dr1).reshape(2, HALF, D),
        dot_tn(a1, du).reshape(D, 2, HIDDEN_HALF).transpose(1, 0, 2),
        dot_tn(hidden, dr2).reshape(2, HIDDEN_HALF, D),
    )
    swap = [(i, i ^ 1) for i in range(PIPE)]
    found = []
    for member in halves:
        part = lax.psum_scatter(member, "dp", scatter_dimension=1, tiled=True)
        keep = lax.dynamic_index_in_dim(part, half, 0, keepdims=False)
        send = lax.dynamic_index_in_dim(part, 1 - half, 0, keepdims=False)
        found.append(keep + lax.ppermute(send.astype(BF), "pipe", swap).astype(F32))
    small = lax.psum(sums, "dp")
    small = small + lax.ppermute(small, "pipe", swap)
    mine = jnp.where(layer == 1, y2, da)
    pieces = lax.all_to_all(mine, "pipe", 0, 0, tiled=False)
    return found + [small, pieces]


def shards(
    n_dp,
    tokens, cotangent, captions, projection, biases, combiner, offsets, scaling, centring,
    expansion, lifting, reduction, settling, stretch, translate,
):
    pipe = lax.axis_index("pipe")
    dp = lax.axis_index("dp")
    half = pipe % 2
    local_rows = tokens.shape[0]
    local_pairs = local_rows // PAIR_ROWS
    pairs = 2 * ((local_pairs + 3) // 4)
    rows = pairs * PAIR_ROWS
    spare = 2 * rows - local_rows
    block = 2 * PAIR_ROWS
    micros = rows // block

    both = jnp.pad(jnp.stack([tokens, cotangent]), ((0, 0), (0, spare), (0, 0)))
    wide = [jnp.pad(v[0], (0, HIDDEN_HALF - v.shape[1])) for v in (
        biases, offsets, scaling, centring, lifting, settling, stretch, translate
    )]
    packed = jnp.pad(jnp.stack(wide), ((0, 8), (0, 0)))
    owned = (projection[0], combiner[0], expansion[0], reduction[0])
    lengths = lax.dynamic_slice_in_dim(jnp.pad(captions, (0, 2 * pairs - local_pairs)), half * pairs, pairs)
    key = jnp.arange(KEYS)[None, :]
    visible = (key < PAIR_ROWS) & ((key >= WORDS) | (key < lengths[:, None]))
    masks = jnp.where(visible, 0.0, NEGATIVE).astype(F32)

    a0, qkv, prob, context, n1, r1, a1, hidden, slope, n2, r2, y2, vectors, pieces, *others = forward(
        micros, block, packed, masks, both, owned
    )
    dr2, du, dr1, dqkv, da, sums = backward(
        micros, block, pieces, vectors, owned, others, n2, r2, slope, n1, r1, qkv, prob
    )
    whole_tiles = HALF % (16 * n_dp) == 0
    collect = weight_gradients if whole_tiles else weight_gradients_by_scatter
    g_proj, g_comb, g_exp, g_red, small, outs = collect(
        n_dp, a0, dqkv, context, dr1, a1, du, hidden, dr2, sums, y2, da
    )
    tokens_grad = jnp.concatenate([outs[0], outs[1]])[:local_rows].astype(F32)
    encoded = jnp.concatenate([outs[2], outs[3]])[:local_rows]

    def own(row, start, width):
        count = width // n_dp
        return lax.dynamic_slice(small, (row, start + half * width + dp * count), (1, count))

    own_bias = lax.dynamic_slice(small, (0, half * 3 * HALF), (1, 3 * HALF))
    per_bias = jnp.concatenate([own_bias[:, :HALF], own_bias[:, D:]], 1)
    g_bias = lax.dynamic_slice(per_bias, (0, dp * (D // n_dp)), (1, D // n_dp))
    return (
        encoded,
        tokens_grad,
        g_proj[None],
        g_bias,
        g_comb[None],
        own(1, 0, HALF),
        own(2, 0, HALF),
        own(3, 0, HALF),
        g_exp[None],
        own(4, 0, HIDDEN_HALF),
        g_red[None],
        own(5, 0, HALF),
        own(6, 0, HALF),
        own(7, 0, HALF),
    )


def solution(mesh):
    rows = P("dp", "pipe")
    matrix = P("pipe", None, None)
    vector = P("pipe", None)
    matrix_out = P("pipe", "dp", None)
    vector_out = P("pipe", "dp")
    in_specs = (
        rows, rows, P("dp"), matrix, vector, matrix, vector, vector, vector,
        matrix, vector, matrix, vector, vector, vector,
    )
    out_specs = (
        rows, rows, matrix_out, vector_out, matrix_out, vector_out, vector_out, vector_out,
        matrix_out, vector_out, matrix_out, vector_out, vector_out, vector_out,
    )
    return jax.shard_map(
        functools.partial(shards, mesh.shape["dp"]),
        mesh=mesh, in_specs=in_specs, out_specs=out_specs, check_vma=False,
    )
```

```python
import functools

import jax
import jax.numpy as jnp
from jax import lax
from jax.experimental import pallas as pl
from jax.experimental.pallas import tpu as pltpu
from jax.sharding import PartitionSpec as P

D = 768
HEADS = 12
HEAD_DIM = 64
FF = 3072
WORDS = 64
PAIR_ROWS = 104
HALF = D // 2
HIDDEN_HALF = FF // 2
QUARTER = D // 4
PIPE = 4
GROUP_WIDTH = 2 * HEAD_DIM
GROUPS = HEADS // 2
STACKED = 2 * PAIR_ROWS

EPSILON = 1e-05
NEGATIVE = -1e30
SCALE = HEAD_DIM ** (-0.5)

MESH = pl.DeviceIdType.MESH
BF = jnp.bfloat16
F32 = jnp.float32
VMEM_LIMIT = 60 << 20


def dot_nn(left, right):
    return lax.dot_general(left, right, (((1,), (0,)), ((), ())), preferred_element_type=F32)


def dot_nt(left, right):
    return lax.dot_general(left, right, (((1,), (1,)), ((), ())), preferred_element_type=F32)


def dot_tn(left, right):
    return lax.dot_general(left, right, (((0,), (0,)), ((), ())), preferred_element_type=F32)


def place():
    pipe = lax.axis_index("pipe")
    dp = lax.axis_index("dp")
    layer = pipe // 2
    half = pipe % 2
    across_x = pipe + 1 - 2 * half
    across_y = (pipe + 2) % 4
    core = dp % 2
    other_core = dp + 1 - 2 * core
    return pipe, dp, layer, half, across_x, across_y, core, other_core


def greet(devices):
    barrier = pltpu.get_barrier_semaphore()
    for device in devices:
        pl.semaphore_signal(barrier, inc=1, device_id=device, device_id_type=MESH)
    pl.semaphore_wait(barrier, len(devices))


def remote(source, target, send, recv, device):
    return pltpu.make_async_remote_copy(
        src_ref=source,
        dst_ref=target,
        send_sem=send,
        recv_sem=recv,
        device_id=device,
        device_id_type=MESH,
    )


WEIGHT_SHAPES = [(D, 3 * HALF), (HALF, D), (D, HIDDEN_HALF), (HIDDEN_HALF, D)]
CHUNKS = [(0, 0, 96), (0, 96, 96), (1, 0, 96), (2, 0, 96), (2, 96, 96), (3, 0, 192), (3, 192, 192)]
ATTENTION_CHUNKS = 3
DEPTH = 3


def left_lanes():
    return lax.broadcasted_iota(jnp.int32, (PAIR_ROWS, GROUP_WIDTH), 1) < HEAD_DIM


def stacked(values, scale=None):
    if scale is not None:
        values = values * scale
    left = left_lanes()
    return jnp.concatenate([jnp.where(left, values, 0.0), jnp.where(left, 0.0, values)], 0).astype(BF)


def own_lanes(values):
    return jnp.where(left_lanes(), values[:PAIR_ROWS], values[PAIR_ROWS:])


def normalized(residual):
    average = jnp.mean(residual, axis=-1, keepdims=True)
    centred = residual - average
    variance = jnp.mean(centred * centred, axis=-1, keepdims=True)
    inverse = lax.rsqrt(variance + EPSILON)
    return centred * inverse, inverse


def norm_backward(gradient, norm, inverse, gain):
    scaled = gradient * gain
    first = jnp.mean(scaled, axis=-1, keepdims=True)
    second = jnp.mean(scaled * norm, axis=-1, keepdims=True)
    return (scaled - first - norm * second) * inverse


def column_sums(value):
    return jnp.sum(value, axis=0, keepdims=True)


def layer_kernel(
    micros, block, local_pairs,
    captions, tokens, cotangent, biases, offsets, scaling, centring, lifting, settling, stretch, translate,
    own_proj, own_comb, own_exp, own_red,
    a0_out, context_out, a1_out, hidden_out, dr2_out, du_out, dr1_out, dqkv_out, sums_out, results_out,
    both, own_vectors, joint, mixing, expand, reduce, pieces, other_vectors, vectors, results,
    slots, outgoing, qkv_keep, prob_keep, n1_keep, r1_keep, n2_keep, r2_keep, slope_keep,
    a_s, qkv_s, context_s, dqkv_s,
    send, recv, x_send, x_recv, z_send, z_recv, near_send, near_recv, far_send, far_recv,
    own_sem, piece_send, piece_recv, vec_sem, result_send, result_recv, result_sem,
):
    pipe, dp, layer, half, across_x, across_y, core, other_core = place()
    step = pl.program_id(0)
    pairs = block // PAIR_ROWS
    rows = micros * block
    diagonal = (across_x + 2) % 4
    parity = (dp // 2) % 2
    across_z = dp + 2 - 4 * parity
    mine = 2 * parity + core
    paired = 2 * (1 - parity) + core
    relatives = (across_x, across_y, diagonal)
    owned = [own_proj, own_comb, own_exp, own_red]
    held = [joint, mixing, expand, reduce]
    n = len(CHUNKS)

    def span(chunk, quarter):
        which, start, count = chunk
        return pl.ds(quarter * (WEIGHT_SHAPES[which][0] // 4) + start, count)

    def x_copy(k):
        at = span(CHUNKS[k], mine)
        which = CHUNKS[k][0]
        return remote(owned[which].at[at], held[which].at[half, at], x_send.at[k], x_recv.at[k], (across_x, dp))

    def z_copy(k):
        region = held[CHUNKS[k][0]].at[1 - half, span(CHUNKS[k], mine)]
        return remote(region, region, z_send.at[k], z_recv.at[k], (pipe, across_z))

    def near_copy(k):
        region = held[CHUNKS[k][0]].at[1 - half, span(CHUNKS[k], mine)]
        return remote(region, region, near_send.at[k], near_recv.at[k], (pipe, other_core))

    def far_copy(k):
        region = held[CHUNKS[k][0]].at[1 - half, span(CHUNKS[k], paired)]
        return remote(region, region, far_send.at[k], far_recv.at[k], (pipe, other_core))

    own_copies = [pltpu.make_async_copy(owned[i], held[i].at[half], own_sem.at[i]) for i in range(4)]
    own_piece = pltpu.make_async_copy(both.at[layer, half], pieces.at[pipe], own_sem.at[4])
    vec_copy = remote(own_vectors, other_vectors, vec_sem.at[0], vec_sem.at[1], (across_x, dp))
    piece_copies = [
        remote(
            both.at[target // 2, target % 2], pieces.at[pipe], piece_send.at[j], piece_recv.at[j], (target, dp)
        )
        for j, target in enumerate(relatives)
    ]

    def send_pieces(to_layer):
        for j, target in enumerate(relatives):
            @pl.when(target // 2 == to_layer)
            def _():
                piece_copies[j].start()

    def gathered(first, last):
        for k in range(first, last):
            x_copy(k).wait_recv()
            z_copy(k).start()
            near_copy(k).start()
            if k + DEPTH < n:
                x_copy(k).wait_send()
                x_copy(k + DEPTH).start()
            if k + DEPTH == n - 1:
                send_pieces(1)
        for k in range(first, last):
            z_copy(k).wait_recv()
            far_copy(k).start()
        for k in range(first, last):
            near_copy(k).wait_recv()
            far_copy(k).wait_recv()

    def rest_gathered():
        gathered(ATTENTION_CHUNKS, n)
        own_copies[2].wait()
        own_copies[3].wait()

    def y_copy(index):
        return remote(outgoing.at[index], slots.at[index], send.at[index], recv.at[index], (across_y, dp))

    def rows_of(index):
        return pl.ds(pl.multiple_of(index * block, 16), block)

    def result_copies(index):
        return [
            remote(
                results.at[target, rows_of(index)], results_out.at[pipe, rows_of(index)],
                result_send.at[j, index], result_recv.at[j, index], (target, dp),
            )
            for j, target in enumerate(relatives)
        ]

    def own_result(index):
        return pltpu.make_async_copy(
            results.at[pipe, rows_of(index)], results_out.at[pipe, rows_of(index)], result_sem.at[index]
        )

    def share_result(index, value):
        for i in range(PIPE):
            results[i, rows_of(index), :] = value[:, i * QUARTER : (i + 1) * QUARTER]
        for copy in result_copies(index):
            copy.start()
        own_result(index).start()

    def from_pieces(index):
        folded = micros // 2
        for k in range(2):
            @pl.when(index // folded == k)
            def _():
                at = pl.ds(pl.multiple_of((index - k * folded) * block, 16), block)
                lanes = slice(k * QUARTER, (k + 1) * QUARTER)
                a_s[...] = jnp.concatenate([pieces[i, at, lanes] for i in range(PIPE)], 1)

    @pl.when(step == 0)
    def _():
        for copy in own_copies:
            copy.start()
        fold = rows // 2
        for t, source in enumerate((tokens, cotangent)):
            for h in range(2):
                blocks = []
                for k in range(2):
                    first = h * rows + k * fold
                    value = source[first : min(first + fold, source.shape[0]), :].astype(F32)
                    if value.shape[0] < fold:
                        value = jnp.concatenate([value, jnp.zeros((fold - value.shape[0], QUARTER), F32)], 0)
                    blocks.append(value)
                both[t, h] = jnp.concatenate(blocks, 1).astype(BF)
        for i, source in enumerate((biases, offsets, scaling, centring, lifting, settling, stretch, translate)):
            own_vectors[i : i + 1, : source.shape[1]] = source[...].astype(F32)
        own_piece.start()
        sums_out[...] = jnp.zeros_like(sums_out)
        greet([(across_x, dp), (across_y, dp), (diagonal, dp), (pipe, across_z), (pipe, other_core)])
        vec_copy.start()
        send_pieces(0)
        for k in range(DEPTH):
            x_copy(k).start()
        vec_copy.wait_recv()
        for which in range(2):
            value = jnp.where(half == which, own_vectors[...], other_vectors[...])
            vectors[0:1, which * 3 * HALF : which * 3 * HALF + HALF] = value[0:1, :HALF]
            vectors[0:1, which * 3 * HALF + HALF : which * 3 * HALF + D] = jnp.zeros((1, HALF), F32)
            vectors[0:1, which * 3 * HALF + D : (which + 1) * 3 * HALF] = value[0:1, HALF:D]
            for i in (1, 2, 3, 5, 6, 7):
                vectors[i : i + 1, which * HALF : (which + 1) * HALF] = value[i : i + 1, :HALF]
            vectors[4:5, which * HIDDEN_HALF : (which + 1) * HIDDEN_HALF] = value[4:5, :]
        own_piece.wait()

        @pl.when(layer == 0)
        def _():
            for copy in piece_copies:
                copy.wait_recv()

        gathered(0, ATTENTION_CHUNKS)
        own_copies[0].wait()
        own_copies[1].wait()

        @pl.when(layer == 1)
        def _():
            rest_gathered()

    @pl.when(step < micros)
    def _():
        micro = step

        @pl.when(layer == 0)
        def _():
            from_pieces(micro)

        @pl.when(layer == 1)
        def _():
            y_copy(micro).wait_recv()
            a_s[...] = slots[micro]

        inputs = a_s[...]
        a0_out[...] = inputs
        for which in range(2):
            value = dot_nn(inputs, joint[which]) + vectors[0:1, which * 3 * HALF : (which + 1) * 3 * HALF]
            for part in range(3):
                cols = slice(part * D + which * HALF, part * D + (which + 1) * HALF)
                found = value[:, part * HALF : (part + 1) * HALF]
                qkv_s[:, cols] = found
                qkv_keep[micro, :, cols] = found.astype(BF)
        over = [(pair, group) for pair in range(pairs) for group in range(GROUPS)]
        spans = [
            (
                slice(pair * PAIR_ROWS, (pair + 1) * PAIR_ROWS),
                [slice(part * D + group * GROUP_WIDTH, part * D + (group + 1) * GROUP_WIDTH) for part in range(3)],
            )
            for pair, group in over
        ]
        key = lax.broadcasted_iota(jnp.int32, (PAIR_ROWS, PAIR_ROWS), 0)
        masks = []
        for pair in range(pairs):
            length = captions[jnp.minimum((half * micros + micro) * pairs + pair, local_pairs - 1)]
            masks.append(jnp.where((key >= WORDS) | (key < length), 0.0, NEGATIVE))
        scores = [
            dot_nt(stacked(qkv_s[at, lanes[1]], SCALE), qkv_s[at, lanes[0]].astype(BF)) for at, lanes in spans
        ]
        values = [stacked(qkv_s[at, lanes[2]]) for at, lanes in spans]
        probs = []
        for k, (pair, group) in enumerate(over):
            found = []
            for i in range(2):
                score = scores[k][i * PAIR_ROWS : (i + 1) * PAIR_ROWS] + masks[pair]
                exponent = jnp.exp(score - jnp.max(score, axis=0, keepdims=True))
                found.append(exponent * (1.0 / jnp.sum(exponent, axis=0, keepdims=True)))
            probs.append(jnp.concatenate(found, 0).astype(BF))
        contexts = [dot_tn(probs[k], values[k]) for k in range(len(over))]
        for k, (at, lanes) in enumerate(spans):
            prob_keep[micro, k] = probs[k]
            context_s[at, lanes[0]] = contexts[k]
        context = context_s[...].astype(BF)
        context_out[...] = context
        residual = inputs.astype(F32) + dot_nn(context, mixing[...].reshape(D, D)) + vectors[1:2, :D]
        norm, inverse = normalized(residual)
        n1_keep[micro] = norm.astype(BF)
        r1_keep[micro] = inverse
        attended = (norm * vectors[2:3, :D] + vectors[3:4, :D]).astype(BF)
        a1_out[...] = attended

        @pl.when((micro == 0) & (layer == 0))
        def _():
            rest_gathered()

        residual = attended.astype(F32) + vectors[5:6, :D]
        for which in range(2):
            cols = slice(which * HIDDEN_HALF, (which + 1) * HIDDEN_HALF)
            raised = dot_nn(attended, expand[which]) + vectors[4:5, cols]
            below = 0.5 * (1.0 + lax.erf(raised * (0.5**0.5)))
            hidden = (raised * below).astype(BF)
            hidden_out[:, cols] = hidden
            density = jnp.exp(raised * raised * (-0.5)) * 0.3989422804014327
            slope_keep[micro, :, cols] = (below + raised * density).astype(BF)
            residual = residual + dot_nn(hidden, reduce[which])
        norm, inverse = normalized(residual)
        n2_keep[micro] = norm.astype(BF)
        r2_keep[micro] = inverse
        result = (norm * vectors[6:7, :D] + vectors[7:8, :D]).astype(BF)

        @pl.when(layer == 0)
        def _():
            outgoing[micro] = result
            y_copy(micro).start()

        @pl.when(layer == 1)
        def _():
            share_result(micro, result)

    def add_sum(row, value):
        width = value.shape[1]
        sums_out[row : row + 1, :width] += column_sums(value)

    @pl.when(step >= micros)
    def _():
        micro = step - micros

        @pl.when((layer == 1) & (micro == 0))
        def _():
            for copy in piece_copies:
                copy.wait_recv()

        @pl.when(layer == 1)
        def _():
            from_pieces(micro)

        @pl.when(layer == 0)
        def _():
            y_copy(micro).wait_recv()
            a_s[...] = slots[micro]

        gradient = a_s[...].astype(F32)
        norm = n2_keep[micro].astype(F32)
        add_sum(6, gradient * norm)
        add_sum(7, gradient)
        grad_residual = norm_backward(gradient, norm, r2_keep[micro], vectors[6:7, :D])
        add_sum(5, grad_residual)
        branch = grad_residual.astype(BF)
        dr2_out[...] = branch
        total = grad_residual
        for which in range(2):
            cols = slice(which * HIDDEN_HALF, (which + 1) * HIDDEN_HALF)
            raised = dot_nt(branch, reduce[which]) * slope_keep[micro, :, cols].astype(F32)
            sums_out[4:5, cols] += column_sums(raised)
            raised = raised.astype(BF)
            du_out[:, cols] = raised
            total = total + dot_nt(raised, expand[which])

        gradient = total.astype(BF).astype(F32)
        norm = n1_keep[micro].astype(F32)
        add_sum(2, gradient * norm)
        add_sum(3, gradient)
        grad_residual = norm_backward(gradient, norm, r1_keep[micro], vectors[2:3, :D])
        add_sum(1, grad_residual)
        branch = grad_residual.astype(BF)
        dr1_out[...] = branch
        context_s[...] = dot_nt(branch, mixing[...].reshape(D, D))
        qkv_s[...] = qkv_keep[micro].astype(F32)
        spans = [
            (
                slice(pair * PAIR_ROWS, (pair + 1) * PAIR_ROWS),
                [slice(part * D + group * GROUP_WIDTH, part * D + (group + 1) * GROUP_WIDTH) for part in range(3)],
            )
            for pair in range(pairs)
            for group in range(GROUPS)
        ]
        over = range(len(spans))
        queries = [qkv_s[at, lanes[0]].astype(BF) for at, lanes in spans]
        keys = [stacked(qkv_s[at, lanes[1]], SCALE) for at, lanes in spans]
        values = [stacked(qkv_s[at, lanes[2]]) for at, lanes in spans]
        grads = [context_s[at, lanes[0]].astype(BF) for at, lanes in spans]
        rounded = [prob_keep[micro, g] for g in over]
        grad_probs = [dot_nt(values[g], grads[g]) for g in over]
        grad_values = [dot_nn(rounded[g], grads[g]) for g in over]
        grad_scores = []
        for g in over:
            probs = rounded[g].astype(F32)
            weighted = probs * grad_probs[g]
            found = []
            for i in range(2):
                at = slice(i * PAIR_ROWS, (i + 1) * PAIR_ROWS)
                found.append(weighted[at] - probs[at] * column_sums(weighted[at]))
            grad_scores.append(jnp.concatenate(found, 0).astype(BF))
        grad_keys = [dot_nn(grad_scores[g], queries[g]) for g in over]
        grad_queries = [dot_tn(grad_scores[g], keys[g]) for g in over]
        for g, (at, lanes) in enumerate(spans):
            dqkv_s[at, lanes[0]] = grad_queries[g]
            dqkv_s[at, lanes[1]] = own_lanes(grad_keys[g]) * SCALE
            dqkv_s[at, lanes[2]] = own_lanes(grad_values[g])
        total = grad_residual
        for which in range(2):
            value = jnp.concatenate(
                [dqkv_s[:, part * D + which * HALF : part * D + (which + 1) * HALF] for part in range(3)], 1
            ).astype(BF)
            cols = slice(which * 3 * HALF, (which + 1) * 3 * HALF)
            dqkv_out[:, cols] = value
            sums_out[0:1, cols] += column_sums(value.astype(F32))
            total = total + dot_nt(value, joint[which])
        result = total.astype(BF)

        @pl.when(layer == 1)
        def _():
            outgoing[micro] = result
            y_copy(micro).start()

        @pl.when(layer == 0)
        def _():
            share_result(micro, result)

    @pl.when(step == 2 * micros - 1)
    def _():
        for index in range(micros):
            y_copy(index).wait_send()
            own_result(index).wait()
            for copy in result_copies(index):
                copy.wait()
        for k in range(n):
            if k + DEPTH >= n:
                x_copy(k).wait_send()
            z_copy(k).wait_send()
            near_copy(k).wait_send()
            far_copy(k).wait_send()
        for copy in piece_copies + [vec_copy]:
            copy.wait_send()


def layer_passes(micros, block, captions, small, tokens, cotangent, owned):
    rows = micros * block
    n = len(CHUNKS)
    vmem = pl.BlockSpec(memory_space=pltpu.VMEM)
    hbm = pl.BlockSpec(memory_space=pl.ANY)

    def forward_rows(width):
        return pl.BlockSpec((block, width), lambda s: (jnp.minimum(s, micros - 1), 0))

    def backward_rows(width):
        return pl.BlockSpec((block, width), lambda s: (jnp.maximum(s - micros, 0), 0))

    forward_widths = [D, D, D, FF]
    backward_widths = [D, FF, D, 3 * D]
    pairs = block // PAIR_ROWS
    return pl.pallas_call(
        functools.partial(layer_kernel, micros, block, captions.shape[0]),
        grid=(2 * micros,),
        out_shape=[jax.ShapeDtypeStruct((rows, w), BF) for w in forward_widths + backward_widths]
        + [jax.ShapeDtypeStruct((8, FF), F32), jax.ShapeDtypeStruct((PIPE, rows, QUARTER), BF)],
        in_specs=[pl.BlockSpec(memory_space=pltpu.SMEM)] + [vmem] * 10 + [hbm] * 4,
        out_specs=[forward_rows(w) for w in forward_widths]
        + [backward_rows(w) for w in backward_widths]
        + [vmem, hbm],
        scratch_shapes=[
            pltpu.VMEM((2, 2, rows // 2, 2 * QUARTER), BF),
            pltpu.VMEM((8, HIDDEN_HALF), F32),
        ]
        + [pltpu.VMEM((2,) + shape, BF) for shape in WEIGHT_SHAPES]
        + [
            pltpu.VMEM((PIPE, rows // 2, 2 * QUARTER), BF),
            pltpu.VMEM((8, HIDDEN_HALF), F32),
            pltpu.VMEM((8, FF), F32),
            pltpu.VMEM((PIPE, rows, QUARTER), BF),
            pltpu.VMEM((micros, block, D), BF),
            pltpu.VMEM((micros, block, D), BF),
            pltpu.VMEM((micros, block, 3 * D), BF),
            pltpu.VMEM((micros, pairs * GROUPS, STACKED, PAIR_ROWS), BF),
            pltpu.VMEM((micros, block, D), BF),
            pltpu.VMEM((micros, block, 1), F32),
            pltpu.VMEM((micros, block, D), BF),
            pltpu.VMEM((micros, block, 1), F32),
            pltpu.VMEM((micros, block, FF), BF),
            pltpu.VMEM((block, D), BF),
            pltpu.VMEM((block, 3 * D), F32),
            pltpu.VMEM((block, D), F32),
            pltpu.VMEM((block, 3 * D), F32),
            pltpu.SemaphoreType.DMA((micros,)),
            pltpu.SemaphoreType.DMA((micros,)),
        ]
        + [pltpu.SemaphoreType.DMA((n,))] * 8
        + [
            pltpu.SemaphoreType.DMA((5,)),
            pltpu.SemaphoreType.DMA((3,)),
            pltpu.SemaphoreType.DMA((3,)),
            pltpu.SemaphoreType.DMA((2,)),
            pltpu.SemaphoreType.DMA((3, micros)),
            pltpu.SemaphoreType.DMA((3, micros)),
            pltpu.SemaphoreType.DMA((micros,)),
        ],
        compiler_params=pltpu.CompilerParams(collective_id=1, has_side_effects=True, vmem_limit_bytes=VMEM_LIMIT),
        name="layer_passes",
    )(captions, tokens, cotangent, *small, *owned)


TILE = 384


def weights_kernel(
    n_dp,
    a0_in, dqkv_in, context_in, dr1_in, a1_in, du_in, hidden_in, dr2_in, sums,
    g_proj, g_comb, g_exp, g_red, sums_out,
    b_proj, b_comb, b_exp, b_red,
    c_proj, c_comb, c_exp, c_red,
    x_proj, x_comb, x_exp, x_red,
    z_proj, z_comb, z_exp, z_red,
    sums_core, sums_x, sums_z, sums_a, sums_b,
    a0, dqkv, context, dr1, a1, du, hidden, dr2,
    core_send, core_recv, x_send, x_recv, z_send, z_recv,
    small_send, small_recv, load_sem,
):
    pipe, dp, layer, half, across_x, across_y, core, other_core = place()
    n_z = n_dp // 2
    z = dp // 2
    offsets = sorted(range(1, n_z), key=lambda off: -min(off, n_z - off)) + [0]
    z_order = [(z + off) % n_z for off in offsets]
    z_others = z_order[:-1]
    loads = [
        pltpu.make_async_copy(source, target, load_sem.at[i])
        for i, (source, target) in enumerate((
            (hidden_in, hidden), (dr2_in, dr2), (a1_in, a1), (du_in, du),
            (a0_in, a0), (dqkv_in, dqkv), (context_in, context), (dr1_in, dr1),
        ))
    ]
    for copy in loads:
        copy.start()
    greet(
        [(across_x, dp), (pipe, other_core)]
        + [(pipe, 2 * other + core) for other in z_others]
    )

    mine = [b_red, b_exp, b_proj, b_comb]
    from_core = [c_red, c_exp, c_proj, c_comb]
    from_x = [x_red, x_exp, x_proj, x_comb]
    from_z = [z_red, z_exp, z_proj, z_comb]
    outs = [g_red, g_exp, g_proj, g_comb]

    def spread(target, tile, cast=BF):
        r = target.shape[-2]
        for k in range(tile.shape[0] // (2 * r)):
            for c in range(2):
                yield c, k, tile[(2 * k + c) * r : (2 * k + c + 1) * r].astype(cast)

    def fill_red(h):
        for part in range(HIDDEN_HALF // D):
            lanes = pl.ds(pl.multiple_of(h * HIDDEN_HALF + part * D, 128), D)
            shards_here = D // (2 * b_red.shape[3])
            for c, k, rows in spread(b_red, dot_tn(hidden[:, lanes], dr2[...])):
                b_red[c, h, part * shards_here + k] = rows

    def fill_exp(step, carry):
        i, h = step // 2, step % 2
        tile = dot_tn(
            a1[:, pl.ds(pl.multiple_of(i * TILE, 128), TILE)],
            du[:, pl.ds(pl.multiple_of(h * HIDDEN_HALF, 128), HIDDEN_HALF)],
        )
        for c, k, rows in spread(b_exp, tile):
            b_exp[c, h, i * (TILE // (2 * b_exp.shape[3])) + k] = rows
        return carry

    def fill_proj(h, carry):
        tile = dot_tn(a0[...], dqkv[:, pl.ds(pl.multiple_of(h * 3 * HALF, 128), 3 * HALF)])
        for c, k, rows in spread(b_proj, tile):
            b_proj[c, h, k] = rows
        return carry

    def fill_comb():
        tile = dot_tn(context[...], dr1[...])
        for h in range(2):
            for c, k, rows in spread(b_comb, tile[h * HALF : (h + 1) * HALF]):
                b_comb[c, h, k] = rows

    def core_copy(a, which):
        at = 1 - half if which == 0 else half
        return remote(
            mine[a].at[1 - core, at], from_core[a].at[at], core_send.at[a, which], core_recv.at[a, which],
            (pipe, other_core),
        )

    def x_copy(k):
        a, i = chunks[k]
        return remote(
            mine[a].at[core, 1 - half, z_order[i]], from_x[a].at[z_order[i]], x_send.at[a, i], x_recv.at[a, i],
            (across_x, dp),
        )

    def z_copy(a, i):
        other = z_order[i]
        return remote(
            mine[a].at[core, half, other], from_z[a].at[i], z_send.at[a, i], z_recv.at[a, i],
            (pipe, 2 * other + core),
        )

    chunks = [(a, i) for a in range(4) for i in range(n_z)]

    def start_x(k):
        if k >= len(chunks):
            return
        a, i = chunks[k]
        at = z_order[i]
        total = mine[a][core, 1 - half, at].astype(F32) + from_core[a][1 - half, at].astype(F32)
        mine[a][core, 1 - half, at] = total.astype(BF)
        x_copy(k).start()

    def after_x(k):
        a, i = chunks[k]
        at = z_order[i]
        x_copy(k).wait()
        start_x(k + DEPTH)
        if i == 0:
            core_copy(a, 1).wait_recv()
        total = mine[a][core, half, at].astype(F32) + from_core[a][half, at].astype(F32) + from_x[a][at].astype(F32)
        if i < n_z - 1:
            mine[a][core, half, at] = total.astype(BF)
            z_copy(a, i).start()
        else:
            outs[a][...] = total

    def after_z(a):
        total = outs[a][...]
        for i in range(n_z - 1):
            z_copy(a, i).wait()
            total = total + from_z[a][i].astype(F32)
        outs[a][...] = total

    sums_copy_core = remote(sums, sums_core, small_send.at[0], small_recv.at[0], (pipe, other_core))
    sums_copy_x = remote(sums_a, sums_x, small_send.at[1], small_recv.at[1], (across_x, dp))
    sums_copies_z = [
        remote(sums_b, sums_z.at[i], small_send.at[2 + i], small_recv.at[2 + i], (pipe, 2 * other + core))
        for i, other in enumerate(z_others)
    ]

    sums_copy_core.start()
    loads[0].wait()
    loads[1].wait()
    fill_red(1 - half)
    core_copy(0, 0).start()
    fill_red(half)
    core_copy(0, 1).start()
    core_copy(0, 0).wait_recv()
    for k in range(DEPTH):
        start_x(k)
    loads[2].wait()
    loads[3].wait()
    lax.fori_loop(0, 2 * D // TILE, fill_exp, 0)
    core_copy(1, 0).start()
    core_copy(1, 1).start()
    sums_copy_core.wait()
    sums_a[...] = sums[...] + sums_core[...]
    sums_copy_x.start()
    core_copy(1, 0).wait_recv()
    after_x(0)
    loads[4].wait()
    loads[5].wait()
    lax.fori_loop(0, 2, fill_proj, 0)
    core_copy(2, 0).start()
    core_copy(2, 1).start()
    after_x(1)
    loads[6].wait()
    loads[7].wait()
    fill_comb()
    core_copy(3, 0).start()
    core_copy(3, 1).start()
    sums_copy_x.wait()
    sums_b[...] = sums_a[...] + sums_x[...]
    for copy in sums_copies_z:
        copy.start()
    core_copy(2, 0).wait_recv()
    core_copy(3, 0).wait_recv()
    for k in range(2, len(chunks)):
        after_x(k)
        if k % n_z == n_z - 2 and k >= n_z:
            after_z(k // n_z - 1)
    after_z(3)
    for a in range(4):
        for which in range(2):
            core_copy(a, which).wait_send()
    total = sums_b[...]
    for i in range(n_z - 1):
        sums_copies_z[i].wait()
        total = total + sums_z[i]
    sums_out[...] = total


def weight_gradients(n_dp, a0, dqkv, context, dr1, a1, du, hidden, dr2, sums):
    vmem = pl.BlockSpec(memory_space=pltpu.VMEM)
    hbm = pl.BlockSpec(memory_space=pl.ANY)
    n_z = n_dp // 2
    shapes = [(D // n_dp, 3 * HALF), (HALF // n_dp, D), (D // n_dp, HIDDEN_HALF), (HIDDEN_HALF // n_dp, D)]
    return pl.pallas_call(
        functools.partial(weights_kernel, n_dp),
        out_shape=[jax.ShapeDtypeStruct(s, F32) for s in shapes]
        + [jax.ShapeDtypeStruct(sums.shape, F32)],
        in_specs=[hbm] * 8 + [vmem],
        out_specs=[vmem] * 5,
        scratch_shapes=[pltpu.VMEM((2, 2, n_z) + s, BF) for s in shapes]
        + [pltpu.VMEM((2, n_z) + s, BF) for s in shapes]
        + [pltpu.VMEM((n_z,) + s, BF) for s in shapes]
        + [pltpu.VMEM((n_z - 1,) + s, BF) for s in shapes]
        + [
            pltpu.VMEM(sums.shape, F32),
            pltpu.VMEM(sums.shape, F32),
            pltpu.VMEM((n_z - 1,) + sums.shape, F32),
            pltpu.VMEM(sums.shape, F32),
            pltpu.VMEM(sums.shape, F32),
        ]
        + [pltpu.VMEM(v.shape, BF) for v in (a0, dqkv, context, dr1, a1, du, hidden, dr2)]
        + [
            pltpu.SemaphoreType.DMA((4, 2)),
            pltpu.SemaphoreType.DMA((4, 2)),
            pltpu.SemaphoreType.DMA((4, n_z)),
            pltpu.SemaphoreType.DMA((4, n_z)),
            pltpu.SemaphoreType.DMA((4, n_z - 1)),
            pltpu.SemaphoreType.DMA((4, n_z - 1)),
            pltpu.SemaphoreType.DMA((n_z + 1,)),
            pltpu.SemaphoreType.DMA((n_z + 1,)),
            pltpu.SemaphoreType.DMA((8,)),
        ],
        compiler_params=pltpu.CompilerParams(collective_id=3, has_side_effects=True, vmem_limit_bytes=VMEM_LIMIT),
        name="weight_gradients",
    )(a0, dqkv, context, dr1, a1, du, hidden, dr2, sums)


def finish_kernel(n_dp, small, results, *refs):
    pipe, dp, layer, half, across_x, across_y, core, other_core = place()
    sources, encoded, tokens_grad, outs, parts = refs[:4], refs[4], refs[5], refs[6:10], refs[10:]
    for source, out in zip(sources, outs):
        out[0] = source[...]
    rows = results.shape[1]
    spare = encoded.shape[0] - rows
    tokens_grad[:rows] = results[0].astype(F32)
    tokens_grad[rows:] = results[1, :spare].astype(F32)
    encoded[:rows] = results[2]
    encoded[rows:] = results[3, :spare]
    for row, out in enumerate(parts):
        count = out.shape[1]
        width = n_dp * count
        found = jnp.zeros(out.shape, F32)
        for h in range(2):
            for d in range(n_dp):
                at = d * count
                if row == 0:
                    at = h * 3 * HALF + at + (HALF if at >= HALF else 0)
                else:
                    at = h * width + at
                found = jnp.where((half == h) & (dp == d), small[row : row + 1, at : at + count], found)
        out[...] = found


def finish(n_dp, local_rows, small, results, grads):
    vmem = pl.BlockSpec(memory_space=pltpu.VMEM)
    widths = [D, HALF, HALF, HALF, HIDDEN_HALF, HALF, HALF, HALF]
    return pl.pallas_call(
        functools.partial(finish_kernel, n_dp),
        out_shape=[
            jax.ShapeDtypeStruct((local_rows, QUARTER), BF),
            jax.ShapeDtypeStruct((local_rows, QUARTER), F32),
        ]
        + [jax.ShapeDtypeStruct((1,) + g.shape, F32) for g in grads]
        + [jax.ShapeDtypeStruct((1, w // n_dp), F32) for w in widths],
        in_specs=[vmem] * 6,
        out_specs=[vmem] * 14,
        compiler_params=pltpu.CompilerParams(vmem_limit_bytes=VMEM_LIMIT),
        name="finish",
    )(small, results, *grads)


def weight_gradients_by_scatter(n_dp, a0, dqkv, context, dr1, a1, du, hidden, dr2, sums):
    half = lax.axis_index("pipe") % 2
    halves = (
        dot_tn(a0, dqkv).reshape(D, 2, 3 * HALF).transpose(1, 0, 2),
        dot_tn(context, dr1).reshape(2, HALF, D),
        dot_tn(a1, du).reshape(D, 2, HIDDEN_HALF).transpose(1, 0, 2),
        dot_tn(hidden, dr2).reshape(2, HIDDEN_HALF, D),
    )
    swap = [(i, i ^ 1) for i in range(PIPE)]
    found = []
    for member in halves:
        part = lax.psum_scatter(member, "dp", scatter_dimension=1, tiled=True)
        keep = lax.dynamic_index_in_dim(part, half, 0, keepdims=False)
        send = lax.dynamic_index_in_dim(part, 1 - half, 0, keepdims=False)
        found.append(keep + lax.ppermute(send.astype(BF), "pipe", swap).astype(F32))
    small = lax.psum(sums, "dp")
    return found + [small + lax.ppermute(small, "pipe", swap)]


def shards(
    n_dp,
    tokens, cotangent, captions, projection, biases, combiner, offsets, scaling, centring,
    expansion, lifting, reduction, settling, stretch, translate,
):
    local_rows = tokens.shape[0]
    local_pairs = local_rows // PAIR_ROWS
    pairs = 2 * ((local_pairs + 3) // 4)
    block = 2 * PAIR_ROWS
    micros = pairs // 2
    owned = (projection[0], combiner[0], expansion[0], reduction[0])
    small = (biases, offsets, scaling, centring, lifting, settling, stretch, translate)
    *kept, results = layer_passes(micros, block, captions, small, tokens, cotangent, owned)
    a0, context, a1, hidden, dr2, du, dr1, dqkv, sums = kept
    whole_tiles = HALF % (16 * n_dp) == 0
    collect = weight_gradients if whole_tiles else weight_gradients_by_scatter
    *grads, sums = collect(n_dp, a0, dqkv, context, dr1, a1, du, hidden, dr2, sums)
    encoded, tokens_grad, g_proj, g_comb, g_exp, g_red, *parts = finish(n_dp, local_rows, sums, results, grads)
    return (
        encoded, tokens_grad, g_proj, parts[0], g_comb, parts[1], parts[2], parts[3],
        g_exp, parts[4], g_red, parts[5], parts[6], parts[7],
    )


def solution(mesh):
    rows = P("dp", "pipe")
    matrix = P("pipe", None, None)
    vector = P("pipe", None)
    matrix_out = P("pipe", "dp", None)
    vector_out = P("pipe", "dp")
    in_specs = (
        rows, rows, P("dp"), matrix, vector, matrix, vector, vector, vector,
        matrix, vector, matrix, vector, vector, vector,
    )
    out_specs = (
        rows, rows, matrix_out, vector_out, matrix_out, vector_out, vector_out, vector_out,
        matrix_out, vector_out, matrix_out, vector_out, vector_out, vector_out,
    )
    return jax.shard_map(
        functools.partial(shards, mesh.shape["dp"]),
        mesh=mesh, in_specs=in_specs, out_specs=out_specs, check_vma=False,
    )
```

```python
import functools

import jax
import jax.numpy as jnp
from jax import lax
from jax.experimental import pallas as pl
from jax.experimental.pallas import tpu as pltpu
from jax.sharding import PartitionSpec as P

D = 768
HEADS = 12
HEAD_DIM = 64
FF = 3072
WORDS = 64
PAIR_ROWS = 104
HALF = D // 2
HIDDEN_HALF = FF // 2
QUARTER = D // 4
PIPE = 4
GROUP_WIDTH = 2 * HEAD_DIM
GROUPS = HEADS // 2
STACKED = 2 * PAIR_ROWS

EPSILON = 1e-05
NEGATIVE = -1e30
SCALE = HEAD_DIM ** (-0.5)

MESH = pl.DeviceIdType.MESH
BF = jnp.bfloat16
F32 = jnp.float32
VMEM_LIMIT = 60 << 20


def dot_nn(left, right):
    return lax.dot_general(left, right, (((1,), (0,)), ((), ())), preferred_element_type=F32)


def dot_nt(left, right):
    return lax.dot_general(left, right, (((1,), (1,)), ((), ())), preferred_element_type=F32)


def dot_tn(left, right):
    return lax.dot_general(left, right, (((0,), (0,)), ((), ())), preferred_element_type=F32)


def place():
    pipe = lax.axis_index("pipe")
    dp = lax.axis_index("dp")
    layer = pipe // 2
    half = pipe % 2
    across_x = pipe + 1 - 2 * half
    across_y = (pipe + 2) % 4
    core = dp % 2
    other_core = dp + 1 - 2 * core
    return pipe, dp, layer, half, across_x, across_y, core, other_core


def greet(devices):
    barrier = pltpu.get_barrier_semaphore()
    for device in devices:
        pl.semaphore_signal(barrier, inc=1, device_id=device, device_id_type=MESH)
    pl.semaphore_wait(barrier, len(devices))


def remote(source, target, send, recv, device):
    return pltpu.make_async_remote_copy(
        src_ref=source,
        dst_ref=target,
        send_sem=send,
        recv_sem=recv,
        device_id=device,
        device_id_type=MESH,
    )


WEIGHT_SHAPES = [(D, 3 * HALF), (HALF, D), (D, HIDDEN_HALF), (HIDDEN_HALF, D)]
CHUNKS = [(0, 0, 96), (0, 96, 96), (1, 0, 96)] + [(2, i*48, 48) for i in range(4)] + [(3, i*96, 96) for i in range(4)]
ATTENTION_CHUNKS = 3
DEPTH = 3
LAG = 2
REDUCE_DEPTH = 3


def left_lanes():
    return lax.broadcasted_iota(jnp.int32, (PAIR_ROWS, GROUP_WIDTH), 1) < HEAD_DIM


def stacked(values, scale=None):
    if scale is not None:
        values = values * scale
    left = left_lanes()
    return jnp.concatenate([jnp.where(left, values, 0.0), jnp.where(left, 0.0, values)], 0).astype(BF)


def own_lanes(values):
    return jnp.where(left_lanes(), values[:PAIR_ROWS], values[PAIR_ROWS:])


def normalized(residual):
    average = jnp.mean(residual, axis=-1, keepdims=True)
    centred = residual - average
    variance = jnp.mean(centred * centred, axis=-1, keepdims=True)
    inverse = lax.rsqrt(variance + EPSILON)
    return centred * inverse, inverse


def norm_backward(gradient, norm, inverse, gain):
    scaled = gradient * gain
    first = jnp.mean(scaled, axis=-1, keepdims=True)
    second = jnp.mean(scaled * norm, axis=-1, keepdims=True)
    return (scaled - first - norm * second) * inverse


def column_sums(value):
    return jnp.sum(value, axis=0, keepdims=True)


def layer_kernel(
    micros, block, local_pairs,
    captions, tokens, cotangent, biases, offsets, scaling, centring, lifting, settling, stretch, translate,
    own_proj, own_comb, own_exp, own_red,
    a0_hbm, context_hbm, a1_hbm, hidden_hbm, dr2_hbm, du_hbm, dr1_hbm, dqkv_hbm, sums_out, results_out, last_out,
    both, own_vectors, joint, mixing, expand, reduce, pieces, unpacked, other_vectors, vectors, results,
    slots, outgoing, qkv_keep, prob_keep, n1_keep, r1_keep, n2_keep, r2_keep, slope_keep,
    a_s, qkv_s, context_s, dqkv_s,
    a0_ring, context_ring, a1_ring, hidden_ring, dr2_ring, du_ring, dr1_ring, dqkv_ring,
    send, recv, x_send, x_recv, z_send, z_recv, near_send, near_recv, far_send, far_recv,
    own_sem, piece_send, piece_recv, vec_sem, result_send, result_recv, result_sem, ring_sem,
):
    pipe, dp, layer, half, across_x, across_y, core, other_core = place()
    step = pl.program_id(0)
    pairs = block // PAIR_ROWS
    rows = micros * block
    diagonal = (across_x + 2) % 4
    parity = (dp // 2) % 2
    across_z = dp + 2 - 4 * parity
    mine = 2 * parity + core
    paired = 2 * (1 - parity) + core
    relatives = (across_x, across_y, diagonal)
    owned = [own_proj, own_comb, own_exp, own_red]
    held = [joint, mixing, expand, reduce]
    n = len(CHUNKS)

    def span(chunk, quarter):
        which, start, count = chunk
        return pl.ds(quarter * (WEIGHT_SHAPES[which][0] // 4) + start, count)

    def x_copy(k):
        at = span(CHUNKS[k], mine)
        which = CHUNKS[k][0]
        return remote(owned[which].at[at], held[which].at[half, at], x_send.at[k], x_recv.at[k], (across_x, dp))

    def z_copy(k):
        region = held[CHUNKS[k][0]].at[1 - half, span(CHUNKS[k], mine)]
        return remote(region, region, z_send.at[k], z_recv.at[k], (pipe, across_z))

    def near_copy(k):
        region = held[CHUNKS[k][0]].at[1 - half, span(CHUNKS[k], mine)]
        return remote(region, region, near_send.at[k], near_recv.at[k], (pipe, other_core))

    def far_copy(k):
        region = held[CHUNKS[k][0]].at[1 - half, span(CHUNKS[k], paired)]
        return remote(region, region, far_send.at[k], far_recv.at[k], (pipe, other_core))

    own_copies = [pltpu.make_async_copy(owned[i], held[i].at[half], own_sem.at[i]) for i in range(4)]
    own_piece = pltpu.make_async_copy(both.at[layer, half], pieces.at[pipe], own_sem.at[4])
    vec_copy = remote(own_vectors, other_vectors, vec_sem.at[0], vec_sem.at[1], (across_x, dp))
    piece_copies = [
        remote(
            both.at[target // 2, target % 2], pieces.at[pipe], piece_send.at[j], piece_recv.at[j], (target, dp)
        )
        for j, target in enumerate(relatives)
    ]

    def send_pieces(to_layer):
        for j, target in enumerate(relatives):
            @pl.when(target // 2 == to_layer)
            def _():
                piece_copies[j].start()

    def hand_on(k):
        z_copy(k).wait_recv()
        far_copy(k).start()

    def arrived(first, last):
        for k in range(first, last):
            near_copy(k).wait_recv()
            far_copy(k).wait_recv()

    def gather_most():
        for k in range(n):
            x_copy(k).wait_recv()
            z_copy(k).start()
            near_copy(k).start()
            if k + DEPTH < n:
                x_copy(k).wait_send()
                x_copy(k + DEPTH).start()
            if k + DEPTH == n - 1:
                send_pieces(1)
            if k >= LAG:
                hand_on(k - LAG)
        arrived(0, ATTENTION_CHUNKS)
        own_copies[0].wait()
        own_copies[1].wait()

    def gather_rest():
        for k in range(n - LAG, n):
            hand_on(k)
        arrived(ATTENTION_CHUNKS, n)
        own_copies[2].wait()
        own_copies[3].wait()

    def y_copy(index):
        return remote(outgoing.at[index], slots.at[index], send.at[index], recv.at[index], (across_y, dp))

    def rows_of(index):
        return pl.ds(pl.multiple_of(index * block, 16), block)

    def result_copies(index):
        return [
            remote(
                results.at[target, rows_of(index)], results_out.at[pipe, rows_of(index)],
                result_send.at[j, index], result_recv.at[j, index], (target, dp),
            )
            for j, target in enumerate(relatives)
        ]

    def own_result(index):
        return pltpu.make_async_copy(
            results.at[pipe, rows_of(index)], results_out.at[pipe, rows_of(index)], result_sem.at[index]
        )

    def share_result(index, value):
        for i in range(PIPE):
            results[i, rows_of(index), :] = value[:, i * QUARTER : (i + 1) * QUARTER]
        for copy in result_copies(index):
            copy.start()
        own_result(index).start()

    def wait_results(index):
        final = index == micros - 1
        for j, copy in enumerate(result_copies(index)):
            if not final:
                copy.wait()
                continue

            @pl.when(layer == 1)
            def _():
                copy.wait_send()

            @pl.when(relatives[j] // 2 == 1)
            def _():
                copy.wait_recv()

        @pl.when((layer == 1) | (not final))
        def _():
            own_result(index).wait()

    rings = [
        (a0_ring, a0_hbm), (context_ring, context_hbm), (a1_ring, a1_hbm), (hidden_ring, hidden_hbm),
        (dr2_ring, dr2_hbm), (du_ring, du_hbm), (dr1_ring, dr1_hbm), (dqkv_ring, dqkv_hbm),
    ]

    def ring_copy(which, index):
        ring, target = rings[which]
        return pltpu.make_async_copy(ring.at[index % 2], target.at[rows_of(index)], ring_sem.at[which, index])

    def ring_slots(first, last, index):
        @pl.when(index >= 2)
        def _():
            for which in range(first, last):
                ring_copy(which, index - 2).wait()

        return [rings[which][0].at[index % 2] for which in range(first, last)]

    def ring_start(first, last, index):
        for which in range(first, last):
            ring_copy(which, index).start()

    def unpack_pieces():
        for copy in piece_copies:
            copy.wait_recv()
        unpacked[...] = pieces[...].reshape(D, rows).astype(F32).T.astype(BF)

    @pl.when(step == 0)
    def _():
        for copy in own_copies:
            copy.start()
        for t, source in enumerate((tokens, cotangent)):
            whole = source[...].astype(F32)
            spare = jnp.zeros((QUARTER, 2 * rows - whole.shape[1]), F32)
            both[t, 0] = whole[:, :rows].astype(BF)
            both[t, 1] = jnp.concatenate([whole[:, rows:], spare], 1).astype(BF)
        for i, source in enumerate((biases, offsets, scaling, centring, lifting, settling, stretch, translate)):
            own_vectors[i : i + 1, : source.shape[1]] = source[...].astype(F32)
        own_piece.start()
        sums_out[...] = jnp.zeros_like(sums_out)
        greet([(across_x, dp), (across_y, dp), (diagonal, dp), (pipe, across_z), (pipe, other_core)])
        vec_copy.start()

        send_pieces(0)
        for k in range(DEPTH):
            x_copy(k).start()
        vec_copy.wait_recv()
        for which in range(2):
            value = jnp.where(half == which, own_vectors[...], other_vectors[...])
            vectors[0:1, which * 3 * HALF : which * 3 * HALF + HALF] = value[0:1, :HALF]
            vectors[0:1, which * 3 * HALF + HALF : which * 3 * HALF + D] = jnp.zeros((1, HALF), F32)
            vectors[0:1, which * 3 * HALF + D : (which + 1) * 3 * HALF] = value[0:1, HALF:D]
            for i in (1, 2, 3, 5, 6, 7):
                vectors[i : i + 1, which * HALF : (which + 1) * HALF] = value[i : i + 1, :HALF]
            vectors[4:5, which * HIDDEN_HALF : (which + 1) * HIDDEN_HALF] = value[4:5, :]
        own_piece.wait()
        gather_most()

        @pl.when(layer == 1)
        def _():
            gather_rest()

    @pl.when(((layer == 0) & (step < micros)) | ((layer == 1) & (step % 2 == 0)))
    def _():
        micro = (1 - layer) * step + layer * (step // 2)
        a0_out, context_out, a1_out, hidden_out = ring_slots(0, 4, micro)

        @pl.when((layer == 0) & (micro == 0))
        def _():
            unpack_pieces()

        @pl.when(layer == 0)
        def _():
            a_s[...] = unpacked[rows_of(micro), :]

        @pl.when(layer == 1)
        def _():
            y_copy(micro).wait_recv()
            a_s[...] = slots[micro]

        inputs = a_s[...]
        a0_out[...] = inputs
        for which in range(2):
            value = dot_nn(inputs, joint[which]) + vectors[0:1, which * 3 * HALF : (which + 1) * 3 * HALF]
            for part in range(3):
                cols = slice(part * D + which * HALF, part * D + (which + 1) * HALF)
                found = value[:, part * HALF : (part + 1) * HALF]
                qkv_s[:, cols] = found
                qkv_keep[micro, :, cols] = found.astype(BF)
        over = [(pair, group) for pair in range(pairs) for group in range(GROUPS)]
        spans = [
            (
                slice(pair * PAIR_ROWS, (pair + 1) * PAIR_ROWS),
                [slice(part * D + group * GROUP_WIDTH, part * D + (group + 1) * GROUP_WIDTH) for part in range(3)],
            )
            for pair, group in over
        ]
        key = lax.broadcasted_iota(jnp.int32, (PAIR_ROWS, PAIR_ROWS), 0)
        masks = []
        for pair in range(pairs):
            length = captions[jnp.minimum((half * micros + micro) * pairs + pair, local_pairs - 1)]
            masks.append(jnp.where((key >= WORDS) | (key < length), 0.0, NEGATIVE))
        scores = [
            dot_nt(stacked(qkv_s[at, lanes[1]], SCALE), qkv_s[at, lanes[0]].astype(BF)) for at, lanes in spans
        ]
        values = [stacked(qkv_s[at, lanes[2]]) for at, lanes in spans]
        probs = []
        for k, (pair, group) in enumerate(over):
            found = []
            for i in range(2):
                score = scores[k][i * PAIR_ROWS : (i + 1) * PAIR_ROWS] + masks[pair]
                exponent = jnp.exp(score - jnp.max(score, axis=0, keepdims=True))
                found.append(exponent * (1.0 / jnp.sum(exponent, axis=0, keepdims=True)))
            probs.append(jnp.concatenate(found, 0).astype(BF))
        contexts = [dot_tn(probs[k], values[k]) for k in range(len(over))]
        for k, (at, lanes) in enumerate(spans):
            prob_keep[micro, k] = probs[k]
            context_s[at, lanes[0]] = contexts[k]
        context = context_s[...].astype(BF)
        context_out[...] = context
        residual = inputs.astype(F32) + dot_nn(context, mixing[...].reshape(D, D)) + vectors[1:2, :D]
        norm, inverse = normalized(residual)
        n1_keep[micro] = norm.astype(BF)
        r1_keep[micro] = inverse
        attended = (norm * vectors[2:3, :D] + vectors[3:4, :D]).astype(BF)
        a1_out[...] = attended

        @pl.when((micro == 0) & (layer == 0))
        def _():
            gather_rest()

        residual = attended.astype(F32) + vectors[5:6, :D]
        for which in range(2):
            cols = slice(which * HIDDEN_HALF, (which + 1) * HIDDEN_HALF)
            raised = dot_nn(attended, expand[which]) + vectors[4:5, cols]
            below = 0.5 * (1.0 + lax.erf(raised * (0.5**0.5)))
            hidden = (raised * below).astype(BF)
            hidden_out[:, cols] = hidden
            density = jnp.exp(raised * raised * (-0.5)) * 0.3989422804014327
            slope_keep[micro, :, cols] = (below + raised * density).astype(BF)
            residual = residual + dot_nn(hidden, reduce[which])
        norm, inverse = normalized(residual)
        n2_keep[micro] = norm.astype(BF)
        r2_keep[micro] = inverse
        result = (norm * vectors[6:7, :D] + vectors[7:8, :D]).astype(BF)

        @pl.when(layer == 0)
        def _():
            outgoing[micro] = result
            y_copy(micro).start()

        @pl.when(layer == 1)
        def _():
            share_result(micro, result)

        ring_start(0, 4, micro)

    def add_sum(row, value):
        width = value.shape[1]
        sums_out[row : row + 1, :width] += column_sums(value)

    @pl.when(((layer == 0) & (step >= micros)) | ((layer == 1) & (step % 2 == 1)))
    def _():
        micro = (1 - layer) * (step - micros) + layer * (step // 2)
        dr2_out, du_out, dr1_out, dqkv_out = ring_slots(4, 8, micro)

        @pl.when((layer == 1) & (micro == 0))
        def _():
            unpack_pieces()

        @pl.when(layer == 1)
        def _():
            a_s[...] = unpacked[rows_of(micro), :]

        @pl.when(layer == 0)
        def _():
            y_copy(micro).wait_recv()
            a_s[...] = slots[micro]

        gradient = a_s[...].astype(F32)
        norm = n2_keep[micro].astype(F32)
        add_sum(6, gradient * norm)
        add_sum(7, gradient)
        grad_residual = norm_backward(gradient, norm, r2_keep[micro], vectors[6:7, :D])
        add_sum(5, grad_residual)
        branch = grad_residual.astype(BF)
        dr2_out[...] = branch
        total = grad_residual
        for which in range(2):
            cols = slice(which * HIDDEN_HALF, (which + 1) * HIDDEN_HALF)
            raised = dot_nt(branch, reduce[which]) * slope_keep[micro, :, cols].astype(F32)
            sums_out[4:5, cols] += column_sums(raised)
            raised = raised.astype(BF)
            du_out[:, cols] = raised
            total = total + dot_nt(raised, expand[which])

        gradient = total.astype(BF).astype(F32)
        norm = n1_keep[micro].astype(F32)
        add_sum(2, gradient * norm)
        add_sum(3, gradient)
        grad_residual = norm_backward(gradient, norm, r1_keep[micro], vectors[2:3, :D])
        add_sum(1, grad_residual)
        branch = grad_residual.astype(BF)
        dr1_out[...] = branch
        context_s[...] = dot_nt(branch, mixing[...].reshape(D, D))
        qkv_s[...] = qkv_keep[micro].astype(F32)
        spans = [
            (
                slice(pair * PAIR_ROWS, (pair + 1) * PAIR_ROWS),
                [slice(part * D + group * GROUP_WIDTH, part * D + (group + 1) * GROUP_WIDTH) for part in range(3)],
            )
            for pair in range(pairs)
            for group in range(GROUPS)
        ]
        over = range(len(spans))
        queries = [qkv_s[at, lanes[0]].astype(BF) for at, lanes in spans]
        keys = [stacked(qkv_s[at, lanes[1]], SCALE) for at, lanes in spans]
        values = [stacked(qkv_s[at, lanes[2]]) for at, lanes in spans]
        grads = [context_s[at, lanes[0]].astype(BF) for at, lanes in spans]
        rounded = [prob_keep[micro, g] for g in over]
        grad_probs = [dot_nt(values[g], grads[g]) for g in over]
        grad_values = [dot_nn(rounded[g], grads[g]) for g in over]
        grad_scores = []
        for g in over:
            probs = rounded[g].astype(F32)
            weighted = probs * grad_probs[g]
            found = []
            for i in range(2):
                at = slice(i * PAIR_ROWS, (i + 1) * PAIR_ROWS)
                found.append(weighted[at] - probs[at] * column_sums(weighted[at]))
            grad_scores.append(jnp.concatenate(found, 0).astype(BF))
        grad_keys = [dot_nn(grad_scores[g], queries[g]) for g in over]
        grad_queries = [dot_tn(grad_scores[g], keys[g]) for g in over]
        for g, (at, lanes) in enumerate(spans):
            dqkv_s[at, lanes[0]] = grad_queries[g]
            dqkv_s[at, lanes[1]] = own_lanes(grad_keys[g]) * SCALE
            dqkv_s[at, lanes[2]] = own_lanes(grad_values[g])
        total = grad_residual
        for which in range(2):
            value = jnp.concatenate(
                [dqkv_s[:, part * D + which * HALF : part * D + (which + 1) * HALF] for part in range(3)], 1
            ).astype(BF)
            cols = slice(which * 3 * HALF, (which + 1) * 3 * HALF)
            dqkv_out[:, cols] = value
            sums_out[0:1, cols] += column_sums(value.astype(F32))
            total = total + dot_nt(value, joint[which])
        result = total.astype(BF)

        @pl.when(layer == 1)
        def _():
            outgoing[micro] = result
            y_copy(micro).start()

        ring_start(4, 8, micro)

        @pl.when((layer == 0) & (micro < micros - 1))
        def _():
            share_result(micro, result)

        @pl.when((layer == 0) & (micro == micros - 1))
        def _():
            for i in range(PIPE):
                last_out[i] = result[:, i * QUARTER : (i + 1) * QUARTER]

    @pl.when(step == 2 * micros - 1)
    def _():
        for index in range(micros):
            y_copy(index).wait_send()
            wait_results(index)
        for index in range(max(micros - 2, 0), micros):
            for which in range(8):
                ring_copy(which, index).wait()
        for k in range(n):
            if k + DEPTH >= n:
                x_copy(k).wait_send()
            z_copy(k).wait_send()
            near_copy(k).wait_send()
            far_copy(k).wait_send()
        for copy in piece_copies + [vec_copy]:
            copy.wait_send()


def layer_passes(micros, block, captions, small, tokens, cotangent, owned):
    rows = micros * block
    n = len(CHUNKS)
    vmem = pl.BlockSpec(memory_space=pltpu.VMEM)
    hbm = pl.BlockSpec(memory_space=pl.ANY)

    forward_widths = [D, D, D, FF]
    backward_widths = [D, FF, D, 3 * D]
    pairs = block // PAIR_ROWS
    return pl.pallas_call(
        functools.partial(layer_kernel, micros, block, captions.shape[0]),
        grid=(2 * micros,),
        out_shape=[jax.ShapeDtypeStruct((rows, w), BF) for w in forward_widths + backward_widths]
        + [
            jax.ShapeDtypeStruct((8, FF), F32),
            jax.ShapeDtypeStruct((PIPE, rows, QUARTER), BF),
            jax.ShapeDtypeStruct((PIPE, block, QUARTER), BF),
        ],
        in_specs=[pl.BlockSpec(memory_space=pltpu.SMEM)] + [vmem] * 10 + [hbm] * 4,
        out_specs=[hbm] * 8 + [vmem, hbm, vmem],
        scratch_shapes=[
            pltpu.VMEM((2, 2, QUARTER, rows), BF),
            pltpu.VMEM((8, HIDDEN_HALF), F32),
        ]
        + [pltpu.VMEM((2,) + shape, BF) for shape in WEIGHT_SHAPES]
        + [
            pltpu.VMEM((PIPE, QUARTER, rows), BF),
            pltpu.VMEM((rows, D), BF),
            pltpu.VMEM((8, HIDDEN_HALF), F32),
            pltpu.VMEM((8, FF), F32),
            pltpu.VMEM((PIPE, rows, QUARTER), BF),
            pltpu.VMEM((micros, block, D), BF),
            pltpu.VMEM((micros, block, D), BF),
            pltpu.VMEM((micros, block, 3 * D), BF),
            pltpu.VMEM((micros, pairs * GROUPS, STACKED, PAIR_ROWS), BF),
            pltpu.VMEM((micros, block, D), BF),
            pltpu.VMEM((micros, block, 1), F32),
            pltpu.VMEM((micros, block, D), BF),
            pltpu.VMEM((micros, block, 1), F32),
            pltpu.VMEM((micros, block, FF), BF),
            pltpu.VMEM((block, D), BF),
            pltpu.VMEM((block, 3 * D), F32),
            pltpu.VMEM((block, D), F32),
            pltpu.VMEM((block, 3 * D), F32),
        ]
        + [pltpu.VMEM((2, block, w), BF) for w in forward_widths + backward_widths]
        + [pltpu.SemaphoreType.DMA((micros,))] * 2
        + [pltpu.SemaphoreType.DMA((n,))] * 8
        + [
            pltpu.SemaphoreType.DMA((5,)),
            pltpu.SemaphoreType.DMA((3,)),
            pltpu.SemaphoreType.DMA((3,)),
            pltpu.SemaphoreType.DMA((2,)),
            pltpu.SemaphoreType.DMA((3, micros)),
            pltpu.SemaphoreType.DMA((3, micros)),
            pltpu.SemaphoreType.DMA((micros,)),
            pltpu.SemaphoreType.DMA((8, micros)),
        ],
        compiler_params=pltpu.CompilerParams(collective_id=1, has_side_effects=True, vmem_limit_bytes=VMEM_LIMIT),
        name="layer_passes",
    )(captions, tokens, cotangent, *small, *owned)


TILE = 384


def weights_kernel(
    n_dp,
    a0_in, dqkv_in, context_in, dr1_in, a1_in, du_in, hidden_in, dr2_in, sums, last,
    g_proj, g_comb, g_exp, g_red, sums_out, last_out,
    b_proj, b_comb, b_exp, b_red,
    c_proj, c_comb, c_exp, c_red,
    x_proj, x_comb, x_exp, x_red,
    p_proj, p_comb, p_exp, p_red,
    z_proj, z_comb, z_exp, z_red,
    sums_core, sums_x, sums_z, sums_a, sums_b, sums_c,
    a0, dqkv, context, dr1, a1, du, hidden, dr2,
    core_send, core_recv, x_send, x_recv, z_send, z_recv,
    small_send, small_recv, load_sem, last_send, last_recv,
):
    pipe, dp, layer, half, across_x, across_y, core, other_core = place()
    n_z = n_dp // 2
    z = dp // 2
    near_z = z + 1 - 2 * (z % 2)
    steps = n_z // 2
    z_order = [(near_z + 2 * (step + 1)) % n_z for step in range(steps - 1)] + [near_z]
    z_order += [(z + 2 * (step + 1)) % n_z for step in range(steps - 1)] + [z]
    same_parity = z_order[steps:-1]
    def hidden_lanes(h):
        return pl.ds(pl.multiple_of(h * HIDDEN_HALF, 128), HIDDEN_HALF)

    loads = [
        pltpu.make_async_copy(source, target, load_sem.at[i])
        for i, (source, target) in enumerate((
            (dr2_in, dr2),
            (hidden_in.at[:, hidden_lanes(1 - half)], hidden.at[:, hidden_lanes(1 - half)]),
            (hidden_in.at[:, hidden_lanes(half)], hidden.at[:, hidden_lanes(half)]),
            (a1_in, a1), (du_in, du), (a0_in, a0), (dqkv_in, dqkv), (context_in, context), (dr1_in, dr1),
        ))
    ]
    for copy in loads:
        copy.start()
    relatives = (across_x, across_y, (across_x + 2) % 4)
    greet(
        [(target, dp) for target in relatives] + [(pipe, other_core)]
        + [(pipe, 2 * other + core) for other in [near_z] + same_parity]
    )

    last_copies = [
        remote(last.at[target], last_out.at[half], last_send.at[j], last_recv.at[j], (target, dp))
        for j, target in enumerate(relatives)
    ]
    last_own = pltpu.make_async_copy(last.at[pipe], last_out.at[half], load_sem.at[9])

    @pl.when(layer == 0)
    def _():
        for copy in last_copies:
            copy.start()
        last_own.start()

    mine = [b_red, b_exp, b_proj, b_comb]
    from_core = [c_red, c_exp, c_proj, c_comb]
    from_x = [x_red, x_exp, x_proj, x_comb]
    from_pair = [p_red, p_exp, p_proj, p_comb]
    from_far = [z_red, z_exp, z_proj, z_comb]
    outs = [g_red, g_exp, g_proj, g_comb]

    def spread(target, tile, cast=BF):
        r = target.shape[-2]
        for k in range(tile.shape[0] // (2 * r)):
            for c in range(2):
                yield c, k, tile[(2 * k + c) * r : (2 * k + c + 1) * r].astype(cast)

    def fill_red(h, at):
        width = 2 * b_red.shape[3]
        lanes = pl.ds(pl.multiple_of(h * HIDDEN_HALF + at * width, 128), width)
        for c, k, rows in spread(b_red, dot_tn(hidden[:, lanes], dr2[...])):
            b_red[c, h, at] = rows

    def fill_exp(step, carry):
        i, h = step // 2, step % 2
        tile = dot_tn(
            a1[:, pl.ds(pl.multiple_of(i * TILE, 128), TILE)],
            du[:, pl.ds(pl.multiple_of(h * HIDDEN_HALF, 128), HIDDEN_HALF)],
        )
        for c, k, rows in spread(b_exp, tile):
            b_exp[c, h, i * (TILE // (2 * b_exp.shape[3])) + k] = rows
        return carry

    def fill_proj(h, carry):
        tile = dot_tn(a0[...], dqkv[:, pl.ds(pl.multiple_of(h * 3 * HALF, 128), 3 * HALF)])
        for c, k, rows in spread(b_proj, tile):
            b_proj[c, h, k] = rows
        return carry

    def fill_comb():
        tile = dot_tn(context[...], dr1[...])
        for h in range(2):
            for c, k, rows in spread(b_comb, tile[h * HALF : (h + 1) * HALF]):
                b_comb[c, h, k] = rows

    def core_copy(a, which, i):
        h = 1 - half if which == 0 else half
        at = z_order[i]
        return remote(
            mine[a].at[1 - core, h, at], from_core[a].at[h, at], core_send.at[a, which, i], core_recv.at[a, which, i],
            (pipe, other_core),
        )

    def send_core(a, which):
        for i in range(n_z):
            core_copy(a, which, i).start()

    def x_copy(k):
        a, i = chunks[k]
        return remote(
            mine[a].at[core, 1 - half, z_order[i]], from_x[a].at[z_order[i]], x_send.at[a, i], x_recv.at[a, i],
            (across_x, dp),
        )

    def pair_copy(a, i):
        return remote(
            mine[a].at[core, half, z_order[i]], from_pair[a].at[i], z_send.at[a, i], z_recv.at[a, i],
            (pipe, 2 * near_z + core),
        )

    def far_copy(a, i):
        other = same_parity[i]
        return remote(
            mine[a].at[core, half, other], from_far[a].at[i], z_send.at[a, steps + i], z_recv.at[a, steps + i],
            (pipe, 2 * other + core),
        )

    chunks = [(a, i) for a in range(4) for i in range(n_z)]

    def start_x(k):
        if k >= len(chunks):
            return
        a, i = chunks[k]
        at = z_order[i]
        core_copy(a, 0, i).wait_recv()
        total = mine[a][core, 1 - half, at].astype(F32) + from_core[a][1 - half, at].astype(F32)
        mine[a][core, 1 - half, at] = total.astype(BF)
        x_copy(k).start()

    def after_x(k):
        a, i = chunks[k]
        at = z_order[i]
        x_copy(k).wait()
        start_x(k + REDUCE_DEPTH)
        core_copy(a, 1, i).wait_recv()
        total = mine[a][core, half, at].astype(F32) + from_core[a][half, at].astype(F32) + from_x[a][at].astype(F32)
        if i < steps:
            mine[a][core, half, at] = total.astype(BF)
            pair_copy(a, i).start()
            return
        pair_copy(a, i - steps).wait_recv()
        total = total + from_pair[a][i - steps].astype(F32)
        if i < n_z - 1:
            mine[a][core, half, at] = total.astype(BF)
            far_copy(a, i - steps).start()
        else:
            outs[a][...] = total

    def after_z(a):
        total = outs[a][...]
        for i in range(steps - 1):
            far_copy(a, i).wait()
            total = total + from_far[a][i].astype(F32)
        outs[a][...] = total
        for i in range(steps):
            pair_copy(a, i).wait_send()

    sums_copy_core = remote(sums, sums_core, small_send.at[0], small_recv.at[0], (pipe, other_core))
    sums_copy_x = remote(sums_a, sums_x, small_send.at[1], small_recv.at[1], (across_x, dp))
    sums_copy_pair = remote(
        sums_b, sums_z.at[steps - 1], small_send.at[2], small_recv.at[2], (pipe, 2 * near_z + core)
    )
    sums_copies_far = [
        remote(sums_c, sums_z.at[i], small_send.at[3 + i], small_recv.at[3 + i], (pipe, 2 * other + core))
        for i, other in enumerate(same_parity)
    ]

    sums_copy_core.start()
    loads[0].wait()
    loads[1].wait()
    for i in range(n_z):
        fill_red(1 - half, z_order[i])
        core_copy(0, 0, i).start()
        if 1 <= i <= REDUCE_DEPTH:
            start_x(i - 1)
    loads[2].wait()
    for i in range(n_z):
        fill_red(half, z_order[i])
        core_copy(0, 1, i).start()
    loads[3].wait()
    loads[4].wait()
    lax.fori_loop(0, 2 * D // TILE, fill_exp, 0)
    send_core(1, 0)
    send_core(1, 1)
    sums_copy_core.wait()
    sums_a[...] = sums[...] + sums_core[...]
    sums_copy_x.start()
    after_x(0)
    loads[5].wait()
    loads[6].wait()
    lax.fori_loop(0, 2, fill_proj, 0)
    send_core(2, 0)
    send_core(2, 1)
    after_x(1)
    loads[7].wait()
    loads[8].wait()
    fill_comb()
    send_core(3, 0)
    send_core(3, 1)
    sums_copy_x.wait()
    sums_b[...] = sums_a[...] + sums_x[...]
    sums_copy_pair.start()
    for k in range(2, len(chunks)):
        after_x(k)
        if k == n_z:
            sums_copy_pair.wait()
            sums_c[...] = sums_b[...] + sums_z[steps - 1]
            for copy in sums_copies_far:
                copy.start()
        if k % n_z == n_z - 2 and k >= n_z:
            after_z(k // n_z - 1)
    after_z(3)
    for a in range(4):
        for which in range(2):
            for i in range(n_z):
                core_copy(a, which, i).wait_send()
    total = sums_c[...]
    for i in range(steps - 1):
        sums_copies_far[i].wait()
        total = total + sums_z[i]
    sums_out[...] = total

    @pl.when(layer == 0)
    def _():
        for copy in last_copies:
            copy.wait_send()
        last_own.wait()

    for j, source in enumerate(relatives):
        @pl.when(source // 2 == 0)
        def _():
            last_copies[j].wait_recv()


def weight_gradients(n_dp, a0, dqkv, context, dr1, a1, du, hidden, dr2, sums, last):
    vmem = pl.BlockSpec(memory_space=pltpu.VMEM)
    hbm = pl.BlockSpec(memory_space=pl.ANY)
    n_z = n_dp // 2
    shapes = [(D // n_dp, 3 * HALF), (HALF // n_dp, D), (D // n_dp, HIDDEN_HALF), (HIDDEN_HALF // n_dp, D)]
    return pl.pallas_call(
        functools.partial(weights_kernel, n_dp),
        out_shape=[jax.ShapeDtypeStruct(s, F32) for s in shapes]
        + [jax.ShapeDtypeStruct(sums.shape, F32), jax.ShapeDtypeStruct((2,) + last.shape[1:], BF)],
        in_specs=[hbm] * 8 + [vmem, hbm],
        out_specs=[vmem] * 5 + [hbm],
        scratch_shapes=[pltpu.VMEM((2, 2, n_z) + s, BF) for s in shapes]
        + [pltpu.VMEM((2, n_z) + s, BF) for s in shapes]
        + [pltpu.VMEM((n_z,) + s, BF) for s in shapes]
        + [pltpu.VMEM((n_z // 2,) + s, BF) for s in shapes]
        + [pltpu.VMEM((max(n_z // 2 - 1, 1),) + s, BF) for s in shapes]
        + [
            pltpu.VMEM(sums.shape, F32),
            pltpu.VMEM(sums.shape, F32),
            pltpu.VMEM((n_z // 2,) + sums.shape, F32),
            pltpu.VMEM(sums.shape, F32),
            pltpu.VMEM(sums.shape, F32),
            pltpu.VMEM(sums.shape, F32),
        ]
        + [pltpu.VMEM(v.shape, BF) for v in (a0, dqkv, context, dr1, a1, du, hidden, dr2)]
        + [
            pltpu.SemaphoreType.DMA((4, 2, n_z)),
            pltpu.SemaphoreType.DMA((4, 2, n_z)),
            pltpu.SemaphoreType.DMA((4, n_z)),
            pltpu.SemaphoreType.DMA((4, n_z)),
            pltpu.SemaphoreType.DMA((4, n_z - 1)),
            pltpu.SemaphoreType.DMA((4, n_z - 1)),
            pltpu.SemaphoreType.DMA((n_z + 1,)),
            pltpu.SemaphoreType.DMA((n_z + 1,)),
            pltpu.SemaphoreType.DMA((10,)),
            pltpu.SemaphoreType.DMA((3,)),
            pltpu.SemaphoreType.DMA((3,)),
        ],
        compiler_params=pltpu.CompilerParams(collective_id=3, has_side_effects=True, vmem_limit_bytes=VMEM_LIMIT),
        name="weight_gradients",
    )(a0, dqkv, context, dr1, a1, du, hidden, dr2, sums, last)


def finish_kernel(n_dp, small, results, last, *refs):
    pipe, dp, layer, half, across_x, across_y, core, other_core = place()
    sources, encoded, tokens_grad, outs, parts = refs[:4], refs[4], refs[5], refs[6:10], refs[10:]
    for source, out in zip(sources, outs):
        out[0] = source[...]
    for first, out in ((0, tokens_grad), (2, encoded)):
        parts_of = []
        for i in (first, first + 1):
            if first == 0:
                parts_of += [results[i, : results.shape[1] - last.shape[1], :], last[i]]
            else:
                parts_of.append(results[i])
        value = jnp.concatenate(parts_of, 0).astype(F32).T
        out[...] = value[:, : out.shape[1]].astype(out.dtype)
    for row, out in enumerate(parts):
        count = out.shape[1]
        width = n_dp * count
        found = jnp.zeros(out.shape, F32)
        for h in range(2):
            for d in range(n_dp):
                at = d * count
                if row == 0:
                    at = h * 3 * HALF + at + (HALF if at >= HALF else 0)
                else:
                    at = h * width + at
                found = jnp.where((half == h) & (dp == d), small[row : row + 1, at : at + count], found)
        out[...] = found


def finish(n_dp, local_rows, small, results, last, grads):
    vmem = pl.BlockSpec(memory_space=pltpu.VMEM)
    widths = [D, HALF, HALF, HALF, HIDDEN_HALF, HALF, HALF, HALF]
    return pl.pallas_call(
        functools.partial(finish_kernel, n_dp),
        out_shape=[
            jax.ShapeDtypeStruct((QUARTER, local_rows), BF),
            jax.ShapeDtypeStruct((QUARTER, local_rows), F32),
        ]
        + [jax.ShapeDtypeStruct((1,) + g.shape, F32) for g in grads]
        + [jax.ShapeDtypeStruct((1, w // n_dp), F32) for w in widths],
        in_specs=[vmem] * 7,
        out_specs=[vmem] * 14,
        compiler_params=pltpu.CompilerParams(vmem_limit_bytes=VMEM_LIMIT),
        name="finish",
    )(small, results, last, *grads)


def weight_gradients_by_scatter(n_dp, a0, dqkv, context, dr1, a1, du, hidden, dr2, sums, last):
    half = lax.axis_index("pipe") % 2
    halves = (
        dot_tn(a0, dqkv).reshape(D, 2, 3 * HALF).transpose(1, 0, 2),
        dot_tn(context, dr1).reshape(2, HALF, D),
        dot_tn(a1, du).reshape(D, 2, HIDDEN_HALF).transpose(1, 0, 2),
        dot_tn(hidden, dr2).reshape(2, HIDDEN_HALF, D),
    )
    swap = [(i, i ^ 1) for i in range(PIPE)]
    found = []
    for member in halves:
        part = lax.psum_scatter(member, "dp", scatter_dimension=1, tiled=True)
        keep = lax.dynamic_index_in_dim(part, half, 0, keepdims=False)
        send = lax.dynamic_index_in_dim(part, 1 - half, 0, keepdims=False)
        found.append(keep + lax.ppermute(send.astype(BF), "pipe", swap).astype(F32))
    small = lax.psum(sums, "dp")
    received = lax.all_to_all(last, "pipe", 0, 0, tiled=False)
    return found + [small + lax.ppermute(small, "pipe", swap), received[:2]]


def shards(
    n_dp,
    tokens, cotangent, captions, projection, biases, combiner, offsets, scaling, centring,
    expansion, lifting, reduction, settling, stretch, translate,
):
    local_rows = tokens.shape[0]
    local_pairs = local_rows // PAIR_ROWS
    pairs = 2 * ((local_pairs + 3) // 4)
    block = 2 * PAIR_ROWS
    micros = pairs // 2
    owned = (projection[0], combiner[0], expansion[0], reduction[0])
    small = (biases, offsets, scaling, centring, lifting, settling, stretch, translate)
    *kept, results, last = layer_passes(micros, block, captions, small, tokens.T, cotangent.T, owned)
    a0, context, a1, hidden, dr2, du, dr1, dqkv, sums = kept
    whole_tiles = HALF % (16 * n_dp) == 0
    collect = weight_gradients if whole_tiles else weight_gradients_by_scatter
    *grads, sums, last = collect(n_dp, a0, dqkv, context, dr1, a1, du, hidden, dr2, sums, last)
    encoded, tokens_grad, g_proj, g_comb, g_exp, g_red, *parts = finish(n_dp, local_rows, sums, results, last, grads)
    return (
        encoded.T, tokens_grad.T, g_proj, parts[0], g_comb, parts[1], parts[2], parts[3],
        g_exp, parts[4], g_red, parts[5], parts[6], parts[7],
    )


def solution(mesh):
    rows = P("dp", "pipe")
    matrix = P("pipe", None, None)
    vector = P("pipe", None)
    matrix_out = P("pipe", "dp", None)
    vector_out = P("pipe", "dp")
    in_specs = (
        rows, rows, P("dp"), matrix, vector, matrix, vector, vector, vector,
        matrix, vector, matrix, vector, vector, vector,
    )
    out_specs = (
        rows, rows, matrix_out, vector_out, matrix_out, vector_out, vector_out, vector_out,
        matrix_out, vector_out, matrix_out, vector_out, vector_out, vector_out,
    )
    return jax.shard_map(
        functools.partial(shards, mesh.shape["dp"]),
        mesh=mesh, in_specs=in_specs, out_specs=out_specs, check_vma=False,
    )
```

```python
import functools

import jax
import jax.numpy as jnp
from jax import lax
from jax.experimental import pallas as pl
from jax.experimental.pallas import tpu as pltpu
from jax.sharding import PartitionSpec as P

D = 768
HEADS = 12
HEAD_DIM = 64
FF = 3072
WORDS = 64
PAIR_ROWS = 104
HALF = D // 2
HIDDEN_HALF = FF // 2
QUARTER = D // 4
PIPE = 4
GROUP_WIDTH = 2 * HEAD_DIM
GROUPS = HEADS // 2
STACKED = 2 * PAIR_ROWS

EPSILON = 1e-05
NEGATIVE = -1e30
SCALE = HEAD_DIM ** (-0.5)

MESH = pl.DeviceIdType.MESH
BF = jnp.bfloat16
F32 = jnp.float32
VMEM_LIMIT = 60 << 20


def dot_nn(left, right):
    return lax.dot_general(left, right, (((1,), (0,)), ((), ())), preferred_element_type=F32)


def dot_nt(left, right):
    return lax.dot_general(left, right, (((1,), (1,)), ((), ())), preferred_element_type=F32)


def dot_tn(left, right):
    return lax.dot_general(left, right, (((0,), (0,)), ((), ())), preferred_element_type=F32)


def place():
    pipe = lax.axis_index("pipe")
    dp = lax.axis_index("dp")
    layer = pipe // 2
    half = pipe % 2
    across_x = pipe + 1 - 2 * half
    across_y = (pipe + 2) % 4
    core = dp % 2
    other_core = dp + 1 - 2 * core
    return pipe, dp, layer, half, across_x, across_y, core, other_core


def greet(devices):
    barrier = pltpu.get_barrier_semaphore()
    for device in devices:
        pl.semaphore_signal(barrier, inc=1, device_id=device, device_id_type=MESH)
    pl.semaphore_wait(barrier, len(devices))


def remote(source, target, send, recv, device):
    return pltpu.make_async_remote_copy(
        src_ref=source,
        dst_ref=target,
        send_sem=send,
        recv_sem=recv,
        device_id=device,
        device_id_type=MESH,
    )


WEIGHT_SHAPES = [(D, 3 * HALF), (HALF, D), (D, HIDDEN_HALF), (HIDDEN_HALF, D)]
CHUNKS = [(0, 0, 96), (0, 96, 96), (1, 0, 96)] + [(2, i*48, 48) for i in range(4)] + [(3, i*96, 96) for i in range(4)]
ATTENTION_CHUNKS = 3
FIRST_LANES = 256
DEPTH = 3
LAG = 2
REDUCE_DEPTH = 3
LOW_AT = (4, 7)


def left_lanes():
    return lax.broadcasted_iota(jnp.int32, (PAIR_ROWS, GROUP_WIDTH), 1) < HEAD_DIM


def stacked(values, scale=None):
    if scale is not None:
        values = values * scale
    left = left_lanes()
    return jnp.concatenate([jnp.where(left, values, 0.0), jnp.where(left, 0.0, values)], 0).astype(BF)


def own_lanes(values):
    return jnp.where(left_lanes(), values[:PAIR_ROWS], values[PAIR_ROWS:])


def normalized(residual):
    average = jnp.mean(residual, axis=-1, keepdims=True)
    centred = residual - average
    variance = jnp.mean(centred * centred, axis=-1, keepdims=True)
    inverse = lax.rsqrt(variance + EPSILON)
    return centred * inverse, inverse


def norm_backward(gradient, norm, inverse, gain):
    scaled = gradient * gain
    first = jnp.mean(scaled, axis=-1, keepdims=True)
    second = jnp.mean(scaled * norm, axis=-1, keepdims=True)
    return (scaled - first - norm * second) * inverse


def column_sums(value):
    return jnp.sum(value, axis=0, keepdims=True)


def layer_kernel(
    micros, block, local_pairs,
    captions, tokens, cotangent, biases, offsets, scaling, centring, lifting, settling, stretch, translate,
    own_proj, own_comb, own_exp, own_red,
    a0_hbm, context_hbm, a1_hbm, hidden_hbm, dr2_hbm, du_hbm, dr1_hbm, dqkv_hbm, sums_out, results_out, last_out,
    both, own_vectors, joint, mixing, expand, reduce, pieces, unpacked, other_vectors, vectors, results,
    slots, outgoing, qkv_keep, prob_keep, n1_keep, r1_keep, n2_keep, r2_keep, slope_keep,
    a_s, qkv_s, context_s, dqkv_s,
    a0_ring, context_ring, a1_ring, hidden_ring, dr2_ring, du_ring, dr1_ring, dqkv_ring,
    send, recv, x_send, x_recv, z_send, z_recv, near_send, near_recv, far_send, far_recv,
    own_sem, piece_send, piece_recv, vec_sem, result_send, result_recv, result_sem, ring_sem,
):
    pipe, dp, layer, half, across_x, across_y, core, other_core = place()
    step = pl.program_id(0)
    pairs = block // PAIR_ROWS
    rows = micros * block
    diagonal = (across_x + 2) % 4
    parity = (dp // 2) % 2
    across_z = dp + 2 - 4 * parity
    mine = 2 * parity + core
    paired = 2 * (1 - parity) + core
    relatives = (across_x, across_y, diagonal)
    owned = [own_proj, own_comb, own_exp, own_red]
    held = [joint, mixing, expand, reduce]
    n = len(CHUNKS)

    def span(chunk, quarter):
        which, start, count = chunk
        return pl.ds(quarter * (WEIGHT_SHAPES[which][0] // 4) + start, count)

    def x_copy(k):
        at = span(CHUNKS[k], mine)
        which = CHUNKS[k][0]
        return remote(owned[which].at[at], held[which].at[half, at], x_send.at[k], x_recv.at[k], (across_x, dp))

    def z_copy(k):
        region = held[CHUNKS[k][0]].at[1 - half, span(CHUNKS[k], mine)]
        return remote(region, region, z_send.at[k], z_recv.at[k], (pipe, across_z))

    def near_copy(k):
        region = held[CHUNKS[k][0]].at[1 - half, span(CHUNKS[k], mine)]
        return remote(region, region, near_send.at[k], near_recv.at[k], (pipe, other_core))

    def far_copy(k):
        region = held[CHUNKS[k][0]].at[1 - half, span(CHUNKS[k], paired)]
        return remote(region, region, far_send.at[k], far_recv.at[k], (pipe, other_core))

    own_copies = [pltpu.make_async_copy(owned[i], held[i].at[half], own_sem.at[i]) for i in range(4)]
    own_piece = pltpu.make_async_copy(both.at[layer, half], pieces.at[pipe], own_sem.at[4])
    lanes_held = both.shape[3]
    lanes_of = (pl.ds(0, FIRST_LANES), pl.ds(FIRST_LANES, lanes_held - FIRST_LANES))
    vec_copy = remote(own_vectors, other_vectors, vec_sem.at[0], vec_sem.at[1], (across_x, dp))
    piece_copies = [
        [
            remote(
                both.at[target // 2, target % 2, :, lanes], pieces.at[pipe, :, lanes],
                piece_send.at[part, j], piece_recv.at[part, j], (target, dp),
            )
            for j, target in enumerate(relatives)
        ]
        for part, lanes in enumerate(lanes_of)
    ]

    def send_pieces(to_layer, part):
        for j, target in enumerate(relatives):
            @pl.when(target // 2 == to_layer)
            def _():
                piece_copies[part][j].start()

    def hand_on(k):
        z_copy(k).wait_recv()
        far_copy(k).start()

    def arrived(first, last):
        for k in range(first, last):
            near_copy(k).wait_recv()
            far_copy(k).wait_recv()

    def gather_most():
        for k in range(n):
            x_copy(k).wait_recv()
            z_copy(k).start()
            near_copy(k).start()
            if k + DEPTH < n:
                x_copy(k).wait_send()
                x_copy(k + DEPTH).start()
            if k + DEPTH == n - 1:
                send_pieces(0, 1)
                send_pieces(1, 0)
                send_pieces(1, 1)
            if k >= LAG:
                hand_on(k - LAG)
        arrived(0, ATTENTION_CHUNKS)
        own_copies[0].wait()
        own_copies[1].wait()

    def gather_rest():
        for k in range(n - LAG, n):
            hand_on(k)
        arrived(ATTENTION_CHUNKS, n)
        own_copies[2].wait()
        own_copies[3].wait()

    def y_copy(index):
        return remote(outgoing.at[index], slots.at[index], send.at[index], recv.at[index], (across_y, dp))

    def rows_of(index):
        return pl.ds(pl.multiple_of(index * block, 16), block)

    def result_copies(index):
        return [
            remote(
                results.at[target, rows_of(index)], results_out.at[pipe, rows_of(index)],
                result_send.at[j, index], result_recv.at[j, index], (target, dp),
            )
            for j, target in enumerate(relatives)
        ]

    def own_result(index):
        return pltpu.make_async_copy(
            results.at[pipe, rows_of(index)], results_out.at[pipe, rows_of(index)], result_sem.at[index]
        )

    def share_result(index, value):
        for i in range(PIPE):
            results[i, rows_of(index), :] = value[:, i * QUARTER : (i + 1) * QUARTER]
        for copy in result_copies(index):
            copy.start()
        own_result(index).start()

    def wait_results(index):
        final = index == micros - 1
        for j, copy in enumerate(result_copies(index)):
            if not final:
                copy.wait()
                continue

            @pl.when(layer == 1)
            def _():
                copy.wait_send()

            @pl.when(relatives[j] // 2 == 1)
            def _():
                copy.wait_recv()

        @pl.when((layer == 1) | (not final))
        def _():
            own_result(index).wait()

    rings = [
        (a0_ring, a0_hbm), (context_ring, context_hbm), (a1_ring, a1_hbm), (hidden_ring, hidden_hbm),
        (dr2_ring, dr2_hbm), (du_ring, du_hbm), (dr1_ring, dr1_hbm), (dqkv_ring, dqkv_hbm),
    ]

    def ring_copy(which, index):
        ring, target = rings[which]
        return pltpu.make_async_copy(ring.at[index % 2], target.at[rows_of(index)], ring_sem.at[which, index])

    def ring_slots(first, last, index):
        @pl.when(index >= 2)
        def _():
            for which in range(first, last):
                ring_copy(which, index - 2).wait()

        return [rings[which][0].at[index % 2] for which in range(first, last)]

    def ring_start(first, last, index):
        for which in range(first, last):
            ring_copy(which, index).start()

    def unpack_pieces(part):
        for copy in piece_copies[part]:
            copy.wait_recv()
        at = lanes_of[part]
        value = pieces[:, :, at.start : at.start + at.size].reshape(D, at.size)
        unpacked[at.start : at.start + at.size, :] = value.astype(F32).T.astype(BF)

    @pl.when(step == 0)
    def _():
        for copy in own_copies:
            copy.start()
        for t, source in enumerate((tokens, cotangent)):
            whole = source[...].astype(F32)
            for h in range(2):
                value = whole[:, h * rows : (h + 1) * rows]
                spare = jnp.zeros((QUARTER, lanes_held - value.shape[1]), F32)
                both[t, h] = jnp.concatenate([value, spare], 1).astype(BF)
        for i, source in enumerate((biases, offsets, scaling, centring, lifting, settling, stretch, translate)):
            own_vectors[i : i + 1, : source.shape[1]] = source[...].astype(F32)
        own_piece.start()
        sums_out[...] = jnp.zeros_like(sums_out)
        greet([(across_x, dp), (across_y, dp), (diagonal, dp), (pipe, across_z), (pipe, other_core)])
        vec_copy.start()

        send_pieces(0, 0)
        for k in range(DEPTH):
            x_copy(k).start()
        vec_copy.wait_recv()
        for which in range(2):
            value = jnp.where(half == which, own_vectors[...], other_vectors[...])
            vectors[0:1, which * 3 * HALF : which * 3 * HALF + HALF] = value[0:1, :HALF]
            vectors[0:1, which * 3 * HALF + HALF : which * 3 * HALF + D] = jnp.zeros((1, HALF), F32)
            vectors[0:1, which * 3 * HALF + D : (which + 1) * 3 * HALF] = value[0:1, HALF:D]
            for i in (1, 2, 3, 5, 6, 7):
                vectors[i : i + 1, which * HALF : (which + 1) * HALF] = value[i : i + 1, :HALF]
            vectors[4:5, which * HIDDEN_HALF : (which + 1) * HIDDEN_HALF] = value[4:5, :]
        own_piece.wait()
        gather_most()

        @pl.when(layer == 1)
        def _():
            gather_rest()

    @pl.when(((layer == 0) & (step < micros)) | ((layer == 1) & (step % 2 == 0)))
    def _():
        micro = (1 - layer) * step + layer * (step // 2)
        a0_out, context_out, a1_out, hidden_out = ring_slots(0, 4, micro)

        for part in range(2):
            @pl.when((layer == 0) & (micro == part))
            def _():
                unpack_pieces(part)

        @pl.when(layer == 0)
        def _():
            a_s[...] = unpacked[rows_of(micro), :]

        @pl.when(layer == 1)
        def _():
            y_copy(micro).wait_recv()
            a_s[...] = slots[micro]

        inputs = a_s[...]
        a0_out[...] = inputs
        for which in range(2):
            value = dot_nn(inputs, joint[which]) + vectors[0:1, which * 3 * HALF : (which + 1) * 3 * HALF]
            for part in range(3):
                cols = slice(part * D + which * HALF, part * D + (which + 1) * HALF)
                found = value[:, part * HALF : (part + 1) * HALF]
                qkv_s[:, cols] = found
                qkv_keep[micro, :, cols] = found.astype(BF)
        over = [(pair, group) for pair in range(pairs) for group in range(GROUPS)]
        spans = [
            (
                slice(pair * PAIR_ROWS, (pair + 1) * PAIR_ROWS),
                [slice(part * D + group * GROUP_WIDTH, part * D + (group + 1) * GROUP_WIDTH) for part in range(3)],
            )
            for pair, group in over
        ]
        key = lax.broadcasted_iota(jnp.int32, (PAIR_ROWS, PAIR_ROWS), 0)
        masks = []
        for pair in range(pairs):
            length = captions[jnp.minimum((half * micros + micro) * pairs + pair, local_pairs - 1)]
            masks.append(jnp.where((key >= WORDS) | (key < length), 0.0, NEGATIVE))
        scores = [
            dot_nt(stacked(qkv_s[at, lanes[1]], SCALE), qkv_s[at, lanes[0]].astype(BF)) for at, lanes in spans
        ]
        values = [stacked(qkv_s[at, lanes[2]]) for at, lanes in spans]
        probs = []
        for k, (pair, group) in enumerate(over):
            found = []
            for i in range(2):
                score = scores[k][i * PAIR_ROWS : (i + 1) * PAIR_ROWS] + masks[pair]
                exponent = jnp.exp(score - jnp.max(score, axis=0, keepdims=True))
                found.append(exponent * (1.0 / jnp.sum(exponent, axis=0, keepdims=True)))
            probs.append(jnp.concatenate(found, 0).astype(BF))
        contexts = [dot_tn(probs[k], values[k]) for k in range(len(over))]
        for k, (at, lanes) in enumerate(spans):
            prob_keep[micro, k] = probs[k]
            context_s[at, lanes[0]] = contexts[k]
        context = context_s[...].astype(BF)
        context_out[...] = context
        residual = inputs.astype(F32) + dot_nn(context, mixing[...].reshape(D, D)) + vectors[1:2, :D]
        norm, inverse = normalized(residual)
        n1_keep[micro] = norm.astype(BF)
        r1_keep[micro] = inverse
        attended = (norm * vectors[2:3, :D] + vectors[3:4, :D]).astype(BF)
        a1_out[...] = attended

        @pl.when((micro == 0) & (layer == 0))
        def _():
            gather_rest()

        residual = attended.astype(F32) + vectors[5:6, :D]
        for which in range(2):
            cols = slice(which * HIDDEN_HALF, (which + 1) * HIDDEN_HALF)
            raised = dot_nn(attended, expand[which]) + vectors[4:5, cols]
            below = 0.5 * (1.0 + lax.erf(raised * (0.5**0.5)))
            hidden = (raised * below).astype(BF)
            hidden_out[:, cols] = hidden
            density = jnp.exp(raised * raised * (-0.5)) * 0.3989422804014327
            slope_keep[micro, :, cols] = (below + raised * density).astype(BF)
            residual = residual + dot_nn(hidden, reduce[which])
        norm, inverse = normalized(residual)
        n2_keep[micro] = norm.astype(BF)
        r2_keep[micro] = inverse
        result = (norm * vectors[6:7, :D] + vectors[7:8, :D]).astype(BF)

        @pl.when(layer == 0)
        def _():
            outgoing[micro] = result
            y_copy(micro).start()

        @pl.when(layer == 1)
        def _():
            share_result(micro, result)

        ring_start(0, 4, micro)

    def add_sum(row, value):
        width = value.shape[1]
        sums_out[row : row + 1, :width] += column_sums(value)

    @pl.when(((layer == 0) & (step >= micros)) | ((layer == 1) & (step % 2 == 1)))
    def _():
        micro = (1 - layer) * (step - micros) + layer * (step // 2)
        dr2_out, du_out, dr1_out, dqkv_out = ring_slots(4, 8, micro)

        @pl.when((layer == 1) & (micro == 0))
        def _():
            unpack_pieces(0)
            unpack_pieces(1)

        @pl.when(layer == 1)
        def _():
            a_s[...] = unpacked[rows_of(micro), :]

        @pl.when(layer == 0)
        def _():
            y_copy(micro).wait_recv()
            a_s[...] = slots[micro]

        gradient = a_s[...].astype(F32)
        norm = n2_keep[micro].astype(F32)
        add_sum(6, gradient * norm)
        add_sum(7, gradient)
        grad_residual = norm_backward(gradient, norm, r2_keep[micro], vectors[6:7, :D])
        add_sum(5, grad_residual)
        branch = grad_residual.astype(BF)
        dr2_out[...] = branch
        total = grad_residual
        for which in range(2):
            cols = slice(which * HIDDEN_HALF, (which + 1) * HIDDEN_HALF)
            raised = dot_nt(branch, reduce[which]) * slope_keep[micro, :, cols].astype(F32)
            sums_out[4:5, cols] += column_sums(raised)
            raised = raised.astype(BF)
            du_out[:, cols] = raised
            total = total + dot_nt(raised, expand[which])

        gradient = total.astype(BF).astype(F32)
        norm = n1_keep[micro].astype(F32)
        add_sum(2, gradient * norm)
        add_sum(3, gradient)
        grad_residual = norm_backward(gradient, norm, r1_keep[micro], vectors[2:3, :D])
        add_sum(1, grad_residual)
        branch = grad_residual.astype(BF)
        dr1_out[...] = branch
        context_s[...] = dot_nt(branch, mixing[...].reshape(D, D))
        qkv_s[...] = qkv_keep[micro].astype(F32)
        spans = [
            (
                slice(pair * PAIR_ROWS, (pair + 1) * PAIR_ROWS),
                [slice(part * D + group * GROUP_WIDTH, part * D + (group + 1) * GROUP_WIDTH) for part in range(3)],
            )
            for pair in range(pairs)
            for group in range(GROUPS)
        ]
        over = range(len(spans))
        queries = [qkv_s[at, lanes[0]].astype(BF) for at, lanes in spans]
        keys = [stacked(qkv_s[at, lanes[1]], SCALE) for at, lanes in spans]
        values = [stacked(qkv_s[at, lanes[2]]) for at, lanes in spans]
        grads = [context_s[at, lanes[0]].astype(BF) for at, lanes in spans]
        rounded = [prob_keep[micro, g] for g in over]
        grad_probs = [dot_nt(values[g], grads[g]) for g in over]
        grad_values = [dot_nn(rounded[g], grads[g]) for g in over]
        grad_scores = []
        for g in over:
            probs = rounded[g].astype(F32)
            weighted = probs * grad_probs[g]
            found = []
            for i in range(2):
                at = slice(i * PAIR_ROWS, (i + 1) * PAIR_ROWS)
                found.append(weighted[at] - probs[at] * column_sums(weighted[at]))
            grad_scores.append(jnp.concatenate(found, 0).astype(BF))
        grad_keys = [dot_nn(grad_scores[g], queries[g]) for g in over]
        grad_queries = [dot_tn(grad_scores[g], keys[g]) for g in over]
        for g, (at, lanes) in enumerate(spans):
            dqkv_s[at, lanes[0]] = grad_queries[g]
            dqkv_s[at, lanes[1]] = own_lanes(grad_keys[g]) * SCALE
            dqkv_s[at, lanes[2]] = own_lanes(grad_values[g])
        total = grad_residual
        for which in range(2):
            value = jnp.concatenate(
                [dqkv_s[:, part * D + which * HALF : part * D + (which + 1) * HALF] for part in range(3)], 1
            ).astype(BF)
            cols = slice(which * 3 * HALF, (which + 1) * 3 * HALF)
            dqkv_out[:, cols] = value
            sums_out[0:1, cols] += column_sums(value.astype(F32))
            total = total + dot_nt(value, joint[which])
        result = total.astype(BF)

        @pl.when(layer == 1)
        def _():
            outgoing[micro] = result
            y_copy(micro).start()

        ring_start(4, 8, micro)

        @pl.when((layer == 0) & (micro < micros - 1))
        def _():
            share_result(micro, result)

        @pl.when((layer == 0) & (micro == micros - 1))
        def _():
            for i in range(PIPE):
                last_out[i] = result[:, i * QUARTER : (i + 1) * QUARTER]

    @pl.when(step == 2 * micros - 1)
    def _():
        for index in range(micros):
            y_copy(index).wait_send()
            wait_results(index)
        for index in range(max(micros - 2, 0), micros):
            for which in range(8):
                ring_copy(which, index).wait()
        for k in range(n):
            if k + DEPTH >= n:
                x_copy(k).wait_send()
            z_copy(k).wait_send()
            near_copy(k).wait_send()
            far_copy(k).wait_send()
        for copy in piece_copies[0] + piece_copies[1] + [vec_copy]:
            copy.wait_send()


def layer_passes(micros, block, captions, small, tokens, cotangent, owned):
    rows = micros * block
    n = len(CHUNKS)
    lanes_held = (rows + 127) // 128 * 128
    vmem = pl.BlockSpec(memory_space=pltpu.VMEM)
    hbm = pl.BlockSpec(memory_space=pl.ANY)

    forward_widths = [D, D, D, FF]
    backward_widths = [D, FF, D, 3 * D]
    pairs = block // PAIR_ROWS
    return pl.pallas_call(
        functools.partial(layer_kernel, micros, block, captions.shape[0]),
        grid=(2 * micros,),
        out_shape=[jax.ShapeDtypeStruct((rows, w), BF) for w in forward_widths + backward_widths]
        + [
            jax.ShapeDtypeStruct((8, FF), F32),
            jax.ShapeDtypeStruct((PIPE, rows, QUARTER), BF),
            jax.ShapeDtypeStruct((PIPE, block, QUARTER), BF),
        ],
        in_specs=[pl.BlockSpec(memory_space=pltpu.SMEM)] + [vmem] * 10 + [hbm] * 4,
        out_specs=[hbm] * 8 + [vmem, hbm, vmem],
        scratch_shapes=[
            pltpu.VMEM((2, 2, QUARTER, lanes_held), BF),
            pltpu.VMEM((8, HIDDEN_HALF), F32),
        ]
        + [pltpu.VMEM((2,) + shape, BF) for shape in WEIGHT_SHAPES]
        + [
            pltpu.VMEM((PIPE, QUARTER, lanes_held), BF),
            pltpu.VMEM((lanes_held, D), BF),
            pltpu.VMEM((8, HIDDEN_HALF), F32),
            pltpu.VMEM((8, FF), F32),
            pltpu.VMEM((PIPE, rows, QUARTER), BF),
            pltpu.VMEM((micros, block, D), BF),
            pltpu.VMEM((micros, block, D), BF),
            pltpu.VMEM((micros, block, 3 * D), BF),
            pltpu.VMEM((micros, pairs * GROUPS, STACKED, PAIR_ROWS), BF),
            pltpu.VMEM((micros, block, D), BF),
            pltpu.VMEM((micros, block, 1), F32),
            pltpu.VMEM((micros, block, D), BF),
            pltpu.VMEM((micros, block, 1), F32),
            pltpu.VMEM((micros, block, FF), BF),
            pltpu.VMEM((block, D), BF),
            pltpu.VMEM((block, 3 * D), F32),
            pltpu.VMEM((block, D), F32),
            pltpu.VMEM((block, 3 * D), F32),
        ]
        + [pltpu.VMEM((2, block, w), BF) for w in forward_widths + backward_widths]
        + [pltpu.SemaphoreType.DMA((micros,))] * 2
        + [pltpu.SemaphoreType.DMA((n,))] * 8
        + [
            pltpu.SemaphoreType.DMA((5,)),
            pltpu.SemaphoreType.DMA((2, 3)),
            pltpu.SemaphoreType.DMA((2, 3)),
            pltpu.SemaphoreType.DMA((2,)),
            pltpu.SemaphoreType.DMA((3, micros)),
            pltpu.SemaphoreType.DMA((3, micros)),
            pltpu.SemaphoreType.DMA((micros,)),
            pltpu.SemaphoreType.DMA((8, micros)),
        ],
        compiler_params=pltpu.CompilerParams(collective_id=1, has_side_effects=True, vmem_limit_bytes=VMEM_LIMIT),
        name="layer_passes",
    )(captions, tokens, cotangent, *small, *owned)


TILE = 384


def weights_kernel(
    n_dp,
    a0_in, dqkv_in, context_in, dr1_in, a1_in, du_in, hidden_in, dr2_in, sums, last,
    g_proj, g_comb, g_exp, g_red, sums_out, last_out,
    b_proj, b_comb, b_exp, b_red,
    c_proj, c_comb, c_exp, c_red,
    x_proj, x_comb, x_exp, x_red,
    p_proj, p_comb, p_exp, p_red,
    z_proj, z_comb, z_exp, z_red,
    sums_core, sums_x, sums_z, sums_a, sums_b, sums_c,
    low_from_pair, low_from_far, low_from_x, low_own,
    a0, dqkv, context, dr1, a1, du, hidden, dr2,
    core_send, core_recv, x_send, x_recv, z_send, z_recv,
    small_send, small_recv, load_sem, last_send, last_recv, low_send, low_recv,
):
    pipe, dp, layer, half, across_x, across_y, core, other_core = place()
    n_z = n_dp // 2
    z = dp // 2
    near_z = z + 1 - 2 * (z % 2)
    steps = n_z // 2
    z_order = [(near_z + 2 * (step + 1)) % n_z for step in range(steps - 1)] + [near_z]
    z_order += [(z + 2 * (step + 1)) % n_z for step in range(steps - 1)] + [z]
    same_parity = z_order[steps:-1]
    def hidden_lanes(h):
        return pl.ds(pl.multiple_of(h * HIDDEN_HALF, 128), HIDDEN_HALF)

    loads = [
        pltpu.make_async_copy(source, target, load_sem.at[i])
        for i, (source, target) in enumerate((
            (dr2_in, dr2),
            (hidden_in.at[:, hidden_lanes(1 - half)], hidden.at[:, hidden_lanes(1 - half)]),
            (hidden_in.at[:, hidden_lanes(half)], hidden.at[:, hidden_lanes(half)]),
            (a1_in, a1), (du_in, du), (a0_in, a0), (dqkv_in, dqkv), (context_in, context), (dr1_in, dr1),
        ))
    ]
    for copy in loads:
        copy.start()
    relatives = (across_x, across_y, (across_x + 2) % 4)
    greet(
        [(target, dp) for target in relatives] + [(pipe, other_core)]
        + [(pipe, 2 * other + core) for other in [near_z] + same_parity]
    )

    last_copies = [
        remote(last.at[target], last_out.at[half], last_send.at[j], last_recv.at[j], (target, dp))
        for j, target in enumerate(relatives)
    ]
    last_own = pltpu.make_async_copy(last.at[pipe], last_out.at[half], load_sem.at[9])

    @pl.when(layer == 0)
    def _():
        for copy in last_copies:
            copy.start()
        last_own.start()

    mine = [b_red, b_exp, b_proj, b_comb]
    from_core = [c_red, c_exp, c_proj, c_comb]
    from_x = [x_red, x_exp, x_proj, x_comb]
    from_pair = [p_red, p_exp, p_proj, p_comb]
    from_far = [z_red, z_exp, z_proj, z_comb]
    outs = [g_red, g_exp, g_proj, g_comb]

    def spread(target, tile, cast=BF):
        r = target.shape[-2]
        for k in range(tile.shape[0] // (2 * r)):
            for c in range(2):
                yield c, k, tile[(2 * k + c) * r : (2 * k + c + 1) * r].astype(cast)

    def fill_red(h, at):
        width = 2 * b_red.shape[3]
        lanes = pl.ds(pl.multiple_of(h * HIDDEN_HALF + at * width, 128), width)
        for c, k, rows in spread(b_red, dot_tn(hidden[:, lanes], dr2[...])):
            b_red[c, h, at] = rows

    def fill_exp(step, carry):
        i, h = step // 2, step % 2
        tile = dot_tn(
            a1[:, pl.ds(pl.multiple_of(i * TILE, 128), TILE)],
            du[:, pl.ds(pl.multiple_of(h * HIDDEN_HALF, 128), HIDDEN_HALF)],
        )
        for c, k, rows in spread(b_exp, tile):
            b_exp[c, h, i * (TILE // (2 * b_exp.shape[3])) + k] = rows
        return carry

    def fill_proj(h, carry):
        tile = dot_tn(a0[...], dqkv[:, pl.ds(pl.multiple_of(h * 3 * HALF, 128), 3 * HALF)])
        for c, k, rows in spread(b_proj, tile):
            b_proj[c, h, k] = rows
        return carry

    def fill_comb():
        tile = dot_tn(context[...], dr1[...])
        for h in range(2):
            for c, k, rows in spread(b_comb, tile[h * HALF : (h + 1) * HALF]):
                b_comb[c, h, k] = rows

    low = b_red.shape[3] // 32 * 16
    low_rows = pl.ds(0, low)
    rows_of = [pl.ds(low, b_red.shape[3] - low)] + [pl.ds(0, b.shape[3]) for b in mine[1:]]

    def half_of(which):
        return 1 - half if which == 0 else half

    def core_copy(a, which, i):
        h, at = half_of(which), z_order[i]
        return remote(
            mine[a].at[1 - core, h, at, rows_of[a]], from_core[a].at[h, at, rows_of[a]],
            core_send.at[a, which, i], core_recv.at[a, which, i], (pipe, other_core),
        )

    def send_core(a, which):
        for i in range(n_z):
            core_copy(a, which, i).start()

    def x_copy(k):
        a, i = chunks[k]
        at = z_order[i]
        return remote(
            mine[a].at[core, 1 - half, at, rows_of[a]], from_x[a].at[at, rows_of[a]],
            x_send.at[a, i], x_recv.at[a, i], (across_x, dp),
        )

    def pair_copy(a, i):
        return remote(
            mine[a].at[core, half, z_order[i], rows_of[a]], from_pair[a].at[i, rows_of[a]],
            z_send.at[a, i], z_recv.at[a, i], (pipe, 2 * near_z + core),
        )

    def far_copy(a, i):
        other = same_parity[i]
        return remote(
            mine[a].at[core, half, other, rows_of[a]], from_far[a].at[i, rows_of[a]],
            z_send.at[a, steps + i], z_recv.at[a, steps + i], (pipe, 2 * other + core),
        )

    chunks = [(a, i) for a in range(4) for i in range(n_z)]

    def start_x(k):
        if k >= len(chunks):
            return
        a, i = chunks[k]
        at, rows = z_order[i], rows_of[a]
        core_copy(a, 0, i).wait_recv()
        total = mine[a][core, 1 - half, at, rows, :].astype(F32) + from_core[a][1 - half, at, rows, :].astype(F32)
        mine[a][core, 1 - half, at, rows, :] = total.astype(BF)
        x_copy(k).start()

    def after_x(k):
        a, i = chunks[k]
        at, rows = z_order[i], rows_of[a]
        x_copy(k).wait()
        start_x(k + REDUCE_DEPTH)
        core_copy(a, 1, i).wait_recv()
        total = mine[a][core, half, at, rows, :].astype(F32) + from_core[a][half, at, rows, :].astype(F32)
        total = total + from_x[a][at, rows, :].astype(F32)
        if i < steps:
            mine[a][core, half, at, rows, :] = total.astype(BF)
            pair_copy(a, i).start()
            return
        pair_copy(a, i - steps).wait_recv()
        total = total + from_pair[a][i - steps, rows, :].astype(F32)
        if i < n_z - 1:
            mine[a][core, half, at, rows, :] = total.astype(BF)
            far_copy(a, i - steps).start()
        else:
            outs[a][rows, :] = total

    def after_z(a):
        rows = rows_of[a]
        total = outs[a][rows, :]
        for i in range(steps - 1):
            far_copy(a, i).wait()
            total = total + from_far[a][i, rows, :].astype(F32)
        outs[a][rows, :] = total
        for i in range(steps):
            pair_copy(a, i).wait_send()

    def low_core(which, i):
        h, at = half_of(which), z_order[i]
        return remote(
            b_red.at[1 - core, h, at, low_rows], c_red.at[h, at, low_rows],
            low_send.at[which, i], low_recv.at[which, i], (pipe, other_core),
        )

    def low_pair(which, i):
        return remote(
            b_red.at[core, half_of(which), z_order[i], low_rows], low_from_pair.at[which, i],
            low_send.at[2 + which, i], low_recv.at[2 + which, i], (pipe, 2 * near_z + core),
        )

    def low_far(which, i):
        other = same_parity[i]
        return remote(
            b_red.at[core, half_of(which), other, low_rows], low_from_far.at[which, i],
            low_send.at[2 + which, steps + i], low_recv.at[2 + which, steps + i], (pipe, 2 * other + core),
        )

    low_x = remote(
        b_red.at[core, 1 - half, z, low_rows], low_from_x,
        low_send.at[2, n_z - 1], low_recv.at[2, n_z - 1], (across_x, dp),
    )

    def low_sum(which, i):
        h, at = half_of(which), z_order[i]
        low_core(which, i).wait_recv()
        return b_red[core, h, at, low_rows, :].astype(F32) + c_red[h, at, low_rows, :].astype(F32)

    def low_to_pair():
        for which in range(2):
            for i in range(steps):
                b_red[core, half_of(which), z_order[i], low_rows, :] = low_sum(which, i).astype(BF)
                low_pair(which, i).start()

    def low_to_far():
        for which in range(2):
            for i in range(steps, n_z):
                total = low_sum(which, i)
                low_pair(which, i - steps).wait_recv()
                total = total + low_from_pair[which, i - steps].astype(F32)
                if i < n_z - 1:
                    b_red[core, half_of(which), z_order[i], low_rows, :] = total.astype(BF)
                    low_far(which, i - steps).start()
                else:
                    low_own[which] = total

    def low_to_x():
        for which in range(2):
            total = low_own[which]
            for i in range(steps - 1):
                low_far(which, i).wait_recv()
                total = total + low_from_far[which, i].astype(F32)
            if which == 0:
                b_red[core, 1 - half, z, low_rows, :] = total.astype(BF)
                low_x.start()
            else:
                g_red[low_rows, :] = total

    def low_done():
        low_x.wait()
        g_red[low_rows, :] = g_red[low_rows, :] + low_from_x[...].astype(F32)
        for which in range(2):
            for i in range(n_z):
                low_core(which, i).wait_send()
            for i in range(steps):
                low_pair(which, i).wait_send()
            for i in range(steps - 1):
                low_far(which, i).wait_send()

    sums_copy_core = remote(sums, sums_core, small_send.at[0], small_recv.at[0], (pipe, other_core))
    sums_copy_x = remote(sums_a, sums_x, small_send.at[1], small_recv.at[1], (across_x, dp))
    sums_copy_pair = remote(
        sums_b, sums_z.at[steps - 1], small_send.at[2], small_recv.at[2], (pipe, 2 * near_z + core)
    )
    sums_copies_far = [
        remote(sums_c, sums_z.at[i], small_send.at[3 + i], small_recv.at[3 + i], (pipe, 2 * other + core))
        for i, other in enumerate(same_parity)
    ]

    sums_copy_core.start()
    loads[0].wait()
    loads[1].wait()
    for i in range(n_z):
        fill_red(1 - half, z_order[i])
        core_copy(0, 0, i).start()
        low_core(0, i).start()
        if 1 <= i <= REDUCE_DEPTH:
            start_x(i - 1)
    loads[2].wait()
    for i in range(n_z):
        fill_red(half, z_order[i])
        low_core(1, i).start()
        core_copy(0, 1, i).start()
    low_to_pair()
    loads[3].wait()
    loads[4].wait()
    lax.fori_loop(0, 2 * D // TILE, fill_exp, 0)
    send_core(1, 0)
    send_core(1, 1)
    sums_copy_core.wait()
    sums_a[...] = sums[...] + sums_core[...]
    sums_copy_x.start()
    after_x(0)
    after_x(1)
    loads[5].wait()
    loads[6].wait()
    lax.fori_loop(0, 2, fill_proj, 0)
    send_core(2, 0)
    send_core(2, 1)
    after_x(2)
    loads[7].wait()
    loads[8].wait()
    fill_comb()
    send_core(3, 0)
    send_core(3, 1)
    sums_copy_x.wait()
    sums_b[...] = sums_a[...] + sums_x[...]
    sums_copy_pair.start()
    for k in range(3, len(chunks)):
        after_x(k)
        if k == LOW_AT[0]:
            low_to_far()
        if k == LOW_AT[1]:
            low_to_x()
        if k == n_z:
            sums_copy_pair.wait()
            sums_c[...] = sums_b[...] + sums_z[steps - 1]
            for copy in sums_copies_far:
                copy.start()
        if k % n_z == n_z - 2 and k >= n_z:
            after_z(k // n_z - 1)
    low_done()
    after_z(3)
    for a in range(4):
        for which in range(2):
            for i in range(n_z):
                core_copy(a, which, i).wait_send()
    total = sums_c[...]
    for i in range(steps - 1):
        sums_copies_far[i].wait()
        total = total + sums_z[i]
    sums_out[...] = total

    @pl.when(layer == 0)
    def _():
        for copy in last_copies:
            copy.wait_send()
        last_own.wait()

    for j, source in enumerate(relatives):
        @pl.when(source // 2 == 0)
        def _():
            last_copies[j].wait_recv()


def weight_gradients(n_dp, a0, dqkv, context, dr1, a1, du, hidden, dr2, sums, last):
    vmem = pl.BlockSpec(memory_space=pltpu.VMEM)
    hbm = pl.BlockSpec(memory_space=pl.ANY)
    n_z = n_dp // 2
    low = HIDDEN_HALF // n_dp // 32 * 16
    shapes = [(D // n_dp, 3 * HALF), (HALF // n_dp, D), (D // n_dp, HIDDEN_HALF), (HIDDEN_HALF // n_dp, D)]
    return pl.pallas_call(
        functools.partial(weights_kernel, n_dp),
        out_shape=[jax.ShapeDtypeStruct(s, F32) for s in shapes]
        + [jax.ShapeDtypeStruct(sums.shape, F32), jax.ShapeDtypeStruct((2,) + last.shape[1:], BF)],
        in_specs=[hbm] * 8 + [vmem, hbm],
        out_specs=[vmem] * 5 + [hbm],
        scratch_shapes=[pltpu.VMEM((2, 2, n_z) + s, BF) for s in shapes]
        + [pltpu.VMEM((2, n_z) + s, BF) for s in shapes]
        + [pltpu.VMEM((n_z,) + s, BF) for s in shapes]
        + [pltpu.VMEM((n_z // 2,) + s, BF) for s in shapes]
        + [pltpu.VMEM((max(n_z // 2 - 1, 1),) + s, BF) for s in shapes]
        + [
            pltpu.VMEM(sums.shape, F32),
            pltpu.VMEM(sums.shape, F32),
            pltpu.VMEM((n_z // 2,) + sums.shape, F32),
            pltpu.VMEM(sums.shape, F32),
            pltpu.VMEM(sums.shape, F32),
            pltpu.VMEM(sums.shape, F32),
            pltpu.VMEM((2, n_z // 2, low, D), BF),
            pltpu.VMEM((2, max(n_z // 2 - 1, 1), low, D), BF),
            pltpu.VMEM((low, D), BF),
            pltpu.VMEM((2, low, D), F32),
        ]
        + [pltpu.VMEM(v.shape, BF) for v in (a0, dqkv, context, dr1, a1, du, hidden, dr2)]
        + [
            pltpu.SemaphoreType.DMA((4, 2, n_z)),
            pltpu.SemaphoreType.DMA((4, 2, n_z)),
            pltpu.SemaphoreType.DMA((4, n_z)),
            pltpu.SemaphoreType.DMA((4, n_z)),
            pltpu.SemaphoreType.DMA((4, n_z - 1)),
            pltpu.SemaphoreType.DMA((4, n_z - 1)),
            pltpu.SemaphoreType.DMA((n_z + 1,)),
            pltpu.SemaphoreType.DMA((n_z + 1,)),
            pltpu.SemaphoreType.DMA((10,)),
            pltpu.SemaphoreType.DMA((3,)),
            pltpu.SemaphoreType.DMA((3,)),
            pltpu.SemaphoreType.DMA((4, n_z)),
            pltpu.SemaphoreType.DMA((4, n_z)),
        ],
        compiler_params=pltpu.CompilerParams(collective_id=3, has_side_effects=True, vmem_limit_bytes=VMEM_LIMIT),
        name="weight_gradients",
    )(a0, dqkv, context, dr1, a1, du, hidden, dr2, sums, last)


def finish_kernel(n_dp, small, results, last, *refs):
    pipe, dp, layer, half, across_x, across_y, core, other_core = place()
    sources, encoded, tokens_grad, outs, parts = refs[:4], refs[4], refs[5], refs[6:10], refs[10:]
    for source, out in zip(sources, outs):
        out[0] = source[...]
    for first, out in ((0, tokens_grad), (2, encoded)):
        parts_of = []
        for i in (first, first + 1):
            if first == 0:
                parts_of += [results[i, : results.shape[1] - last.shape[1], :], last[i]]
            else:
                parts_of.append(results[i])
        value = jnp.concatenate(parts_of, 0).astype(F32).T
        out[...] = value[:, : out.shape[1]].astype(out.dtype)
    for row, out in enumerate(parts):
        count = out.shape[1]
        width = n_dp * count
        found = jnp.zeros(out.shape, F32)
        for h in range(2):
            for d in range(n_dp):
                at = d * count
                if row == 0:
                    at = h * 3 * HALF + at + (HALF if at >= HALF else 0)
                else:
                    at = h * width + at
                found = jnp.where((half == h) & (dp == d), small[row : row + 1, at : at + count], found)
        out[...] = found


def finish(n_dp, local_rows, small, results, last, grads):
    vmem = pl.BlockSpec(memory_space=pltpu.VMEM)
    widths = [D, HALF, HALF, HALF, HIDDEN_HALF, HALF, HALF, HALF]
    return pl.pallas_call(
        functools.partial(finish_kernel, n_dp),
        out_shape=[
            jax.ShapeDtypeStruct((QUARTER, local_rows), BF),
            jax.ShapeDtypeStruct((QUARTER, local_rows), F32),
        ]
        + [jax.ShapeDtypeStruct((1,) + g.shape, F32) for g in grads]
        + [jax.ShapeDtypeStruct((1, w // n_dp), F32) for w in widths],
        in_specs=[vmem] * 7,
        out_specs=[vmem] * 14,
        compiler_params=pltpu.CompilerParams(vmem_limit_bytes=VMEM_LIMIT),
        name="finish",
    )(small, results, last, *grads)


def weight_gradients_by_scatter(n_dp, a0, dqkv, context, dr1, a1, du, hidden, dr2, sums, last):
    half = lax.axis_index("pipe") % 2
    halves = (
        dot_tn(a0, dqkv).reshape(D, 2, 3 * HALF).transpose(1, 0, 2),
        dot_tn(context, dr1).reshape(2, HALF, D),
        dot_tn(a1, du).reshape(D, 2, HIDDEN_HALF).transpose(1, 0, 2),
        dot_tn(hidden, dr2).reshape(2, HIDDEN_HALF, D),
    )
    swap = [(i, i ^ 1) for i in range(PIPE)]
    found = []
    for member in halves:
        part = lax.psum_scatter(member, "dp", scatter_dimension=1, tiled=True)
        keep = lax.dynamic_index_in_dim(part, half, 0, keepdims=False)
        send = lax.dynamic_index_in_dim(part, 1 - half, 0, keepdims=False)
        found.append(keep + lax.ppermute(send.astype(BF), "pipe", swap).astype(F32))
    small = lax.psum(sums, "dp")
    received = lax.all_to_all(last, "pipe", 0, 0, tiled=False)
    return found + [small + lax.ppermute(small, "pipe", swap), received[:2]]


def shards(
    n_dp,
    tokens, cotangent, captions, projection, biases, combiner, offsets, scaling, centring,
    expansion, lifting, reduction, settling, stretch, translate,
):
    local_rows = tokens.shape[0]
    local_pairs = local_rows // PAIR_ROWS
    pairs = 2 * ((local_pairs + 3) // 4)
    block = 2 * PAIR_ROWS
    micros = pairs // 2
    owned = (projection[0], combiner[0], expansion[0], reduction[0])
    small = (biases, offsets, scaling, centring, lifting, settling, stretch, translate)
    *kept, results, last = layer_passes(micros, block, captions, small, tokens.T, cotangent.T, owned)
    a0, context, a1, hidden, dr2, du, dr1, dqkv, sums = kept
    whole_tiles = HALF % (16 * n_dp) == 0
    collect = weight_gradients if whole_tiles else weight_gradients_by_scatter
    *grads, sums, last = collect(n_dp, a0, dqkv, context, dr1, a1, du, hidden, dr2, sums, last)
    encoded, tokens_grad, g_proj, g_comb, g_exp, g_red, *parts = finish(n_dp, local_rows, sums, results, last, grads)
    return (
        encoded.T, tokens_grad.T, g_proj, parts[0], g_comb, parts[1], parts[2], parts[3],
        g_exp, parts[4], g_red, parts[5], parts[6], parts[7],
    )


def solution(mesh):
    rows = P("dp", "pipe")
    matrix = P("pipe", None, None)
    vector = P("pipe", None)
    matrix_out = P("pipe", "dp", None)
    vector_out = P("pipe", "dp")
    in_specs = (
        rows, rows, P("dp"), matrix, vector, matrix, vector, vector, vector,
        matrix, vector, matrix, vector, vector, vector,
    )
    out_specs = (
        rows, rows, matrix_out, vector_out, matrix_out, vector_out, vector_out, vector_out,
        matrix_out, vector_out, matrix_out, vector_out, vector_out, vector_out,
    )
    return jax.shard_map(
        functools.partial(shards, mesh.shape["dp"]),
        mesh=mesh, in_specs=in_specs, out_specs=out_specs, check_vma=False,
    )
```

```python
import functools

import jax
import jax.numpy as jnp
from jax import lax
from jax.experimental import pallas as pl
from jax.experimental.pallas import tpu as pltpu
from jax.sharding import PartitionSpec as P

D = 768
HEADS = 12
HEAD_DIM = 64
FF = 3072
WORDS = 64
PAIR_ROWS = 104
HALF = D // 2
HIDDEN_HALF = FF // 2
QUARTER = D // 4
PIPE = 4
GROUP_WIDTH = 2 * HEAD_DIM
GROUPS = HEADS // 2
STACKED = 2 * PAIR_ROWS

EPSILON = 1e-05
NEGATIVE = -1e30
SCALE = HEAD_DIM ** (-0.5)

MESH = pl.DeviceIdType.MESH
BF = jnp.bfloat16
F32 = jnp.float32
VMEM_LIMIT = 60 << 20


def dot_nn(left, right):
    return lax.dot_general(left, right, (((1,), (0,)), ((), ())), preferred_element_type=F32)


def dot_nt(left, right):
    return lax.dot_general(left, right, (((1,), (1,)), ((), ())), preferred_element_type=F32)


def dot_tn(left, right):
    return lax.dot_general(left, right, (((0,), (0,)), ((), ())), preferred_element_type=F32)


def place():
    pipe = lax.axis_index("pipe")
    dp = lax.axis_index("dp")
    layer = pipe // 2
    half = pipe % 2
    across_x = pipe + 1 - 2 * half
    across_y = (pipe + 2) % 4
    core = dp % 2
    other_core = dp + 1 - 2 * core
    return pipe, dp, layer, half, across_x, across_y, core, other_core


def greet(devices):
    barrier = pltpu.get_barrier_semaphore()
    for device in devices:
        pl.semaphore_signal(barrier, inc=1, device_id=device, device_id_type=MESH)
    pl.semaphore_wait(barrier, len(devices))


def remote(source, target, send, recv, device):
    return pltpu.make_async_remote_copy(
        src_ref=source,
        dst_ref=target,
        send_sem=send,
        recv_sem=recv,
        device_id=device,
        device_id_type=MESH,
    )


WEIGHT_SHAPES = [(D, 3 * HALF), (HALF, D), (D, HIDDEN_HALF), (HIDDEN_HALF, D)]
CHUNKS = [(0, 0, 96), (0, 96, 96), (1, 0, 96)] + [(2, i*48, 48) for i in range(4)] + [(3, i*96, 96) for i in range(4)]
ATTENTION_CHUNKS = 3
FIRST_LANES = 256
DEPTH = 3
LAG = 2
REDUCE_DEPTH = 3
LOW_AT = (4, 7)


def left_lanes():
    return lax.broadcasted_iota(jnp.int32, (PAIR_ROWS, GROUP_WIDTH), 1) < HEAD_DIM


def stacked(values, scale=None):
    if scale is not None:
        values = values * scale
    left = left_lanes()
    return jnp.concatenate([jnp.where(left, values, 0.0), jnp.where(left, 0.0, values)], 0).astype(BF)


def own_lanes(values):
    return jnp.where(left_lanes(), values[:PAIR_ROWS], values[PAIR_ROWS:])


def normalized(residual):
    average = jnp.mean(residual, axis=-1, keepdims=True)
    centred = residual - average
    variance = jnp.mean(centred * centred, axis=-1, keepdims=True)
    inverse = lax.rsqrt(variance + EPSILON)
    return centred * inverse, inverse


def norm_backward(gradient, norm, inverse, gain):
    scaled = gradient * gain
    first = jnp.mean(scaled, axis=-1, keepdims=True)
    second = jnp.mean(scaled * norm, axis=-1, keepdims=True)
    return (scaled - first - norm * second) * inverse


def column_sums(value):
    return jnp.sum(value, axis=0, keepdims=True)


def layer_kernel(
    micros, block, local_pairs,
    captions, tokens_hbm, cotangent_hbm, biases, offsets, scaling, centring, lifting, settling, stretch, translate,
    own_proj, own_comb, own_exp, own_red,
    a0_hbm, context_hbm, a1_hbm, hidden_hbm, dr2_hbm, du_hbm, dr1_hbm, dqkv_hbm, sums_out, results_out, last_out,
    tokens, cotangent, both, own_vectors, joint, mixing, expand, reduce, pieces, unpacked, other_vectors, vectors, results,
    slots, outgoing, qkv_keep, prob_keep, n1_keep, r1_keep, n2_keep, r2_keep, slope_keep,
    a_s, qkv_s, context_s, dqkv_s,
    a0_ring, context_ring, a1_ring, hidden_ring, dr2_ring, du_ring, dr1_ring, dqkv_ring,
    send, recv, x_send, x_recv, z_send, z_recv, near_send, near_recv, far_send, far_recv,
    own_sem, piece_send, piece_recv, vec_sem, result_send, result_recv, result_sem, ring_sem, row_sem,
):
    pipe, dp, layer, half, across_x, across_y, core, other_core = place()
    step = pl.program_id(0)
    pairs = block // PAIR_ROWS
    rows = micros * block
    diagonal = (across_x + 2) % 4
    parity = (dp // 2) % 2
    across_z = dp + 2 - 4 * parity
    mine = 2 * parity + core
    paired = 2 * (1 - parity) + core
    relatives = (across_x, across_y, diagonal)
    owned = [own_proj, own_comb, own_exp, own_red]
    held = [joint, mixing, expand, reduce]
    n = len(CHUNKS)

    def span(chunk, quarter):
        which, start, count = chunk
        return pl.ds(quarter * (WEIGHT_SHAPES[which][0] // 4) + start, count)

    def x_copy(k):
        at = span(CHUNKS[k], mine)
        which = CHUNKS[k][0]
        return remote(owned[which].at[at], held[which].at[half, at], x_send.at[k], x_recv.at[k], (across_x, dp))

    def z_copy(k):
        region = held[CHUNKS[k][0]].at[1 - half, span(CHUNKS[k], mine)]
        return remote(region, region, z_send.at[k], z_recv.at[k], (pipe, across_z))

    def near_copy(k):
        region = held[CHUNKS[k][0]].at[1 - half, span(CHUNKS[k], mine)]
        return remote(region, region, near_send.at[k], near_recv.at[k], (pipe, other_core))

    def far_copy(k):
        region = held[CHUNKS[k][0]].at[1 - half, span(CHUNKS[k], paired)]
        return remote(region, region, far_send.at[k], far_recv.at[k], (pipe, other_core))

    own_copies = [pltpu.make_async_copy(owned[i], held[i].at[half], own_sem.at[i]) for i in range(4)]
    own_piece = pltpu.make_async_copy(both.at[layer, half], pieces.at[pipe], own_sem.at[4])
    lanes_held = both.shape[3]
    lanes_of = (pl.ds(0, FIRST_LANES), pl.ds(FIRST_LANES, lanes_held - FIRST_LANES))
    vec_copy = remote(own_vectors, other_vectors, vec_sem.at[0], vec_sem.at[1], (across_x, dp))
    piece_copies = [
        [
            remote(
                both.at[target // 2, target % 2, :, lanes], pieces.at[pipe, :, lanes],
                piece_send.at[part, j], piece_recv.at[part, j], (target, dp),
            )
            for j, target in enumerate(relatives)
        ]
        for part, lanes in enumerate(lanes_of)
    ]

    def send_pieces(to_layer, part):
        for j, target in enumerate(relatives):
            @pl.when(target // 2 == to_layer)
            def _():
                piece_copies[part][j].start()

    def hand_on(k):
        z_copy(k).wait_recv()
        far_copy(k).start()

    def arrived(first, last):
        for k in range(first, last):
            near_copy(k).wait_recv()
            far_copy(k).wait_recv()

    def gather_most():
        for k in range(n):
            x_copy(k).wait_recv()
            z_copy(k).start()
            near_copy(k).start()
            if k + DEPTH < n:
                x_copy(k).wait_send()
                x_copy(k + DEPTH).start()
            if k + DEPTH == n - 1:
                send_pieces(0, 1)
                send_pieces(1, 0)
                send_pieces(1, 1)
            if k >= LAG:
                hand_on(k - LAG)
        arrived(0, ATTENTION_CHUNKS)
        own_copies[0].wait()
        own_copies[1].wait()

    def gather_rest():
        for k in range(n - LAG, n):
            hand_on(k)
        arrived(ATTENTION_CHUNKS, n)
        own_copies[2].wait()
        own_copies[3].wait()

    def y_copy(index):
        return remote(outgoing.at[index], slots.at[index], send.at[index], recv.at[index], (across_y, dp))

    def rows_of(index):
        return pl.ds(pl.multiple_of(index * block, 16), block)

    def result_copies(index):
        return [
            remote(
                results.at[target, rows_of(index)], results_out.at[pipe, rows_of(index)],
                result_send.at[j, index], result_recv.at[j, index], (target, dp),
            )
            for j, target in enumerate(relatives)
        ]

    def own_result(index):
        return pltpu.make_async_copy(
            results.at[pipe, rows_of(index)], results_out.at[pipe, rows_of(index)], result_sem.at[index]
        )

    def share_result(index, value):
        for i in range(PIPE):
            results[i, rows_of(index), :] = value[:, i * QUARTER : (i + 1) * QUARTER]
        for copy in result_copies(index):
            copy.start()
        own_result(index).start()

    def wait_results(index):
        final = index == micros - 1
        for j, copy in enumerate(result_copies(index)):
            if not final:
                copy.wait()
                continue

            @pl.when(layer == 1)
            def _():
                copy.wait_send()

            @pl.when(relatives[j] // 2 == 1)
            def _():
                copy.wait_recv()

        @pl.when((layer == 1) | (not final))
        def _():
            own_result(index).wait()

    rings = [
        (a0_ring, a0_hbm), (context_ring, context_hbm), (a1_ring, a1_hbm), (hidden_ring, hidden_hbm),
        (dr2_ring, dr2_hbm), (du_ring, du_hbm), (dr1_ring, dr1_hbm), (dqkv_ring, dqkv_hbm),
    ]

    def ring_copy(which, index):
        ring, target = rings[which]
        return pltpu.make_async_copy(ring.at[index % 2], target.at[rows_of(index)], ring_sem.at[which, index])

    def ring_slots(first, last, index):
        @pl.when(index >= 2)
        def _():
            for which in range(first, last):
                ring_copy(which, index - 2).wait()

        return [rings[which][0].at[index % 2] for which in range(first, last)]

    def ring_start(first, last, index):
        for which in range(first, last):
            ring_copy(which, index).start()

    def unpack_pieces(part):
        for copy in piece_copies[part]:
            copy.wait_recv()
        at = lanes_of[part]
        value = pieces[:, :, at.start : at.start + at.size].reshape(D, at.size)
        unpacked[at.start : at.start + at.size, :] = value.astype(F32).T.astype(BF)

    @pl.when(step == 0)
    def _():
        row_copies = [
            pltpu.make_async_copy(tokens_hbm, tokens, row_sem.at[0]),
            pltpu.make_async_copy(cotangent_hbm, cotangent, row_sem.at[1]),
        ]
        for copy in row_copies:
            copy.start()
        greet([(across_x, dp), (across_y, dp), (diagonal, dp), (pipe, across_z), (pipe, other_core)])
        for i, source in enumerate((biases, offsets, scaling, centring, lifting, settling, stretch, translate)):
            own_vectors[i : i + 1, : source.shape[1]] = source[...].astype(F32)
        vec_copy.start()
        for t, source in enumerate((tokens, cotangent)):
            row_copies[t].wait()
            whole = source[...].astype(F32)
            for h in range(2):
                value = whole[:, h * rows : (h + 1) * rows]
                spare = jnp.zeros((QUARTER, lanes_held - value.shape[1]), F32)
                both[t, h] = jnp.concatenate([value, spare], 1).astype(BF)
            if t == 0:
                send_pieces(0, 0)
                for k in range(DEPTH):
                    x_copy(k).start()
        for copy in own_copies:
            copy.start()
        own_piece.start()
        sums_out[...] = jnp.zeros_like(sums_out)
        vec_copy.wait_recv()
        for which in range(2):
            value = jnp.where(half == which, own_vectors[...], other_vectors[...])
            vectors[0:1, which * 3 * HALF : which * 3 * HALF + HALF] = value[0:1, :HALF]
            vectors[0:1, which * 3 * HALF + HALF : which * 3 * HALF + D] = jnp.zeros((1, HALF), F32)
            vectors[0:1, which * 3 * HALF + D : (which + 1) * 3 * HALF] = value[0:1, HALF:D]
            for i in (1, 2, 3, 5, 6, 7):
                vectors[i : i + 1, which * HALF : (which + 1) * HALF] = value[i : i + 1, :HALF]
            vectors[4:5, which * HIDDEN_HALF : (which + 1) * HIDDEN_HALF] = value[4:5, :]
        own_piece.wait()
        gather_most()

        @pl.when(layer == 1)
        def _():
            gather_rest()

    @pl.when(((layer == 0) & (step < micros)) | ((layer == 1) & (step % 2 == 0)))
    def _():
        micro = (1 - layer) * step + layer * (step // 2)
        a0_out, context_out, a1_out, hidden_out = ring_slots(0, 4, micro)

        for part in range(2):
            @pl.when((layer == 0) & (micro == part))
            def _():
                unpack_pieces(part)

        @pl.when(layer == 0)
        def _():
            a_s[...] = unpacked[rows_of(micro), :]

        @pl.when(layer == 1)
        def _():
            y_copy(micro).wait_recv()
            a_s[...] = slots[micro]

        inputs = a_s[...]
        a0_out[...] = inputs
        for which in range(2):
            value = dot_nn(inputs, joint[which]) + vectors[0:1, which * 3 * HALF : (which + 1) * 3 * HALF]
            for part in range(3):
                cols = slice(part * D + which * HALF, part * D + (which + 1) * HALF)
                found = value[:, part * HALF : (part + 1) * HALF]
                qkv_s[:, cols] = found
                qkv_keep[micro, :, cols] = found.astype(BF)
        over = [(pair, group) for pair in range(pairs) for group in range(GROUPS)]
        spans = [
            (
                slice(pair * PAIR_ROWS, (pair + 1) * PAIR_ROWS),
                [slice(part * D + group * GROUP_WIDTH, part * D + (group + 1) * GROUP_WIDTH) for part in range(3)],
            )
            for pair, group in over
        ]
        key = lax.broadcasted_iota(jnp.int32, (PAIR_ROWS, PAIR_ROWS), 0)
        masks = []
        for pair in range(pairs):
            length = captions[jnp.minimum((half * micros + micro) * pairs + pair, local_pairs - 1)]
            masks.append(jnp.where((key >= WORDS) | (key < length), 0.0, NEGATIVE))
        scores = [
            dot_nt(stacked(qkv_s[at, lanes[1]], SCALE), qkv_s[at, lanes[0]].astype(BF)) for at, lanes in spans
        ]
        values = [stacked(qkv_s[at, lanes[2]]) for at, lanes in spans]
        probs = []
        for k, (pair, group) in enumerate(over):
            found = []
            for i in range(2):
                score = scores[k][i * PAIR_ROWS : (i + 1) * PAIR_ROWS] + masks[pair]
                exponent = jnp.exp(score - jnp.max(score, axis=0, keepdims=True))
                found.append(exponent * (1.0 / jnp.sum(exponent, axis=0, keepdims=True)))
            probs.append(jnp.concatenate(found, 0).astype(BF))
        contexts = [dot_tn(probs[k], values[k]) for k in range(len(over))]
        for k, (at, lanes) in enumerate(spans):
            prob_keep[micro, k] = probs[k]
            context_s[at, lanes[0]] = contexts[k]
        context = context_s[...].astype(BF)
        context_out[...] = context
        residual = inputs.astype(F32) + dot_nn(context, mixing[...].reshape(D, D)) + vectors[1:2, :D]
        norm, inverse = normalized(residual)
        n1_keep[micro] = norm.astype(BF)
        r1_keep[micro] = inverse
        attended = (norm * vectors[2:3, :D] + vectors[3:4, :D]).astype(BF)
        a1_out[...] = attended

        @pl.when((micro == 0) & (layer == 0))
        def _():
            gather_rest()

        residual = attended.astype(F32) + vectors[5:6, :D]
        for which in range(2):
            cols = slice(which * HIDDEN_HALF, (which + 1) * HIDDEN_HALF)
            raised = dot_nn(attended, expand[which]) + vectors[4:5, cols]
            below = 0.5 * (1.0 + lax.erf(raised * (0.5**0.5)))
            hidden = (raised * below).astype(BF)
            hidden_out[:, cols] = hidden
            density = jnp.exp(raised * raised * (-0.5)) * 0.3989422804014327
            slope_keep[micro, :, cols] = (below + raised * density).astype(BF)
            residual = residual + dot_nn(hidden, reduce[which])
        norm, inverse = normalized(residual)
        n2_keep[micro] = norm.astype(BF)
        r2_keep[micro] = inverse
        result = (norm * vectors[6:7, :D] + vectors[7:8, :D]).astype(BF)

        @pl.when(layer == 0)
        def _():
            outgoing[micro] = result
            y_copy(micro).start()

        @pl.when(layer == 1)
        def _():
            share_result(micro, result)

        ring_start(0, 4, micro)

    def add_sum(row, value):
        width = value.shape[1]
        sums_out[row : row + 1, :width] += column_sums(value)

    @pl.when(((layer == 0) & (step >= micros)) | ((layer == 1) & (step % 2 == 1)))
    def _():
        micro = (1 - layer) * (step - micros) + layer * (step // 2)
        dr2_out, du_out, dr1_out, dqkv_out = ring_slots(4, 8, micro)

        @pl.when((layer == 1) & (micro == 0))
        def _():
            unpack_pieces(0)
            unpack_pieces(1)

        @pl.when(layer == 1)
        def _():
            a_s[...] = unpacked[rows_of(micro), :]

        @pl.when(layer == 0)
        def _():
            y_copy(micro).wait_recv()
            a_s[...] = slots[micro]

        gradient = a_s[...].astype(F32)
        norm = n2_keep[micro].astype(F32)
        add_sum(6, gradient * norm)
        add_sum(7, gradient)
        grad_residual = norm_backward(gradient, norm, r2_keep[micro], vectors[6:7, :D])
        add_sum(5, grad_residual)
        branch = grad_residual.astype(BF)
        dr2_out[...] = branch
        total = grad_residual
        for which in range(2):
            cols = slice(which * HIDDEN_HALF, (which + 1) * HIDDEN_HALF)
            raised = dot_nt(branch, reduce[which]) * slope_keep[micro, :, cols].astype(F32)
            sums_out[4:5, cols] += column_sums(raised)
            raised = raised.astype(BF)
            du_out[:, cols] = raised
            total = total + dot_nt(raised, expand[which])

        gradient = total.astype(BF).astype(F32)
        norm = n1_keep[micro].astype(F32)
        add_sum(2, gradient * norm)
        add_sum(3, gradient)
        grad_residual = norm_backward(gradient, norm, r1_keep[micro], vectors[2:3, :D])
        add_sum(1, grad_residual)
        branch = grad_residual.astype(BF)
        dr1_out[...] = branch
        context_s[...] = dot_nt(branch, mixing[...].reshape(D, D))
        qkv_s[...] = qkv_keep[micro].astype(F32)
        spans = [
            (
                slice(pair * PAIR_ROWS, (pair + 1) * PAIR_ROWS),
                [slice(part * D + group * GROUP_WIDTH, part * D + (group + 1) * GROUP_WIDTH) for part in range(3)],
            )
            for pair in range(pairs)
            for group in range(GROUPS)
        ]
        over = range(len(spans))
        queries = [qkv_s[at, lanes[0]].astype(BF) for at, lanes in spans]
        keys = [stacked(qkv_s[at, lanes[1]], SCALE) for at, lanes in spans]
        values = [stacked(qkv_s[at, lanes[2]]) for at, lanes in spans]
        grads = [context_s[at, lanes[0]].astype(BF) for at, lanes in spans]
        rounded = [prob_keep[micro, g] for g in over]
        grad_probs = [dot_nt(values[g], grads[g]) for g in over]
        grad_values = [dot_nn(rounded[g], grads[g]) for g in over]
        grad_scores = []
        for g in over:
            probs = rounded[g].astype(F32)
            weighted = probs * grad_probs[g]
            found = []
            for i in range(2):
                at = slice(i * PAIR_ROWS, (i + 1) * PAIR_ROWS)
                found.append(weighted[at] - probs[at] * column_sums(weighted[at]))
            grad_scores.append(jnp.concatenate(found, 0).astype(BF))
        grad_keys = [dot_nn(grad_scores[g], queries[g]) for g in over]
        grad_queries = [dot_tn(grad_scores[g], keys[g]) for g in over]
        for g, (at, lanes) in enumerate(spans):
            dqkv_s[at, lanes[0]] = grad_queries[g]
            dqkv_s[at, lanes[1]] = own_lanes(grad_keys[g]) * SCALE
            dqkv_s[at, lanes[2]] = own_lanes(grad_values[g])
        total = grad_residual
        for which in range(2):
            value = jnp.concatenate(
                [dqkv_s[:, part * D + which * HALF : part * D + (which + 1) * HALF] for part in range(3)], 1
            ).astype(BF)
            cols = slice(which * 3 * HALF, (which + 1) * 3 * HALF)
            dqkv_out[:, cols] = value
            sums_out[0:1, cols] += column_sums(value.astype(F32))
            total = total + dot_nt(value, joint[which])
        result = total.astype(BF)

        @pl.when(layer == 1)
        def _():
            outgoing[micro] = result
            y_copy(micro).start()

        ring_start(4, 8, micro)

        @pl.when((layer == 0) & (micro < micros - 1))
        def _():
            share_result(micro, result)

        @pl.when((layer == 0) & (micro == micros - 1))
        def _():
            for i in range(PIPE):
                last_out[i] = result[:, i * QUARTER : (i + 1) * QUARTER]

    @pl.when(step == 2 * micros - 1)
    def _():
        for index in range(micros):
            y_copy(index).wait_send()
            wait_results(index)
        for index in range(max(micros - 2, 0), micros):
            for which in range(8):
                ring_copy(which, index).wait()
        for k in range(n):
            if k + DEPTH >= n:
                x_copy(k).wait_send()
            z_copy(k).wait_send()
            near_copy(k).wait_send()
            far_copy(k).wait_send()
        for copy in piece_copies[0] + piece_copies[1] + [vec_copy]:
            copy.wait_send()


def layer_passes(micros, block, captions, small, tokens, cotangent, owned):
    rows = micros * block
    n = len(CHUNKS)
    lanes_held = (rows + 127) // 128 * 128
    vmem = pl.BlockSpec(memory_space=pltpu.VMEM)
    hbm = pl.BlockSpec(memory_space=pl.ANY)

    forward_widths = [D, D, D, FF]
    backward_widths = [D, FF, D, 3 * D]
    pairs = block // PAIR_ROWS
    return pl.pallas_call(
        functools.partial(layer_kernel, micros, block, captions.shape[0]),
        grid=(2 * micros,),
        out_shape=[jax.ShapeDtypeStruct((rows, w), BF) for w in forward_widths + backward_widths]
        + [
            jax.ShapeDtypeStruct((8, FF), F32),
            jax.ShapeDtypeStruct((PIPE, rows, QUARTER), BF),
            jax.ShapeDtypeStruct((PIPE, block, QUARTER), BF),
        ],
        in_specs=[pl.BlockSpec(memory_space=pltpu.SMEM)] + [hbm] * 2 + [vmem] * 8 + [hbm] * 4,
        out_specs=[hbm] * 8 + [vmem, hbm, vmem],
        scratch_shapes=[
            pltpu.VMEM(tokens.shape, BF),
            pltpu.VMEM(cotangent.shape, BF),
            pltpu.VMEM((2, 2, QUARTER, lanes_held), BF),
            pltpu.VMEM((8, HIDDEN_HALF), F32),
        ]
        + [pltpu.VMEM((2,) + shape, BF) for shape in WEIGHT_SHAPES]
        + [
            pltpu.VMEM((PIPE, QUARTER, lanes_held), BF),
            pltpu.VMEM((lanes_held, D), BF),
            pltpu.VMEM((8, HIDDEN_HALF), F32),
            pltpu.VMEM((8, FF), F32),
            pltpu.VMEM((PIPE, rows, QUARTER), BF),
            pltpu.VMEM((micros, block, D), BF),
            pltpu.VMEM((micros, block, D), BF),
            pltpu.VMEM((micros, block, 3 * D), BF),
            pltpu.VMEM((micros, pairs * GROUPS, STACKED, PAIR_ROWS), BF),
            pltpu.VMEM((micros, block, D), BF),
            pltpu.VMEM((micros, block, 1), F32),
            pltpu.VMEM((micros, block, D), BF),
            pltpu.VMEM((micros, block, 1), F32),
            pltpu.VMEM((micros, block, FF), BF),
            pltpu.VMEM((block, D), BF),
            pltpu.VMEM((block, 3 * D), F32),
            pltpu.VMEM((block, D), F32),
            pltpu.VMEM((block, 3 * D), F32),
        ]
        + [pltpu.VMEM((2, block, w), BF) for w in forward_widths + backward_widths]
        + [pltpu.SemaphoreType.DMA((micros,))] * 2
        + [pltpu.SemaphoreType.DMA((n,))] * 8
        + [
            pltpu.SemaphoreType.DMA((5,)),
            pltpu.SemaphoreType.DMA((2, 3)),
            pltpu.SemaphoreType.DMA((2, 3)),
            pltpu.SemaphoreType.DMA((2,)),
            pltpu.SemaphoreType.DMA((3, micros)),
            pltpu.SemaphoreType.DMA((3, micros)),
            pltpu.SemaphoreType.DMA((micros,)),
            pltpu.SemaphoreType.DMA((8, micros)),
            pltpu.SemaphoreType.DMA((2,)),
        ],
        compiler_params=pltpu.CompilerParams(collective_id=1, has_side_effects=True, vmem_limit_bytes=VMEM_LIMIT),
        name="layer_passes",
    )(captions, tokens, cotangent, *small, *owned)


TILE = 384


def weights_kernel(
    n_dp,
    a0_in, dqkv_in, context_in, dr1_in, a1_in, du_in, hidden_in, dr2_in, sums, last,
    g_proj, g_comb, g_exp, g_red, sums_out, last_out,
    b_proj, b_comb, b_exp, b_red,
    c_proj, c_comb, c_exp, c_red,
    x_proj, x_comb, x_exp, x_red,
    p_proj, p_comb, p_exp, p_red,
    z_proj, z_comb, z_exp, z_red,
    sums_core, sums_x, sums_z, sums_a, sums_b, sums_c,
    low_from_pair, low_from_far, low_from_x, low_own,
    a0, dqkv, context, dr1, a1, du, hidden, dr2,
    core_send, core_recv, x_send, x_recv, z_send, z_recv,
    small_send, small_recv, load_sem, hidden_sem, last_send, last_recv, low_send, low_recv,
):
    pipe, dp, layer, half, across_x, across_y, core, other_core = place()
    n_z = n_dp // 2
    z = dp // 2
    near_z = z + 1 - 2 * (z % 2)
    steps = n_z // 2
    z_order = [(near_z + 2 * (step + 1)) % n_z for step in range(steps - 1)] + [near_z]
    z_order += [(z + 2 * (step + 1)) % n_z for step in range(steps - 1)] + [z]
    same_parity = z_order[steps:-1]
    def hidden_load(which, i):
        h = 1 - half if which == 0 else half
        width = 2 * b_red.shape[3]
        lanes = pl.ds(pl.multiple_of(h * HIDDEN_HALF + z_order[i] * width, 128), width)
        return pltpu.make_async_copy(hidden_in.at[:, lanes], hidden.at[:, lanes], hidden_sem.at[which, i])

    loads = [
        pltpu.make_async_copy(source, target, load_sem.at[i])
        for i, (source, target) in enumerate((
            (dr2_in, dr2), (a1_in, a1), (du_in, du), (a0_in, a0), (dqkv_in, dqkv), (context_in, context), (dr1_in, dr1),
        ))
    ]
    loads[0].start()
    for which in range(2):
        for i in range(n_z):
            hidden_load(which, i).start()
    for copy in loads[1:]:
        copy.start()
    relatives = (across_x, across_y, (across_x + 2) % 4)
    greet(
        [(target, dp) for target in relatives] + [(pipe, other_core)]
        + [(pipe, 2 * other + core) for other in [near_z] + same_parity]
    )

    last_copies = [
        remote(last.at[target], last_out.at[half], last_send.at[j], last_recv.at[j], (target, dp))
        for j, target in enumerate(relatives)
    ]
    last_own = pltpu.make_async_copy(last.at[pipe], last_out.at[half], load_sem.at[7])

    @pl.when(layer == 0)
    def _():
        for copy in last_copies:
            copy.start()
        last_own.start()

    mine = [b_red, b_exp, b_proj, b_comb]
    from_core = [c_red, c_exp, c_proj, c_comb]
    from_x = [x_red, x_exp, x_proj, x_comb]
    from_pair = [p_red, p_exp, p_proj, p_comb]
    from_far = [z_red, z_exp, z_proj, z_comb]
    outs = [g_red, g_exp, g_proj, g_comb]

    def spread(target, tile, cast=BF):
        r = target.shape[-2]
        for k in range(tile.shape[0] // (2 * r)):
            for c in range(2):
                yield c, k, tile[(2 * k + c) * r : (2 * k + c + 1) * r].astype(cast)

    def fill_red(h, at):
        width = 2 * b_red.shape[3]
        lanes = pl.ds(pl.multiple_of(h * HIDDEN_HALF + at * width, 128), width)
        for c, k, rows in spread(b_red, dot_tn(hidden[:, lanes], dr2[...])):
            b_red[c, h, at] = rows

    def fill_exp(step, carry):
        i, h = step // 2, step % 2
        tile = dot_tn(
            a1[:, pl.ds(pl.multiple_of(i * TILE, 128), TILE)],
            du[:, pl.ds(pl.multiple_of(h * HIDDEN_HALF, 128), HIDDEN_HALF)],
        )
        for c, k, rows in spread(b_exp, tile):
            b_exp[c, h, i * (TILE // (2 * b_exp.shape[3])) + k] = rows
        return carry

    def fill_proj(h, carry):
        tile = dot_tn(a0[...], dqkv[:, pl.ds(pl.multiple_of(h * 3 * HALF, 128), 3 * HALF)])
        for c, k, rows in spread(b_proj, tile):
            b_proj[c, h, k] = rows
        return carry

    def fill_comb():
        tile = dot_tn(context[...], dr1[...])
        for h in range(2):
            for c, k, rows in spread(b_comb, tile[h * HALF : (h + 1) * HALF]):
                b_comb[c, h, k] = rows

    low = b_red.shape[3] // 48 * 16
    low_rows = pl.ds(0, low)
    rows_of = [pl.ds(low, b_red.shape[3] - low)] + [pl.ds(0, b.shape[3]) for b in mine[1:]]

    def half_of(which):
        return 1 - half if which == 0 else half

    def core_copy(a, which, i):
        h, at = half_of(which), z_order[i]
        return remote(
            mine[a].at[1 - core, h, at, rows_of[a]], from_core[a].at[h, at, rows_of[a]],
            core_send.at[a, which, i], core_recv.at[a, which, i], (pipe, other_core),
        )

    def send_core(a, which):
        for i in range(n_z):
            core_copy(a, which, i).start()

    def x_copy(k):
        a, i = chunks[k]
        at = z_order[i]
        return remote(
            mine[a].at[core, 1 - half, at, rows_of[a]], from_x[a].at[at, rows_of[a]],
            x_send.at[a, i], x_recv.at[a, i], (across_x, dp),
        )

    def pair_copy(a, i):
        return remote(
            mine[a].at[core, half, z_order[i], rows_of[a]], from_pair[a].at[i, rows_of[a]],
            z_send.at[a, i], z_recv.at[a, i], (pipe, 2 * near_z + core),
        )

    def far_copy(a, i):
        other = same_parity[i]
        return remote(
            mine[a].at[core, half, other, rows_of[a]], from_far[a].at[i, rows_of[a]],
            z_send.at[a, steps + i], z_recv.at[a, steps + i], (pipe, 2 * other + core),
        )

    chunks = [(a, i) for a in range(4) for i in range(n_z)]

    def start_x(k):
        if k >= len(chunks):
            return
        a, i = chunks[k]
        at, rows = z_order[i], rows_of[a]
        core_copy(a, 0, i).wait_recv()
        total = mine[a][core, 1 - half, at, rows, :].astype(F32) + from_core[a][1 - half, at, rows, :].astype(F32)
        mine[a][core, 1 - half, at, rows, :] = total.astype(BF)
        x_copy(k).start()

    def after_x(k):
        a, i = chunks[k]
        at, rows = z_order[i], rows_of[a]
        x_copy(k).wait()
        start_x(k + REDUCE_DEPTH)
        core_copy(a, 1, i).wait_recv()
        total = mine[a][core, half, at, rows, :].astype(F32) + from_core[a][half, at, rows, :].astype(F32)
        total = total + from_x[a][at, rows, :].astype(F32)
        if i < steps:
            mine[a][core, half, at, rows, :] = total.astype(BF)
            pair_copy(a, i).start()
            return
        pair_copy(a, i - steps).wait_recv()
        total = total + from_pair[a][i - steps, rows, :].astype(F32)
        if i < n_z - 1:
            mine[a][core, half, at, rows, :] = total.astype(BF)
            far_copy(a, i - steps).start()
        else:
            outs[a][rows, :] = total

    def after_z(a):
        rows = rows_of[a]
        total = outs[a][rows, :]
        for i in range(steps - 1):
            far_copy(a, i).wait()
            total = total + from_far[a][i, rows, :].astype(F32)
        outs[a][rows, :] = total
        for i in range(steps):
            pair_copy(a, i).wait_send()

    def low_core(which, i):
        h, at = half_of(which), z_order[i]
        return remote(
            b_red.at[1 - core, h, at, low_rows], c_red.at[h, at, low_rows],
            low_send.at[which, i], low_recv.at[which, i], (pipe, other_core),
        )

    def low_pair(which, i):
        return remote(
            b_red.at[core, half_of(which), z_order[i], low_rows], low_from_pair.at[which, i],
            low_send.at[2 + which, i], low_recv.at[2 + which, i], (pipe, 2 * near_z + core),
        )

    def low_far(which, i):
        other = same_parity[i]
        return remote(
            b_red.at[core, half_of(which), other, low_rows], low_from_far.at[which, i],
            low_send.at[2 + which, steps + i], low_recv.at[2 + which, steps + i], (pipe, 2 * other + core),
        )

    low_x = remote(
        b_red.at[core, 1 - half, z, low_rows], low_from_x,
        low_send.at[2, n_z - 1], low_recv.at[2, n_z - 1], (across_x, dp),
    )

    def low_sum(which, i):
        h, at = half_of(which), z_order[i]
        low_core(which, i).wait_recv()
        return b_red[core, h, at, low_rows, :].astype(F32) + c_red[h, at, low_rows, :].astype(F32)

    def low_to_pair():
        for which in range(2):
            for i in range(steps):
                b_red[core, half_of(which), z_order[i], low_rows, :] = low_sum(which, i).astype(BF)
                low_pair(which, i).start()

    def low_to_far():
        for which in range(2):
            for i in range(steps, n_z):
                total = low_sum(which, i)
                low_pair(which, i - steps).wait_recv()
                total = total + low_from_pair[which, i - steps].astype(F32)
                if i < n_z - 1:
                    b_red[core, half_of(which), z_order[i], low_rows, :] = total.astype(BF)
                    low_far(which, i - steps).start()
                else:
                    low_own[which] = total

    def low_to_x():
        for which in range(2):
            total = low_own[which]
            for i in range(steps - 1):
                low_far(which, i).wait_recv()
                total = total + low_from_far[which, i].astype(F32)
            if which == 0:
                b_red[core, 1 - half, z, low_rows, :] = total.astype(BF)
                low_x.start()
            else:
                g_red[low_rows, :] = total

    def low_done():
        low_x.wait()
        g_red[low_rows, :] = g_red[low_rows, :] + low_from_x[...].astype(F32)
        for which in range(2):
            for i in range(n_z):
                low_core(which, i).wait_send()
            for i in range(steps):
                low_pair(which, i).wait_send()
            for i in range(steps - 1):
                low_far(which, i).wait_send()

    sums_copy_core = remote(sums, sums_core, small_send.at[0], small_recv.at[0], (pipe, other_core))
    sums_copy_x = remote(sums_a, sums_x, small_send.at[1], small_recv.at[1], (across_x, dp))
    sums_copy_pair = remote(
        sums_b, sums_z.at[steps - 1], small_send.at[2], small_recv.at[2], (pipe, 2 * near_z + core)
    )
    sums_copies_far = [
        remote(sums_c, sums_z.at[i], small_send.at[3 + i], small_recv.at[3 + i], (pipe, 2 * other + core))
        for i, other in enumerate(same_parity)
    ]

    sums_copy_core.start()
    loads[0].wait()
    for i in range(n_z):
        hidden_load(0, i).wait()
        fill_red(1 - half, z_order[i])
        core_copy(0, 0, i).start()
        low_core(0, i).start()
        if 1 <= i <= REDUCE_DEPTH:
            start_x(i - 1)
    for i in range(n_z):
        hidden_load(1, i).wait()
        fill_red(half, z_order[i])
        low_core(1, i).start()
        core_copy(0, 1, i).start()
    low_to_pair()
    loads[1].wait()
    loads[2].wait()
    lax.fori_loop(0, 2 * D // TILE, fill_exp, 0)
    send_core(1, 0)
    send_core(1, 1)
    sums_copy_core.wait()
    sums_a[...] = sums[...] + sums_core[...]
    sums_copy_x.start()
    after_x(0)
    after_x(1)
    loads[3].wait()
    loads[4].wait()
    lax.fori_loop(0, 2, fill_proj, 0)
    send_core(2, 0)
    send_core(2, 1)
    after_x(2)
    loads[5].wait()
    loads[6].wait()
    fill_comb()
    send_core(3, 0)
    send_core(3, 1)
    sums_copy_x.wait()
    sums_b[...] = sums_a[...] + sums_x[...]
    sums_copy_pair.start()
    for k in range(3, len(chunks)):
        after_x(k)
        if k == LOW_AT[0]:
            low_to_far()
        if k == LOW_AT[1]:
            low_to_x()
        if k == n_z:
            sums_copy_pair.wait()
            sums_c[...] = sums_b[...] + sums_z[steps - 1]
            for copy in sums_copies_far:
                copy.start()
        if k % n_z == n_z - 2 and k >= n_z:
            after_z(k // n_z - 1)
    low_done()
    after_z(3)
    for a in range(4):
        for which in range(2):
            for i in range(n_z):
                core_copy(a, which, i).wait_send()
    total = sums_c[...]
    for i in range(steps - 1):
        sums_copies_far[i].wait()
        total = total + sums_z[i]
    sums_out[...] = total

    @pl.when(layer == 0)
    def _():
        for copy in last_copies:
            copy.wait_send()
        last_own.wait()

    for j, source in enumerate(relatives):
        @pl.when(source // 2 == 0)
        def _():
            last_copies[j].wait_recv()


def weight_gradients(n_dp, a0, dqkv, context, dr1, a1, du, hidden, dr2, sums, last):
    vmem = pl.BlockSpec(memory_space=pltpu.VMEM)
    hbm = pl.BlockSpec(memory_space=pl.ANY)
    n_z = n_dp // 2
    low = HIDDEN_HALF // n_dp // 48 * 16
    shapes = [(D // n_dp, 3 * HALF), (HALF // n_dp, D), (D // n_dp, HIDDEN_HALF), (HIDDEN_HALF // n_dp, D)]
    return pl.pallas_call(
        functools.partial(weights_kernel, n_dp),
        out_shape=[jax.ShapeDtypeStruct(s, F32) for s in shapes]
        + [jax.ShapeDtypeStruct(sums.shape, F32), jax.ShapeDtypeStruct((2,) + last.shape[1:], BF)],
        in_specs=[hbm] * 8 + [vmem, hbm],
        out_specs=[vmem] * 5 + [hbm],
        scratch_shapes=[pltpu.VMEM((2, 2, n_z) + s, BF) for s in shapes]
        + [pltpu.VMEM((2, n_z) + s, BF) for s in shapes]
        + [pltpu.VMEM((n_z,) + s, BF) for s in shapes]
        + [pltpu.VMEM((n_z // 2,) + s, BF) for s in shapes]
        + [pltpu.VMEM((max(n_z // 2 - 1, 1),) + s, BF) for s in shapes]
        + [
            pltpu.VMEM(sums.shape, F32),
            pltpu.VMEM(sums.shape, F32),
            pltpu.VMEM((n_z // 2,) + sums.shape, F32),
            pltpu.VMEM(sums.shape, F32),
            pltpu.VMEM(sums.shape, F32),
            pltpu.VMEM(sums.shape, F32),
            pltpu.VMEM((2, n_z // 2, low, D), BF),
            pltpu.VMEM((2, max(n_z // 2 - 1, 1), low, D), BF),
            pltpu.VMEM((low, D), BF),
            pltpu.VMEM((2, low, D), F32),
        ]
        + [pltpu.VMEM(v.shape, BF) for v in (a0, dqkv, context, dr1, a1, du, hidden, dr2)]
        + [
            pltpu.SemaphoreType.DMA((4, 2, n_z)),
            pltpu.SemaphoreType.DMA((4, 2, n_z)),
            pltpu.SemaphoreType.DMA((4, n_z)),
            pltpu.SemaphoreType.DMA((4, n_z)),
            pltpu.SemaphoreType.DMA((4, n_z - 1)),
            pltpu.SemaphoreType.DMA((4, n_z - 1)),
            pltpu.SemaphoreType.DMA((n_z + 1,)),
            pltpu.SemaphoreType.DMA((n_z + 1,)),
            pltpu.SemaphoreType.DMA((8,)),
            pltpu.SemaphoreType.DMA((2, n_z)),
            pltpu.SemaphoreType.DMA((3,)),
            pltpu.SemaphoreType.DMA((3,)),
            pltpu.SemaphoreType.DMA((4, n_z)),
            pltpu.SemaphoreType.DMA((4, n_z)),
        ],
        compiler_params=pltpu.CompilerParams(collective_id=3, has_side_effects=True, vmem_limit_bytes=VMEM_LIMIT),
        name="weight_gradients",
    )(a0, dqkv, context, dr1, a1, du, hidden, dr2, sums, last)


def finish_kernel(n_dp, small, results_hbm, last_hbm, *refs):
    pipe, dp, layer, half, across_x, across_y, core, other_core = place()
    sources, encoded_hbm, tokens_hbm, outs, parts = refs[:4], refs[4], refs[5], refs[6:10], refs[10:18]
    results, last, encoded, tokens_grad = refs[18:22]
    held, in_sem, out_sem = refs[22:26], refs[26], refs[27]
    loads = [
        pltpu.make_async_copy(source, target, in_sem.at[i])
        for i, (source, target) in enumerate(zip(
            (results_hbm, last_hbm) + sources, (results, last) + held
        ))
    ]
    stores = [
        pltpu.make_async_copy(source, target, out_sem.at[i])
        for i, (source, target) in enumerate(zip(
            (tokens_grad, encoded) + held, (tokens_hbm, encoded_hbm) + tuple(out.at[0] for out in outs)
        ))
    ]
    for copy in loads:
        copy.start()
    loads[0].wait()
    loads[1].wait()
    for k, (first, out) in enumerate(((0, tokens_grad), (2, encoded))):
        parts_of = []
        for i in (first, first + 1):
            if first == 0:
                parts_of += [results[i, : results.shape[1] - last.shape[1], :], last[i]]
            else:
                parts_of.append(results[i])
        value = jnp.concatenate(parts_of, 0).astype(F32).T
        out[...] = value[:, : out.shape[1]].astype(out.dtype)
        stores[k].start()
        for i in (2 + 2 * k, 3 + 2 * k):
            loads[i].wait()
            stores[i].start()
    for row, out in enumerate(parts):
        count = out.shape[1]
        width = n_dp * count
        found = jnp.zeros(out.shape, F32)
        for h in range(2):
            for d in range(n_dp):
                at = d * count
                if row == 0:
                    at = h * 3 * HALF + at + (HALF if at >= HALF else 0)
                else:
                    at = h * width + at
                found = jnp.where((half == h) & (dp == d), small[row : row + 1, at : at + count], found)
        out[...] = found
    for copy in stores:
        copy.wait()


def finish(n_dp, local_rows, small, results, last, grads):
    vmem = pl.BlockSpec(memory_space=pltpu.VMEM)
    hbm = pl.BlockSpec(memory_space=pl.ANY)
    widths = [D, HALF, HALF, HALF, HIDDEN_HALF, HALF, HALF, HALF]
    return pl.pallas_call(
        functools.partial(finish_kernel, n_dp),
        out_shape=[
            jax.ShapeDtypeStruct((QUARTER, local_rows), BF),
            jax.ShapeDtypeStruct((QUARTER, local_rows), F32),
        ]
        + [jax.ShapeDtypeStruct((1,) + g.shape, F32) for g in grads]
        + [jax.ShapeDtypeStruct((1, w // n_dp), F32) for w in widths],
        in_specs=[vmem] + [hbm] * 6,
        out_specs=[hbm] * 6 + [vmem] * 8,
        scratch_shapes=[
            pltpu.VMEM(results.shape, BF),
            pltpu.VMEM(last.shape, BF),
            pltpu.VMEM((QUARTER, local_rows), BF),
            pltpu.VMEM((QUARTER, local_rows), F32),
        ]
        + [pltpu.VMEM(g.shape, F32) for g in grads]
        + [pltpu.SemaphoreType.DMA((6,))] * 2,
        compiler_params=pltpu.CompilerParams(vmem_limit_bytes=VMEM_LIMIT),
        name="finish",
    )(small, results, last, *grads)


def weight_gradients_by_scatter(n_dp, a0, dqkv, context, dr1, a1, du, hidden, dr2, sums, last):
    half = lax.axis_index("pipe") % 2
    halves = (
        dot_tn(a0, dqkv).reshape(D, 2, 3 * HALF).transpose(1, 0, 2),
        dot_tn(context, dr1).reshape(2, HALF, D),
        dot_tn(a1, du).reshape(D, 2, HIDDEN_HALF).transpose(1, 0, 2),
        dot_tn(hidden, dr2).reshape(2, HIDDEN_HALF, D),
    )
    swap = [(i, i ^ 1) for i in range(PIPE)]
    found = []
    for member in halves:
        part = lax.psum_scatter(member, "dp", scatter_dimension=1, tiled=True)
        keep = lax.dynamic_index_in_dim(part, half, 0, keepdims=False)
        send = lax.dynamic_index_in_dim(part, 1 - half, 0, keepdims=False)
        found.append(keep + lax.ppermute(send.astype(BF), "pipe", swap).astype(F32))
    small = lax.psum(sums, "dp")
    received = lax.all_to_all(last, "pipe", 0, 0, tiled=False)
    return found + [small + lax.ppermute(small, "pipe", swap), received[:2]]


def shards(
    n_dp,
    tokens, cotangent, captions, projection, biases, combiner, offsets, scaling, centring,
    expansion, lifting, reduction, settling, stretch, translate,
):
    local_rows = tokens.shape[0]
    local_pairs = local_rows // PAIR_ROWS
    pairs = 2 * ((local_pairs + 3) // 4)
    block = 2 * PAIR_ROWS
    micros = pairs // 2
    owned = (projection[0], combiner[0], expansion[0], reduction[0])
    small = (biases, offsets, scaling, centring, lifting, settling, stretch, translate)
    *kept, results, last = layer_passes(micros, block, captions, small, tokens.T, cotangent.T, owned)
    a0, context, a1, hidden, dr2, du, dr1, dqkv, sums = kept
    whole_tiles = HALF % (16 * n_dp) == 0
    collect = weight_gradients if whole_tiles else weight_gradients_by_scatter
    *grads, sums, last = collect(n_dp, a0, dqkv, context, dr1, a1, du, hidden, dr2, sums, last)
    encoded, tokens_grad, g_proj, g_comb, g_exp, g_red, *parts = finish(n_dp, local_rows, sums, results, last, grads)
    return (
        encoded.T, tokens_grad.T, g_proj, parts[0], g_comb, parts[1], parts[2], parts[3],
        g_exp, parts[4], g_red, parts[5], parts[6], parts[7],
    )


def solution(mesh):
    rows = P("dp", "pipe")
    matrix = P("pipe", None, None)
    vector = P("pipe", None)
    matrix_out = P("pipe", "dp", None)
    vector_out = P("pipe", "dp")
    in_specs = (
        rows, rows, P("dp"), matrix, vector, matrix, vector, vector, vector,
        matrix, vector, matrix, vector, vector, vector,
    )
    out_specs = (
        rows, rows, matrix_out, vector_out, matrix_out, vector_out, vector_out, vector_out,
        matrix_out, vector_out, matrix_out, vector_out, vector_out, vector_out,
    )
    return jax.shard_map(
        functools.partial(shards, mesh.shape["dp"]),
        mesh=mesh, in_specs=in_specs, out_specs=out_specs, check_vma=False,
    )
```

```python
import functools

import jax
import jax.numpy as jnp
from jax import lax
from jax.experimental import pallas as pl
from jax.experimental.pallas import tpu as pltpu
from jax.sharding import PartitionSpec as P

D = 768
HEADS = 12
HEAD_DIM = 64
FF = 3072
WORDS = 64
PAIR_ROWS = 104
HALF = D // 2
HIDDEN_HALF = FF // 2
QUARTER = D // 4
PIPE = 4
GROUP_WIDTH = 2 * HEAD_DIM
GROUPS = HEADS // 2
STACKED = 2 * PAIR_ROWS

EPSILON = 1e-05
NEGATIVE = -1e30
SCALE = HEAD_DIM ** (-0.5)

MESH = pl.DeviceIdType.MESH
BF = jnp.bfloat16
F32 = jnp.float32
VMEM_LIMIT = 60 << 20


def dot_nn(left, right):
    return lax.dot_general(left, right, (((1,), (0,)), ((), ())), preferred_element_type=F32)


def dot_nt(left, right):
    return lax.dot_general(left, right, (((1,), (1,)), ((), ())), preferred_element_type=F32)


def dot_tn(left, right):
    return lax.dot_general(left, right, (((0,), (0,)), ((), ())), preferred_element_type=F32)


def place():
    pipe = lax.axis_index("pipe")
    dp = lax.axis_index("dp")
    layer = pipe // 2
    half = pipe % 2
    across_x = pipe + 1 - 2 * half
    across_y = (pipe + 2) % 4
    core = dp % 2
    other_core = dp + 1 - 2 * core
    return pipe, dp, layer, half, across_x, across_y, core, other_core


def greet(devices):
    barrier = pltpu.get_barrier_semaphore()
    for device in devices:
        pl.semaphore_signal(barrier, inc=1, device_id=device, device_id_type=MESH)
    pl.semaphore_wait(barrier, len(devices))


def remote(source, target, send, recv, device):
    return pltpu.make_async_remote_copy(
        src_ref=source,
        dst_ref=target,
        send_sem=send,
        recv_sem=recv,
        device_id=device,
        device_id_type=MESH,
    )


WEIGHT_SHAPES = [(D, 3 * HALF), (HALF, D), (D, HIDDEN_HALF), (HIDDEN_HALF, D)]
CHUNKS = [(0, 0, 96), (0, 96, 96), (1, 0, 96)] + [(2, i*48, 48) for i in range(4)] + [(3, i*96, 96) for i in range(4)]
ATTENTION_CHUNKS = 3
FIRST_LANES = 256
DEPTH = 3
LAG = 2
REDUCE_DEPTH = 3
LOW_AT = (4, 10, 14)


def left_lanes():
    return lax.broadcasted_iota(jnp.int32, (PAIR_ROWS, GROUP_WIDTH), 1) < HEAD_DIM


def stacked(values, scale=None):
    if scale is not None:
        values = values * scale
    left = left_lanes()
    return jnp.concatenate([jnp.where(left, values, 0.0), jnp.where(left, 0.0, values)], 0).astype(BF)


def own_lanes(values):
    return jnp.where(left_lanes(), values[:PAIR_ROWS], values[PAIR_ROWS:])


def normalized(residual):
    average = jnp.mean(residual, axis=-1, keepdims=True)
    centred = residual - average
    variance = jnp.mean(centred * centred, axis=-1, keepdims=True)
    inverse = lax.rsqrt(variance + EPSILON)
    return centred * inverse, inverse


def norm_backward(gradient, norm, inverse, gain):
    scaled = gradient * gain
    first = jnp.mean(scaled, axis=-1, keepdims=True)
    second = jnp.mean(scaled * norm, axis=-1, keepdims=True)
    return (scaled - first - norm * second) * inverse


def column_sums(value):
    return jnp.sum(value, axis=0, keepdims=True)


def layer_kernel(
    micros, block, local_pairs,
    captions, tokens_hbm, cotangent_hbm, biases, offsets, scaling, centring, lifting, settling, stretch, translate,
    own_proj, own_comb, own_exp, own_red,
    a0_hbm, context_hbm, a1_hbm, hidden_hbm, dr2_hbm, du_hbm, dr1_hbm, dqkv_hbm, sums_out, results_out, last_out,
    tokens, cotangent, both, own_vectors, joint, mixing, expand, reduce, pieces, unpacked, other_vectors, vectors, results,
    slots, outgoing, qkv_keep, prob_keep, n1_keep, r1_keep, n2_keep, r2_keep, slope_keep,
    a_s, qkv_s, context_s, dqkv_s,
    a0_ring, context_ring, a1_ring, hidden_ring, dr2_ring, du_ring, dr1_ring, dqkv_ring,
    send, recv, x_send, x_recv, z_send, z_recv, near_send, near_recv, far_send, far_recv,
    own_sem, piece_send, piece_recv, vec_sem, result_send, result_recv, result_sem, ring_sem, row_sem,
):
    pipe, dp, layer, half, across_x, across_y, core, other_core = place()
    step = pl.program_id(0)
    pairs = block // PAIR_ROWS
    rows = micros * block
    diagonal = (across_x + 2) % 4
    parity = (dp // 2) % 2
    across_z = dp + 2 - 4 * parity
    mine = 2 * parity + core
    paired = 2 * (1 - parity) + core
    relatives = (across_x, across_y, diagonal)
    owned = [own_proj, own_comb, own_exp, own_red]
    held = [joint, mixing, expand, reduce]
    n = len(CHUNKS)

    def span(chunk, quarter):
        which, start, count = chunk
        return pl.ds(quarter * (WEIGHT_SHAPES[which][0] // 4) + start, count)

    def x_copy(k):
        at = span(CHUNKS[k], mine)
        which = CHUNKS[k][0]
        return remote(owned[which].at[at], held[which].at[half, at], x_send.at[k], x_recv.at[k], (across_x, dp))

    def z_copy(k):
        region = held[CHUNKS[k][0]].at[1 - half, span(CHUNKS[k], mine)]
        return remote(region, region, z_send.at[k], z_recv.at[k], (pipe, across_z))

    def near_copy(k):
        region = held[CHUNKS[k][0]].at[1 - half, span(CHUNKS[k], mine)]
        return remote(region, region, near_send.at[k], near_recv.at[k], (pipe, other_core))

    def far_copy(k):
        region = held[CHUNKS[k][0]].at[1 - half, span(CHUNKS[k], paired)]
        return remote(region, region, far_send.at[k], far_recv.at[k], (pipe, other_core))

    own_copies = [pltpu.make_async_copy(owned[i], held[i].at[half], own_sem.at[i]) for i in range(4)]
    own_piece = pltpu.make_async_copy(both.at[layer, half], pieces.at[pipe], own_sem.at[4])
    lanes_held = both.shape[3]
    lanes_of = (pl.ds(0, FIRST_LANES), pl.ds(FIRST_LANES, lanes_held - FIRST_LANES))
    vec_copy = remote(own_vectors, other_vectors, vec_sem.at[0], vec_sem.at[1], (across_x, dp))
    piece_copies = [
        [
            remote(
                both.at[target // 2, target % 2, :, lanes], pieces.at[pipe, :, lanes],
                piece_send.at[part, j], piece_recv.at[part, j], (target, dp),
            )
            for j, target in enumerate(relatives)
        ]
        for part, lanes in enumerate(lanes_of)
    ]

    def send_pieces(to_layer, part):
        for j, target in enumerate(relatives):
            @pl.when(target // 2 == to_layer)
            def _():
                piece_copies[part][j].start()

    def hand_on(k):
        z_copy(k).wait_recv()
        far_copy(k).start()

    def arrived(first, last):
        for k in range(first, last):
            near_copy(k).wait_recv()
            far_copy(k).wait_recv()

    def gather_most():
        for k in range(n):
            x_copy(k).wait_recv()
            z_copy(k).start()
            near_copy(k).start()
            if k + DEPTH < n:
                x_copy(k).wait_send()
                x_copy(k + DEPTH).start()
            if k + DEPTH == n - 1:
                send_pieces(0, 1)
                send_pieces(1, 0)
                send_pieces(1, 1)
            if k >= LAG:
                hand_on(k - LAG)
        arrived(0, ATTENTION_CHUNKS)
        own_copies[0].wait()
        own_copies[1].wait()

    def gather_rest():
        for k in range(n - LAG, n):
            hand_on(k)
        arrived(ATTENTION_CHUNKS, n)
        own_copies[2].wait()
        own_copies[3].wait()

    def y_copy(index):
        return remote(outgoing.at[index], slots.at[index], send.at[index], recv.at[index], (across_y, dp))

    def rows_of(index):
        return pl.ds(pl.multiple_of(index * block, 16), block)

    def result_copies(index):
        return [
            remote(
                results.at[target, rows_of(index)], results_out.at[pipe, rows_of(index)],
                result_send.at[j, index], result_recv.at[j, index], (target, dp),
            )
            for j, target in enumerate(relatives)
        ]

    def own_result(index):
        return pltpu.make_async_copy(
            results.at[pipe, rows_of(index)], results_out.at[pipe, rows_of(index)], result_sem.at[index]
        )

    def share_result(index, value):
        for i in range(PIPE):
            results[i, rows_of(index), :] = value[:, i * QUARTER : (i + 1) * QUARTER]
        for copy in result_copies(index):
            copy.start()
        own_result(index).start()

    def wait_results(index):
        final = index == micros - 1
        for j, copy in enumerate(result_copies(index)):
            if not final:
                copy.wait()
                continue

            @pl.when(layer == 1)
            def _():
                copy.wait_send()

            @pl.when(relatives[j] // 2 == 1)
            def _():
                copy.wait_recv()

        @pl.when((layer == 1) | (not final))
        def _():
            own_result(index).wait()

    rings = [
        (a0_ring, a0_hbm), (context_ring, context_hbm), (a1_ring, a1_hbm), (hidden_ring, hidden_hbm),
        (dr2_ring, dr2_hbm), (du_ring, du_hbm), (dr1_ring, dr1_hbm), (dqkv_ring, dqkv_hbm),
    ]

    def ring_copy(which, index):
        ring, target = rings[which]
        return pltpu.make_async_copy(ring.at[index % 2], target.at[rows_of(index)], ring_sem.at[which, index])

    def ring_slots(first, last, index):
        @pl.when(index >= 2)
        def _():
            for which in range(first, last):
                ring_copy(which, index - 2).wait()

        return [rings[which][0].at[index % 2] for which in range(first, last)]

    def ring_start(first, last, index):
        for which in range(first, last):
            ring_copy(which, index).start()

    def unpack_pieces(part):
        for copy in piece_copies[part]:
            copy.wait_recv()
        at = lanes_of[part]
        value = pieces[:, :, at.start : at.start + at.size].reshape(D, at.size)
        unpacked[at.start : at.start + at.size, :] = value.astype(F32).T.astype(BF)

    @pl.when(step == 0)
    def _():
        row_copies = [
            pltpu.make_async_copy(tokens_hbm, tokens, row_sem.at[0]),
            pltpu.make_async_copy(cotangent_hbm, cotangent, row_sem.at[1]),
        ]
        for copy in row_copies:
            copy.start()
        greet([(across_x, dp), (across_y, dp), (diagonal, dp), (pipe, across_z), (pipe, other_core)])
        for i, source in enumerate((biases, offsets, scaling, centring, lifting, settling, stretch, translate)):
            own_vectors[i : i + 1, : source.shape[1]] = source[...].astype(F32)
        vec_copy.start()
        for t, source in enumerate((tokens, cotangent)):
            row_copies[t].wait()
            whole = source[...].astype(F32)
            for h in range(2):
                value = whole[:, h * rows : (h + 1) * rows]
                spare = jnp.zeros((QUARTER, lanes_held - value.shape[1]), F32)
                both[t, h] = jnp.concatenate([value, spare], 1).astype(BF)
            if t == 0:
                send_pieces(0, 0)
                for k in range(DEPTH):
                    x_copy(k).start()
        for copy in own_copies:
            copy.start()
        own_piece.start()
        sums_out[...] = jnp.zeros_like(sums_out)
        vec_copy.wait_recv()
        for which in range(2):
            value = jnp.where(half == which, own_vectors[...], other_vectors[...])
            vectors[0:1, which * 3 * HALF : which * 3 * HALF + HALF] = value[0:1, :HALF]
            vectors[0:1, which * 3 * HALF + HALF : which * 3 * HALF + D] = jnp.zeros((1, HALF), F32)
            vectors[0:1, which * 3 * HALF + D : (which + 1) * 3 * HALF] = value[0:1, HALF:D]
            for i in (1, 2, 3, 5, 6, 7):
                vectors[i : i + 1, which * HALF : (which + 1) * HALF] = value[i : i + 1, :HALF]
            vectors[4:5, which * HIDDEN_HALF : (which + 1) * HIDDEN_HALF] = value[4:5, :]
        own_piece.wait()
        gather_most()

        @pl.when(layer == 1)
        def _():
            gather_rest()

    @pl.when(((layer == 0) & (step < micros)) | ((layer == 1) & (step % 2 == 0)))
    def _():
        micro = (1 - layer) * step + layer * (step // 2)
        a0_out, context_out, a1_out, hidden_out = ring_slots(0, 4, micro)

        for part in range(2):
            @pl.when((layer == 0) & (micro == part))
            def _():
                unpack_pieces(part)

        @pl.when(layer == 0)
        def _():
            a_s[...] = unpacked[rows_of(micro), :]

        @pl.when(layer == 1)
        def _():
            y_copy(micro).wait_recv()
            a_s[...] = slots[micro]

        inputs = a_s[...]
        a0_out[...] = inputs
        for which in range(2):
            value = dot_nn(inputs, joint[which]) + vectors[0:1, which * 3 * HALF : (which + 1) * 3 * HALF]
            for part in range(3):
                cols = slice(part * D + which * HALF, part * D + (which + 1) * HALF)
                found = value[:, part * HALF : (part + 1) * HALF]
                qkv_s[:, cols] = found
                qkv_keep[micro, :, cols] = found.astype(BF)
        over = [(pair, group) for pair in range(pairs) for group in range(GROUPS)]
        spans = [
            (
                slice(pair * PAIR_ROWS, (pair + 1) * PAIR_ROWS),
                [slice(part * D + group * GROUP_WIDTH, part * D + (group + 1) * GROUP_WIDTH) for part in range(3)],
            )
            for pair, group in over
        ]
        key = lax.broadcasted_iota(jnp.int32, (PAIR_ROWS, PAIR_ROWS), 0)
        masks = []
        for pair in range(pairs):
            length = captions[jnp.minimum((half * micros + micro) * pairs + pair, local_pairs - 1)]
            masks.append(jnp.where((key >= WORDS) | (key < length), 0.0, NEGATIVE))
        scores = [
            dot_nt(stacked(qkv_s[at, lanes[1]], SCALE), qkv_s[at, lanes[0]].astype(BF)) for at, lanes in spans
        ]
        values = [stacked(qkv_s[at, lanes[2]]) for at, lanes in spans]
        probs = []
        for k, (pair, group) in enumerate(over):
            found = []
            for i in range(2):
                score = scores[k][i * PAIR_ROWS : (i + 1) * PAIR_ROWS] + masks[pair]
                exponent = jnp.exp(score - jnp.max(score, axis=0, keepdims=True))
                found.append(exponent * (1.0 / jnp.sum(exponent, axis=0, keepdims=True)))
            probs.append(jnp.concatenate(found, 0).astype(BF))
        contexts = [dot_tn(probs[k], values[k]) for k in range(len(over))]
        for k, (at, lanes) in enumerate(spans):
            prob_keep[micro, k] = probs[k]
            context_s[at, lanes[0]] = contexts[k]
        context = context_s[...].astype(BF)
        context_out[...] = context
        residual = inputs.astype(F32) + dot_nn(context, mixing[...].reshape(D, D)) + vectors[1:2, :D]
        norm, inverse = normalized(residual)
        n1_keep[micro] = norm.astype(BF)
        r1_keep[micro] = inverse
        attended = (norm * vectors[2:3, :D] + vectors[3:4, :D]).astype(BF)
        a1_out[...] = attended

        @pl.when((micro == 0) & (layer == 0))
        def _():
            gather_rest()

        residual = attended.astype(F32) + vectors[5:6, :D]
        for which in range(2):
            cols = slice(which * HIDDEN_HALF, (which + 1) * HIDDEN_HALF)
            raised = dot_nn(attended, expand[which]) + vectors[4:5, cols]
            below = 0.5 * (1.0 + lax.erf(raised * (0.5**0.5)))
            hidden = (raised * below).astype(BF)
            hidden_out[:, cols] = hidden
            density = jnp.exp(raised * raised * (-0.5)) * 0.3989422804014327
            slope_keep[micro, :, cols] = (below + raised * density).astype(BF)
            residual = residual + dot_nn(hidden, reduce[which])
        norm, inverse = normalized(residual)
        n2_keep[micro] = norm.astype(BF)
        r2_keep[micro] = inverse
        result = (norm * vectors[6:7, :D] + vectors[7:8, :D]).astype(BF)

        @pl.when(layer == 0)
        def _():
            outgoing[micro] = result
            y_copy(micro).start()

        @pl.when(layer == 1)
        def _():
            share_result(micro, result)

        ring_start(0, 4, micro)

    def add_sum(row, value):
        width = value.shape[1]
        sums_out[row : row + 1, :width] += column_sums(value)

    @pl.when(((layer == 0) & (step >= micros)) | ((layer == 1) & (step % 2 == 1)))
    def _():
        micro = (1 - layer) * (step - micros) + layer * (step // 2)
        dr2_out, du_out, dr1_out, dqkv_out = ring_slots(4, 8, micro)

        @pl.when((layer == 1) & (micro == 0))
        def _():
            unpack_pieces(0)
            unpack_pieces(1)

        @pl.when(layer == 1)
        def _():
            a_s[...] = unpacked[rows_of(micro), :]

        @pl.when(layer == 0)
        def _():
            y_copy(micro).wait_recv()
            a_s[...] = slots[micro]

        gradient = a_s[...].astype(F32)
        norm = n2_keep[micro].astype(F32)
        add_sum(6, gradient * norm)
        add_sum(7, gradient)
        grad_residual = norm_backward(gradient, norm, r2_keep[micro], vectors[6:7, :D])
        add_sum(5, grad_residual)
        branch = grad_residual.astype(BF)
        dr2_out[...] = branch
        total = grad_residual
        for which in range(2):
            cols = slice(which * HIDDEN_HALF, (which + 1) * HIDDEN_HALF)
            raised = dot_nt(branch, reduce[which]) * slope_keep[micro, :, cols].astype(F32)
            sums_out[4:5, cols] += column_sums(raised)
            raised = raised.astype(BF)
            du_out[:, cols] = raised
            total = total + dot_nt(raised, expand[which])

        gradient = total.astype(BF).astype(F32)
        norm = n1_keep[micro].astype(F32)
        add_sum(2, gradient * norm)
        add_sum(3, gradient)
        grad_residual = norm_backward(gradient, norm, r1_keep[micro], vectors[2:3, :D])
        add_sum(1, grad_residual)
        branch = grad_residual.astype(BF)
        dr1_out[...] = branch
        context_s[...] = dot_nt(branch, mixing[...].reshape(D, D))
        qkv_s[...] = qkv_keep[micro].astype(F32)
        spans = [
            (
                slice(pair * PAIR_ROWS, (pair + 1) * PAIR_ROWS),
                [slice(part * D + group * GROUP_WIDTH, part * D + (group + 1) * GROUP_WIDTH) for part in range(3)],
            )
            for pair in range(pairs)
            for group in range(GROUPS)
        ]
        over = range(len(spans))
        queries = [qkv_s[at, lanes[0]].astype(BF) for at, lanes in spans]
        keys = [stacked(qkv_s[at, lanes[1]], SCALE) for at, lanes in spans]
        values = [stacked(qkv_s[at, lanes[2]]) for at, lanes in spans]
        grads = [context_s[at, lanes[0]].astype(BF) for at, lanes in spans]
        rounded = [prob_keep[micro, g] for g in over]
        grad_probs = [dot_nt(values[g], grads[g]) for g in over]
        grad_values = [dot_nn(rounded[g], grads[g]) for g in over]
        grad_scores = []
        for g in over:
            probs = rounded[g].astype(F32)
            weighted = probs * grad_probs[g]
            found = []
            for i in range(2):
                at = slice(i * PAIR_ROWS, (i + 1) * PAIR_ROWS)
                found.append(weighted[at] - probs[at] * column_sums(weighted[at]))
            grad_scores.append(jnp.concatenate(found, 0).astype(BF))
        grad_keys = [dot_nn(grad_scores[g], queries[g]) for g in over]
        grad_queries = [dot_tn(grad_scores[g], keys[g]) for g in over]
        for g, (at, lanes) in enumerate(spans):
            dqkv_s[at, lanes[0]] = grad_queries[g]
            dqkv_s[at, lanes[1]] = own_lanes(grad_keys[g]) * SCALE
            dqkv_s[at, lanes[2]] = own_lanes(grad_values[g])
        total = grad_residual
        for which in range(2):
            value = jnp.concatenate(
                [dqkv_s[:, part * D + which * HALF : part * D + (which + 1) * HALF] for part in range(3)], 1
            ).astype(BF)
            cols = slice(which * 3 * HALF, (which + 1) * 3 * HALF)
            dqkv_out[:, cols] = value
            sums_out[0:1, cols] += column_sums(value.astype(F32))
            total = total + dot_nt(value, joint[which])
        result = total.astype(BF)

        @pl.when(layer == 1)
        def _():
            outgoing[micro] = result
            y_copy(micro).start()

        ring_start(4, 8, micro)

        @pl.when((layer == 0) & (micro < micros - 1))
        def _():
            share_result(micro, result)

        @pl.when((layer == 0) & (micro == micros - 1))
        def _():
            for i in range(PIPE):
                last_out[i] = result[:, i * QUARTER : (i + 1) * QUARTER]

    @pl.when(step == 2 * micros - 1)
    def _():
        for index in range(micros):
            y_copy(index).wait_send()
            wait_results(index)
        for index in range(max(micros - 2, 0), micros):
            for which in range(8):
                ring_copy(which, index).wait()
        for k in range(n):
            if k + DEPTH >= n:
                x_copy(k).wait_send()
            z_copy(k).wait_send()
            near_copy(k).wait_send()
            far_copy(k).wait_send()
        for copy in piece_copies[0] + piece_copies[1] + [vec_copy]:
            copy.wait_send()


def layer_passes(micros, block, captions, small, tokens, cotangent, owned):
    rows = micros * block
    n = len(CHUNKS)
    lanes_held = (rows + 127) // 128 * 128
    vmem = pl.BlockSpec(memory_space=pltpu.VMEM)
    hbm = pl.BlockSpec(memory_space=pl.ANY)

    forward_widths = [D, D, D, FF]
    backward_widths = [D, FF, D, 3 * D]
    pairs = block // PAIR_ROWS
    return pl.pallas_call(
        functools.partial(layer_kernel, micros, block, captions.shape[0]),
        grid=(2 * micros,),
        out_shape=[jax.ShapeDtypeStruct((rows, w), BF) for w in forward_widths + backward_widths]
        + [
            jax.ShapeDtypeStruct((8, FF), F32),
            jax.ShapeDtypeStruct((PIPE, rows, QUARTER), BF),
            jax.ShapeDtypeStruct((PIPE, block, QUARTER), BF),
        ],
        in_specs=[pl.BlockSpec(memory_space=pltpu.SMEM)] + [hbm] * 2 + [vmem] * 8 + [hbm] * 4,
        out_specs=[hbm] * 8 + [vmem, hbm, vmem],
        scratch_shapes=[
            pltpu.VMEM(tokens.shape, BF),
            pltpu.VMEM(cotangent.shape, BF),
            pltpu.VMEM((2, 2, QUARTER, lanes_held), BF),
            pltpu.VMEM((8, HIDDEN_HALF), F32),
        ]
        + [pltpu.VMEM((2,) + shape, BF) for shape in WEIGHT_SHAPES]
        + [
            pltpu.VMEM((PIPE, QUARTER, lanes_held), BF),
            pltpu.VMEM((lanes_held, D), BF),
            pltpu.VMEM((8, HIDDEN_HALF), F32),
            pltpu.VMEM((8, FF), F32),
            pltpu.VMEM((PIPE, rows, QUARTER), BF),
            pltpu.VMEM((micros, block, D), BF),
            pltpu.VMEM((micros, block, D), BF),
            pltpu.VMEM((micros, block, 3 * D), BF),
            pltpu.VMEM((micros, pairs * GROUPS, STACKED, PAIR_ROWS), BF),
            pltpu.VMEM((micros, block, D), BF),
            pltpu.VMEM((micros, block, 1), F32),
            pltpu.VMEM((micros, block, D), BF),
            pltpu.VMEM((micros, block, 1), F32),
            pltpu.VMEM((micros, block, FF), BF),
            pltpu.VMEM((block, D), BF),
            pltpu.VMEM((block, 3 * D), F32),
            pltpu.VMEM((block, D), F32),
            pltpu.VMEM((block, 3 * D), F32),
        ]
        + [pltpu.VMEM((2, block, w), BF) for w in forward_widths + backward_widths]
        + [pltpu.SemaphoreType.DMA((micros,))] * 2
        + [pltpu.SemaphoreType.DMA((n,))] * 8
        + [
            pltpu.SemaphoreType.DMA((5,)),
            pltpu.SemaphoreType.DMA((2, 3)),
            pltpu.SemaphoreType.DMA((2, 3)),
            pltpu.SemaphoreType.DMA((2,)),
            pltpu.SemaphoreType.DMA((3, micros)),
            pltpu.SemaphoreType.DMA((3, micros)),
            pltpu.SemaphoreType.DMA((micros,)),
            pltpu.SemaphoreType.DMA((8, micros)),
            pltpu.SemaphoreType.DMA((2,)),
        ],
        compiler_params=pltpu.CompilerParams(collective_id=1, has_side_effects=True, vmem_limit_bytes=VMEM_LIMIT),
        name="layer_passes",
    )(captions, tokens, cotangent, *small, *owned)


TILE = 384


def weights_kernel(
    n_dp,
    a0_in, dqkv_in, context_in, dr1_in, a1_in, du_in, hidden_in, dr2_in, sums, last,
    g_proj_hbm, g_comb_hbm, g_exp_hbm, g_red_hbm, sums_out, last_out,
    g_proj, g_comb, g_exp, g_red,
    b_proj, b_comb, b_exp, b_red,
    c_proj, c_comb, c_exp, c_red,
    x_proj, x_comb, x_exp, x_red,
    p_proj, p_comb, p_exp, p_red,
    z_proj, z_comb, z_exp, z_red,
    sums_core, sums_x, sums_z, sums_a, sums_b, sums_c,
    low_from_pair, low_from_far, low_from_x, low_own,
    a0, dqkv, context, dr1, a1, du, hidden, dr2,
    core_send, core_recv, x_send, x_recv, z_send, z_recv,
    small_send, small_recv, load_sem, hidden_sem, last_send, last_recv, low_send, low_recv, out_sem,
):
    pipe, dp, layer, half, across_x, across_y, core, other_core = place()
    n_z = n_dp // 2
    z = dp // 2
    near_z = z + 1 - 2 * (z % 2)
    steps = n_z // 2
    z_order = [(near_z + 2 * (step + 1)) % n_z for step in range(steps - 1)] + [near_z]
    z_order += [(z + 2 * (step + 1)) % n_z for step in range(steps - 1)] + [z]
    same_parity = z_order[steps:-1]
    def hidden_load(which, i):
        h = 1 - half if which == 0 else half
        width = 2 * b_red.shape[3]
        lanes = pl.ds(pl.multiple_of(h * HIDDEN_HALF + z_order[i] * width, 128), width)
        return pltpu.make_async_copy(hidden_in.at[:, lanes], hidden.at[:, lanes], hidden_sem.at[which, i])

    loads = [
        pltpu.make_async_copy(source, target, load_sem.at[i])
        for i, (source, target) in enumerate((
            (dr2_in, dr2), (a1_in, a1), (du_in, du), (a0_in, a0), (dqkv_in, dqkv), (context_in, context), (dr1_in, dr1),
        ))
    ]
    loads[0].start()
    for which in range(2):
        for i in range(n_z):
            hidden_load(which, i).start()
    for copy in loads[1:]:
        copy.start()
    relatives = (across_x, across_y, (across_x + 2) % 4)
    greet(
        [(target, dp) for target in relatives] + [(pipe, other_core)]
        + [(pipe, 2 * other + core) for other in [near_z] + same_parity]
    )

    last_copies = [
        remote(last.at[target], last_out.at[half], last_send.at[j], last_recv.at[j], (target, dp))
        for j, target in enumerate(relatives)
    ]
    last_own = pltpu.make_async_copy(last.at[pipe], last_out.at[half], load_sem.at[7])

    @pl.when(layer == 0)
    def _():
        for copy in last_copies:
            copy.start()
        last_own.start()

    mine = [b_red, b_exp, b_proj, b_comb]
    from_core = [c_red, c_exp, c_proj, c_comb]
    from_x = [x_red, x_exp, x_proj, x_comb]
    from_pair = [p_red, p_exp, p_proj, p_comb]
    from_far = [z_red, z_exp, z_proj, z_comb]
    outs = [g_red, g_exp, g_proj, g_comb]
    out_copies = [
        pltpu.make_async_copy(source, target, out_sem.at[a])
        for a, (source, target) in enumerate(zip(outs, (g_red_hbm, g_exp_hbm, g_proj_hbm, g_comb_hbm)))
    ]

    def spread(target, tile, cast=BF):
        r = target.shape[-2]
        for k in range(tile.shape[0] // (2 * r)):
            for c in range(2):
                yield c, k, tile[(2 * k + c) * r : (2 * k + c + 1) * r].astype(cast)

    def fill_red(h, at):
        width = 2 * b_red.shape[3]
        lanes = pl.ds(pl.multiple_of(h * HIDDEN_HALF + at * width, 128), width)
        for c, k, rows in spread(b_red, dot_tn(hidden[:, lanes], dr2[...])):
            b_red[c, h, at] = rows

    def fill_exp(step, carry):
        i, h = step // 2, step % 2
        tile = dot_tn(
            a1[:, pl.ds(pl.multiple_of(i * TILE, 128), TILE)],
            du[:, pl.ds(pl.multiple_of(h * HIDDEN_HALF, 128), HIDDEN_HALF)],
        )
        for c, k, rows in spread(b_exp, tile):
            b_exp[c, h, i * (TILE // (2 * b_exp.shape[3])) + k] = rows
        return carry

    def fill_proj(h, carry):
        tile = dot_tn(a0[...], dqkv[:, pl.ds(pl.multiple_of(h * 3 * HALF, 128), 3 * HALF)])
        for c, k, rows in spread(b_proj, tile):
            b_proj[c, h, k] = rows
        return carry

    def fill_comb():
        tile = dot_tn(context[...], dr1[...])
        for h in range(2):
            for c, k, rows in spread(b_comb, tile[h * HALF : (h + 1) * HALF]):
                b_comb[c, h, k] = rows

    low = b_red.shape[3] // 48 * 16
    low_rows = pl.ds(0, low)
    rows_of = [pl.ds(low, b_red.shape[3] - low)] + [pl.ds(0, b.shape[3]) for b in mine[1:]]

    def half_of(which):
        return 1 - half if which == 0 else half

    def core_copy(a, which, i):
        h, at = half_of(which), z_order[i]
        return remote(
            mine[a].at[1 - core, h, at, rows_of[a]], from_core[a].at[h, at, rows_of[a]],
            core_send.at[a, which, i], core_recv.at[a, which, i], (pipe, other_core),
        )

    def send_core(a, which):
        for i in range(n_z):
            core_copy(a, which, i).start()

    def x_copy(k):
        a, i = chunks[k]
        at = z_order[i]
        return remote(
            mine[a].at[core, 1 - half, at, rows_of[a]], from_x[a].at[at, rows_of[a]],
            x_send.at[a, i], x_recv.at[a, i], (across_x, dp),
        )

    def pair_copy(a, i):
        return remote(
            mine[a].at[core, half, z_order[i], rows_of[a]], from_pair[a].at[i, rows_of[a]],
            z_send.at[a, i], z_recv.at[a, i], (pipe, 2 * near_z + core),
        )

    def far_copy(a, i):
        other = same_parity[i]
        return remote(
            mine[a].at[core, half, other, rows_of[a]], from_far[a].at[i, rows_of[a]],
            z_send.at[a, steps + i], z_recv.at[a, steps + i], (pipe, 2 * other + core),
        )

    chunks = [(a, i) for a in range(4) for i in range(n_z)]

    def start_x(k):
        if k >= len(chunks):
            return
        a, i = chunks[k]
        at, rows = z_order[i], rows_of[a]
        core_copy(a, 0, i).wait_recv()
        total = mine[a][core, 1 - half, at, rows, :].astype(F32) + from_core[a][1 - half, at, rows, :].astype(F32)
        mine[a][core, 1 - half, at, rows, :] = total.astype(BF)
        x_copy(k).start()

    def after_x(k):
        a, i = chunks[k]
        at, rows = z_order[i], rows_of[a]
        x_copy(k).wait()
        start_x(k + REDUCE_DEPTH)
        core_copy(a, 1, i).wait_recv()
        total = mine[a][core, half, at, rows, :].astype(F32) + from_core[a][half, at, rows, :].astype(F32)
        total = total + from_x[a][at, rows, :].astype(F32)
        if i < steps:
            mine[a][core, half, at, rows, :] = total.astype(BF)
            pair_copy(a, i).start()
            return
        pair_copy(a, i - steps).wait_recv()
        total = total + from_pair[a][i - steps, rows, :].astype(F32)
        if i < n_z - 1:
            mine[a][core, half, at, rows, :] = total.astype(BF)
            far_copy(a, i - steps).start()
        else:
            outs[a][rows, :] = total

    def after_z(a):
        rows = rows_of[a]
        total = outs[a][rows, :]
        for i in range(steps - 1):
            far_copy(a, i).wait()
            total = total + from_far[a][i, rows, :].astype(F32)
        outs[a][rows, :] = total
        for i in range(steps):
            pair_copy(a, i).wait_send()

    def low_core(which, i):
        h, at = half_of(which), z_order[i]
        return remote(
            b_red.at[1 - core, h, at, low_rows], c_red.at[h, at, low_rows],
            low_send.at[which, i], low_recv.at[which, i], (pipe, other_core),
        )

    def low_pair(which, i):
        return remote(
            b_red.at[core, half_of(which), z_order[i], low_rows], low_from_pair.at[which, i],
            low_send.at[2 + which, i], low_recv.at[2 + which, i], (pipe, 2 * near_z + core),
        )

    def low_far(which, i):
        other = same_parity[i]
        return remote(
            b_red.at[core, half_of(which), other, low_rows], low_from_far.at[which, i],
            low_send.at[2 + which, steps + i], low_recv.at[2 + which, steps + i], (pipe, 2 * other + core),
        )

    low_x = remote(
        b_red.at[core, 1 - half, z, low_rows], low_from_x,
        low_send.at[2, n_z - 1], low_recv.at[2, n_z - 1], (across_x, dp),
    )

    def low_sum(which, i):
        h, at = half_of(which), z_order[i]
        low_core(which, i).wait_recv()
        return b_red[core, h, at, low_rows, :].astype(F32) + c_red[h, at, low_rows, :].astype(F32)

    def low_to_pair():
        for which in range(2):
            for i in range(steps):
                b_red[core, half_of(which), z_order[i], low_rows, :] = low_sum(which, i).astype(BF)
                low_pair(which, i).start()

    def low_to_far():
        for which in range(2):
            for i in range(steps, n_z):
                total = low_sum(which, i)
                low_pair(which, i - steps).wait_recv()
                total = total + low_from_pair[which, i - steps].astype(F32)
                if i < n_z - 1:
                    b_red[core, half_of(which), z_order[i], low_rows, :] = total.astype(BF)
                    low_far(which, i - steps).start()
                else:
                    low_own[which] = total

    def low_to_x():
        for which in range(2):
            total = low_own[which]
            for i in range(steps - 1):
                low_far(which, i).wait_recv()
                total = total + low_from_far[which, i].astype(F32)
            if which == 0:
                b_red[core, 1 - half, z, low_rows, :] = total.astype(BF)
                low_x.start()
            else:
                g_red[low_rows, :] = total

    def low_done():
        low_x.wait()
        g_red[low_rows, :] = g_red[low_rows, :] + low_from_x[...].astype(F32)
        for which in range(2):
            for i in range(n_z):
                low_core(which, i).wait_send()
            for i in range(steps):
                low_pair(which, i).wait_send()
            for i in range(steps - 1):
                low_far(which, i).wait_send()

    sums_copy_core = remote(sums, sums_core, small_send.at[0], small_recv.at[0], (pipe, other_core))
    sums_copy_x = remote(sums_a, sums_x, small_send.at[1], small_recv.at[1], (across_x, dp))
    sums_copy_pair = remote(
        sums_b, sums_z.at[steps - 1], small_send.at[2], small_recv.at[2], (pipe, 2 * near_z + core)
    )
    sums_copies_far = [
        remote(sums_c, sums_z.at[i], small_send.at[3 + i], small_recv.at[3 + i], (pipe, 2 * other + core))
        for i, other in enumerate(same_parity)
    ]

    sums_copy_core.start()
    loads[0].wait()
    for i in range(n_z):
        hidden_load(0, i).wait()
        fill_red(1 - half, z_order[i])
        core_copy(0, 0, i).start()
        low_core(0, i).start()
        if 1 <= i <= REDUCE_DEPTH:
            start_x(i - 1)
    for i in range(n_z):
        hidden_load(1, i).wait()
        fill_red(half, z_order[i])
        low_core(1, i).start()
        core_copy(0, 1, i).start()
    low_to_pair()
    loads[1].wait()
    loads[2].wait()
    lax.fori_loop(0, 2 * D // TILE, fill_exp, 0)
    send_core(1, 0)
    send_core(1, 1)
    sums_copy_core.wait()
    sums_a[...] = sums[...] + sums_core[...]
    sums_copy_x.start()
    after_x(0)
    after_x(1)
    loads[3].wait()
    loads[4].wait()
    lax.fori_loop(0, 2, fill_proj, 0)
    send_core(2, 0)
    send_core(2, 1)
    after_x(2)
    loads[5].wait()
    loads[6].wait()
    fill_comb()
    send_core(3, 0)
    send_core(3, 1)
    sums_copy_x.wait()
    sums_b[...] = sums_a[...] + sums_x[...]
    sums_copy_pair.start()
    for k in range(3, len(chunks)):
        after_x(k)
        if k == LOW_AT[0]:
            low_to_far()
        if k == LOW_AT[1]:
            low_to_x()
        if k == LOW_AT[2]:
            low_done()
            out_copies[0].start()
        if k == n_z:
            sums_copy_pair.wait()
            sums_c[...] = sums_b[...] + sums_z[steps - 1]
            for copy in sums_copies_far:
                copy.start()
        if k % n_z == n_z - 2 and k >= n_z:
            after_z(k // n_z - 1)
            if k // n_z > 1:
                out_copies[k // n_z - 1].start()
    after_z(3)
    out_copies[3].start()
    for a in range(4):
        for which in range(2):
            for i in range(n_z):
                core_copy(a, which, i).wait_send()
    total = sums_c[...]
    for i in range(steps - 1):
        sums_copies_far[i].wait()
        total = total + sums_z[i]
    sums_out[...] = total
    for copy in out_copies:
        copy.wait()

    @pl.when(layer == 0)
    def _():
        for copy in last_copies:
            copy.wait_send()
        last_own.wait()

    for j, source in enumerate(relatives):
        @pl.when(source // 2 == 0)
        def _():
            last_copies[j].wait_recv()


def weight_gradients(n_dp, a0, dqkv, context, dr1, a1, du, hidden, dr2, sums, last):
    vmem = pl.BlockSpec(memory_space=pltpu.VMEM)
    hbm = pl.BlockSpec(memory_space=pl.ANY)
    n_z = n_dp // 2
    low = HIDDEN_HALF // n_dp // 48 * 16
    shapes = [(D // n_dp, 3 * HALF), (HALF // n_dp, D), (D // n_dp, HIDDEN_HALF), (HIDDEN_HALF // n_dp, D)]
    return pl.pallas_call(
        functools.partial(weights_kernel, n_dp),
        out_shape=[jax.ShapeDtypeStruct(s, F32) for s in shapes]
        + [jax.ShapeDtypeStruct(sums.shape, F32), jax.ShapeDtypeStruct((2,) + last.shape[1:], BF)],
        in_specs=[hbm] * 8 + [vmem, hbm],
        out_specs=[hbm] * 4 + [vmem, hbm],
        scratch_shapes=[pltpu.VMEM(s, F32) for s in shapes]
        + [pltpu.VMEM((2, 2, n_z) + s, BF) for s in shapes]
        + [pltpu.VMEM((2, n_z) + s, BF) for s in shapes]
        + [pltpu.VMEM((n_z,) + s, BF) for s in shapes]
        + [pltpu.VMEM((n_z // 2,) + s, BF) for s in shapes]
        + [pltpu.VMEM((max(n_z // 2 - 1, 1),) + s, BF) for s in shapes]
        + [
            pltpu.VMEM(sums.shape, F32),
            pltpu.VMEM(sums.shape, F32),
            pltpu.VMEM((n_z // 2,) + sums.shape, F32),
            pltpu.VMEM(sums.shape, F32),
            pltpu.VMEM(sums.shape, F32),
            pltpu.VMEM(sums.shape, F32),
            pltpu.VMEM((2, n_z // 2, low, D), BF),
            pltpu.VMEM((2, max(n_z // 2 - 1, 1), low, D), BF),
            pltpu.VMEM((low, D), BF),
            pltpu.VMEM((2, low, D), F32),
        ]
        + [pltpu.VMEM(v.shape, BF) for v in (a0, dqkv, context, dr1, a1, du, hidden, dr2)]
        + [
            pltpu.SemaphoreType.DMA((4, 2, n_z)),
            pltpu.SemaphoreType.DMA((4, 2, n_z)),
            pltpu.SemaphoreType.DMA((4, n_z)),
            pltpu.SemaphoreType.DMA((4, n_z)),
            pltpu.SemaphoreType.DMA((4, n_z - 1)),
            pltpu.SemaphoreType.DMA((4, n_z - 1)),
            pltpu.SemaphoreType.DMA((n_z + 1,)),
            pltpu.SemaphoreType.DMA((n_z + 1,)),
            pltpu.SemaphoreType.DMA((8,)),
            pltpu.SemaphoreType.DMA((2, n_z)),
            pltpu.SemaphoreType.DMA((3,)),
            pltpu.SemaphoreType.DMA((3,)),
            pltpu.SemaphoreType.DMA((4, n_z)),
            pltpu.SemaphoreType.DMA((4, n_z)),
            pltpu.SemaphoreType.DMA((4,)),
        ],
        compiler_params=pltpu.CompilerParams(collective_id=3, has_side_effects=True, vmem_limit_bytes=VMEM_LIMIT),
        name="weight_gradients",
    )(a0, dqkv, context, dr1, a1, du, hidden, dr2, sums, last)


def finish_kernel(n_dp, small, results_hbm, last_hbm, *refs):
    pipe, dp, layer, half, across_x, across_y, core, other_core = place()
    sources, encoded_hbm, tokens_hbm, outs, parts = refs[:4], refs[4], refs[5], refs[6:10], refs[10:18]
    results, last, encoded, tokens_grad = refs[18:22]
    held, in_sem, out_sem = refs[22:26], refs[26], refs[27]
    loads = [
        pltpu.make_async_copy(source, target, in_sem.at[i])
        for i, (source, target) in enumerate(zip(
            (results_hbm, last_hbm) + sources, (results, last) + held
        ))
    ]
    stores = [
        pltpu.make_async_copy(source, target, out_sem.at[i])
        for i, (source, target) in enumerate(zip(
            (tokens_grad, encoded) + held, (tokens_hbm, encoded_hbm) + tuple(out.at[0] for out in outs)
        ))
    ]
    for copy in loads:
        copy.start()
    loads[0].wait()
    loads[1].wait()
    for k, (first, out) in enumerate(((0, tokens_grad), (2, encoded))):
        parts_of = []
        for i in (first, first + 1):
            if first == 0:
                parts_of += [results[i, : results.shape[1] - last.shape[1], :], last[i]]
            else:
                parts_of.append(results[i])
        value = jnp.concatenate(parts_of, 0).astype(F32).T
        out[...] = value[:, : out.shape[1]].astype(out.dtype)
        stores[k].start()
        for i in (2 + 2 * k, 3 + 2 * k):
            loads[i].wait()
            stores[i].start()
    for row, out in enumerate(parts):
        count = out.shape[1]
        width = n_dp * count
        found = jnp.zeros(out.shape, F32)
        for h in range(2):
            for d in range(n_dp):
                at = d * count
                if row == 0:
                    at = h * 3 * HALF + at + (HALF if at >= HALF else 0)
                else:
                    at = h * width + at
                found = jnp.where((half == h) & (dp == d), small[row : row + 1, at : at + count], found)
        out[...] = found
    for copy in stores:
        copy.wait()


def finish(n_dp, local_rows, small, results, last, grads):
    vmem = pl.BlockSpec(memory_space=pltpu.VMEM)
    hbm = pl.BlockSpec(memory_space=pl.ANY)
    widths = [D, HALF, HALF, HALF, HIDDEN_HALF, HALF, HALF, HALF]
    return pl.pallas_call(
        functools.partial(finish_kernel, n_dp),
        out_shape=[
            jax.ShapeDtypeStruct((QUARTER, local_rows), BF),
            jax.ShapeDtypeStruct((QUARTER, local_rows), F32),
        ]
        + [jax.ShapeDtypeStruct((1,) + g.shape, F32) for g in grads]
        + [jax.ShapeDtypeStruct((1, w // n_dp), F32) for w in widths],
        in_specs=[vmem] + [hbm] * 6,
        out_specs=[hbm] * 6 + [vmem] * 8,
        scratch_shapes=[
            pltpu.VMEM(results.shape, BF),
            pltpu.VMEM(last.shape, BF),
            pltpu.VMEM((QUARTER, local_rows), BF),
            pltpu.VMEM((QUARTER, local_rows), F32),
        ]
        + [pltpu.VMEM(g.shape, F32) for g in grads]
        + [pltpu.SemaphoreType.DMA((6,))] * 2,
        compiler_params=pltpu.CompilerParams(vmem_limit_bytes=VMEM_LIMIT),
        name="finish",
    )(small, results, last, *grads)


def weight_gradients_by_scatter(n_dp, a0, dqkv, context, dr1, a1, du, hidden, dr2, sums, last):
    half = lax.axis_index("pipe") % 2
    halves = (
        dot_tn(a0, dqkv).reshape(D, 2, 3 * HALF).transpose(1, 0, 2),
        dot_tn(context, dr1).reshape(2, HALF, D),
        dot_tn(a1, du).reshape(D, 2, HIDDEN_HALF).transpose(1, 0, 2),
        dot_tn(hidden, dr2).reshape(2, HIDDEN_HALF, D),
    )
    swap = [(i, i ^ 1) for i in range(PIPE)]
    found = []
    for member in halves:
        part = lax.psum_scatter(member, "dp", scatter_dimension=1, tiled=True)
        keep = lax.dynamic_index_in_dim(part, half, 0, keepdims=False)
        send = lax.dynamic_index_in_dim(part, 1 - half, 0, keepdims=False)
        found.append(keep + lax.ppermute(send.astype(BF), "pipe", swap).astype(F32))
    small = lax.psum(sums, "dp")
    received = lax.all_to_all(last, "pipe", 0, 0, tiled=False)
    return found + [small + lax.ppermute(small, "pipe", swap), received[:2]]


def shards(
    n_dp,
    tokens, cotangent, captions, projection, biases, combiner, offsets, scaling, centring,
    expansion, lifting, reduction, settling, stretch, translate,
):
    local_rows = tokens.shape[0]
    local_pairs = local_rows // PAIR_ROWS
    pairs = 2 * ((local_pairs + 3) // 4)
    block = 2 * PAIR_ROWS
    micros = pairs // 2
    owned = (projection[0], combiner[0], expansion[0], reduction[0])
    small = (biases, offsets, scaling, centring, lifting, settling, stretch, translate)
    *kept, results, last = layer_passes(micros, block, captions, small, tokens.T, cotangent.T, owned)
    a0, context, a1, hidden, dr2, du, dr1, dqkv, sums = kept
    whole_tiles = HALF % (16 * n_dp) == 0
    collect = weight_gradients if whole_tiles else weight_gradients_by_scatter
    *grads, sums, last = collect(n_dp, a0, dqkv, context, dr1, a1, du, hidden, dr2, sums, last)
    encoded, tokens_grad, g_proj, g_comb, g_exp, g_red, *parts = finish(n_dp, local_rows, sums, results, last, grads)
    return (
        encoded.T, tokens_grad.T, g_proj, parts[0], g_comb, parts[1], parts[2], parts[3],
        g_exp, parts[4], g_red, parts[5], parts[6], parts[7],
    )


def solution(mesh):
    rows = P("dp", "pipe")
    matrix = P("pipe", None, None)
    vector = P("pipe", None)
    matrix_out = P("pipe", "dp", None)
    vector_out = P("pipe", "dp")
    in_specs = (
        rows, rows, P("dp"), matrix, vector, matrix, vector, vector, vector,
        matrix, vector, matrix, vector, vector, vector,
    )
    out_specs = (
        rows, rows, matrix_out, vector_out, matrix_out, vector_out, vector_out, vector_out,
        matrix_out, vector_out, matrix_out, vector_out, vector_out, vector_out,
    )
    return jax.shard_map(
        functools.partial(shards, mesh.shape["dp"]),
        mesh=mesh, in_specs=in_specs, out_specs=out_specs, check_vma=False,
    )
```

```python
import functools

import jax
import jax.numpy as jnp
from jax import lax
from jax.experimental import pallas as pl
from jax.experimental.pallas import tpu as pltpu
from jax.sharding import PartitionSpec as P

D = 768
HEADS = 12
HEAD_DIM = 64
FF = 3072
WORDS = 64
PAIR_ROWS = 104
HALF = D // 2
HIDDEN_HALF = FF // 2
QUARTER = D // 4
PIPE = 4
GROUP_WIDTH = 2 * HEAD_DIM
GROUPS = HEADS // 2
STACKED = 2 * PAIR_ROWS

EPSILON = 1e-05
NEGATIVE = -1e30
SCALE = HEAD_DIM ** (-0.5)

MESH = pl.DeviceIdType.MESH
BF = jnp.bfloat16
F32 = jnp.float32
VMEM_LIMIT = 60 << 20


def dot_nn(left, right):
    return lax.dot_general(left, right, (((1,), (0,)), ((), ())), preferred_element_type=F32)


def dot_nt(left, right):
    return lax.dot_general(left, right, (((1,), (1,)), ((), ())), preferred_element_type=F32)


def dot_tn(left, right):
    return lax.dot_general(left, right, (((0,), (0,)), ((), ())), preferred_element_type=F32)


def place():
    pipe = lax.axis_index("pipe")
    dp = lax.axis_index("dp")
    layer = pipe // 2
    half = pipe % 2
    across_x = pipe + 1 - 2 * half
    across_y = (pipe + 2) % 4
    core = dp % 2
    other_core = dp + 1 - 2 * core
    return pipe, dp, layer, half, across_x, across_y, core, other_core


def greet(devices):
    barrier = pltpu.get_barrier_semaphore()
    for device in devices:
        pl.semaphore_signal(barrier, inc=1, device_id=device, device_id_type=MESH)
    pl.semaphore_wait(barrier, len(devices))


def remote(source, target, send, recv, device):
    return pltpu.make_async_remote_copy(
        src_ref=source,
        dst_ref=target,
        send_sem=send,
        recv_sem=recv,
        device_id=device,
        device_id_type=MESH,
    )


WEIGHT_SHAPES = [(D, 3 * HALF), (HALF, D), (D, HIDDEN_HALF), (HIDDEN_HALF, D)]
CHUNKS = [(0, 0, 96), (0, 96, 96), (1, 0, 96), (2, 0, 96), (2, 96, 96), (3, 0, 96), (3, 96, 96), (3, 192, 96), (3, 288, 48), (3, 336, 48)]
ATTENTION_CHUNKS = 3
FIRST_LANES = 256
DEPTH = 3
LAG = 2
ATTEND_AT = 5
REDUCE_DEPTH = 3
LOW_AT = (4, 10, 14)


def left_lanes():
    return lax.broadcasted_iota(jnp.int32, (PAIR_ROWS, GROUP_WIDTH), 1) < HEAD_DIM


def stacked(values, scale=None):
    if scale is not None:
        values = values * scale
    left = left_lanes()
    return jnp.concatenate([jnp.where(left, values, 0.0), jnp.where(left, 0.0, values)], 0).astype(BF)


def own_lanes(values):
    return jnp.where(left_lanes(), values[:PAIR_ROWS], values[PAIR_ROWS:])


def normalized(residual):
    average = jnp.mean(residual, axis=-1, keepdims=True)
    centred = residual - average
    variance = jnp.mean(centred * centred, axis=-1, keepdims=True)
    inverse = lax.rsqrt(variance + EPSILON)
    return centred * inverse, inverse


def norm_backward(gradient, norm, inverse, gain):
    scaled = gradient * gain
    first = jnp.mean(scaled, axis=-1, keepdims=True)
    second = jnp.mean(scaled * norm, axis=-1, keepdims=True)
    return (scaled - first - norm * second) * inverse


def column_sums(value):
    return jnp.sum(value, axis=0, keepdims=True)


def layer_kernel(
    micros, block, local_pairs,
    captions, tokens_hbm, cotangent_hbm, biases, offsets, scaling, centring, lifting, settling, stretch, translate,
    own_proj, own_comb, own_exp, own_red,
    a0_hbm, context_hbm, a1_hbm, hidden_hbm, dr2_hbm, du_hbm, dr1_hbm, dqkv_hbm, sums_out, results_out, last_out,
    tokens, cotangent, both, own_vectors, joint, mixing, expand, reduce, pieces, unpacked, other_vectors, vectors, results,
    slots, outgoing, qkv_keep, prob_keep, n1_keep, r1_keep, n2_keep, r2_keep, slope_keep,
    a_s, qkv_s, context_s, dqkv_s,
    a0_ring, context_ring, a1_ring, hidden_ring, dr2_ring, du_ring, dr1_ring, dqkv_ring,
    send, recv, x_send, x_recv, z_send, z_recv, near_send, near_recv, far_send, far_recv,
    own_sem, piece_send, piece_recv, vec_sem, result_send, result_recv, result_sem, ring_sem, row_sem,
):
    pipe, dp, layer, half, across_x, across_y, core, other_core = place()
    step = pl.program_id(0)
    pairs = block // PAIR_ROWS
    rows = micros * block
    diagonal = (across_x + 2) % 4
    parity = (dp // 2) % 2
    across_z = dp + 2 - 4 * parity
    mine = 2 * parity + core
    paired = 2 * (1 - parity) + core
    relatives = (across_x, across_y, diagonal)
    owned = [own_proj, own_comb, own_exp, own_red]
    held = [joint, mixing, expand, reduce]
    n = len(CHUNKS)

    def span(chunk, quarter):
        which, start, count = chunk
        return pl.ds(quarter * (WEIGHT_SHAPES[which][0] // 4) + start, count)

    def x_copy(k):
        at = span(CHUNKS[k], mine)
        which = CHUNKS[k][0]
        return remote(owned[which].at[at], held[which].at[half, at], x_send.at[k], x_recv.at[k], (across_x, dp))

    def z_copy(k):
        region = held[CHUNKS[k][0]].at[1 - half, span(CHUNKS[k], mine)]
        return remote(region, region, z_send.at[k], z_recv.at[k], (pipe, across_z))

    def near_copy(k):
        region = held[CHUNKS[k][0]].at[1 - half, span(CHUNKS[k], mine)]
        return remote(region, region, near_send.at[k], near_recv.at[k], (pipe, other_core))

    def far_copy(k):
        region = held[CHUNKS[k][0]].at[1 - half, span(CHUNKS[k], paired)]
        return remote(region, region, far_send.at[k], far_recv.at[k], (pipe, other_core))

    own_copies = [pltpu.make_async_copy(owned[i], held[i].at[half], own_sem.at[i]) for i in range(4)]
    own_piece = pltpu.make_async_copy(both.at[layer, half], pieces.at[pipe], own_sem.at[4])
    lanes_held = both.shape[3]
    lanes_of = (pl.ds(0, FIRST_LANES), pl.ds(FIRST_LANES, lanes_held - FIRST_LANES))
    vec_copy = remote(own_vectors, other_vectors, vec_sem.at[0], vec_sem.at[1], (across_x, dp))
    piece_copies = [
        [
            remote(
                both.at[target // 2, target % 2, :, lanes], pieces.at[pipe, :, lanes],
                piece_send.at[part, j], piece_recv.at[part, j], (target, dp),
            )
            for j, target in enumerate(relatives)
        ]
        for part, lanes in enumerate(lanes_of)
    ]

    def send_pieces(to_layer, part):
        for j, target in enumerate(relatives):
            @pl.when(target // 2 == to_layer)
            def _():
                piece_copies[part][j].start()

    def hand_on(k):
        z_copy(k).wait_recv()
        far_copy(k).start()

    def arrived(first, last):
        for k in range(first, last):
            near_copy(k).wait_recv()
            far_copy(k).wait_recv()

    def gather_most():
        for k in range(n):
            x_copy(k).wait_recv()
            z_copy(k).start()
            near_copy(k).start()
            if k + DEPTH < n:
                x_copy(k).wait_send()
                x_copy(k + DEPTH).start()
            if k + DEPTH == n - 1:
                send_pieces(0, 1)
                send_pieces(1, 0)
                send_pieces(1, 1)
            if k >= LAG:
                hand_on(k - LAG)
            if k == ATTEND_AT:
                arrived(0, ATTENTION_CHUNKS)
                own_copies[0].wait()
                own_copies[1].wait()

                @pl.when(layer == 0)
                def _():
                    attend(0, *[ring.at[0] for ring, _ in rings[:3]])

    def gather_rest():
        for k in range(n - LAG, n):
            hand_on(k)
        arrived(ATTENTION_CHUNKS, n)
        own_copies[2].wait()
        own_copies[3].wait()

    def y_copy(index):
        return remote(outgoing.at[index], slots.at[index], send.at[index], recv.at[index], (across_y, dp))

    def rows_of(index):
        return pl.ds(pl.multiple_of(index * block, 16), block)

    def result_copies(index):
        return [
            remote(
                results.at[target, rows_of(index)], results_out.at[pipe, rows_of(index)],
                result_send.at[j, index], result_recv.at[j, index], (target, dp),
            )
            for j, target in enumerate(relatives)
        ]

    def own_result(index):
        return pltpu.make_async_copy(
            results.at[pipe, rows_of(index)], results_out.at[pipe, rows_of(index)], result_sem.at[index]
        )

    def share_result(index, value):
        for i in range(PIPE):
            results[i, rows_of(index), :] = value[:, i * QUARTER : (i + 1) * QUARTER]
        for copy in result_copies(index):
            copy.start()
        own_result(index).start()

    def wait_results(index):
        final = index == micros - 1
        for j, copy in enumerate(result_copies(index)):
            if not final:
                copy.wait()
                continue

            @pl.when(layer == 1)
            def _():
                copy.wait_send()

            @pl.when(relatives[j] // 2 == 1)
            def _():
                copy.wait_recv()

        @pl.when((layer == 1) | (not final))
        def _():
            own_result(index).wait()

    rings = [
        (a0_ring, a0_hbm), (context_ring, context_hbm), (a1_ring, a1_hbm), (hidden_ring, hidden_hbm),
        (dr2_ring, dr2_hbm), (du_ring, du_hbm), (dr1_ring, dr1_hbm), (dqkv_ring, dqkv_hbm),
    ]

    def ring_copy(which, index):
        ring, target = rings[which]
        return pltpu.make_async_copy(ring.at[index % 2], target.at[rows_of(index)], ring_sem.at[which, index])

    def ring_slots(first, last, index):
        @pl.when(index >= 2)
        def _():
            for which in range(first, last):
                ring_copy(which, index - 2).wait()

        return [rings[which][0].at[index % 2] for which in range(first, last)]

    def ring_start(first, last, index):
        for which in range(first, last):
            ring_copy(which, index).start()

    def unpack_pieces(part):
        for copy in piece_copies[part]:
            copy.wait_recv()
        at = lanes_of[part]
        value = pieces[:, :, at.start : at.start + at.size].reshape(D, at.size)
        unpacked[at.start : at.start + at.size, :] = value.astype(F32).T.astype(BF)

    def attend(micro, a0_out, context_out, a1_out):
        for part in range(2):
            @pl.when((layer == 0) & (micro == part))
            def _():
                unpack_pieces(part)

        @pl.when(layer == 0)
        def _():
            a_s[...] = unpacked[rows_of(micro), :]

        @pl.when(layer == 1)
        def _():
            y_copy(micro).wait_recv()
            a_s[...] = slots[micro]

        inputs = a_s[...]
        a0_out[...] = inputs
        for which in range(2):
            value = dot_nn(inputs, joint[which]) + vectors[0:1, which * 3 * HALF : (which + 1) * 3 * HALF]
            for part in range(3):
                cols = slice(part * D + which * HALF, part * D + (which + 1) * HALF)
                found = value[:, part * HALF : (part + 1) * HALF]
                qkv_s[:, cols] = found
                qkv_keep[micro, :, cols] = found.astype(BF)
        over = [(pair, group) for pair in range(pairs) for group in range(GROUPS)]
        spans = [
            (
                slice(pair * PAIR_ROWS, (pair + 1) * PAIR_ROWS),
                [slice(part * D + group * GROUP_WIDTH, part * D + (group + 1) * GROUP_WIDTH) for part in range(3)],
            )
            for pair, group in over
        ]
        key = lax.broadcasted_iota(jnp.int32, (PAIR_ROWS, PAIR_ROWS), 0)
        masks = []
        for pair in range(pairs):
            length = captions[jnp.minimum((half * micros + micro) * pairs + pair, local_pairs - 1)]
            masks.append(jnp.where((key >= WORDS) | (key < length), 0.0, NEGATIVE))
        scores = [
            dot_nt(stacked(qkv_s[at, lanes[1]], SCALE), qkv_s[at, lanes[0]].astype(BF)) for at, lanes in spans
        ]
        values = [stacked(qkv_s[at, lanes[2]]) for at, lanes in spans]
        probs = []
        for k, (pair, group) in enumerate(over):
            found = []
            for i in range(2):
                score = scores[k][i * PAIR_ROWS : (i + 1) * PAIR_ROWS] + masks[pair]
                exponent = jnp.exp(score - jnp.max(score, axis=0, keepdims=True))
                found.append(exponent * (1.0 / jnp.sum(exponent, axis=0, keepdims=True)))
            probs.append(jnp.concatenate(found, 0).astype(BF))
        contexts = [dot_tn(probs[k], values[k]) for k in range(len(over))]
        for k, (at, lanes) in enumerate(spans):
            prob_keep[micro, k] = probs[k]
            context_s[at, lanes[0]] = contexts[k]
        context = context_s[...].astype(BF)
        context_out[...] = context
        residual = inputs.astype(F32) + dot_nn(context, mixing[...].reshape(D, D)) + vectors[1:2, :D]
        norm, inverse = normalized(residual)
        n1_keep[micro] = norm.astype(BF)
        r1_keep[micro] = inverse
        attended = (norm * vectors[2:3, :D] + vectors[3:4, :D]).astype(BF)
        a1_out[...] = attended

    @pl.when(step == 0)
    def _():
        row_copies = [
            pltpu.make_async_copy(tokens_hbm, tokens, row_sem.at[0]),
            pltpu.make_async_copy(cotangent_hbm, cotangent, row_sem.at[1]),
        ]
        for copy in row_copies:
            copy.start()
        greet([(across_x, dp), (across_y, dp), (diagonal, dp), (pipe, across_z), (pipe, other_core)])
        own_vectors[0:1, :] = biases[...].astype(F32)
        for i, (first, second) in enumerate(((offsets, scaling), (centring, settling), (stretch, translate)), 1):
            own_vectors[i : i + 1, :HALF] = first[...].astype(F32)
            own_vectors[i : i + 1, HALF:] = second[...].astype(F32)
        own_vectors[4:5, :] = lifting[:, :D].astype(F32)
        own_vectors[5:6, :] = lifting[:, D:].astype(F32)
        own_vectors[6:8, :] = jnp.zeros((2, D), F32)
        vec_copy.start()
        for t, source in enumerate((tokens, cotangent)):
            row_copies[t].wait()
            whole = source[...].astype(F32)
            for h in range(2):
                value = whole[:, h * rows : (h + 1) * rows]
                spare = jnp.zeros((QUARTER, lanes_held - value.shape[1]), F32)
                both[t, h] = jnp.concatenate([value, spare], 1).astype(BF)
            if t == 0:
                send_pieces(0, 0)
                for k in range(DEPTH):
                    x_copy(k).start()
        for copy in own_copies:
            copy.start()
        own_piece.start()
        sums_out[...] = jnp.zeros_like(sums_out)
        vec_copy.wait_recv()
        for which in range(2):
            value = jnp.where(half == which, own_vectors[...], other_vectors[...])
            vectors[0:1, which * 3 * HALF : which * 3 * HALF + HALF] = value[0:1, :HALF]
            vectors[0:1, which * 3 * HALF + HALF : which * 3 * HALF + D] = jnp.zeros((1, HALF), F32)
            vectors[0:1, which * 3 * HALF + D : (which + 1) * 3 * HALF] = value[0:1, HALF:D]
            for row, pair in enumerate(((1, 2), (3, 5), (6, 7)), 1):
                for k, i in enumerate(pair):
                    vectors[i : i + 1, which * HALF : (which + 1) * HALF] = value[row : row + 1, k * HALF : (k + 1) * HALF]
            for k in range(2):
                first = which * HIDDEN_HALF + k * D
                vectors[4:5, first : first + D] = value[4 + k : 5 + k, :]
        own_piece.wait()
        gather_most()

        @pl.when(layer == 1)
        def _():
            gather_rest()

    @pl.when(((layer == 0) & (step < micros)) | ((layer == 1) & (step % 2 == 0)))
    def _():
        micro = (1 - layer) * step + layer * (step // 2)
        a0_out, context_out, a1_out, hidden_out = ring_slots(0, 4, micro)

        @pl.when((layer == 1) | (step > 0))
        def _():
            attend(micro, a0_out, context_out, a1_out)

        @pl.when((micro == 0) & (layer == 0))
        def _():
            gather_rest()

        attended = a1_out[...]
        residual = attended.astype(F32) + vectors[5:6, :D]
        for which in range(2):
            cols = slice(which * HIDDEN_HALF, (which + 1) * HIDDEN_HALF)
            raised = dot_nn(attended, expand[which]) + vectors[4:5, cols]
            below = 0.5 * (1.0 + lax.erf(raised * (0.5**0.5)))
            hidden = (raised * below).astype(BF)
            hidden_out[:, cols] = hidden
            density = jnp.exp(raised * raised * (-0.5)) * 0.3989422804014327
            slope_keep[micro, :, cols] = (below + raised * density).astype(BF)
            residual = residual + dot_nn(hidden, reduce[which])
        norm, inverse = normalized(residual)
        n2_keep[micro] = norm.astype(BF)
        r2_keep[micro] = inverse
        result = (norm * vectors[6:7, :D] + vectors[7:8, :D]).astype(BF)

        @pl.when(layer == 0)
        def _():
            outgoing[micro] = result
            y_copy(micro).start()

        @pl.when(layer == 1)
        def _():
            share_result(micro, result)

        ring_start(0, 4, micro)

    def add_sum(row, value):
        width = value.shape[1]
        sums_out[row : row + 1, :width] += column_sums(value)

    @pl.when(((layer == 0) & (step >= micros)) | ((layer == 1) & (step % 2 == 1)))
    def _():
        micro = (1 - layer) * (step - micros) + layer * (step // 2)
        dr2_out, du_out, dr1_out, dqkv_out = ring_slots(4, 8, micro)

        @pl.when((layer == 1) & (micro == 0))
        def _():
            unpack_pieces(0)
            unpack_pieces(1)

        @pl.when(layer == 1)
        def _():
            a_s[...] = unpacked[rows_of(micro), :]

        @pl.when(layer == 0)
        def _():
            y_copy(micro).wait_recv()
            a_s[...] = slots[micro]

        gradient = a_s[...].astype(F32)
        norm = n2_keep[micro].astype(F32)
        add_sum(6, gradient * norm)
        add_sum(7, gradient)
        grad_residual = norm_backward(gradient, norm, r2_keep[micro], vectors[6:7, :D])
        add_sum(5, grad_residual)
        branch = grad_residual.astype(BF)
        dr2_out[...] = branch
        total = grad_residual
        for which in range(2):
            cols = slice(which * HIDDEN_HALF, (which + 1) * HIDDEN_HALF)
            raised = dot_nt(branch, reduce[which]) * slope_keep[micro, :, cols].astype(F32)
            sums_out[4:5, cols] += column_sums(raised)
            raised = raised.astype(BF)
            du_out[:, cols] = raised
            total = total + dot_nt(raised, expand[which])

        gradient = total.astype(BF).astype(F32)
        norm = n1_keep[micro].astype(F32)
        add_sum(2, gradient * norm)
        add_sum(3, gradient)
        grad_residual = norm_backward(gradient, norm, r1_keep[micro], vectors[2:3, :D])
        add_sum(1, grad_residual)
        branch = grad_residual.astype(BF)
        dr1_out[...] = branch
        context_s[...] = dot_nt(branch, mixing[...].reshape(D, D))
        qkv_s[...] = qkv_keep[micro].astype(F32)
        spans = [
            (
                slice(pair * PAIR_ROWS, (pair + 1) * PAIR_ROWS),
                [slice(part * D + group * GROUP_WIDTH, part * D + (group + 1) * GROUP_WIDTH) for part in range(3)],
            )
            for pair in range(pairs)
            for group in range(GROUPS)
        ]
        over = range(len(spans))
        queries = [qkv_s[at, lanes[0]].astype(BF) for at, lanes in spans]
        keys = [stacked(qkv_s[at, lanes[1]], SCALE) for at, lanes in spans]
        values = [stacked(qkv_s[at, lanes[2]]) for at, lanes in spans]
        grads = [context_s[at, lanes[0]].astype(BF) for at, lanes in spans]
        rounded = [prob_keep[micro, g] for g in over]
        grad_probs = [dot_nt(values[g], grads[g]) for g in over]
        grad_values = [dot_nn(rounded[g], grads[g]) for g in over]
        grad_scores = []
        for g in over:
            probs = rounded[g].astype(F32)
            weighted = probs * grad_probs[g]
            found = []
            for i in range(2):
                at = slice(i * PAIR_ROWS, (i + 1) * PAIR_ROWS)
                found.append(weighted[at] - probs[at] * column_sums(weighted[at]))
            grad_scores.append(jnp.concatenate(found, 0).astype(BF))
        grad_keys = [dot_nn(grad_scores[g], queries[g]) for g in over]
        grad_queries = [dot_tn(grad_scores[g], keys[g]) for g in over]
        for g, (at, lanes) in enumerate(spans):
            dqkv_s[at, lanes[0]] = grad_queries[g]
            dqkv_s[at, lanes[1]] = own_lanes(grad_keys[g]) * SCALE
            dqkv_s[at, lanes[2]] = own_lanes(grad_values[g])
        total = grad_residual
        for which in range(2):
            value = jnp.concatenate(
                [dqkv_s[:, part * D + which * HALF : part * D + (which + 1) * HALF] for part in range(3)], 1
            ).astype(BF)
            cols = slice(which * 3 * HALF, (which + 1) * 3 * HALF)
            dqkv_out[:, cols] = value
            sums_out[0:1, cols] += column_sums(value.astype(F32))
            total = total + dot_nt(value, joint[which])
        result = total.astype(BF)

        @pl.when(layer == 1)
        def _():
            outgoing[micro] = result
            y_copy(micro).start()

        ring_start(4, 8, micro)

        @pl.when((layer == 0) & (micro < micros - 1))
        def _():
            share_result(micro, result)

        @pl.when((layer == 0) & (micro == micros - 1))
        def _():
            for i in range(PIPE):
                last_out[i] = result[:, i * QUARTER : (i + 1) * QUARTER]

    @pl.when(step == 2 * micros - 1)
    def _():
        for index in range(micros):
            y_copy(index).wait_send()
            wait_results(index)
        for index in range(max(micros - 2, 0), micros):
            for which in range(8):
                ring_copy(which, index).wait()
        for k in range(n):
            if k + DEPTH >= n:
                x_copy(k).wait_send()
            z_copy(k).wait_send()
            near_copy(k).wait_send()
            far_copy(k).wait_send()
        for copy in piece_copies[0] + piece_copies[1] + [vec_copy]:
            copy.wait_send()


def layer_passes(micros, block, captions, small, tokens, cotangent, owned):
    rows = micros * block
    n = len(CHUNKS)
    lanes_held = (rows + 127) // 128 * 128
    vmem = pl.BlockSpec(memory_space=pltpu.VMEM)
    hbm = pl.BlockSpec(memory_space=pl.ANY)

    forward_widths = [D, D, D, FF]
    backward_widths = [D, FF, D, 3 * D]
    pairs = block // PAIR_ROWS
    return pl.pallas_call(
        functools.partial(layer_kernel, micros, block, captions.shape[0]),
        grid=(2 * micros,),
        out_shape=[jax.ShapeDtypeStruct((rows, w), BF) for w in forward_widths + backward_widths]
        + [
            jax.ShapeDtypeStruct((8, FF), F32),
            jax.ShapeDtypeStruct((PIPE, rows, QUARTER), BF),
            jax.ShapeDtypeStruct((PIPE, block, QUARTER), BF),
        ],
        in_specs=[pl.BlockSpec(memory_space=pltpu.SMEM)] + [hbm] * 2 + [vmem] * 8 + [hbm] * 4,
        out_specs=[hbm] * 8 + [vmem, hbm, vmem],
        scratch_shapes=[
            pltpu.VMEM(tokens.shape, BF),
            pltpu.VMEM(cotangent.shape, BF),
            pltpu.VMEM((2, 2, QUARTER, lanes_held), BF),
            pltpu.VMEM((8, D), F32),
        ]
        + [pltpu.VMEM((2,) + shape, BF) for shape in WEIGHT_SHAPES]
        + [
            pltpu.VMEM((PIPE, QUARTER, lanes_held), BF),
            pltpu.VMEM((lanes_held, D), BF),
            pltpu.VMEM((8, D), F32),
            pltpu.VMEM((8, FF), F32),
            pltpu.VMEM((PIPE, rows, QUARTER), BF),
            pltpu.VMEM((micros, block, D), BF),
            pltpu.VMEM((micros, block, D), BF),
            pltpu.VMEM((micros, block, 3 * D), BF),
            pltpu.VMEM((micros, pairs * GROUPS, STACKED, PAIR_ROWS), BF),
            pltpu.VMEM((micros, block, D), BF),
            pltpu.VMEM((micros, block, 1), F32),
            pltpu.VMEM((micros, block, D), BF),
            pltpu.VMEM((micros, block, 1), F32),
            pltpu.VMEM((micros, block, FF), BF),
            pltpu.VMEM((block, D), BF),
            pltpu.VMEM((block, 3 * D), F32),
            pltpu.VMEM((block, D), F32),
            pltpu.VMEM((block, 3 * D), F32),
        ]
        + [pltpu.VMEM((2, block, w), BF) for w in forward_widths + backward_widths]
        + [pltpu.SemaphoreType.DMA((micros,))] * 2
        + [pltpu.SemaphoreType.DMA((n,))] * 8
        + [
            pltpu.SemaphoreType.DMA((5,)),
            pltpu.SemaphoreType.DMA((2, 3)),
            pltpu.SemaphoreType.DMA((2, 3)),
            pltpu.SemaphoreType.DMA((2,)),
            pltpu.SemaphoreType.DMA((3, micros)),
            pltpu.SemaphoreType.DMA((3, micros)),
            pltpu.SemaphoreType.DMA((micros,)),
            pltpu.SemaphoreType.DMA((8, micros)),
            pltpu.SemaphoreType.DMA((2,)),
        ],
        compiler_params=pltpu.CompilerParams(collective_id=1, has_side_effects=True, vmem_limit_bytes=VMEM_LIMIT),
        name="layer_passes",
    )(captions, tokens, cotangent, *small, *owned)


TILE = 384


def weights_kernel(
    n_dp,
    a0_in, dqkv_in, context_in, dr1_in, a1_in, du_in, hidden_in, dr2_in, sums, last,
    g_proj_hbm, g_comb_hbm, g_exp_hbm, g_red_hbm, sums_out, last_out,
    g_proj, g_comb, g_exp, g_red,
    b_proj, b_comb, b_exp, b_red,
    c_proj, c_comb, c_exp, c_red,
    x_proj, x_comb, x_exp, x_red,
    p_proj, p_comb, p_exp, p_red,
    z_proj, z_comb, z_exp, z_red,
    sums_core, sums_x, sums_z, sums_a, sums_b, sums_c,
    low_from_pair, low_from_far, low_from_x, low_own,
    a0, dqkv, context, dr1, a1, du, hidden, dr2,
    core_send, core_recv, x_send, x_recv, z_send, z_recv,
    small_send, small_recv, load_sem, hidden_sem, last_send, last_recv, low_send, low_recv, out_sem,
):
    pipe, dp, layer, half, across_x, across_y, core, other_core = place()
    n_z = n_dp // 2
    z = dp // 2
    near_z = z + 1 - 2 * (z % 2)
    steps = n_z // 2
    z_order = [(near_z + 2 * (step + 1)) % n_z for step in range(steps - 1)] + [near_z]
    z_order += [(z + 2 * (step + 1)) % n_z for step in range(steps - 1)] + [z]
    same_parity = z_order[steps:-1]
    def hidden_load(which, i):
        h = 1 - half if which == 0 else half
        width = 2 * b_red.shape[3]
        lanes = pl.ds(pl.multiple_of(h * HIDDEN_HALF + z_order[i] * width, 128), width)
        return pltpu.make_async_copy(hidden_in.at[:, lanes], hidden.at[:, lanes], hidden_sem.at[which, i])

    loads = [
        pltpu.make_async_copy(source, target, load_sem.at[i])
        for i, (source, target) in enumerate((
            (dr2_in, dr2), (a1_in, a1), (du_in, du), (a0_in, a0), (dqkv_in, dqkv), (context_in, context), (dr1_in, dr1),
        ))
    ]
    loads[0].start()
    for which in range(2):
        for i in range(n_z):
            hidden_load(which, i).start()
    for copy in loads[1:]:
        copy.start()
    relatives = (across_x, across_y, (across_x + 2) % 4)
    greet(
        [(target, dp) for target in relatives] + [(pipe, other_core)]
        + [(pipe, 2 * other + core) for other in [near_z] + same_parity]
    )

    last_copies = [
        remote(last.at[target], last_out.at[half], last_send.at[j], last_recv.at[j], (target, dp))
        for j, target in enumerate(relatives)
    ]
    last_own = pltpu.make_async_copy(last.at[pipe], last_out.at[half], load_sem.at[7])

    @pl.when(layer == 0)
    def _():
        for copy in last_copies:
            copy.start()
        last_own.start()

    mine = [b_red, b_exp, b_proj, b_comb]
    from_core = [c_red, c_exp, c_proj, c_comb]
    from_x = [x_red, x_exp, x_proj, x_comb]
    from_pair = [p_red, p_exp, p_proj, p_comb]
    from_far = [z_red, z_exp, z_proj, z_comb]
    outs = [g_red, g_exp, g_proj, g_comb]
    out_copies = [
        pltpu.make_async_copy(source, target, out_sem.at[a])
        for a, (source, target) in enumerate(zip(outs, (g_red_hbm, g_exp_hbm, g_proj_hbm, g_comb_hbm)))
    ]

    def spread(target, tile, cast=BF):
        r = target.shape[-2]
        for k in range(tile.shape[0] // (2 * r)):
            for c in range(2):
                yield c, k, tile[(2 * k + c) * r : (2 * k + c + 1) * r].astype(cast)

    def fill_red(h, at):
        width = 2 * b_red.shape[3]
        lanes = pl.ds(pl.multiple_of(h * HIDDEN_HALF + at * width, 128), width)
        for c, k, rows in spread(b_red, dot_tn(hidden[:, lanes], dr2[...])):
            b_red[c, h, at] = rows

    def fill_exp(step, carry):
        i, h = step // 2, step % 2
        tile = dot_tn(
            a1[:, pl.ds(pl.multiple_of(i * TILE, 128), TILE)],
            du[:, pl.ds(pl.multiple_of(h * HIDDEN_HALF, 128), HIDDEN_HALF)],
        )
        for c, k, rows in spread(b_exp, tile):
            b_exp[c, h, i * (TILE // (2 * b_exp.shape[3])) + k] = rows
        return carry

    def fill_proj(h, carry):
        tile = dot_tn(a0[...], dqkv[:, pl.ds(pl.multiple_of(h * 3 * HALF, 128), 3 * HALF)])
        for c, k, rows in spread(b_proj, tile):
            b_proj[c, h, k] = rows
        return carry

    def fill_comb():
        tile = dot_tn(context[...], dr1[...])
        for h in range(2):
            for c, k, rows in spread(b_comb, tile[h * HALF : (h + 1) * HALF]):
                b_comb[c, h, k] = rows

    low = b_red.shape[3] // 48 * 16
    low_rows = pl.ds(0, low)
    rows_of = [pl.ds(low, b_red.shape[3] - low)] + [pl.ds(0, b.shape[3]) for b in mine[1:]]

    def half_of(which):
        return 1 - half if which == 0 else half

    def core_copy(a, which, i):
        h, at = half_of(which), z_order[i]
        return remote(
            mine[a].at[1 - core, h, at, rows_of[a]], from_core[a].at[h, at, rows_of[a]],
            core_send.at[a, which, i], core_recv.at[a, which, i], (pipe, other_core),
        )

    def send_core(a, which):
        for i in range(n_z):
            core_copy(a, which, i).start()

    def x_copy(k):
        a, i = chunks[k]
        at = z_order[i]
        return remote(
            mine[a].at[core, 1 - half, at, rows_of[a]], from_x[a].at[at, rows_of[a]],
            x_send.at[a, i], x_recv.at[a, i], (across_x, dp),
        )

    def pair_copy(a, i):
        return remote(
            mine[a].at[core, half, z_order[i], rows_of[a]], from_pair[a].at[i, rows_of[a]],
            z_send.at[a, i], z_recv.at[a, i], (pipe, 2 * near_z + core),
        )

    def far_copy(a, i):
        other = same_parity[i]
        return remote(
            mine[a].at[core, half, other, rows_of[a]], from_far[a].at[i, rows_of[a]],
            z_send.at[a, steps + i], z_recv.at[a, steps + i], (pipe, 2 * other + core),
        )

    chunks = [(a, i) for a in range(4) for i in range(n_z)]

    def start_x(k):
        if k >= len(chunks):
            return
        a, i = chunks[k]
        at, rows = z_order[i], rows_of[a]
        core_copy(a, 0, i).wait_recv()
        total = mine[a][core, 1 - half, at, rows, :].astype(F32) + from_core[a][1 - half, at, rows, :].astype(F32)
        mine[a][core, 1 - half, at, rows, :] = total.astype(BF)
        x_copy(k).start()

    def after_x(k):
        a, i = chunks[k]
        at, rows = z_order[i], rows_of[a]
        x_copy(k).wait()
        start_x(k + REDUCE_DEPTH)
        core_copy(a, 1, i).wait_recv()
        total = mine[a][core, half, at, rows, :].astype(F32) + from_core[a][half, at, rows, :].astype(F32)
        total = total + from_x[a][at, rows, :].astype(F32)
        if i < steps:
            mine[a][core, half, at, rows, :] = total.astype(BF)
            pair_copy(a, i).start()
            return
        pair_copy(a, i - steps).wait_recv()
        total = total + from_pair[a][i - steps, rows, :].astype(F32)
        if i < n_z - 1:
            mine[a][core, half, at, rows, :] = total.astype(BF)
            far_copy(a, i - steps).start()
        else:
            outs[a][rows, :] = total

    def after_z(a):
        rows = rows_of[a]
        total = outs[a][rows, :]
        for i in range(steps - 1):
            far_copy(a, i).wait()
            total = total + from_far[a][i, rows, :].astype(F32)
        outs[a][rows, :] = total
        for i in range(steps):
            pair_copy(a, i).wait_send()

    def low_core(which, i):
        h, at = half_of(which), z_order[i]
        return remote(
            b_red.at[1 - core, h, at, low_rows], c_red.at[h, at, low_rows],
            low_send.at[which, i], low_recv.at[which, i], (pipe, other_core),
        )

    def low_pair(which, i):
        return remote(
            b_red.at[core, half_of(which), z_order[i], low_rows], low_from_pair.at[which, i],
            low_send.at[2 + which, i], low_recv.at[2 + which, i], (pipe, 2 * near_z + core),
        )

    def low_far(which, i):
        other = same_parity[i]
        return remote(
            b_red.at[core, half_of(which), other, low_rows], low_from_far.at[which, i],
            low_send.at[2 + which, steps + i], low_recv.at[2 + which, steps + i], (pipe, 2 * other + core),
        )

    low_x = remote(
        b_red.at[core, 1 - half, z, low_rows], low_from_x,
        low_send.at[2, n_z - 1], low_recv.at[2, n_z - 1], (across_x, dp),
    )

    def low_sum(which, i):
        h, at = half_of(which), z_order[i]
        low_core(which, i).wait_recv()
        return b_red[core, h, at, low_rows, :].astype(F32) + c_red[h, at, low_rows, :].astype(F32)

    def low_to_pair():
        for which in range(2):
            for i in range(steps):
                b_red[core, half_of(which), z_order[i], low_rows, :] = low_sum(which, i).astype(BF)
                low_pair(which, i).start()

    def low_to_far():
        for which in range(2):
            for i in range(steps, n_z):
                total = low_sum(which, i)
                low_pair(which, i - steps).wait_recv()
                total = total + low_from_pair[which, i - steps].astype(F32)
                if i < n_z - 1:
                    b_red[core, half_of(which), z_order[i], low_rows, :] = total.astype(BF)
                    low_far(which, i - steps).start()
                else:
                    low_own[which] = total

    def low_to_x():
        for which in range(2):
            total = low_own[which]
            for i in range(steps - 1):
                low_far(which, i).wait_recv()
                total = total + low_from_far[which, i].astype(F32)
            if which == 0:
                b_red[core, 1 - half, z, low_rows, :] = total.astype(BF)
                low_x.start()
            else:
                g_red[low_rows, :] = total

    def low_done():
        low_x.wait()
        g_red[low_rows, :] = g_red[low_rows, :] + low_from_x[...].astype(F32)
        for which in range(2):
            for i in range(n_z):
                low_core(which, i).wait_send()
            for i in range(steps):
                low_pair(which, i).wait_send()
            for i in range(steps - 1):
                low_far(which, i).wait_send()

    sums_copy_core = remote(sums, sums_core, small_send.at[0], small_recv.at[0], (pipe, other_core))
    sums_copy_x = remote(sums_a, sums_x, small_send.at[1], small_recv.at[1], (across_x, dp))
    sums_copy_pair = remote(
        sums_b, sums_z.at[steps - 1], small_send.at[2], small_recv.at[2], (pipe, 2 * near_z + core)
    )
    sums_copies_far = [
        remote(sums_c, sums_z.at[i], small_send.at[3 + i], small_recv.at[3 + i], (pipe, 2 * other + core))
        for i, other in enumerate(same_parity)
    ]

    sums_copy_core.start()
    loads[0].wait()
    for i in range(n_z):
        hidden_load(0, i).wait()
        fill_red(1 - half, z_order[i])
        core_copy(0, 0, i).start()
        low_core(0, i).start()
        if 1 <= i <= REDUCE_DEPTH:
            start_x(i - 1)
    for i in range(n_z):
        hidden_load(1, i).wait()
        fill_red(half, z_order[i])
        low_core(1, i).start()
        core_copy(0, 1, i).start()
    low_to_pair()
    loads[1].wait()
    loads[2].wait()
    lax.fori_loop(0, 2 * D // TILE, fill_exp, 0)
    send_core(1, 0)
    send_core(1, 1)
    sums_copy_core.wait()
    sums_a[...] = sums[...] + sums_core[...]
    sums_copy_x.start()
    after_x(0)
    after_x(1)
    loads[3].wait()
    loads[4].wait()
    lax.fori_loop(0, 2, fill_proj, 0)
    send_core(2, 0)
    send_core(2, 1)
    after_x(2)
    loads[5].wait()
    loads[6].wait()
    fill_comb()
    send_core(3, 0)
    send_core(3, 1)
    sums_copy_x.wait()
    sums_b[...] = sums_a[...] + sums_x[...]
    sums_copy_pair.start()
    for k in range(3, len(chunks)):
        after_x(k)
        if k == LOW_AT[0]:
            low_to_far()
        if k == LOW_AT[1]:
            low_to_x()
        if k == LOW_AT[2]:
            low_done()
            out_copies[0].start()
        if k == n_z:
            sums_copy_pair.wait()
            sums_c[...] = sums_b[...] + sums_z[steps - 1]
            for copy in sums_copies_far:
                copy.start()
        if k % n_z == n_z - 2 and k >= n_z:
            after_z(k // n_z - 1)
            if k // n_z > 1:
                out_copies[k // n_z - 1].start()
    after_z(3)
    out_copies[3].start()
    for a in range(4):
        for which in range(2):
            for i in range(n_z):
                core_copy(a, which, i).wait_send()
    total = sums_c[...]
    for i in range(steps - 1):
        sums_copies_far[i].wait()
        total = total + sums_z[i]
    sums_out[...] = total
    for copy in out_copies:
        copy.wait()

    @pl.when(layer == 0)
    def _():
        for copy in last_copies:
            copy.wait_send()
        last_own.wait()

    for j, source in enumerate(relatives):
        @pl.when(source // 2 == 0)
        def _():
            last_copies[j].wait_recv()


def weight_gradients(n_dp, a0, dqkv, context, dr1, a1, du, hidden, dr2, sums, last):
    vmem = pl.BlockSpec(memory_space=pltpu.VMEM)
    hbm = pl.BlockSpec(memory_space=pl.ANY)
    n_z = n_dp // 2
    low = HIDDEN_HALF // n_dp // 48 * 16
    shapes = [(D // n_dp, 3 * HALF), (HALF // n_dp, D), (D // n_dp, HIDDEN_HALF), (HIDDEN_HALF // n_dp, D)]
    return pl.pallas_call(
        functools.partial(weights_kernel, n_dp),
        out_shape=[jax.ShapeDtypeStruct(s, F32) for s in shapes]
        + [jax.ShapeDtypeStruct(sums.shape, F32), jax.ShapeDtypeStruct((2,) + last.shape[1:], BF)],
        in_specs=[hbm] * 8 + [vmem, hbm],
        out_specs=[hbm] * 4 + [vmem, hbm],
        scratch_shapes=[pltpu.VMEM(s, F32) for s in shapes]
        + [pltpu.VMEM((2, 2, n_z) + s, BF) for s in shapes]
        + [pltpu.VMEM((2, n_z) + s, BF) for s in shapes]
        + [pltpu.VMEM((n_z,) + s, BF) for s in shapes]
        + [pltpu.VMEM((n_z // 2,) + s, BF) for s in shapes]
        + [pltpu.VMEM((max(n_z // 2 - 1, 1),) + s, BF) for s in shapes]
        + [
            pltpu.VMEM(sums.shape, F32),
            pltpu.VMEM(sums.shape, F32),
            pltpu.VMEM((n_z // 2,) + sums.shape, F32),
            pltpu.VMEM(sums.shape, F32),
            pltpu.VMEM(sums.shape, F32),
            pltpu.VMEM(sums.shape, F32),
            pltpu.VMEM((2, n_z // 2, low, D), BF),
            pltpu.VMEM((2, max(n_z // 2 - 1, 1), low, D), BF),
            pltpu.VMEM((low, D), BF),
            pltpu.VMEM((2, low, D), F32),
        ]
        + [pltpu.VMEM(v.shape, BF) for v in (a0, dqkv, context, dr1, a1, du, hidden, dr2)]
        + [
            pltpu.SemaphoreType.DMA((4, 2, n_z)),
            pltpu.SemaphoreType.DMA((4, 2, n_z)),
            pltpu.SemaphoreType.DMA((4, n_z)),
            pltpu.SemaphoreType.DMA((4, n_z)),
            pltpu.SemaphoreType.DMA((4, n_z - 1)),
            pltpu.SemaphoreType.DMA((4, n_z - 1)),
            pltpu.SemaphoreType.DMA((n_z + 1,)),
            pltpu.SemaphoreType.DMA((n_z + 1,)),
            pltpu.SemaphoreType.DMA((8,)),
            pltpu.SemaphoreType.DMA((2, n_z)),
            pltpu.SemaphoreType.DMA((3,)),
            pltpu.SemaphoreType.DMA((3,)),
            pltpu.SemaphoreType.DMA((4, n_z)),
            pltpu.SemaphoreType.DMA((4, n_z)),
            pltpu.SemaphoreType.DMA((4,)),
        ],
        compiler_params=pltpu.CompilerParams(collective_id=3, has_side_effects=True, vmem_limit_bytes=VMEM_LIMIT),
        name="weight_gradients",
    )(a0, dqkv, context, dr1, a1, du, hidden, dr2, sums, last)


def finish_kernel(n_dp, small, results_hbm, last_hbm, *refs):
    pipe, dp, layer, half, across_x, across_y, core, other_core = place()
    sources, encoded_hbm, tokens_hbm, outs, parts = refs[:4], refs[4], refs[5], refs[6:10], refs[10:18]
    results, last, encoded, tokens_grad = refs[18:22]
    held, in_sem, out_sem = refs[22:26], refs[26], refs[27]
    loads = [
        pltpu.make_async_copy(source, target, in_sem.at[i])
        for i, (source, target) in enumerate(zip(
            (results_hbm, last_hbm) + sources, (results, last) + held
        ))
    ]
    stores = [
        pltpu.make_async_copy(source, target, out_sem.at[i])
        for i, (source, target) in enumerate(zip(
            (tokens_grad, encoded) + held, (tokens_hbm, encoded_hbm) + tuple(out.at[0] for out in outs)
        ))
    ]
    for copy in loads:
        copy.start()
    loads[0].wait()
    loads[1].wait()
    for k, (first, out) in enumerate(((0, tokens_grad), (2, encoded))):
        parts_of = []
        for i in (first, first + 1):
            if first == 0:
                parts_of += [results[i, : results.shape[1] - last.shape[1], :], last[i]]
            else:
                parts_of.append(results[i])
        value = jnp.concatenate(parts_of, 0).astype(F32).T
        out[...] = value[:, : out.shape[1]].astype(out.dtype)
        stores[k].start()
        for i in (2 + 2 * k, 3 + 2 * k):
            loads[i].wait()
            stores[i].start()
    for row, out in enumerate(parts):
        count = out.shape[1]
        width = n_dp * count
        found = jnp.zeros(out.shape, F32)
        for h in range(2):
            for d in range(n_dp):
                at = d * count
                if row == 0:
                    at = h * 3 * HALF + at + (HALF if at >= HALF else 0)
                else:
                    at = h * width + at
                found = jnp.where((half == h) & (dp == d), small[row : row + 1, at : at + count], found)
        out[...] = found
    for copy in stores:
        copy.wait()


def finish(n_dp, local_rows, small, results, last, grads):
    vmem = pl.BlockSpec(memory_space=pltpu.VMEM)
    hbm = pl.BlockSpec(memory_space=pl.ANY)
    widths = [D, HALF, HALF, HALF, HIDDEN_HALF, HALF, HALF, HALF]
    return pl.pallas_call(
        functools.partial(finish_kernel, n_dp),
        out_shape=[
            jax.ShapeDtypeStruct((QUARTER, local_rows), BF),
            jax.ShapeDtypeStruct((QUARTER, local_rows), F32),
        ]
        + [jax.ShapeDtypeStruct((1,) + g.shape, F32) for g in grads]
        + [jax.ShapeDtypeStruct((1, w // n_dp), F32) for w in widths],
        in_specs=[vmem] + [hbm] * 6,
        out_specs=[hbm] * 6 + [vmem] * 8,
        scratch_shapes=[
            pltpu.VMEM(results.shape, BF),
            pltpu.VMEM(last.shape, BF),
            pltpu.VMEM((QUARTER, local_rows), BF),
            pltpu.VMEM((QUARTER, local_rows), F32),
        ]
        + [pltpu.VMEM(g.shape, F32) for g in grads]
        + [pltpu.SemaphoreType.DMA((6,))] * 2,
        compiler_params=pltpu.CompilerParams(vmem_limit_bytes=VMEM_LIMIT),
        name="finish",
    )(small, results, last, *grads)


def weight_gradients_by_scatter(n_dp, a0, dqkv, context, dr1, a1, du, hidden, dr2, sums, last):
    half = lax.axis_index("pipe") % 2
    halves = (
        dot_tn(a0, dqkv).reshape(D, 2, 3 * HALF).transpose(1, 0, 2),
        dot_tn(context, dr1).reshape(2, HALF, D),
        dot_tn(a1, du).reshape(D, 2, HIDDEN_HALF).transpose(1, 0, 2),
        dot_tn(hidden, dr2).reshape(2, HIDDEN_HALF, D),
    )
    swap = [(i, i ^ 1) for i in range(PIPE)]
    found = []
    for member in halves:
        part = lax.psum_scatter(member, "dp", scatter_dimension=1, tiled=True)
        keep = lax.dynamic_index_in_dim(part, half, 0, keepdims=False)
        send = lax.dynamic_index_in_dim(part, 1 - half, 0, keepdims=False)
        found.append(keep + lax.ppermute(send.astype(BF), "pipe", swap).astype(F32))
    small = lax.psum(sums, "dp")
    received = lax.all_to_all(last, "pipe", 0, 0, tiled=False)
    return found + [small + lax.ppermute(small, "pipe", swap), received[:2]]


def shards(
    n_dp,
    tokens, cotangent, captions, projection, biases, combiner, offsets, scaling, centring,
    expansion, lifting, reduction, settling, stretch, translate,
):
    local_rows = tokens.shape[0]
    local_pairs = local_rows // PAIR_ROWS
    pairs = 2 * ((local_pairs + 3) // 4)
    block = 2 * PAIR_ROWS
    micros = pairs // 2
    owned = (projection[0], combiner[0], expansion[0], reduction[0])
    small = (biases, offsets, scaling, centring, lifting, settling, stretch, translate)
    *kept, results, last = layer_passes(micros, block, captions, small, tokens.T, cotangent.T, owned)
    a0, context, a1, hidden, dr2, du, dr1, dqkv, sums = kept
    whole_tiles = HALF % (16 * n_dp) == 0
    collect = weight_gradients if whole_tiles else weight_gradients_by_scatter
    *grads, sums, last = collect(n_dp, a0, dqkv, context, dr1, a1, du, hidden, dr2, sums, last)
    encoded, tokens_grad, g_proj, g_comb, g_exp, g_red, *parts = finish(n_dp, local_rows, sums, results, last, grads)
    return (
        encoded.T, tokens_grad.T, g_proj, parts[0], g_comb, parts[1], parts[2], parts[3],
        g_exp, parts[4], g_red, parts[5], parts[6], parts[7],
    )


def solution(mesh):
    rows = P("dp", "pipe")
    matrix = P("pipe", None, None)
    vector = P("pipe", None)
    matrix_out = P("pipe", "dp", None)
    vector_out = P("pipe", "dp")
    in_specs = (
        rows, rows, P("dp"), matrix, vector, matrix, vector, vector, vector,
        matrix, vector, matrix, vector, vector, vector,
    )
    out_specs = (
        rows, rows, matrix_out, vector_out, matrix_out, vector_out, vector_out, vector_out,
        matrix_out, vector_out, matrix_out, vector_out, vector_out, vector_out,
    )
    return jax.shard_map(
        functools.partial(shards, mesh.shape["dp"]),
        mesh=mesh, in_specs=in_specs, out_specs=out_specs, check_vma=False,
    )
```

```python
import functools

import jax
import jax.numpy as jnp
from jax import lax
from jax.experimental import pallas as pl
from jax.experimental.pallas import tpu as pltpu
from jax.sharding import PartitionSpec as P

D = 768
HEADS = 12
HEAD_DIM = 64
FF = 3072
WORDS = 64
PAIR_ROWS = 104
HALF = D // 2
HIDDEN_HALF = FF // 2
QUARTER = D // 4
PIPE = 4
GROUP_WIDTH = 2 * HEAD_DIM
GROUPS = HEADS // 2
STACKED = 2 * PAIR_ROWS

EPSILON = 1e-05
NEGATIVE = -1e30
SCALE = HEAD_DIM ** (-0.5)

MESH = pl.DeviceIdType.MESH
BF = jnp.bfloat16
F32 = jnp.float32
VMEM_LIMIT = 60 << 20


def dot_nn(left, right):
    return lax.dot_general(left, right, (((1,), (0,)), ((), ())), preferred_element_type=F32)


def dot_nt(left, right):
    return lax.dot_general(left, right, (((1,), (1,)), ((), ())), preferred_element_type=F32)


def dot_tn(left, right):
    return lax.dot_general(left, right, (((0,), (0,)), ((), ())), preferred_element_type=F32)


def place():
    pipe = lax.axis_index("pipe")
    dp = lax.axis_index("dp")
    layer = pipe // 2
    half = pipe % 2
    across_x = pipe + 1 - 2 * half
    across_y = (pipe + 2) % 4
    core = dp % 2
    other_core = dp + 1 - 2 * core
    return pipe, dp, layer, half, across_x, across_y, core, other_core


def greet(devices):
    barrier = pltpu.get_barrier_semaphore()
    for device in devices:
        pl.semaphore_signal(barrier, inc=1, device_id=device, device_id_type=MESH)
    pl.semaphore_wait(barrier, len(devices))


def remote(source, target, send, recv, device):
    return pltpu.make_async_remote_copy(
        src_ref=source,
        dst_ref=target,
        send_sem=send,
        recv_sem=recv,
        device_id=device,
        device_id_type=MESH,
    )


WEIGHT_SHAPES = [(D, 3 * HALF), (HALF, D), (D, HIDDEN_HALF), (HIDDEN_HALF, D)]
CHUNKS = [(0, 0, 96), (0, 96, 96), (1, 0, 96), (2, 0, 96), (2, 96, 96), (3, 0, 96), (3, 96, 96), (3, 192, 96), (3, 288, 48), (3, 336, 48)]
ATTENTION_CHUNKS = 3
FIRST_LANES = 256
DEPTH = 3
LAG = 2
ATTEND_AT = 5
REDUCE_DEPTH = 3
LOW_AT = (4, 10, 14)


def left_lanes():
    return lax.broadcasted_iota(jnp.int32, (PAIR_ROWS, GROUP_WIDTH), 1) < HEAD_DIM


def stacked(values, scale=None):
    if scale is not None:
        values = values * scale
    left = left_lanes()
    return jnp.concatenate([jnp.where(left, values, 0.0), jnp.where(left, 0.0, values)], 0).astype(BF)


def own_lanes(values):
    return jnp.where(left_lanes(), values[:PAIR_ROWS], values[PAIR_ROWS:])


def normalized(residual):
    average = jnp.mean(residual, axis=-1, keepdims=True)
    centred = residual - average
    variance = jnp.mean(centred * centred, axis=-1, keepdims=True)
    inverse = lax.rsqrt(variance + EPSILON)
    return centred * inverse, inverse


def norm_backward(gradient, norm, inverse, gain):
    scaled = gradient * gain
    first = jnp.mean(scaled, axis=-1, keepdims=True)
    second = jnp.mean(scaled * norm, axis=-1, keepdims=True)
    return (scaled - first - norm * second) * inverse


def column_sums(value):
    return jnp.sum(value, axis=0, keepdims=True)


def layer_kernel(
    micros, block, local_pairs,
    captions, tokens_hbm, cotangent_hbm, biases, offsets, scaling, centring, lifting, settling, stretch, translate,
    own_proj, own_comb, own_exp, own_red,
    a0_hbm, context_hbm, a1_hbm, hidden_hbm, dr2_hbm, du_hbm, dr1_hbm, dqkv_hbm, sums_out, results_out, last_out,
    tokens, cotangent, both, own_vectors, joint, mixing, expand, reduce, pieces, unpacked, other_vectors, vectors, results,
    slots, outgoing, qkv_keep, prob_keep, n1_keep, r1_keep, n2_keep, r2_keep, slope_keep,
    a_s, qkv_s, context_s, dqkv_s,
    a0_ring, context_ring, a1_ring, hidden_ring, dr2_ring, du_ring, dr1_ring, dqkv_ring,
    send, recv, x_send, x_recv, z_send, z_recv, near_send, near_recv, far_send, far_recv,
    own_sem, piece_send, piece_recv, vec_sem, result_send, result_recv, result_sem, ring_sem, row_sem,
):
    pipe, dp, layer, half, across_x, across_y, core, other_core = place()
    step = pl.program_id(0)
    pairs = block // PAIR_ROWS
    rows = micros * block
    diagonal = (across_x + 2) % 4
    parity = (dp // 2) % 2
    across_z = dp + 2 - 4 * parity
    mine = 2 * parity + core
    paired = 2 * (1 - parity) + core
    relatives = (across_x, across_y, diagonal)
    owned = [own_proj, own_comb, own_exp, own_red]
    held = [joint, mixing, expand, reduce]
    n = len(CHUNKS)

    def span(chunk, quarter):
        which, start, count = chunk
        return pl.ds(quarter * (WEIGHT_SHAPES[which][0] // 4) + start, count)

    def x_copy(k):
        at = span(CHUNKS[k], mine)
        which = CHUNKS[k][0]
        return remote(owned[which].at[at], held[which].at[half, at], x_send.at[k], x_recv.at[k], (across_x, dp))

    def z_copy(k):
        region = held[CHUNKS[k][0]].at[1 - half, span(CHUNKS[k], mine)]
        return remote(region, region, z_send.at[k], z_recv.at[k], (pipe, across_z))

    def near_copy(k):
        region = held[CHUNKS[k][0]].at[1 - half, span(CHUNKS[k], mine)]
        return remote(region, region, near_send.at[k], near_recv.at[k], (pipe, other_core))

    def far_copy(k):
        region = held[CHUNKS[k][0]].at[1 - half, span(CHUNKS[k], paired)]
        return remote(region, region, far_send.at[k], far_recv.at[k], (pipe, other_core))

    own_copies = [pltpu.make_async_copy(owned[i], held[i].at[half], own_sem.at[i]) for i in range(4)]
    own_piece = pltpu.make_async_copy(both.at[layer, half], pieces.at[pipe], own_sem.at[4])
    lanes_held = both.shape[3]
    lanes_of = (pl.ds(0, FIRST_LANES), pl.ds(FIRST_LANES, lanes_held - FIRST_LANES))
    vec_copy = remote(own_vectors, other_vectors, vec_sem.at[0], vec_sem.at[1], (across_x, dp))
    piece_copies = [
        [
            remote(
                both.at[target // 2, target % 2, :, lanes], pieces.at[pipe, :, lanes],
                piece_send.at[part, j], piece_recv.at[part, j], (target, dp),
            )
            for j, target in enumerate(relatives)
        ]
        for part, lanes in enumerate(lanes_of)
    ]

    def send_pieces(to_layer, part):
        for j, target in enumerate(relatives):
            @pl.when(target // 2 == to_layer)
            def _():
                piece_copies[part][j].start()

    def hand_on(k):
        z_copy(k).wait_recv()
        far_copy(k).start()

    def arrived(first, last):
        for k in range(first, last):
            near_copy(k).wait_recv()
            far_copy(k).wait_recv()

    def gather_most():
        for k in range(n):
            x_copy(k).wait_recv()
            z_copy(k).start()
            near_copy(k).start()
            if k + DEPTH < n:
                x_copy(k).wait_send()
                x_copy(k + DEPTH).start()
            if k + DEPTH == n - 1:
                send_pieces(0, 1)
                send_pieces(1, 0)
                send_pieces(1, 1)
            if k >= LAG:
                hand_on(k - LAG)
            if k == ATTEND_AT:
                arrived(0, ATTENTION_CHUNKS)
                own_copies[0].wait()
                own_copies[1].wait()

                @pl.when(layer == 0)
                def _():
                    attend(0, *[ring.at[0] for ring, _ in rings[:3]])

    def gather_rest():
        for k in range(n - LAG, n):
            hand_on(k)
        arrived(ATTENTION_CHUNKS, n)
        own_copies[2].wait()
        own_copies[3].wait()

    def y_copy(index):
        return remote(outgoing.at[index], slots.at[index], send.at[index], recv.at[index], (across_y, dp))

    def rows_of(index):
        return pl.ds(pl.multiple_of(index * block, 16), block)

    def result_copies(index):
        return [
            remote(
                results.at[target, rows_of(index)], results_out.at[pipe, rows_of(index)],
                result_send.at[j, index], result_recv.at[j, index], (target, dp),
            )
            for j, target in enumerate(relatives)
        ]

    def own_result(index):
        return pltpu.make_async_copy(
            results.at[pipe, rows_of(index)], results_out.at[pipe, rows_of(index)], result_sem.at[index]
        )

    def share_result(index, value):
        for i in range(PIPE):
            results[i, rows_of(index), :] = value[:, i * QUARTER : (i + 1) * QUARTER]
        for copy in result_copies(index):
            copy.start()
        own_result(index).start()

    def wait_results(index):
        final = index == micros - 1
        for j, copy in enumerate(result_copies(index)):
            if not final:
                copy.wait()
                continue

            @pl.when(layer == 1)
            def _():
                copy.wait_send()

            @pl.when(relatives[j] // 2 == 1)
            def _():
                copy.wait_recv()

        @pl.when((layer == 1) | (not final))
        def _():
            own_result(index).wait()

    rings = [
        (a0_ring, a0_hbm), (context_ring, context_hbm), (a1_ring, a1_hbm), (hidden_ring, hidden_hbm),
        (dr2_ring, dr2_hbm), (du_ring, du_hbm), (dr1_ring, dr1_hbm), (dqkv_ring, dqkv_hbm),
    ]

    def ring_copy(which, index):
        ring, target = rings[which]
        return pltpu.make_async_copy(ring.at[index % 2], target.at[rows_of(index)], ring_sem.at[which, index])

    def ring_slots(first, last, index):
        @pl.when(index >= 2)
        def _():
            for which in range(first, last):
                ring_copy(which, index - 2).wait()

        return [rings[which][0].at[index % 2] for which in range(first, last)]

    def ring_start(first, last, index):
        for which in range(first, last):
            ring_copy(which, index).start()

    def unpack_pieces(part):
        for copy in piece_copies[part]:
            copy.wait_recv()
        at = lanes_of[part]
        value = pieces[:, :, at.start : at.start + at.size].reshape(D, at.size)
        unpacked[at.start : at.start + at.size, :] = value.astype(F32).T.astype(BF)

    def attend(micro, a0_out, context_out, a1_out):
        for part in range(2):
            @pl.when((layer == 0) & (micro == part))
            def _():
                unpack_pieces(part)

        @pl.when(layer == 0)
        def _():
            a_s[...] = unpacked[rows_of(micro), :]

        @pl.when(layer == 1)
        def _():
            y_copy(micro).wait_recv()
            a_s[...] = slots[micro]

        inputs = a_s[...]
        a0_out[...] = inputs
        for which in range(2):
            value = dot_nn(inputs, joint[which]) + vectors[0:1, which * 3 * HALF : (which + 1) * 3 * HALF]
            for part in range(3):
                cols = slice(part * D + which * HALF, part * D + (which + 1) * HALF)
                found = value[:, part * HALF : (part + 1) * HALF]
                qkv_s[:, cols] = found
                qkv_keep[micro, :, cols] = found.astype(BF)
        over = [(pair, group) for pair in range(pairs) for group in range(GROUPS)]
        spans = [
            (
                slice(pair * PAIR_ROWS, (pair + 1) * PAIR_ROWS),
                [slice(part * D + group * GROUP_WIDTH, part * D + (group + 1) * GROUP_WIDTH) for part in range(3)],
            )
            for pair, group in over
        ]
        key = lax.broadcasted_iota(jnp.int32, (PAIR_ROWS, PAIR_ROWS), 0)
        masks = []
        for pair in range(pairs):
            length = captions[jnp.minimum((half * micros + micro) * pairs + pair, local_pairs - 1)]
            masks.append(jnp.where((key >= WORDS) | (key < length), 0.0, NEGATIVE))
        scores = [
            dot_nt(stacked(qkv_s[at, lanes[1]], SCALE), qkv_s[at, lanes[0]].astype(BF)) for at, lanes in spans
        ]
        values = [stacked(qkv_s[at, lanes[2]]) for at, lanes in spans]
        probs = []
        for k, (pair, group) in enumerate(over):
            found = []
            for i in range(2):
                score = scores[k][i * PAIR_ROWS : (i + 1) * PAIR_ROWS] + masks[pair]
                exponent = jnp.exp(score - jnp.max(score, axis=0, keepdims=True))
                found.append(exponent * (1.0 / jnp.sum(exponent, axis=0, keepdims=True)))
            probs.append(jnp.concatenate(found, 0).astype(BF))
        contexts = [dot_tn(probs[k], values[k]) for k in range(len(over))]
        for k, (at, lanes) in enumerate(spans):
            prob_keep[micro, k] = probs[k]
            context_s[at, lanes[0]] = contexts[k]
        context = context_s[...].astype(BF)
        context_out[...] = context
        residual = inputs.astype(F32) + dot_nn(context, mixing[...].reshape(D, D)) + vectors[1:2, :D]
        norm, inverse = normalized(residual)
        n1_keep[micro] = norm.astype(BF)
        r1_keep[micro] = inverse
        attended = (norm * vectors[2:3, :D] + vectors[3:4, :D]).astype(BF)
        a1_out[...] = attended

    @pl.when(step == 0)
    def _():
        row_copies = [
            pltpu.make_async_copy(tokens_hbm, tokens, row_sem.at[0]),
            pltpu.make_async_copy(cotangent_hbm, cotangent, row_sem.at[1]),
        ]
        for copy in row_copies:
            copy.start()
        greet([(across_x, dp), (across_y, dp), (diagonal, dp), (pipe, across_z), (pipe, other_core)])
        own_vectors[0:1, :] = biases[...].astype(F32)
        for i, (first, second) in enumerate(((offsets, scaling), (centring, settling), (stretch, translate)), 1):
            own_vectors[i : i + 1, :HALF] = first[...].astype(F32)
            own_vectors[i : i + 1, HALF:] = second[...].astype(F32)
        own_vectors[4:5, :] = lifting[:, :D].astype(F32)
        own_vectors[5:6, :] = lifting[:, D:].astype(F32)
        own_vectors[6:8, :] = jnp.zeros((2, D), F32)
        vec_copy.start()
        for t, source in enumerate((tokens, cotangent)):
            row_copies[t].wait()
            whole = source[...].astype(F32)
            for h in range(2):
                value = whole[:, h * rows : (h + 1) * rows]
                spare = jnp.zeros((QUARTER, lanes_held - value.shape[1]), F32)
                both[t, h] = jnp.concatenate([value, spare], 1).astype(BF)
            if t == 0:
                send_pieces(0, 0)
                for k in range(DEPTH):
                    x_copy(k).start()
        for copy in own_copies:
            copy.start()
        own_piece.start()
        sums_out[...] = jnp.zeros_like(sums_out)
        vec_copy.wait_recv()
        for which in range(2):
            value = jnp.where(half == which, own_vectors[...], other_vectors[...])
            vectors[0:1, which * 3 * HALF : which * 3 * HALF + HALF] = value[0:1, :HALF]
            vectors[0:1, which * 3 * HALF + HALF : which * 3 * HALF + D] = jnp.zeros((1, HALF), F32)
            vectors[0:1, which * 3 * HALF + D : (which + 1) * 3 * HALF] = value[0:1, HALF:D]
            for row, pair in enumerate(((1, 2), (3, 5), (6, 7)), 1):
                for k, i in enumerate(pair):
                    vectors[i : i + 1, which * HALF : (which + 1) * HALF] = value[row : row + 1, k * HALF : (k + 1) * HALF]
            for k in range(2):
                first = which * HIDDEN_HALF + k * D
                vectors[4:5, first : first + D] = value[4 + k : 5 + k, :]
        own_piece.wait()
        gather_most()

        @pl.when(layer == 1)
        def _():
            gather_rest()

    @pl.when(((layer == 0) & (step < micros)) | ((layer == 1) & (step % 2 == 0)))
    def _():
        micro = (1 - layer) * step + layer * (step // 2)
        a0_out, context_out, a1_out, hidden_out = ring_slots(0, 4, micro)

        @pl.when((layer == 1) | (step > 0))
        def _():
            attend(micro, a0_out, context_out, a1_out)

        @pl.when((micro == 0) & (layer == 0))
        def _():
            gather_rest()

        attended = a1_out[...]
        residual = attended.astype(F32) + vectors[5:6, :D]
        for which in range(2):
            cols = slice(which * HIDDEN_HALF, (which + 1) * HIDDEN_HALF)
            raised = dot_nn(attended, expand[which]) + vectors[4:5, cols]
            below = 0.5 * (1.0 + lax.erf(raised * (0.5**0.5)))
            hidden = (raised * below).astype(BF)
            hidden_out[:, cols] = hidden
            density = jnp.exp(raised * raised * (-0.5)) * 0.3989422804014327
            slope_keep[micro, :, cols] = (below + raised * density).astype(BF)
            residual = residual + dot_nn(hidden, reduce[which])
        norm, inverse = normalized(residual)
        n2_keep[micro] = norm.astype(BF)
        r2_keep[micro] = inverse
        result = (norm * vectors[6:7, :D] + vectors[7:8, :D]).astype(BF)

        @pl.when(layer == 0)
        def _():
            outgoing[micro] = result
            y_copy(micro).start()

        @pl.when(layer == 1)
        def _():
            share_result(micro, result)

        ring_start(0, 4, micro)

    def add_sum(row, value):
        width = value.shape[1]
        sums_out[row : row + 1, :width] += column_sums(value)

    @pl.when(((layer == 0) & (step >= micros)) | ((layer == 1) & (step % 2 == 1)))
    def _():
        micro = (1 - layer) * (step - micros) + layer * (step // 2)
        dr2_out, du_out, dr1_out, dqkv_out = ring_slots(4, 8, micro)

        @pl.when((layer == 1) & (micro == 0))
        def _():
            unpack_pieces(0)
            unpack_pieces(1)

        @pl.when(layer == 1)
        def _():
            a_s[...] = unpacked[rows_of(micro), :]

        @pl.when(layer == 0)
        def _():
            y_copy(micro).wait_recv()
            a_s[...] = slots[micro]

        gradient = a_s[...].astype(F32)
        norm = n2_keep[micro].astype(F32)
        add_sum(6, gradient * norm)
        add_sum(7, gradient)
        grad_residual = norm_backward(gradient, norm, r2_keep[micro], vectors[6:7, :D])
        add_sum(5, grad_residual)
        branch = grad_residual.astype(BF)
        dr2_out[...] = branch
        total = grad_residual
        for which in range(2):
            cols = slice(which * HIDDEN_HALF, (which + 1) * HIDDEN_HALF)
            raised = dot_nt(branch, reduce[which]) * slope_keep[micro, :, cols].astype(F32)
            sums_out[4:5, cols] += column_sums(raised)
            raised = raised.astype(BF)
            du_out[:, cols] = raised
            total = total + dot_nt(raised, expand[which])

        gradient = total.astype(BF).astype(F32)
        norm = n1_keep[micro].astype(F32)
        add_sum(2, gradient * norm)
        add_sum(3, gradient)
        grad_residual = norm_backward(gradient, norm, r1_keep[micro], vectors[2:3, :D])
        add_sum(1, grad_residual)
        branch = grad_residual.astype(BF)
        dr1_out[...] = branch
        context_s[...] = dot_nt(branch, mixing[...].reshape(D, D))
        qkv_s[...] = qkv_keep[micro].astype(F32)
        spans = [
            (
                slice(pair * PAIR_ROWS, (pair + 1) * PAIR_ROWS),
                [slice(part * D + group * GROUP_WIDTH, part * D + (group + 1) * GROUP_WIDTH) for part in range(3)],
            )
            for pair in range(pairs)
            for group in range(GROUPS)
        ]
        over = range(len(spans))
        queries = [qkv_s[at, lanes[0]].astype(BF) for at, lanes in spans]
        keys = [stacked(qkv_s[at, lanes[1]], SCALE) for at, lanes in spans]
        values = [stacked(qkv_s[at, lanes[2]]) for at, lanes in spans]
        grads = [context_s[at, lanes[0]].astype(BF) for at, lanes in spans]
        rounded = [prob_keep[micro, g] for g in over]
        grad_probs = [dot_nt(values[g], grads[g]) for g in over]
        grad_values = [dot_nn(rounded[g], grads[g]) for g in over]
        grad_scores = []
        for g in over:
            probs = rounded[g].astype(F32)
            weighted = probs * grad_probs[g]
            found = []
            for i in range(2):
                at = slice(i * PAIR_ROWS, (i + 1) * PAIR_ROWS)
                found.append(weighted[at] - probs[at] * column_sums(weighted[at]))
            grad_scores.append(jnp.concatenate(found, 0).astype(BF))
        grad_keys = [dot_nn(grad_scores[g], queries[g]) for g in over]
        grad_queries = [dot_tn(grad_scores[g], keys[g]) for g in over]
        for g, (at, lanes) in enumerate(spans):
            dqkv_s[at, lanes[0]] = grad_queries[g]
            dqkv_s[at, lanes[1]] = own_lanes(grad_keys[g]) * SCALE
            dqkv_s[at, lanes[2]] = own_lanes(grad_values[g])
        total = grad_residual
        for which in range(2):
            value = jnp.concatenate(
                [dqkv_s[:, part * D + which * HALF : part * D + (which + 1) * HALF] for part in range(3)], 1
            ).astype(BF)
            cols = slice(which * 3 * HALF, (which + 1) * 3 * HALF)
            dqkv_out[:, cols] = value
            sums_out[0:1, cols] += column_sums(value.astype(F32))
            total = total + dot_nt(value, joint[which])
        result = total.astype(BF)

        @pl.when(layer == 1)
        def _():
            outgoing[micro] = result
            y_copy(micro).start()

        ring_start(4, 8, micro)

        @pl.when((layer == 0) & (micro < micros - 1))
        def _():
            share_result(micro, result)

        @pl.when((layer == 0) & (micro == micros - 1))
        def _():
            for i in range(PIPE):
                last_out[i] = result[:, i * QUARTER : (i + 1) * QUARTER]

    @pl.when(step == 2 * micros - 1)
    def _():
        for index in range(micros):
            y_copy(index).wait_send()
            wait_results(index)
        for index in range(max(micros - 2, 0), micros):
            for which in range(8):
                ring_copy(which, index).wait()
        for k in range(n):
            if k + DEPTH >= n:
                x_copy(k).wait_send()
            z_copy(k).wait_send()
            near_copy(k).wait_send()
            far_copy(k).wait_send()
        for copy in piece_copies[0] + piece_copies[1] + [vec_copy]:
            copy.wait_send()


def layer_passes(micros, block, captions, small, tokens, cotangent, owned):
    rows = micros * block
    n = len(CHUNKS)
    lanes_held = (rows + 127) // 128 * 128
    vmem = pl.BlockSpec(memory_space=pltpu.VMEM)
    hbm = pl.BlockSpec(memory_space=pl.ANY)

    forward_widths = [D, D, D, FF]
    backward_widths = [D, FF, D, 3 * D]
    pairs = block // PAIR_ROWS
    return pl.pallas_call(
        functools.partial(layer_kernel, micros, block, captions.shape[0]),
        grid=(2 * micros,),
        out_shape=[jax.ShapeDtypeStruct((rows, w), BF) for w in forward_widths + backward_widths]
        + [
            jax.ShapeDtypeStruct((8, FF), F32),
            jax.ShapeDtypeStruct((PIPE, rows, QUARTER), BF),
            jax.ShapeDtypeStruct((PIPE, block, QUARTER), BF),
        ],
        in_specs=[pl.BlockSpec(memory_space=pltpu.SMEM)] + [hbm] * 2 + [vmem] * 8 + [hbm] * 4,
        out_specs=[hbm] * 8 + [vmem, hbm, vmem],
        scratch_shapes=[
            pltpu.VMEM(tokens.shape, BF),
            pltpu.VMEM(cotangent.shape, BF),
            pltpu.VMEM((2, 2, QUARTER, lanes_held), BF),
            pltpu.VMEM((8, D), F32),
        ]
        + [pltpu.VMEM((2,) + shape, BF) for shape in WEIGHT_SHAPES]
        + [
            pltpu.VMEM((PIPE, QUARTER, lanes_held), BF),
            pltpu.VMEM((lanes_held, D), BF),
            pltpu.VMEM((8, D), F32),
            pltpu.VMEM((8, FF), F32),
            pltpu.VMEM((PIPE, rows, QUARTER), BF),
            pltpu.VMEM((micros, block, D), BF),
            pltpu.VMEM((micros, block, D), BF),
            pltpu.VMEM((micros, block, 3 * D), BF),
            pltpu.VMEM((micros, pairs * GROUPS, STACKED, PAIR_ROWS), BF),
            pltpu.VMEM((micros, block, D), BF),
            pltpu.VMEM((micros, block, 1), F32),
            pltpu.VMEM((micros, block, D), BF),
            pltpu.VMEM((micros, block, 1), F32),
            pltpu.VMEM((micros, block, FF), BF),
            pltpu.VMEM((block, D), BF),
            pltpu.VMEM((block, 3 * D), F32),
            pltpu.VMEM((block, D), F32),
            pltpu.VMEM((block, 3 * D), F32),
        ]
        + [pltpu.VMEM((2, block, w), BF) for w in forward_widths + backward_widths]
        + [pltpu.SemaphoreType.DMA((micros,))] * 2
        + [pltpu.SemaphoreType.DMA((n,))] * 8
        + [
            pltpu.SemaphoreType.DMA((5,)),
            pltpu.SemaphoreType.DMA((2, 3)),
            pltpu.SemaphoreType.DMA((2, 3)),
            pltpu.SemaphoreType.DMA((2,)),
            pltpu.SemaphoreType.DMA((3, micros)),
            pltpu.SemaphoreType.DMA((3, micros)),
            pltpu.SemaphoreType.DMA((micros,)),
            pltpu.SemaphoreType.DMA((8, micros)),
            pltpu.SemaphoreType.DMA((2,)),
        ],
        compiler_params=pltpu.CompilerParams(collective_id=1, has_side_effects=True, vmem_limit_bytes=VMEM_LIMIT),
        name="layer_passes",
    )(captions, tokens, cotangent, *small, *owned)


TILE = 384


def weights_kernel(
    n_dp,
    a0_in, dqkv_in, context_in, dr1_in, a1_in, du_in, hidden_in, dr2_in, sums, last,
    g_proj_hbm, g_comb_hbm, g_exp_hbm, g_red_hbm, sums_out, last_out,
    g_proj, g_comb, g_exp, g_red,
    b_proj, b_comb, b_exp, b_red,
    c_proj, c_comb, c_exp, c_red,
    x_proj, x_comb, x_exp, x_red,
    p_proj, p_comb, p_exp, p_red,
    z_proj, z_comb, z_exp, z_red,
    sums_core, sums_x, sums_z, sums_a, sums_b, sums_c,
    low_from_pair, low_from_far, low_from_x, low_own,
    a0, dqkv, context, dr1, a1, du, hidden, dr2,
    core_send, core_recv, x_send, x_recv, z_send, z_recv,
    small_send, small_recv, load_sem, hidden_sem, last_send, last_recv, low_send, low_recv, out_sem,
):
    pipe, dp, layer, half, across_x, across_y, core, other_core = place()
    n_z = n_dp // 2
    z = dp // 2
    near_z = z + 1 - 2 * (z % 2)
    steps = n_z // 2
    z_order = [(near_z + 2 * (step + 1)) % n_z for step in range(steps - 1)] + [near_z]
    z_order += [(z + 2 * (step + 1)) % n_z for step in range(steps - 1)] + [z]
    same_parity = z_order[steps:-1]
    def hidden_load(which, i):
        h = 1 - half if which == 0 else half
        width = 2 * b_red.shape[3]
        lanes = pl.ds(pl.multiple_of(h * HIDDEN_HALF + z_order[i] * width, 128), width)
        return pltpu.make_async_copy(hidden_in.at[:, lanes], hidden.at[:, lanes], hidden_sem.at[which, i])

    loads = [
        pltpu.make_async_copy(source, target, load_sem.at[i])
        for i, (source, target) in enumerate((
            (dr2_in, dr2), (a1_in, a1), (du_in, du), (a0_in, a0), (dqkv_in, dqkv), (context_in, context), (dr1_in, dr1),
        ))
    ]
    loads[0].start()
    for which in range(2):
        for i in range(n_z):
            hidden_load(which, i).start()
    for copy in loads[1:]:
        copy.start()
    relatives = (across_x, across_y, (across_x + 2) % 4)
    greet(
        [(target, dp) for target in relatives] + [(pipe, other_core)]
        + [(pipe, 2 * other + core) for other in [near_z] + same_parity]
    )

    last_copies = [
        remote(last.at[target], last_out.at[half], last_send.at[j], last_recv.at[j], (target, dp))
        for j, target in enumerate(relatives)
    ]
    last_own = pltpu.make_async_copy(last.at[pipe], last_out.at[half], load_sem.at[7])

    @pl.when(layer == 0)
    def _():
        for copy in last_copies:
            copy.start()
        last_own.start()

    mine = [b_red, b_exp, b_proj, b_comb]
    from_core = [c_red, c_exp, c_proj, c_comb]
    from_x = [x_red, x_exp, x_proj, x_comb]
    from_pair = [p_red, p_exp, p_proj, p_comb]
    from_far = [z_red, z_exp, z_proj, z_comb]
    outs = [g_red, g_exp, g_proj, g_comb]
    out_copies = [
        pltpu.make_async_copy(source, target, out_sem.at[a])
        for a, (source, target) in enumerate(zip(outs, (g_red_hbm, g_exp_hbm, g_proj_hbm, g_comb_hbm)))
    ]

    def spread(target, tile, cast=BF):
        r = target.shape[-2]
        for k in range(tile.shape[0] // (2 * r)):
            for c in range(2):
                yield c, k, tile[(2 * k + c) * r : (2 * k + c + 1) * r].astype(cast)

    def fill_red(h, at):
        width = 2 * b_red.shape[3]
        lanes = pl.ds(pl.multiple_of(h * HIDDEN_HALF + at * width, 128), width)
        for c, k, rows in spread(b_red, dot_tn(hidden[:, lanes], dr2[...])):
            b_red[c, h, at] = rows

    def fill_exp(step, carry):
        i, h = step // 2, step % 2
        tile = dot_tn(
            a1[:, pl.ds(pl.multiple_of(i * TILE, 128), TILE)],
            du[:, pl.ds(pl.multiple_of(h * HIDDEN_HALF, 128), HIDDEN_HALF)],
        )
        for c, k, rows in spread(b_exp, tile):
            b_exp[c, h, i * (TILE // (2 * b_exp.shape[3])) + k] = rows
        return carry

    def fill_proj(h, carry):
        tile = dot_tn(a0[...], dqkv[:, pl.ds(pl.multiple_of(h * 3 * HALF, 128), 3 * HALF)])
        for c, k, rows in spread(b_proj, tile):
            b_proj[c, h, k] = rows
        return carry

    def fill_comb():
        tile = dot_tn(context[...], dr1[...])
        for h in range(2):
            for c, k, rows in spread(b_comb, tile[h * HALF : (h + 1) * HALF]):
                b_comb[c, h, k] = rows

    low = b_red.shape[3] // 48 * 16
    low_rows = pl.ds(0, low)
    rows_of = [pl.ds(low, b_red.shape[3] - low)] + [pl.ds(0, b.shape[3]) for b in mine[1:]]

    def half_of(which):
        return 1 - half if which == 0 else half

    def core_copy(a, which, i):
        h, at = half_of(which), z_order[i]
        return remote(
            mine[a].at[1 - core, h, at, rows_of[a]], from_core[a].at[h, at, rows_of[a]],
            core_send.at[a, which, i], core_recv.at[a, which, i], (pipe, other_core),
        )

    def send_core(a, which):
        for i in range(n_z):
            core_copy(a, which, i).start()

    def x_copy(k):
        a, i = chunks[k]
        at = z_order[i]
        return remote(
            mine[a].at[core, 1 - half, at, rows_of[a]], from_x[a].at[at, rows_of[a]],
            x_send.at[a, i], x_recv.at[a, i], (across_x, dp),
        )

    def pair_copy(a, i):
        return remote(
            mine[a].at[core, half, z_order[i], rows_of[a]], from_pair[a].at[i, rows_of[a]],
            z_send.at[a, i], z_recv.at[a, i], (pipe, 2 * near_z + core),
        )

    def far_copy(a, i):
        other = same_parity[i]
        return remote(
            mine[a].at[core, half, other, rows_of[a]], from_far[a].at[i, rows_of[a]],
            z_send.at[a, steps + i], z_recv.at[a, steps + i], (pipe, 2 * other + core),
        )

    chunks = [(a, i) for a in range(4) for i in range(n_z)]

    def start_x(k):
        if k >= len(chunks):
            return
        a, i = chunks[k]
        at, rows = z_order[i], rows_of[a]
        core_copy(a, 0, i).wait_recv()
        total = mine[a][core, 1 - half, at, rows, :].astype(F32) + from_core[a][1 - half, at, rows, :].astype(F32)
        mine[a][core, 1 - half, at, rows, :] = total.astype(BF)
        x_copy(k).start()

    def after_x(k):
        a, i = chunks[k]
        at, rows = z_order[i], rows_of[a]
        x_copy(k).wait()
        start_x(k + REDUCE_DEPTH)
        core_copy(a, 1, i).wait_recv()
        total = mine[a][core, half, at, rows, :].astype(F32) + from_core[a][half, at, rows, :].astype(F32)
        total = total + from_x[a][at, rows, :].astype(F32)
        if i < steps:
            mine[a][core, half, at, rows, :] = total.astype(BF)
            pair_copy(a, i).start()
            return
        pair_copy(a, i - steps).wait_recv()
        total = total + from_pair[a][i - steps, rows, :].astype(F32)
        if i < n_z - 1:
            mine[a][core, half, at, rows, :] = total.astype(BF)
            far_copy(a, i - steps).start()
        else:
            outs[a][rows, :] = total

    def after_z(a):
        rows = rows_of[a]
        total = outs[a][rows, :]
        for i in range(steps - 1):
            far_copy(a, i).wait()
            total = total + from_far[a][i, rows, :].astype(F32)
        outs[a][rows, :] = total
        for i in range(steps):
            pair_copy(a, i).wait_send()

    def low_core(which, i):
        h, at = half_of(which), z_order[i]
        return remote(
            b_red.at[1 - core, h, at, low_rows], c_red.at[h, at, low_rows],
            low_send.at[which, i], low_recv.at[which, i], (pipe, other_core),
        )

    def low_pair(which, i):
        return remote(
            b_red.at[core, half_of(which), z_order[i], low_rows], low_from_pair.at[which, i],
            low_send.at[2 + which, i], low_recv.at[2 + which, i], (pipe, 2 * near_z + core),
        )

    def low_far(which, i):
        other = same_parity[i]
        return remote(
            b_red.at[core, half_of(which), other, low_rows], low_from_far.at[which, i],
            low_send.at[2 + which, steps + i], low_recv.at[2 + which, steps + i], (pipe, 2 * other + core),
        )

    low_x = remote(
        b_red.at[core, 1 - half, z, low_rows], low_from_x,
        low_send.at[2, n_z - 1], low_recv.at[2, n_z - 1], (across_x, dp),
    )

    def low_sum(which, i):
        h, at = half_of(which), z_order[i]
        low_core(which, i).wait_recv()
        return b_red[core, h, at, low_rows, :].astype(F32) + c_red[h, at, low_rows, :].astype(F32)

    def low_to_pair():
        for which in range(2):
            for i in range(steps):
                b_red[core, half_of(which), z_order[i], low_rows, :] = low_sum(which, i).astype(BF)
                low_pair(which, i).start()

    def low_to_far():
        for which in range(2):
            for i in range(steps, n_z):
                total = low_sum(which, i)
                low_pair(which, i - steps).wait_recv()
                total = total + low_from_pair[which, i - steps].astype(F32)
                if i < n_z - 1:
                    b_red[core, half_of(which), z_order[i], low_rows, :] = total.astype(BF)
                    low_far(which, i - steps).start()
                else:
                    low_own[which] = total

    def low_to_x():
        for which in range(2):
            total = low_own[which]
            for i in range(steps - 1):
                low_far(which, i).wait_recv()
                total = total + low_from_far[which, i].astype(F32)
            if which == 0:
                b_red[core, 1 - half, z, low_rows, :] = total.astype(BF)
                low_x.start()
            else:
                g_red[low_rows, :] = total

    def low_done():
        low_x.wait()
        g_red[low_rows, :] = g_red[low_rows, :] + low_from_x[...].astype(F32)
        for which in range(2):
            for i in range(n_z):
                low_core(which, i).wait_send()
            for i in range(steps):
                low_pair(which, i).wait_send()
            for i in range(steps - 1):
                low_far(which, i).wait_send()

    sums_copy_core = remote(sums, sums_core, small_send.at[0], small_recv.at[0], (pipe, other_core))
    sums_copy_x = remote(sums_a, sums_x, small_send.at[1], small_recv.at[1], (across_x, dp))
    sums_copy_pair = remote(
        sums_b, sums_z.at[steps - 1], small_send.at[2], small_recv.at[2], (pipe, 2 * near_z + core)
    )
    sums_copies_far = [
        remote(sums_c, sums_z.at[i], small_send.at[3 + i], small_recv.at[3 + i], (pipe, 2 * other + core))
        for i, other in enumerate(same_parity)
    ]

    sums_copy_core.start()
    loads[0].wait()
    for i in range(n_z):
        hidden_load(0, i).wait()
        fill_red(1 - half, z_order[i])
        core_copy(0, 0, i).start()
        low_core(0, i).start()
        if 1 <= i <= REDUCE_DEPTH:
            start_x(i - 1)
    for i in range(n_z):
        hidden_load(1, i).wait()
        fill_red(half, z_order[i])
        low_core(1, i).start()
        core_copy(0, 1, i).start()
    low_to_pair()
    loads[1].wait()
    loads[2].wait()
    lax.fori_loop(0, 2 * D // TILE, fill_exp, 0)
    send_core(1, 0)
    send_core(1, 1)
    sums_copy_core.wait()
    sums_a[...] = sums[...] + sums_core[...]
    sums_copy_x.start()
    after_x(0)
    after_x(1)
    loads[3].wait()
    loads[4].wait()
    lax.fori_loop(0, 2, fill_proj, 0)
    send_core(2, 0)
    send_core(2, 1)
    after_x(2)
    loads[5].wait()
    loads[6].wait()
    fill_comb()
    send_core(3, 0)
    send_core(3, 1)
    sums_copy_x.wait()
    sums_b[...] = sums_a[...] + sums_x[...]
    sums_copy_pair.start()
    for k in range(3, len(chunks)):
        after_x(k)
        if k == LOW_AT[0]:
            low_to_far()
        if k == LOW_AT[1]:
            low_to_x()
        if k == LOW_AT[2]:
            low_done()
            out_copies[0].start()
        if k == n_z:
            sums_copy_pair.wait()
            sums_c[...] = sums_b[...] + sums_z[steps - 1]
            for copy in sums_copies_far:
                copy.start()
        if k % n_z == n_z - 2 and k >= n_z:
            after_z(k // n_z - 1)
            if k // n_z > 1:
                out_copies[k // n_z - 1].start()
    after_z(3)
    out_copies[3].start()
    for a in range(4):
        for which in range(2):
            for i in range(n_z):
                core_copy(a, which, i).wait_send()
    total = sums_c[...]
    for i in range(steps - 1):
        sums_copies_far[i].wait()
        total = total + sums_z[i]
    sums_out[...] = total
    for copy in out_copies:
        copy.wait()

    @pl.when(layer == 0)
    def _():
        for copy in last_copies:
            copy.wait_send()
        last_own.wait()

    for j, source in enumerate(relatives):
        @pl.when(source // 2 == 0)
        def _():
            last_copies[j].wait_recv()


def weight_gradients(n_dp, a0, dqkv, context, dr1, a1, du, hidden, dr2, sums, last):
    vmem = pl.BlockSpec(memory_space=pltpu.VMEM)
    hbm = pl.BlockSpec(memory_space=pl.ANY)
    n_z = n_dp // 2
    low = HIDDEN_HALF // n_dp // 48 * 16
    shapes = [(D // n_dp, 3 * HALF), (HALF // n_dp, D), (D // n_dp, HIDDEN_HALF), (HIDDEN_HALF // n_dp, D)]
    return pl.pallas_call(
        functools.partial(weights_kernel, n_dp),
        out_shape=[jax.ShapeDtypeStruct(s, F32) for s in shapes]
        + [jax.ShapeDtypeStruct(sums.shape, F32), jax.ShapeDtypeStruct((2,) + last.shape[1:], BF)],
        in_specs=[hbm] * 8 + [vmem, hbm],
        out_specs=[hbm] * 4 + [vmem, hbm],
        scratch_shapes=[pltpu.VMEM(s, F32) for s in shapes]
        + [pltpu.VMEM((2, 2, n_z) + s, BF) for s in shapes]
        + [pltpu.VMEM((2, n_z) + s, BF) for s in shapes]
        + [pltpu.VMEM((n_z,) + s, BF) for s in shapes]
        + [pltpu.VMEM((n_z // 2,) + s, BF) for s in shapes]
        + [pltpu.VMEM((max(n_z // 2 - 1, 1),) + s, BF) for s in shapes]
        + [
            pltpu.VMEM(sums.shape, F32),
            pltpu.VMEM(sums.shape, F32),
            pltpu.VMEM((n_z // 2,) + sums.shape, F32),
            pltpu.VMEM(sums.shape, F32),
            pltpu.VMEM(sums.shape, F32),
            pltpu.VMEM(sums.shape, F32),
            pltpu.VMEM((2, n_z // 2, low, D), BF),
            pltpu.VMEM((2, max(n_z // 2 - 1, 1), low, D), BF),
            pltpu.VMEM((low, D), BF),
            pltpu.VMEM((2, low, D), F32),
        ]
        + [pltpu.VMEM(v.shape, BF) for v in (a0, dqkv, context, dr1, a1, du, hidden, dr2)]
        + [
            pltpu.SemaphoreType.DMA((4, 2, n_z)),
            pltpu.SemaphoreType.DMA((4, 2, n_z)),
            pltpu.SemaphoreType.DMA((4, n_z)),
            pltpu.SemaphoreType.DMA((4, n_z)),
            pltpu.SemaphoreType.DMA((4, n_z - 1)),
            pltpu.SemaphoreType.DMA((4, n_z - 1)),
            pltpu.SemaphoreType.DMA((n_z + 1,)),
            pltpu.SemaphoreType.DMA((n_z + 1,)),
            pltpu.SemaphoreType.DMA((8,)),
            pltpu.SemaphoreType.DMA((2, n_z)),
            pltpu.SemaphoreType.DMA((3,)),
            pltpu.SemaphoreType.DMA((3,)),
            pltpu.SemaphoreType.DMA((4, n_z)),
            pltpu.SemaphoreType.DMA((4, n_z)),
            pltpu.SemaphoreType.DMA((4,)),
        ],
        compiler_params=pltpu.CompilerParams(collective_id=3, has_side_effects=True, vmem_limit_bytes=VMEM_LIMIT),
        name="weight_gradients",
    )(a0, dqkv, context, dr1, a1, du, hidden, dr2, sums, last)


def finish_kernel(n_dp, small, results_hbm, last_hbm, *refs):
    pipe, dp, layer, half, across_x, across_y, core, other_core = place()
    sources, encoded_hbm, tokens_hbm, outs, parts = refs[:4], refs[4], refs[5], refs[6:10], refs[10:18]
    results, last, encoded, tokens_grad = refs[18:22]
    held, in_sem, out_sem = refs[22:26], refs[26], refs[27]
    loads = [
        pltpu.make_async_copy(source, target, in_sem.at[i])
        for i, (source, target) in enumerate(zip(
            (results_hbm, last_hbm) + sources, (results, last) + held
        ))
    ]
    stores = [
        pltpu.make_async_copy(source, target, out_sem.at[i])
        for i, (source, target) in enumerate(zip(
            (tokens_grad, encoded) + held, (tokens_hbm, encoded_hbm) + tuple(out.at[0] for out in outs)
        ))
    ]
    for copy in loads:
        copy.start()
    for i in range(2, 6):
        loads[i].wait()
        stores[i].start()
    loads[0].wait()
    loads[1].wait()
    for k, (first, out) in enumerate(((0, tokens_grad), (2, encoded))):
        parts_of = []
        for i in (first, first + 1):
            if first == 0:
                parts_of += [results[i, : results.shape[1] - last.shape[1], :], last[i]]
            else:
                parts_of.append(results[i])
        value = jnp.concatenate(parts_of, 0).astype(F32).T
        out[...] = value[:, : out.shape[1]].astype(out.dtype)
        stores[k].start()
    for row, out in enumerate(parts):
        count = out.shape[1]
        width = n_dp * count
        found = jnp.zeros(out.shape, F32)
        for h in range(2):
            for d in range(n_dp):
                at = d * count
                if row == 0:
                    at = h * 3 * HALF + at + (HALF if at >= HALF else 0)
                else:
                    at = h * width + at
                found = jnp.where((half == h) & (dp == d), small[row : row + 1, at : at + count], found)
        out[...] = found
    for copy in stores:
        copy.wait()


def finish(n_dp, local_rows, small, results, last, grads):
    vmem = pl.BlockSpec(memory_space=pltpu.VMEM)
    hbm = pl.BlockSpec(memory_space=pl.ANY)
    widths = [D, HALF, HALF, HALF, HIDDEN_HALF, HALF, HALF, HALF]
    return pl.pallas_call(
        functools.partial(finish_kernel, n_dp),
        out_shape=[
            jax.ShapeDtypeStruct((QUARTER, local_rows), BF),
            jax.ShapeDtypeStruct((QUARTER, local_rows), F32),
        ]
        + [jax.ShapeDtypeStruct((1,) + g.shape, F32) for g in grads]
        + [jax.ShapeDtypeStruct((1, w // n_dp), F32) for w in widths],
        in_specs=[vmem] + [hbm] * 6,
        out_specs=[hbm] * 6 + [vmem] * 8,
        scratch_shapes=[
            pltpu.VMEM(results.shape, BF),
            pltpu.VMEM(last.shape, BF),
            pltpu.VMEM((QUARTER, local_rows), BF),
            pltpu.VMEM((QUARTER, local_rows), F32),
        ]
        + [pltpu.VMEM(g.shape, F32) for g in grads]
        + [pltpu.SemaphoreType.DMA((6,))] * 2,
        compiler_params=pltpu.CompilerParams(vmem_limit_bytes=VMEM_LIMIT),
        name="finish",
    )(small, results, last, *grads)


def weight_gradients_by_scatter(n_dp, a0, dqkv, context, dr1, a1, du, hidden, dr2, sums, last):
    half = lax.axis_index("pipe") % 2
    halves = (
        dot_tn(a0, dqkv).reshape(D, 2, 3 * HALF).transpose(1, 0, 2),
        dot_tn(context, dr1).reshape(2, HALF, D),
        dot_tn(a1, du).reshape(D, 2, HIDDEN_HALF).transpose(1, 0, 2),
        dot_tn(hidden, dr2).reshape(2, HIDDEN_HALF, D),
    )
    swap = [(i, i ^ 1) for i in range(PIPE)]
    found = []
    for member in halves:
        part = lax.psum_scatter(member, "dp", scatter_dimension=1, tiled=True)
        keep = lax.dynamic_index_in_dim(part, half, 0, keepdims=False)
        send = lax.dynamic_index_in_dim(part, 1 - half, 0, keepdims=False)
        found.append(keep + lax.ppermute(send.astype(BF), "pipe", swap).astype(F32))
    small = lax.psum(sums, "dp")
    received = lax.all_to_all(last, "pipe", 0, 0, tiled=False)
    return found + [small + lax.ppermute(small, "pipe", swap), received[:2]]


def shards(
    n_dp,
    tokens, cotangent, captions, projection, biases, combiner, offsets, scaling, centring,
    expansion, lifting, reduction, settling, stretch, translate,
):
    local_rows = tokens.shape[0]
    local_pairs = local_rows // PAIR_ROWS
    pairs = 2 * ((local_pairs + 3) // 4)
    block = 2 * PAIR_ROWS
    micros = pairs // 2
    owned = (projection[0], combiner[0], expansion[0], reduction[0])
    small = (biases, offsets, scaling, centring, lifting, settling, stretch, translate)
    *kept, results, last = layer_passes(micros, block, captions, small, tokens.T, cotangent.T, owned)
    a0, context, a1, hidden, dr2, du, dr1, dqkv, sums = kept
    whole_tiles = HALF % (16 * n_dp) == 0
    collect = weight_gradients if whole_tiles else weight_gradients_by_scatter
    *grads, sums, last = collect(n_dp, a0, dqkv, context, dr1, a1, du, hidden, dr2, sums, last)
    encoded, tokens_grad, g_proj, g_comb, g_exp, g_red, *parts = finish(n_dp, local_rows, sums, results, last, grads)
    return (
        encoded.T, tokens_grad.T, g_proj, parts[0], g_comb, parts[1], parts[2], parts[3],
        g_exp, parts[4], g_red, parts[5], parts[6], parts[7],
    )


def solution(mesh):
    rows = P("dp", "pipe")
    matrix = P("pipe", None, None)
    vector = P("pipe", None)
    matrix_out = P("pipe", "dp", None)
    vector_out = P("pipe", "dp")
    in_specs = (
        rows, rows, P("dp"), matrix, vector, matrix, vector, vector, vector,
        matrix, vector, matrix, vector, vector, vector,
    )
    out_specs = (
        rows, rows, matrix_out, vector_out, matrix_out, vector_out, vector_out, vector_out,
        matrix_out, vector_out, matrix_out, vector_out, vector_out, vector_out,
    )
    return jax.shard_map(
        functools.partial(shards, mesh.shape["dp"]),
        mesh=mesh, in_specs=in_specs, out_specs=out_specs, check_vma=False,
    )
```
